32 devices in a mesh: dp: 4 (over y, x), row: 2 (over core), col: 4 (over z).
Axes of the slice: x: 2, y: 2, z: 4, core: 2. Of those that a mesh axis runs over, the one named last changes fastest.
Arguments:
- tokens: bfloat16 [4096, 2048], P(('dp', 'row'), 'col'), may hold values from -6 to 6
- attention_norm_gain: float32 [2048], P('col'), may hold values from 0.5 to 1.5
- attention_norm_bias: float32 [2048], P('col'), may hold values from -3 to 3
- qkv_weight: bfloat16 [2048, 3, 2048], P('col', None, 'row'), may hold values from -0.125 to 0.125
- qkv_bias: float32 [3, 2048], P(None, ('row', 'col')), may hold values from -4 to 4
- out_weight: bfloat16 [2048, 2048], P('row', 'col'), may hold values from -1 to 1
- feedforward_norm_gain: float32 [2048], P('col'), may hold values from 0.5 to 1.5
- feedforward_norm_bias: float32 [2048], P('col'), may hold values from -3 to 3
- gate_up_weight: bfloat16 [2048, 2, 5632], P('col', None, 'row'), may hold values from -0.125 to 0.125
- down_weight: bfloat16 [5632, 2048], P('row', 'col'), may hold values from -0.078125 to 0.078125
- cotangent: bfloat16 [4096, 2048], P(('dp', 'row'), 'col'), may hold values from -6 to 6
Outputs:
- mixed: bfloat16 [4096, 2048], P(('dp', 'row'), 'col')
- input_token_gradient: float32 [4096, 2048], P(('dp', 'row'), 'col')
- grad_first_gain: float32 [2048], P('col')
- grad_first_shift: float32 [2048], P('col')
- grad_qkv_weight: float32 [2048, 3, 2048], P('col', None, 'row')
- grad_qkv_bias: float32 [3, 2048], P(None, ('row', 'col'))
- grad_out_weight: float32 [2048, 2048], P('row', 'col')
- grad_second_gain: float32 [2048], P('col')
- grad_second_shift: float32 [2048], P('col')
- grad_gate_up: float32 [2048, 2, 5632], P('col', None, 'row')
- grad_down: float32 [5632, 2048], P('row', 'col')
The draws below stay inside these ranges and needn't reach their ends.
All inputs are finite; a program needn't handle non-finite values.
Results may differ from the reference program's by a relative error of at most 0.012.
Values may be sent and summed in bfloat16 or wider, within the bound.
A program may use at most 192 MiB of HBM per device.

```python
import jax
import jax.numpy as jnp
from jax import lax

MODEL_WIDTH = 2048
H = 32
HD = 64
FF = 5632
ROT = 16
SEQ = 1024
TOKENS = 4096


def steps_of(own_key, extent, pieces, smallest, top_value):
    def one(dim, parts):
        steps = jax.random.uniform(jax.random.fold_in(jax.random.fold_in(own_key, 6), dim), (parts,), jnp.float32, smallest / len(pieces), top_value / len(pieces))
        return jnp.repeat(jnp.exp(steps), extent[dim] // parts).reshape((-1,) + (1,) * (len(extent) - dim - 1))

    loudness = one(*pieces[0])
    for cut in pieces[1:]:
        loudness = loudness * one(*cut)
    return loudness


def normal_values(own_key, shape, scale, bound, split=(), kind=jnp.bfloat16):
    gain = steps_of(own_key, shape, split, -0.22, 0.18) if split else 1.0
    entries = jax.random.normal(own_key, shape, jnp.float32) * scale * gain
    return jnp.minimum(jnp.maximum(entries, -bound), bound).astype(kind)


def setup_inputs(seed: int = 0) -> dict:
    arg_keys = jax.random.split(jax.random.key(seed), 12)
    return {
        "tokens": normal_values(arg_keys[0], (TOKENS, MODEL_WIDTH), 1.0, 6.0, ((0, 8), (1, 4))),
        "attention_norm_gain": jnp.clip(1.0 + 0.1 * jax.random.normal(arg_keys[1], (MODEL_WIDTH,), jnp.float32), 0.5, 1.5),
        "attention_norm_bias": normal_values(arg_keys[2], (MODEL_WIDTH,), 0.3, 3.0, ((0, 4),), jnp.float32),
        "qkv_weight": normal_values(arg_keys[3], (MODEL_WIDTH, 3, MODEL_WIDTH), MODEL_WIDTH ** -0.5, 0.125, ((0, 4), (2, 2))),
        "qkv_bias": normal_values(arg_keys[4], (3, MODEL_WIDTH), 0.5, 4.0, ((1, 8),), jnp.float32),
        "out_weight": normal_values(arg_keys[5], (MODEL_WIDTH, MODEL_WIDTH), (MODEL_WIDTH // 64) ** -0.5, 1.0, ((0, 2), (1, 4))),
        "feedforward_norm_gain": jnp.clip(1.0 + 0.1 * jax.random.normal(arg_keys[6], (MODEL_WIDTH,), jnp.float32), 0.5, 1.5),
        "feedforward_norm_bias": normal_values(arg_keys[7], (MODEL_WIDTH,), 0.3, 3.0, ((0, 4),), jnp.float32),
        "gate_up_weight": normal_values(arg_keys[8], (MODEL_WIDTH, 2, FF), MODEL_WIDTH ** -0.5, 0.125, ((0, 4), (2, 2))),
        "down_weight": normal_values(arg_keys[9], (FF, MODEL_WIDTH), FF ** -0.5, 0.078125, ((0, 2), (1, 4))),
        "cotangent": normal_values(arg_keys[10], (TOKENS, MODEL_WIDTH), 1.0, 6.0, ((0, 8), (1, 4))),
    }


EPSILON = 1e-05
ROPE_BASE = 10000.0
NEG_LARGE = -1e+30
PRECISE = lax.Precision.HIGHEST

@jax.custom_vjp
def low(v):
    return lax.optimization_barrier(v.astype(jnp.bfloat16)).astype(jnp.float32)

@jax.custom_vjp
def low_back(v):
    return v

def low_keep(v):
    return (low(v), None)

def low_pass(kept, grad):
    return (grad,)

def back_keep(v):
    return (v, None)

def back_low(kept, grad):
    return (low(grad),)
low.defvjp(low_keep, low_pass)
low_back.defvjp(back_keep, back_low)

def layer_norm(inputs, norm_gain_vector, shift):
    row_mean = lax.optimization_barrier(jnp.mean(inputs, axis=-1, keepdims=True))
    centered = inputs - row_mean
    spread = lax.optimization_barrier(jnp.mean(centered * centered, axis=-1, keepdims=True))
    return centered * lax.rsqrt(spread + EPSILON) * norm_gain_vector + shift

def rotate(inputs, positions):
    half_rot = ROT // 2
    inverse = ROPE_BASE ** (-2.0 * jnp.arange(half_rot).astype(jnp.float32) / ROT)
    angles = positions[:, None] * inverse[None, :]
    cosine = jnp.cos(angles)[:, None, :]
    sine_part = jnp.sin(angles)[:, None, :]
    lower_half = inputs[..., :half_rot]
    upper_half = inputs[..., half_rot:ROT]
    return jnp.concatenate([lower_half * cosine - upper_half * sine_part, upper_half * cosine + lower_half * sine_part, inputs[..., ROT:]], axis=-1)

def attend(queries, key_rows, value_rows):
    length = queries.shape[0]
    block_rows = min(512, length)
    blocks = length // block_rows
    scale = HD ** (-0.5)
    query_blocks = queries.reshape(blocks, block_rows, H, HD)
    offsets = jnp.arange(blocks) * block_rows

    def one_block(packed):
        query_block, offset = packed
        scores = jnp.einsum('qhd,khd->hqk', query_block, key_rows, precision=PRECISE) * scale
        scores = low_back(scores)
        allowed = (offset + jnp.arange(block_rows))[:, None] >= jnp.arange(length)[None, :]
        scores = jnp.where(allowed[None], scores, NEG_LARGE)
        attn_probs = low(jax.nn.softmax(scores, axis=-1))
        return jnp.einsum('hqk,khd->qhd', attn_probs, value_rows, precision=PRECISE)
    result = lax.map(jax.checkpoint(one_block), (query_blocks, offsets))
    return result.reshape(length, H, HD)

def forward(residual_stream, attention_norm_gain, attention_norm_bias, qkv_weight, qkv_bias, out_weight, feedforward_norm_gain, feedforward_norm_bias, gate_up_weight, down_weight):
    length = residual_stream.shape[0]
    positions = jnp.arange(length).astype(jnp.float32)
    attention_normalized = low(layer_norm(residual_stream, attention_norm_gain, attention_norm_bias))
    qkv = jnp.einsum('td,dkf->tkf', attention_normalized, qkv_weight, precision=PRECISE) + qkv_bias[None]
    qkv = low_back(qkv)
    queries = low(rotate(qkv[:, 0].reshape(length, H, HD), positions))
    key_rows = low(rotate(qkv[:, 1].reshape(length, H, HD), positions))
    value_rows = low(qkv[:, 2].reshape(length, H, HD))
    attn = attend(queries, key_rows, value_rows).reshape(length, MODEL_WIDTH)
    attn = low(low_back(attn))
    branch = low_back(jnp.dot(attn, out_weight, precision=PRECISE))
    middle_state = residual_stream + branch
    feedforward_normalized = low(layer_norm(middle_state, feedforward_norm_gain, feedforward_norm_bias))
    gate_up = low_back(jnp.einsum('td,dkf->tkf', feedforward_normalized, gate_up_weight, precision=PRECISE))
    hidden = low(jax.nn.silu(gate_up[:, 0]) * gate_up[:, 1])
    return middle_state + jnp.dot(hidden, down_weight, precision=PRECISE)

def reference(tokens, attention_norm_gain, attention_norm_bias, qkv_weight, qkv_bias, out_weight, feedforward_norm_gain, feedforward_norm_bias, gate_up_weight, down_weight, cotangent):
    floats = tuple((weight_arg.astype(jnp.float32) for weight_arg in (attention_norm_gain, attention_norm_bias, qkv_weight, qkv_bias, out_weight, feedforward_norm_gain, feedforward_norm_bias, gate_up_weight, down_weight)))
    seq_tokens = tokens.astype(jnp.float32).reshape(-1, SEQ, MODEL_WIDTH)
    seq_cotan = cotangent.astype(jnp.float32).reshape(-1, SEQ, MODEL_WIDTH)

    def advance(totals, packed):
        inputs, cotan = packed
        result, pullback = jax.vjp(forward, inputs, *floats)
        gradients = pullback(cotan)
        totals = tuple((running + addend for running, addend in zip(totals, gradients[1:])))
        return (totals, (result, gradients[0]))
    initial = tuple((jnp.zeros_like(weight_arg) for weight_arg in floats))
    totals, (results, grad_seqs) = lax.scan(advance, initial, (seq_tokens, seq_cotan))
    return (results.reshape(-1, MODEL_WIDTH).astype(jnp.bfloat16), grad_seqs.reshape(-1, MODEL_WIDTH), totals[0], totals[1], totals[2], totals[3], totals[4], totals[5], totals[6], totals[7], totals[8])
```

```python
import jax
import jax.numpy as jnp
from jax import lax
from jax.sharding import PartitionSpec as P

MODEL_WIDTH = 2048
HD = 64
ROT = 16
SEQ = 1024
EPSILON = 1e-05
ROPE_BASE = 10000.0
NEG_LARGE = -1e30
F32 = jnp.float32
BF16 = jnp.bfloat16


def rope_tables(length):
    half_rot = ROT // 2
    inverse = ROPE_BASE ** (-2.0 * jnp.arange(half_rot).astype(F32) / ROT)
    angles = jnp.arange(length).astype(F32)[:, None] * inverse[None, :]
    return jnp.cos(angles)[:, None, :], jnp.sin(angles)[:, None, :]


def rotate(inputs, cosine, sine):
    half_rot = ROT // 2
    lower_half = inputs[..., :half_rot]
    upper_half = inputs[..., half_rot:ROT]
    return jnp.concatenate(
        [
            lower_half * cosine - upper_half * sine,
            upper_half * cosine + lower_half * sine,
            inputs[..., ROT:],
        ],
        axis=-1,
    )


def dot(spec, a, b):
    return jnp.einsum(spec, a, b, preferred_element_type=F32)


def fetch_columns(block, sizes):
    dp, col = sizes["dp"], sizes["col"]
    depth, k, wide = block.shape
    part = depth // dp
    piece = lax.dynamic_slice_in_dim(block, lax.axis_index("dp") * part, part, 0)
    piece = piece.reshape(part, k, col, wide // col).transpose(2, 0, 1, 3)
    piece = lax.all_to_all(piece, "col", 0, 0, tiled=True)
    whole = lax.all_gather(piece, "dp", axis=0)
    return whole.transpose(1, 0, 2, 3, 4).reshape(col * depth, k, wide // col)


def return_columns(grad, sizes):
    dp, col = sizes["dp"], sizes["col"]
    width, k, narrow = grad.shape
    part = width // col // dp
    pieces = grad.astype(BF16).reshape(col, dp, part, k * narrow).transpose(1, 0, 2, 3)
    piece = lax.psum_scatter(pieces, "dp", scatter_dimension=0, tiled=True)[0]
    piece = lax.all_to_all(piece, "col", 0, 0, tiled=True)
    piece = piece.reshape(col, part, k, narrow).transpose(1, 2, 0, 3).reshape(part, k, col * narrow)
    return lax.all_gather(piece, "dp", axis=0, tiled=True).astype(F32)


def fetch_rows(block, sizes):
    dp, col = sizes["dp"], sizes["col"]
    tall, depth = block.shape
    part = tall // col // dp
    piece = lax.dynamic_index_in_dim(
        block.reshape(col, dp, part, depth), lax.axis_index("dp"), 1, False
    )
    piece = lax.all_to_all(piece, "col", 0, 0, tiled=True)
    piece = piece.transpose(1, 0, 2).reshape(part, col * depth)
    return lax.all_gather(piece, "dp", axis=0, tiled=True)


def return_rows(grad, sizes):
    dp, col = sizes["dp"], sizes["col"]
    short, width = grad.shape
    part, depth = short // dp, width // col
    piece = lax.psum_scatter(grad.astype(BF16), "dp", scatter_dimension=0, tiled=True)
    piece = piece.reshape(part, col, depth).transpose(1, 0, 2)
    piece = lax.all_to_all(piece, "col", 0, 0, tiled=True)
    whole = lax.all_gather(piece, "dp", axis=0)
    return whole.transpose(1, 0, 2, 3).reshape(col * short, depth).astype(F32)


def sum_tokens(partial, sizes):
    half = lax.psum_scatter(partial.astype(BF16), "row", scatter_dimension=0, tiled=True)
    return lax.psum_scatter(half, "col", scatter_dimension=0, tiled=True)


def sum_features(partial, sizes):
    half = lax.psum_scatter(partial.astype(BF16), "row", scatter_dimension=0, tiled=True)
    return lax.psum_scatter(half, "col", scatter_dimension=1, tiled=True)


def gather_tokens(own):
    return lax.all_gather(lax.all_gather(own, "col", axis=0, tiled=True), "row", axis=0, tiled=True)


def stats(rows):
    mean = jnp.mean(rows, axis=1, keepdims=True)
    centered = rows - mean
    return mean, lax.rsqrt(jnp.mean(centered * centered, axis=1, keepdims=True) + EPSILON)


def block_scores(query_block, key_rows, offset):
    block_rows = query_block.shape[0]
    scores = dot("qhd,khd->hqk", query_block, key_rows) * HD ** (-0.5)
    allowed = (offset + jnp.arange(block_rows))[:, None] >= jnp.arange(key_rows.shape[0])[None, :]
    return jnp.where(allowed[None], scores, NEG_LARGE)


def attention_forward(queries, key_rows, value_rows):
    def one_seq(packed):
        seq_queries, seq_keys, seq_values = packed
        length = seq_queries.shape[0]
        block_rows = min(512, length)
        blocks = length // block_rows
        query_blocks = seq_queries.reshape((blocks, block_rows) + seq_queries.shape[1:])
        offsets = jnp.arange(blocks) * block_rows

        def one_block(element):
            query_block, offset = element
            scores = block_scores(query_block, seq_keys, offset)
            row_max = jnp.max(scores, axis=2, keepdims=True)
            expo = jnp.exp(scores - row_max)
            denominator = jnp.sum(expo, axis=2, keepdims=True)
            attn_probs = (expo / denominator).astype(BF16)
            result = dot("hqk,khd->qhd", attn_probs, seq_values)
            return (result, (row_max + jnp.log(denominator))[:, :, 0])

        results, log_sums = lax.map(one_block, (query_blocks, offsets))
        return (results.reshape(seq_queries.shape), log_sums)

    return lax.map(one_seq, (queries, key_rows, value_rows))


def attention_backward(queries, key_rows, value_rows, log_sums, grad_attn):
    def one_seq(packed):
        seq_queries, seq_keys, seq_values, seq_sums, seq_grad = packed
        length = seq_queries.shape[0]
        block_rows = min(512, length)
        blocks = length // block_rows
        block_shape = (blocks, block_rows) + seq_queries.shape[1:]
        offsets = jnp.arange(blocks) * block_rows

        def advance(running, element):
            query_block, offset, sum_block, grad_block = element
            scores = block_scores(query_block, seq_keys, offset)
            attn_probs = jnp.exp(scores - sum_block[:, :, None])
            grad_probs = dot("qhd,khd->hqk", grad_block, seq_values)
            delta = jnp.sum(grad_probs * attn_probs, axis=2, keepdims=True)
            grad_scores = (attn_probs * (grad_probs - delta)).astype(BF16)
            grad_query = dot("hqk,khd->qhd", grad_scores, seq_keys) * HD ** (-0.5)
            grad_key = dot("hqk,qhd->khd", grad_scores, query_block) * HD ** (-0.5)
            grad_value = dot("hqk,qhd->khd", attn_probs.astype(BF16), grad_block)
            return ((running[0] + grad_key, running[1] + grad_value), grad_query)

        empty_grad = jnp.zeros(seq_keys.shape, F32)
        (grad_keys, grad_values), grad_queries = lax.scan(
            advance,
            (empty_grad, empty_grad),
            (seq_queries.reshape(block_shape), offsets, seq_sums, seq_grad.reshape(block_shape)),
        )
        return (grad_queries.reshape(seq_queries.shape), grad_keys, grad_values)

    return lax.map(one_seq, (queries, key_rows, value_rows, log_sums, grad_attn))


def make_body(sizes):
    col = sizes["col"]

    def body(
        tokens,
        attention_norm_gain,
        attention_norm_bias,
        qkv_weight,
        qkv_bias,
        out_weight,
        feedforward_norm_gain,
        feedforward_norm_bias,
        gate_up_weight,
        down_weight,
        cotangent,
    ):
        my_col = lax.axis_index("col")
        depth = tokens.shape[1]
        qkv_w = fetch_columns(qkv_weight, sizes)
        out_w = fetch_rows(out_weight, sizes)
        gate_up_w = fetch_columns(gate_up_weight, sizes)
        down_w = fetch_rows(down_weight, sizes)
        vectors = lax.all_gather(
            jnp.stack(
                [
                    attention_norm_gain,
                    attention_norm_bias,
                    feedforward_norm_gain,
                    feedforward_norm_bias,
                ]
            ),
            "col",
            axis=1,
            tiled=True,
        )
        rows_half = lax.all_gather(tokens, "col", axis=1, tiled=True)
        cotan_half = lax.all_gather(cotangent, "col", axis=1, tiled=True)
        cotan_rows = lax.all_gather(cotan_half, "row", axis=0, tiled=True)
        half_f = rows_half.astype(F32)
        mean_one, rstd_one = stats(half_f)
        normed_half = ((half_f - mean_one) * rstd_one * vectors[0] + vectors[1]).astype(BF16)
        normed_one = lax.all_gather(normed_half, "row", axis=0, tiled=True)
        group_rows = normed_one.shape[0]
        heads = qkv_bias.shape[1] // HD
        seqs = group_rows // SEQ
        head_shape = (group_rows, heads, HD)
        seq_shape = (seqs, SEQ, heads, HD)
        cosine, sine = rope_tables(SEQ)
        cosine, sine = jnp.tile(cosine, (seqs, 1, 1)), jnp.tile(sine, (seqs, 1, 1))
        qkv = dot("td,dkf->tkf", normed_one, qkv_w) + qkv_bias[None]
        queries = rotate(qkv[:, 0].reshape(head_shape), cosine, sine).astype(BF16).reshape(seq_shape)
        keys = rotate(qkv[:, 1].reshape(head_shape), cosine, sine).astype(BF16).reshape(seq_shape)
        values = qkv[:, 2].astype(BF16).reshape(seq_shape)
        attn_out, log_sums = attention_forward(queries, keys, values)
        attn = attn_out.reshape(group_rows, heads * HD).astype(BF16)
        own = group_rows // sizes["row"] // col
        branch = sum_tokens(dot("tf,fd->td", attn, out_w), sizes).astype(F32)

        def own_rows(half):
            return lax.dynamic_slice_in_dim(half, my_col * own, own, 0).astype(F32)

        middle = own_rows(rows_half) + branch
        mean_two, rstd_two = stats(middle)
        xhat_two = (middle - mean_two) * rstd_two
        normed_two = gather_tokens((xhat_two * vectors[2] + vectors[3]).astype(BF16))
        gate_up = dot("td,dkf->tkf", normed_two, gate_up_w)
        gate, up = gate_up[:, 0], gate_up[:, 1]
        sig = jax.nn.sigmoid(gate)
        hidden = (gate * sig * up).astype(BF16)
        mixed_part = dot("tf,fd->td", hidden, down_w)
        start = lax.axis_index("row") * (own * col) + my_col * own
        mine = lax.dynamic_slice_in_dim(mixed_part, start, own, 0)
        mixed_part = lax.dynamic_update_slice_in_dim(mixed_part, mine + middle, start, 0)
        mixed = sum_features(mixed_part, sizes)
        grad_down = return_rows(dot("tf,td->fd", hidden, cotan_rows), sizes)
        grad_hidden = dot("td,fd->tf", cotan_rows, down_w)
        grad_gu = jnp.stack(
            [grad_hidden * up * sig * (1.0 + gate * (1.0 - sig)), grad_hidden * gate * sig], axis=1
        ).astype(BF16)
        grad_gate_up = return_columns(dot("td,tkf->dkf", normed_two, grad_gu), sizes)
        grad_normed_two = sum_tokens(dot("tkf,dkf->td", grad_gu, gate_up_w), sizes).astype(F32)
        second = jnp.stack(
            [jnp.sum(grad_normed_two * xhat_two, axis=0), jnp.sum(grad_normed_two, axis=0)]
        )
        scaled = grad_normed_two * vectors[2]
        grad_middle = own_rows(cotan_half) + rstd_two * (
            scaled
            - jnp.mean(scaled, axis=1, keepdims=True)
            - xhat_two * jnp.mean(scaled * xhat_two, axis=1, keepdims=True)
        )
        grad_middle_rows = gather_tokens(grad_middle.astype(BF16))
        grad_out = return_rows(dot("tf,td->fd", attn, grad_middle_rows), sizes)
        grad_attn = dot("td,fd->tf", grad_middle_rows, out_w).astype(BF16).reshape(seq_shape)
        grad_queries, grad_keys, grad_values = attention_backward(
            queries, keys, values, log_sums, grad_attn
        )
        grad_qkv = jnp.stack(
            [
                rotate(grad_queries.reshape(head_shape), cosine, -sine),
                rotate(grad_keys.reshape(head_shape), cosine, -sine),
                grad_values.reshape(head_shape),
            ],
            axis=1,
        )
        grad_qkv = grad_qkv.reshape(group_rows, 3, heads * HD).astype(BF16)
        bias_part = jnp.sum(grad_qkv, axis=0, dtype=F32)
        grad_qkv_weight = return_columns(dot("td,tkf->dkf", normed_one, grad_qkv), sizes)
        normed_part = dot("tkf,dkf->td", grad_qkv, qkv_w)
        grad_normed_one = sum_features(normed_part, sizes).astype(F32)
        xhat_one = (tokens.astype(F32) - mean_one) * rstd_one
        scaled_one = grad_normed_one * attention_norm_gain
        sums = lax.psum(
            jnp.stack([jnp.sum(scaled_one, axis=1), jnp.sum(scaled_one * xhat_one, axis=1)]), "col"
        )
        own_grad = sum_features_residual(grad_middle_rows, depth, my_col)
        input_grad = own_grad + rstd_one * (
            scaled_one - sums[0][:, None] / MODEL_WIDTH - xhat_one * sums[1][:, None] / MODEL_WIDTH
        )
        first = jnp.stack(
            [jnp.sum(grad_normed_one * xhat_one, axis=0), jnp.sum(grad_normed_one, axis=0)]
        )
        second = lax.psum_scatter(second, "col", scatter_dimension=1, tiled=True)
        norms = lax.psum(jnp.concatenate([first, second]), ("dp", "row"))
        bias = lax.psum(bias_part, "dp")
        return (
            mixed,
            input_grad,
            norms[0],
            norms[1],
            grad_qkv_weight,
            bias,
            grad_out,
            norms[2],
            norms[3],
            grad_gate_up,
            grad_down,
        )

    return body


def sum_features_residual(grad_middle_rows, depth, my_col):
    half = grad_middle_rows.shape[0] // 2
    rows = lax.dynamic_slice_in_dim(grad_middle_rows, lax.axis_index("row") * half, half, 0)
    return lax.dynamic_slice_in_dim(rows, my_col * depth, depth, 1).astype(F32)


def solution(mesh):
    specs = (
        P(("dp", "row"), "col"),
        P("col"),
        P("col"),
        P("col", None, "row"),
        P(None, ("row", "col")),
        P("row", "col"),
        P("col"),
        P("col"),
        P("col", None, "row"),
        P("row", "col"),
    )
    return jax.shard_map(
        make_body(dict(mesh.shape)),
        mesh=mesh,
        in_specs=specs + (P(("dp", "row"), "col"),),
        out_specs=(P(("dp", "row"), "col"),) + specs,
        check_vma=False,
    )
```

```python
import functools

import jax
import jax.numpy as jnp
from jax import lax
from jax.experimental import pallas as pl
from jax.experimental.pallas import tpu as pltpu
from jax.sharding import PartitionSpec as P

MODEL_WIDTH = 2048
HD = 64
ROT = 16
SEQ = 1024
EPSILON = 1e-05
ROPE_BASE = 10000.0
NEG_LARGE = -1e30
F32 = jnp.float32
BF16 = jnp.bfloat16
MESH = pl.DeviceIdType.MESH
VMEM_LIMIT = 56 * 1024 * 1024
SUBS = 4


def send(src, dst, send_sem, recv_sem, **where):
    return pltpu.make_async_remote_copy(
        src_ref=src,
        dst_ref=dst,
        send_sem=send_sem,
        recv_sem=recv_sem,
        device_id=where,
        device_id_type=MESH,
    )


def enter(cols, everyone=False):
    r, c = lax.axis_index("row"), lax.axis_index("col")
    barrier = pltpu.get_barrier_semaphore()
    pl.semaphore_signal(barrier, inc=1, device_id={"row": 1 - r}, device_id_type=MESH)
    if everyone:
        for k in range(1, cols):
            pl.semaphore_signal(
                barrier, inc=1, device_id={"col": lax.rem(c + k, cols)}, device_id_type=MESH
            )
        pl.semaphore_wait(barrier, cols)
        return

    @pl.when(c > 0)
    def _():
        pl.semaphore_signal(barrier, inc=1, device_id={"col": c - 1}, device_id_type=MESH)

    @pl.when(c < cols - 1)
    def _():
        pl.semaphore_signal(barrier, inc=1, device_id={"col": c + 1}, device_id_type=MESH)

    inner = (c > 0) & (c < cols - 1)

    @pl.when(inner)
    def _():
        pl.semaphore_wait(barrier, 3)

    @pl.when(jnp.logical_not(inner))
    def _():
        pl.semaphore_wait(barrier, 2)


class Reduce:
    def __init__(self, cols, subs, spot, part, twin, going, coming, sems, add=None):
        self.cols, self.subs, self.spot, self.add = cols, subs, spot, add
        self.part, self.twin, self.going, self.coming = part, twin, going, coming
        self.twin_send, self.twin_recv, self.send, self.recv = sems
        self.r, self.c = lax.axis_index("row"), lax.axis_index("col")
        self.half = part.shape[0] // 2

    def in_half(self, r, d, s):
        row, rows, column, columns = self.spot(d, s)
        return pl.ds(pl.multiple_of(r * self.half + row, 16), rows), pl.ds(column, columns)

    def in_twin(self, d, s):
        row, rows, column, columns = self.spot(d, s)
        return pl.ds(row, rows), pl.ds(column, columns)

    def twin_copy(self, d, s):
        return send(
            self.part.at[self.in_half(1 - self.r, d, s)],
            self.twin.at[self.in_twin(d, s)],
            self.twin_send.at[d, s],
            self.twin_recv.at[d, s],
            row=1 - self.r,
        )

    def start(self):
        order = []
        for j in range(self.cols):
            d = self.cols - 1 - j // 2 if j % 2 == 0 else j // 2
            order.append(d)
        for s in range(self.subs):
            for d in order:
                self.twin_copy(d, s).start()

    def hop(self, way, d, s):
        spot = self.in_twin(d, s)
        target = self.c + 1 if way == 0 else self.c - 1
        return send(
            self.going.at[(way,) + spot],
            self.coming.at[(way,) + spot],
            self.send.at[way, d, s],
            self.recv.at[way, d, s],
            col=target,
        )

    def own(self, d, s):
        self.twin_copy(d, s).wait_recv()
        value = self.part[self.in_half(self.r, d, s)].astype(F32)
        value = value + self.twin[self.in_twin(d, s)].astype(F32)
        if self.add is not None:
            value = value + self.add(d, s)
        return value

    def pass_on(self, way, d, s):
        spot = (way,) + self.in_twin(d, s)
        first = 0 if way == 0 else self.cols - 1

        @pl.when(self.c < d if way == 0 else self.c > d)
        def _():
            value = self.own(d, s)

            @pl.when(self.c == first)
            def _():
                self.going[spot] = value.astype(BF16)

            @pl.when(self.c != first)
            def _():
                self.hop(way, d, s).wait_recv()
                self.going[spot] = (value + self.coming[spot].astype(F32)).astype(BF16)

            self.hop(way, d, s).start()

    def relay(self, s):
        for j in range(self.cols - 1):
            self.pass_on(0, self.cols - 1 - j, s)
            self.pass_on(1, j, s)

    def land(self, s, total):
        for d in range(self.cols):

            @pl.when(self.c == d)
            def _():
                value = self.own(d, s)
                spot = self.in_twin(d, s)
                if d > 0:
                    self.hop(0, d, s).wait_recv()
                    value = value + self.coming[(0,) + spot].astype(F32)
                if d < self.cols - 1:
                    self.hop(1, d, s).wait_recv()
                    value = value + self.coming[(1,) + spot].astype(F32)
                total[...] = value

    def finish(self):
        for s in range(self.subs):
            for d in range(self.cols):
                self.twin_copy(d, s).wait_send()

                @pl.when(self.c < d)
                def _():
                    self.hop(0, d, s).wait_send()

                @pl.when(self.c > d)
                def _():
                    self.hop(1, d, s).wait_send()

    @staticmethod
    def scratch(cols, subs, half, width):
        return [
            pltpu.VMEM((half, width), BF16),
            pltpu.VMEM((2, half, width), BF16),
            pltpu.VMEM((2, half, width), BF16),
            pltpu.SemaphoreType.DMA((cols, subs)),
            pltpu.SemaphoreType.DMA((cols, subs)),
            pltpu.SemaphoreType.DMA((2, cols, subs)),
            pltpu.SemaphoreType.DMA((2, cols, subs)),
        ]


class Gather:
    def __init__(self, cols, subs, spot, whole, sems, pair=True):
        self.cols, self.subs, self.spot, self.whole, self.pair = cols, subs, spot, whole, pair
        self.send, self.recv, self.pair_send, self.pair_recv = sems
        self.r, self.c = lax.axis_index("row"), lax.axis_index("col")

    def hop(self, way, source, s):
        where = self.whole.at[self.spot(self.r, source, s)]
        return send(
            where,
            where,
            self.send.at[way, source, s],
            self.recv.at[way, source, s],
            col=self.c + 1 if way == 0 else self.c - 1,
        )

    def across(self, r, source, s):
        where = self.whole.at[self.spot(r, source, s)]
        return send(
            where, where, self.pair_send.at[source, s], self.pair_recv.at[source, s], row=1 - self.r
        )

    def start(self, s):
        @pl.when(self.c < self.cols - 1)
        def _():
            self.hop(0, self.c, s).start()

        @pl.when(self.c > 0)
        def _():
            self.hop(1, self.c, s).start()

        if self.pair:
            self.across(self.r, self.c, s).start()

    def relay(self, s):
        for k in range(1, self.cols):

            @pl.when(self.c >= k)
            def _():
                self.hop(0, self.c - k, s).wait_recv()

                @pl.when(self.c < self.cols - 1)
                def _():
                    self.hop(0, self.c - k, s).start()

                if self.pair:
                    self.across(self.r, self.c - k, s).start()

            @pl.when(self.c + k < self.cols)
            def _():
                self.hop(1, self.c + k, s).wait_recv()

                @pl.when(self.c > 0)
                def _():
                    self.hop(1, self.c + k, s).start()

                if self.pair:
                    self.across(self.r, self.c + k, s).start()

    def finish(self):
        for s in range(self.subs):
            for source in range(self.cols):
                if self.pair:
                    self.across(1 - self.r, source, s).wait_recv()
                    self.across(self.r, source, s).wait_send()

                @pl.when((self.c >= source) & (self.c < self.cols - 1))
                def _():
                    self.hop(0, source, s).wait_send()

                @pl.when((self.c <= source) & (self.c > 0))
                def _():
                    self.hop(1, source, s).wait_send()

    @staticmethod
    def scratch(cols, subs):
        return [
            pltpu.SemaphoreType.DMA((2, cols, subs)),
            pltpu.SemaphoreType.DMA((2, cols, subs)),
            pltpu.SemaphoreType.DMA((cols, subs)),
            pltpu.SemaphoreType.DMA((cols, subs)),
        ]


def moments(rows):
    mean = jnp.mean(rows, axis=1, keepdims=True)
    centered = rows - mean
    return centered, lax.rsqrt(jnp.mean(centered * centered, axis=1, keepdims=True) + EPSILON)


def params(number):
    return pltpu.CompilerParams(
        collective_id=number, has_side_effects=True, vmem_limit_bytes=VMEM_LIMIT
    )


VM = pl.BlockSpec(memory_space=pltpu.VMEM)


def row_spot(own, step, half, width):
    def spot(r, source, s):
        return pl.ds(pl.multiple_of(r * half + source * own + s * step, 16), step), pl.ds(0, width)

    return spot


def norm_two_kernel(cols, part, tokens_own, vectors, normed, middle, *scratch):
    half, width = part.shape[0] // 2, part.shape[1]
    own = half // cols
    step = own // SUBS
    total = scratch[11]
    enter(cols)
    summing = Reduce(
        cols, SUBS, lambda d, s: (d * own + s * step, step, 0, width), part, *scratch[:3], scratch[3:7]
    )
    spread = Gather(cols, SUBS, row_spot(own, step, half, width), normed, scratch[7:11])
    summing.start()
    for s in range(SUBS):
        summing.relay(s)
        if s > 0:
            spread.relay(s - 1)
        summing.land(s, total)
        rows = pl.ds(s * step, step)
        state = tokens_own[rows, :].astype(F32) + total[...]
        middle[rows, :] = state
        centered, rstd = moments(state)
        result = centered * rstd * vectors[2:3, :] + vectors[3:4, :]
        normed[spread.spot(spread.r, spread.c, s)] = result.astype(BF16)
        spread.start(s)
    spread.relay(SUBS - 1)
    spread.finish()
    summing.finish()


def norm_two(cols, part, tokens_own, vectors):
    group, width = part.shape
    return pl.pallas_call(
        functools.partial(norm_two_kernel, cols),
        out_shape=(
            jax.ShapeDtypeStruct((group, width), BF16),
            jax.ShapeDtypeStruct(tokens_own.shape, F32),
        ),
        in_specs=[VM] * 3,
        out_specs=(VM, VM),
        scratch_shapes=Reduce.scratch(cols, SUBS, group // 2, width)
        + Gather.scratch(cols, SUBS)
        + [pltpu.VMEM((group // 2 // cols // SUBS, width), F32)],
        compiler_params=params(2),
        name="out_sum_norm_gather",
    )(part, tokens_own, vectors)


def norm_two_back_kernel(cols, part, middle, cotan_own, vectors, grads, sums, *scratch):
    half, width = part.shape[0] // 2, part.shape[1]
    own = half // cols
    step = own // SUBS
    total = scratch[11]
    enter(cols)
    summing = Reduce(
        cols, SUBS, lambda d, s: (d * own + s * step, step, 0, width), part, *scratch[:3], scratch[3:7]
    )
    spread = Gather(cols, SUBS, row_spot(own, step, half, width), grads, scratch[7:11])
    summing.start()
    sums[...] = jnp.zeros_like(sums)
    for s in range(SUBS):
        summing.relay(s)
        if s > 0:
            spread.relay(s - 1)
        summing.land(s, total)
        rows = pl.ds(s * step, step)
        centered, rstd = moments(middle[rows, :])
        xhat = centered * rstd
        grad = total[...]
        sums[0:1, :] += jnp.sum(grad * xhat, axis=0, keepdims=True)
        sums[1:2, :] += jnp.sum(grad, axis=0, keepdims=True)
        scaled = grad * vectors[2:3, :]
        inner = (
            scaled
            - jnp.mean(scaled, axis=1, keepdims=True)
            - xhat * jnp.mean(scaled * xhat, axis=1, keepdims=True)
        )
        result = cotan_own[rows, :].astype(F32) + rstd * inner
        grads[spread.spot(spread.r, spread.c, s)] = result.astype(BF16)
        spread.start(s)
    spread.relay(SUBS - 1)
    spread.finish()
    summing.finish()


def norm_two_back(cols, part, middle, cotan_own, vectors):
    group, width = part.shape
    return pl.pallas_call(
        functools.partial(norm_two_back_kernel, cols),
        out_shape=(
            jax.ShapeDtypeStruct((group, width), BF16),
            jax.ShapeDtypeStruct((8, width), F32),
        ),
        in_specs=[VM] * 4,
        out_specs=(VM, VM),
        scratch_shapes=Reduce.scratch(cols, SUBS, group // 2, width)
        + Gather.scratch(cols, SUBS)
        + [pltpu.VMEM((group // 2 // cols // SUBS, width), F32)],
        compiler_params=params(3),
        name="grad_sum_norm_gather",
    )(part, middle, cotan_own, vectors)


def mixed_kernel(cols, part, middle, mixed, *scratch):
    half, width = part.shape[0] // 2, part.shape[1]
    step, depth = half // cols, width // cols
    total = scratch[7]
    enter(cols)
    c = lax.axis_index("col")

    def add(d, s):
        return jnp.where(c == s, middle[:, d * depth : (d + 1) * depth], 0.0)

    summing = Reduce(
        cols,
        cols,
        lambda d, s: (s * step, step, d * depth, depth),
        part,
        *scratch[:3],
        scratch[3:7],
        add=add,
    )
    summing.start()
    for s in range(cols):
        summing.relay(s)
        summing.land(s, total)
        mixed[s * step : (s + 1) * step, :] = total[...].astype(BF16)
    summing.finish()


def sum_mixed(cols, part, middle):
    group, width = part.shape
    return pl.pallas_call(
        functools.partial(mixed_kernel, cols),
        out_shape=jax.ShapeDtypeStruct((group // 2, width // cols), BF16),
        in_specs=[VM] * 2,
        out_specs=VM,
        scratch_shapes=Reduce.scratch(cols, cols, group // 2, width)
        + [pltpu.VMEM((group // 2 // cols, width // cols), F32)],
        compiler_params=params(4),
        name="mixed_sum",
    )(part, middle)


def first_kernel(cols, part, xhat, rstd, gain, grad_middle, result, sums, *scratch):
    half, width = part.shape[0] // 2, part.shape[1]
    step, depth = half // cols, width // cols
    total, grad, mine, theirs, out_sem, in_sem = scratch[7:]
    enter(cols, everyone=True)
    c = lax.axis_index("col")
    summing = Reduce(
        cols,
        cols,
        lambda d, s: (s * step, step, d * depth, depth),
        part,
        *scratch[:3],
        scratch[3:7],
    )
    summing.start()
    sums[...] = jnp.zeros_like(sums)
    lanes = lax.broadcasted_iota(jnp.int32, (step, 128), 1)
    for s in range(cols):
        rows = slice(s * step, (s + 1) * step)
        summing.relay(s)
        summing.land(s, total)
        grad[rows, :] = total[...]
        standard = xhat[rows, :]
        sums[0:1, :] += jnp.sum(total[...] * standard, axis=0, keepdims=True)
        sums[1:2, :] += jnp.sum(total[...], axis=0, keepdims=True)
        scaled = total[...] * gain[0:1, :]
        one = jnp.sum(scaled, axis=1, keepdims=True)
        two = jnp.sum(scaled * standard, axis=1, keepdims=True)
        both = jnp.where(lanes == 0, one, jnp.where(lanes == 1, two, 0.0))
        mine[:, rows] = both.T[0:8, :]

    def exchange(k):
        return send(
            mine, theirs.at[k - 1], out_sem.at[k - 1], in_sem.at[k - 1], col=lax.rem(c + k, cols)
        )

    for k in range(1, cols):
        exchange(k).start()
    for k in range(1, cols):
        exchange(k).wait_recv()
    for s in range(cols):
        rows = slice(s * step, (s + 1) * step)
        both = mine[:, rows]
        for k in range(1, cols):
            both = both + theirs[k - 1, :, rows]
        both = jnp.concatenate([both, jnp.zeros((120, step), F32)], axis=0).T / (depth * cols)
        scaled = grad[rows, :] * gain[0:1, :]
        inner = scaled - both[:, 0:1] - xhat[rows, :] * both[:, 1:2]
        result[rows, :] = grad_middle[rows, :].astype(F32) + rstd[rows, 0:1] * inner
    for k in range(1, cols):
        exchange(k).wait_send()
    summing.finish()


def sum_first(cols, part, xhat, rstd, gain, grad_middle):
    group, width = part.shape
    half, depth = group // 2, width // cols
    return pl.pallas_call(
        functools.partial(first_kernel, cols),
        out_shape=(
            jax.ShapeDtypeStruct((half, depth), F32),
            jax.ShapeDtypeStruct((8, depth), F32),
        ),
        in_specs=[VM] * 5,
        out_specs=(VM, VM),
        scratch_shapes=Reduce.scratch(cols, cols, half, width)
        + [
            pltpu.VMEM((half // cols, depth), F32),
            pltpu.VMEM((half, depth), F32),
            pltpu.VMEM((8, half), F32),
            pltpu.VMEM((cols - 1, 8, half), F32),
            pltpu.SemaphoreType.DMA((cols - 1,)),
            pltpu.SemaphoreType.DMA((cols - 1,)),
        ],
        compiler_params=params(5),
        name="input_grad_sum",
    )(part, xhat, rstd, gain, grad_middle)


def norm_one_kernel(cols, tokens, vector, normed, tokens_own, xhat, rstd, vectors, *scratch):
    half, depth = tokens.shape
    width = depth * cols
    step = half // cols
    full = scratch[0]
    enter(cols)
    r, c = lax.axis_index("row"), lax.axis_index("col")

    def columns(source):
        return pl.ds(pl.multiple_of(source * depth, 128), depth)

    names = Gather(
        cols, 1, lambda r, source, s: (pl.ds(0, 8), columns(source)), vectors, scratch[1:5], pair=False
    )
    spread = Gather(
        cols,
        cols,
        lambda r, source, s: (pl.ds(s * step, step), columns(source)),
        full,
        scratch[5:9],
        pair=False,
    )
    pair_send, pair_recv = scratch[9:11]
    vectors[:, columns(c)] = vector[...]
    names.start(0)
    for s in range(cols):
        rows = pl.ds(s * step, step)
        full[rows, columns(c)] = tokens[rows, :]
        spread.start(s)

    def across(r, s):
        where = normed.at[pl.ds(pl.multiple_of(r * half + s * step, 16), step), :]
        return send(
            where,
            where,
            pair_send.at[s],
            pair_recv.at[s],
            row=1 - lax.axis_index("row"),
        )

    names.relay(0)
    for s in range(cols):
        spread.relay(s)
        rows = slice(s * step, (s + 1) * step)
        state = full[rows, :].astype(F32)
        centered, inverse = moments(state)
        standard = centered * inverse
        out = standard * vectors[0:1, :] + vectors[1:2, :]
        normed[pl.ds(pl.multiple_of(r * half + s * step, 16), step), :] = out.astype(BF16)
        across(r, s).start()
        rstd[rows, :] = jnp.broadcast_to(inverse, (step, 128))
        mean = jnp.mean(state, axis=1, keepdims=True)
        xhat[rows, :] = (tokens[rows, :].astype(F32) - mean) * inverse

        @pl.when(c == s)
        def _():
            tokens_own[...] = full[rows, :]

    for s in range(cols):
        across(1 - r, s).wait_recv()
        across(r, s).wait_send()
    names.finish()
    spread.finish()


def norm_one(cols, tokens, vector):
    half, depth = tokens.shape
    width = depth * cols
    return pl.pallas_call(
        functools.partial(norm_one_kernel, cols),
        out_shape=(
            jax.ShapeDtypeStruct((2 * half, width), BF16),
            jax.ShapeDtypeStruct((half // cols, width), BF16),
            jax.ShapeDtypeStruct((half, depth), F32),
            jax.ShapeDtypeStruct((half, 128), F32),
            jax.ShapeDtypeStruct((8, width), F32),
        ),
        in_specs=[VM] * 2,
        out_specs=(VM,) * 5,
        scratch_shapes=[pltpu.VMEM((half, width), BF16)]
        + Gather.scratch(cols, 1)
        + Gather.scratch(cols, cols)
        + [pltpu.SemaphoreType.DMA((cols,)), pltpu.SemaphoreType.DMA((cols,))],
        compiler_params=params(1),
        name="gather_norm_one",
    )(tokens, vector)


def rope_tables(length):
    half_rot = ROT // 2
    lane = jnp.arange(2 * HD) % HD
    inverse = ROPE_BASE ** (-2.0 * (lane % half_rot).astype(F32) / ROT)
    angles = jnp.arange(length).astype(F32)[:, None] * inverse[None, :]
    turning = lane < ROT
    cosine = jnp.where(turning, jnp.cos(angles), 1.0)
    sine = jnp.where(turning, jnp.sin(angles), 0.0)
    lower = jnp.where(lane < half_rot, -sine, 0.0)
    upper = jnp.where(lane >= half_rot, sine, 0.0)
    return jnp.stack([cosine, lower, upper])


def turn(x, tables, back=False):
    half_rot = ROT // 2
    width = x.shape[1]
    sines = pltpu.roll(x, width - half_rot, 1) * tables[1] + pltpu.roll(x, half_rot, 1) * tables[2]
    return x * tables[0] - sines if back else x * tables[0] + sines


def dot_nt(a, b):
    return lax.dot_general(a, b, (((1,), (1,)), ((), ())), preferred_element_type=F32)


def dot_tn(a, b):
    return lax.dot_general(a, b, (((0,), (0,)), ((), ())), preferred_element_type=F32)


def dot_nn(a, b):
    return jnp.dot(a, b, preferred_element_type=F32)


BLOCK = 256


def causal(rows):
    return lax.broadcasted_iota(jnp.int32, (rows, rows), 0) >= lax.broadcasted_iota(
        jnp.int32, (rows, rows), 1
    )


def attend_kernel(qkv, bias, tables, heads_in, attn, logs):
    length, wide = attn.shape
    two = 2 * HD
    first_head = lax.broadcasted_iota(jnp.int32, (BLOCK, two), 1) < HD

    @pl.loop(0, wide // two)
    def _(pair):
        def lanes(k):
            return pl.ds(pl.multiple_of(k * wide + pair * two, two), two)

        for k in range(3):
            x = qkv[:, lanes(k)] + bias[0:1, lanes(k)]
            if k < 2:
                x = turn(x, tables)
            if k == 0:
                x = x * HD ** (-0.5)
            heads_in[:, lanes(k)] = x.astype(BF16)
        for i in range(length // BLOCK):
            keep = (i + 1) * BLOCK
            rows = slice(i * BLOCK, keep)
            query = heads_in[rows, lanes(0)]
            keys = heads_in[0:keep, lanes(1)]
            values = heads_in[0:keep, lanes(2)]
            outs = []
            for h in range(2):
                mine = first_head if h == 0 else ~first_head
                scores = dot_nt(jnp.where(mine, query, jnp.zeros_like(query)), keys)
                last = jnp.where(causal(BLOCK), scores[:, i * BLOCK :], NEG_LARGE)
                scores = last if i == 0 else jnp.concatenate([scores[:, : i * BLOCK], last], axis=1)
                top = jnp.max(scores, axis=1, keepdims=True)
                expo = jnp.exp(scores - top)
                total = jnp.sum(expo, axis=1, keepdims=True)
                probs = (expo * (1.0 / total)).astype(BF16)
                outs.append(dot_nn(probs, values))
                logs[pair, h, rows, :] = jnp.broadcast_to(top + jnp.log(total), (BLOCK, 128))
            attn[rows, pl.ds(pl.multiple_of(pair * two, two), two)] = jnp.where(
                first_head, outs[0], outs[1]
            ).astype(BF16)


def attend(qkv, bias, tables):
    length, wide = qkv.shape[0], qkv.shape[1] // 3
    return pl.pallas_call(
        attend_kernel,
        out_shape=(
            jax.ShapeDtypeStruct(qkv.shape, BF16),
            jax.ShapeDtypeStruct((length, wide), BF16),
            jax.ShapeDtypeStruct((wide // (2 * HD), 2, length, 128), F32),
        ),
        in_specs=[VM] * 3,
        out_specs=(VM,) * 3,
        compiler_params=pltpu.CompilerParams(vmem_limit_bytes=VMEM_LIMIT),
        cost_estimate=pl.CostEstimate(flops=8 * 10**9, bytes_accessed=10**7, transcendentals=4 * 10**6),
        name="attention",
    )(qkv, bias, tables)


def attend_back_kernel(heads_in, logs, grad, tables, result, sums, queries_grad, keys_grad, values_grad):
    length, wide = grad.shape
    two = 2 * HD
    first_head = lax.broadcasted_iota(jnp.int32, (BLOCK, two), 1) < HD

    @pl.loop(0, wide // two)
    def _(pair):
        def lanes(k):
            return pl.ds(pl.multiple_of(k * wide + pair * two, two), two)

        keys_grad[...] = jnp.zeros_like(keys_grad)
        values_grad[...] = jnp.zeros_like(values_grad)
        for i in range(length // BLOCK):
            keep = (i + 1) * BLOCK
            rows = slice(i * BLOCK, keep)
            query = heads_in[rows, lanes(0)]
            keys = heads_in[0:keep, lanes(1)]
            values = heads_in[0:keep, lanes(2)]
            out_grad = grad[rows, lanes(0)]
            outs = []
            for h in range(2):
                mine = first_head if h == 0 else ~first_head
                query_h = jnp.where(mine, query, jnp.zeros_like(query))
                grad_h = jnp.where(mine, out_grad, jnp.zeros_like(out_grad))
                scores = dot_nt(query_h, keys)
                probs = jnp.exp(scores - logs[pair, h, rows, 0:1])
                last = jnp.where(causal(BLOCK), probs[:, i * BLOCK :], 0.0)
                probs = last if i == 0 else jnp.concatenate([probs[:, : i * BLOCK], last], axis=1)
                probs_grad = dot_nt(grad_h, values)
                delta = jnp.sum(probs * probs_grad, axis=1, keepdims=True)
                scores_grad = (probs * (probs_grad - delta)).astype(BF16)
                outs.append(dot_nn(scores_grad, keys))
                keys_grad[0:keep, :] += dot_tn(scores_grad, query_h)
                values_grad[0:keep, :] += dot_tn(probs.astype(BF16), grad_h)
            queries_grad[rows, :] = jnp.where(first_head, outs[0], outs[1]) * HD ** (-0.5)
        grads = (
            turn(queries_grad[...], tables, back=True),
            turn(keys_grad[...], tables, back=True),
            values_grad[...],
        )
        for k in range(3):
            low = grads[k].astype(BF16)
            result[:, lanes(k)] = low
            total = jnp.sum(low.astype(F32), axis=0, keepdims=True)
            sums[:, lanes(k)] = jnp.broadcast_to(total, (8, two))


def attend_back(heads_in, logs, grad, tables):
    length, wide = grad.shape
    return pl.pallas_call(
        attend_back_kernel,
        out_shape=(
            jax.ShapeDtypeStruct(heads_in.shape, BF16),
            jax.ShapeDtypeStruct((8, 3 * wide), F32),
        ),
        in_specs=[VM] * 4,
        out_specs=(VM,) * 2,
        scratch_shapes=[pltpu.VMEM((length, 2 * HD), F32)] * 3,
        compiler_params=pltpu.CompilerParams(vmem_limit_bytes=VMEM_LIMIT),
        cost_estimate=pl.CostEstimate(flops=20 * 10**9, bytes_accessed=10**7, transcendentals=4 * 10**6),
        name="attention_back",
    )(heads_in, logs, grad, tables)


def dot(spec, a, b):
    return jnp.einsum(spec, a, b, preferred_element_type=F32)


def columns_piece(block, sizes):
    dp, col = sizes["dp"], sizes["col"]
    depth, k, wide = block.shape
    part = depth // dp
    piece = lax.dynamic_slice_in_dim(block, lax.axis_index("dp") * part, part, 0)
    piece = piece.reshape(part, k, col, wide // col).transpose(2, 0, 1, 3)
    return piece.reshape(col, part, k * wide // col)


def columns_whole(piece, sizes):
    whole = lax.all_gather(piece, "dp", axis=0)
    return whole.transpose(1, 0, 2, 3).reshape(-1, piece.shape[-1])


def rows_piece(block, sizes):
    dp, col = sizes["dp"], sizes["col"]
    tall, depth = block.shape
    return lax.dynamic_index_in_dim(
        block.reshape(col, dp, tall // col // dp, depth), lax.axis_index("dp"), 1, False
    )


def rows_whole(piece, sizes):
    col, part, depth = piece.shape
    return lax.all_gather(
        piece.transpose(1, 0, 2).reshape(part, col * depth), "dp", axis=0, tiled=True
    )


def exchange(pieces):
    return lax.all_to_all(pieces, "col", 0, 0, tiled=True)


def exchange_later(pieces, cols):
    me = lax.axis_index("col")
    out = jnp.zeros_like(pieces)
    out = lax.dynamic_update_index_in_dim(
        out, lax.dynamic_index_in_dim(pieces, me, 0, True), me, 0
    )
    for k in range(1, cols):
        going = lax.dynamic_index_in_dim(pieces, lax.rem(me + k, cols), 0, True)
        coming = lax.ppermute(going, "col", [(i, (i + k) % cols) for i in range(cols)])
        out = lax.dynamic_update_index_in_dim(out, coming, lax.rem(me + cols - k, cols), 0)
    return out


def columns_sum(grad, sizes):
    dp, col = sizes["dp"], sizes["col"]
    width, narrow = grad.shape
    part = width // col // dp
    pieces = grad.astype(BF16).reshape(col, dp, part, narrow).transpose(1, 0, 2, 3)
    piece = lax.psum_scatter(
        pieces.reshape(width, narrow), "dp", scatter_dimension=0, tiled=True
    )
    return piece.reshape(col, part, narrow)


def columns_return(piece, k):
    col, part, narrow = piece.shape
    piece = piece.reshape(col, part, k, narrow // k).transpose(1, 2, 0, 3)
    piece = piece.reshape(part, k, col * narrow // k)
    return lax.all_gather(piece, "dp", axis=0, tiled=True).astype(F32)


def rows_sum(grad, sizes):
    dp, col = sizes["dp"], sizes["col"]
    short, width = grad.shape
    piece = lax.psum_scatter(grad.astype(BF16), "dp", scatter_dimension=0, tiled=True)
    return piece.reshape(short // dp, col, width // col).transpose(1, 0, 2)


def rows_return(piece):
    col, part, depth = piece.shape
    whole = lax.all_gather(piece, "dp", axis=0)
    return whole.transpose(1, 0, 2, 3).reshape(-1, depth).astype(F32)


def line_gather(block, cols):
    me = lax.axis_index("col")
    right, left = [block], [block]
    for k in range(1, cols):
        right.append(lax.ppermute(right[-1], "col", [(i, i + 1) for i in range(k - 1, cols - 1)]))
        left.append(lax.ppermute(left[-1], "col", [(i + 1, i) for i in range(cols - k)]))
    depth = block.shape[1]
    out = jnp.zeros((block.shape[0], cols * depth), block.dtype)
    for k in range(cols):
        source = lax.rem(me + cols - k, cols)
        value = block if k == 0 else jnp.where(me >= k, right[k], left[cols - k])
        out = lax.dynamic_update_slice_in_dim(out, value, source * depth, 1)
    return out


def pair_gather(half):
    other = lax.ppermute(half, "row", [(0, 1), (1, 0)])
    first = lax.axis_index("row") == 0
    return jnp.concatenate([jnp.where(first, half, other), jnp.where(first, other, half)])


def make_body(sizes):
    cols = sizes["col"]

    def body(
        tokens,
        attention_norm_gain,
        attention_norm_bias,
        qkv_weight,
        qkv_bias,
        out_weight,
        feedforward_norm_gain,
        feedforward_norm_bias,
        gate_up_weight,
        down_weight,
        cotangent,
    ):
        my_row, my_col, my_dp = (lax.axis_index(name) for name in ("row", "col", "dp"))
        half, depth = tokens.shape
        own = half // cols
        heads_wide = qkv_bias.shape[1]
        tables = rope_tables(SEQ)
        vector = jnp.stack(
            [attention_norm_gain, attention_norm_bias, feedforward_norm_gain, feedforward_norm_bias]
        )
        vector = jnp.concatenate([vector, jnp.zeros_like(vector)])
        qkv_piece = exchange(columns_piece(qkv_weight, sizes))
        out_piece = exchange(rows_piece(out_weight, sizes))
        qkv_w = columns_whole(qkv_piece, sizes)
        out_w = rows_whole(out_piece, sizes)
        tokens, qkv_piece = lax.optimization_barrier((tokens, qkv_piece))
        normed_one, tokens_own, xhat_one, rstd_one, vectors = norm_one(cols, tokens, vector)
        gate_up_block, down_block, cotan_block, normed_one = lax.optimization_barrier(
            (gate_up_weight, down_weight, cotangent, normed_one)
        )
        gate_up_w = columns_whole(exchange_later(columns_piece(gate_up_block, sizes), cols), sizes)
        down_w = rows_whole(exchange_later(rows_piece(down_block, sizes), cols), sizes)
        cotan_half = line_gather(cotan_block, cols)
        cotan_rows = pair_gather(cotan_half)
        cotan_own = lax.dynamic_slice_in_dim(cotan_half, my_col * own, own, 0)

        qkv = dot_nn(normed_one, qkv_w)
        heads_in, attn, logs = attend(qkv, qkv_bias.reshape(1, -1), tables)
        normed_two, middle = norm_two(cols, dot_nn(attn, out_w).astype(BF16), tokens_own, vectors)

        gate_up = dot_nn(normed_two, gate_up_w)
        wide = gate_up.shape[1] // 2
        gate, up = gate_up[:, :wide], gate_up[:, wide:]
        sig = jax.nn.sigmoid(gate)
        hidden = (gate * sig * up).astype(BF16)
        grad_hidden = dot_nt(cotan_rows, down_w)
        grad_gu = jnp.concatenate(
            [grad_hidden * up * sig * (1.0 + gate * (1.0 - sig)), grad_hidden * gate * sig], axis=1
        ).astype(BF16)
        grad_middle, second = norm_two_back(
            cols, dot_nt(grad_gu, gate_up_w).astype(BF16), middle, cotan_own, vectors
        )
        mixed = sum_mixed(cols, dot_nn(hidden, down_w).astype(BF16), middle)
        down_piece = exchange_later(rows_sum(dot_tn(hidden, cotan_rows), sizes), cols)
        gate_up_piece = exchange_later(columns_sum(dot_tn(normed_two, grad_gu), sizes), cols)
        out_piece = exchange_later(rows_sum(dot_tn(attn, grad_middle), sizes), cols)
        grad_attn = dot_nt(grad_middle, out_w).astype(BF16)
        grad_qkv, bias_part = attend_back(heads_in, logs, grad_attn, tables)
        qkv_piece = exchange_later(columns_sum(dot_tn(normed_one, grad_qkv), sizes), cols)
        grad_block = lax.dynamic_slice(grad_middle, (my_row * half, my_col * depth), (half, depth))
        input_grad, first = sum_first(
            cols,
            dot_nt(grad_qkv, qkv_w).astype(BF16),
            xhat_one,
            rstd_one,
            attention_norm_gain.reshape(1, -1),
            grad_block,
        )
        mine = jnp.zeros((4, cols * depth), F32)
        mine = lax.dynamic_update_slice(mine, first[:2], (0, my_col * depth))
        mine = lax.dynamic_update_slice(mine, second[:2], (2, 0))
        biases = jnp.zeros((sizes["row"] * cols, 3 * heads_wide), F32)
        biases = lax.dynamic_update_slice(biases, bias_part[:1], (my_row * cols + my_col, 0))
        small = lax.psum(
            jnp.concatenate([mine.reshape(-1), biases.reshape(-1)]), ("dp", "row", "col")
        )
        norms = lax.dynamic_slice_in_dim(
            small[: mine.size].reshape(mine.shape), my_col * depth, depth, 1
        )
        bias = lax.dynamic_index_in_dim(
            small[mine.size :].reshape(biases.shape), my_row * cols + my_col, 0, False
        ).reshape(3, heads_wide)
        return (
            mixed,
            input_grad,
            norms[0],
            norms[1],
            columns_return(qkv_piece, 3),
            bias,
            rows_return(out_piece),
            norms[2],
            norms[3],
            columns_return(gate_up_piece, 2),
            rows_return(down_piece),
        )

    return body


def solution(mesh):
    specs = (
        P(("dp", "row"), "col"),
        P("col"),
        P("col"),
        P("col", None, "row"),
        P(None, ("row", "col")),
        P("row", "col"),
        P("col"),
        P("col"),
        P("col", None, "row"),
        P("row", "col"),
    )
    return jax.shard_map(
        make_body(dict(mesh.shape)),
        mesh=mesh,
        in_specs=specs + (P(("dp", "row"), "col"),),
        out_specs=(P(("dp", "row"), "col"),) + specs,
        check_vma=False,
    )
```

```python
import functools

import jax
import jax.numpy as jnp
from jax import lax
from jax.experimental import pallas as pl
from jax.experimental.pallas import tpu as pltpu
from jax.sharding import PartitionSpec as P

MODEL_WIDTH = 2048
HD = 64
ROT = 16
SEQ = 1024
EPSILON = 1e-05
ROPE_BASE = 10000.0
NEG_LARGE = -1e30
F32 = jnp.float32
BF16 = jnp.bfloat16
MESH = pl.DeviceIdType.MESH
VMEM_LIMIT = 56 * 1024 * 1024
SUBS = 8


def send(src, dst, send_sem, recv_sem, **where):
    return pltpu.make_async_remote_copy(
        src_ref=src,
        dst_ref=dst,
        send_sem=send_sem,
        recv_sem=recv_sem,
        device_id=where,
        device_id_type=MESH,
    )


def enter(cols, everyone=False):
    r, c = lax.axis_index("row"), lax.axis_index("col")
    barrier = pltpu.get_barrier_semaphore()
    pl.semaphore_signal(barrier, inc=1, device_id={"row": 1 - r}, device_id_type=MESH)
    if everyone:
        for k in range(1, cols):
            pl.semaphore_signal(
                barrier, inc=1, device_id={"col": lax.rem(c + k, cols)}, device_id_type=MESH
            )
        pl.semaphore_wait(barrier, cols)
        return

    @pl.when(c > 0)
    def _():
        pl.semaphore_signal(barrier, inc=1, device_id={"col": c - 1}, device_id_type=MESH)

    @pl.when(c < cols - 1)
    def _():
        pl.semaphore_signal(barrier, inc=1, device_id={"col": c + 1}, device_id_type=MESH)

    inner = (c > 0) & (c < cols - 1)

    @pl.when(inner)
    def _():
        pl.semaphore_wait(barrier, 3)

    @pl.when(jnp.logical_not(inner))
    def _():
        pl.semaphore_wait(barrier, 2)


LAG = 3


class Reduce:
    def __init__(self, cols, subs, spot, part, twin, going, coming, sems, add=None):
        self.cols, self.subs, self.spot, self.add = cols, subs, spot, add
        self.part, self.twin, self.going, self.coming = part, twin, going, coming
        self.twin_send, self.twin_recv, self.send, self.recv = sems
        self.r, self.c = lax.axis_index("row"), lax.axis_index("col")
        self.half = part.shape[0] // 2
        self.per_sub = cols - 1
        self.landing = LAG * (cols - 1)
        self.slots = self.per_sub * (subs - 1) + self.landing + 1

    def place(self, d, s, base=0):
        row, rows, column, columns = self.spot(d, s)
        if not isinstance(column, int):
            column = pl.multiple_of(column, 128)
        return pl.ds(pl.multiple_of(base + row, 16), rows), pl.ds(column, columns)

    def twin_copy(self, d, s):
        return send(
            self.part.at[self.place(d, s, (1 - self.r) * self.half)],
            self.twin.at[self.place(d, s)],
            self.twin_send.at[d, s],
            self.twin_recv.at[d, s],
            row=1 - self.r,
        )

    def start(self):
        @pl.loop(0, self.subs)
        def _(s):
            for j in range(self.cols):
                self.twin_copy(self.cols - 1 - j // 2 if j % 2 == 0 else j // 2, s).start()

    def hop(self, way, d, s):
        place = self.place(d, s)
        return send(
            self.going.at[(way,) + place],
            self.coming.at[(way,) + place],
            self.send.at[way, d, s],
            self.recv.at[way, d, s],
            col=self.c + 1 if way == 0 else self.c - 1,
        )

    def own(self, d, s):
        self.twin_copy(d, s).wait_recv()
        value = self.part[self.place(d, s, self.r * self.half)].astype(F32)
        value = value + self.twin[self.place(d, s)].astype(F32)
        if self.add is not None:
            value = value + self.add(d, s)
        return value

    def pass_on(self, way, d, s):
        place = (way,) + self.place(d, s)
        first = 0 if way == 0 else self.cols - 1

        @pl.when(self.c == first)
        def _():
            self.going[place] = self.own(d, s).astype(BF16)

        @pl.when(self.c != first)
        def _():
            value = self.own(d, s)
            self.hop(way, d, s).wait_recv()
            self.going[place] = (value + self.coming[place].astype(F32)).astype(BF16)

        self.hop(way, d, s).start()

    def slot(self, t):
        for way in range(2):
            made = self.c if way == 0 else self.cols - 1 - self.c
            event = t - LAG * made

            @pl.when((event >= 0) & (event < self.per_sub * self.subs))
            def _():
                s, j = lax.div(event, self.per_sub), lax.rem(event, self.per_sub)
                d = self.cols - 1 - j if way == 0 else j

                @pl.when(self.c < d if way == 0 else self.c > d)
                def _():
                    self.pass_on(way, d, s)

    def landed(self, t, do):
        after = t - self.landing

        @pl.when((after >= 0) & (lax.rem(after + self.per_sub * self.cols, self.per_sub) == 0))
        def _():
            s = lax.div(after, self.per_sub)

            @pl.when(s < self.subs)
            def _():
                do(s)

    def land(self, s, total):
        place = self.place(self.c, s)
        total[...] = self.own(self.c, s)

        @pl.when(self.c > 0)
        def _():
            self.hop(0, self.c, s).wait_recv()
            total[...] += self.coming[(0,) + place].astype(F32)

        @pl.when(self.c < self.cols - 1)
        def _():
            self.hop(1, self.c, s).wait_recv()
            total[...] += self.coming[(1,) + place].astype(F32)

    def finish(self):
        @pl.loop(0, self.subs)
        def _(s):
            for d in range(self.cols):
                self.twin_copy(d, s).wait_send()

                @pl.when(self.c < d)
                def _():
                    self.hop(0, d, s).wait_send()

                @pl.when(self.c > d)
                def _():
                    self.hop(1, d, s).wait_send()

    @staticmethod
    def scratch(cols, subs, half, width):
        return [
            pltpu.VMEM((half, width), BF16),
            pltpu.VMEM((2, half, width), BF16),
            pltpu.VMEM((2, half, width), BF16),
            pltpu.SemaphoreType.DMA((cols, subs)),
            pltpu.SemaphoreType.DMA((cols, subs)),
            pltpu.SemaphoreType.DMA((2, cols, subs)),
            pltpu.SemaphoreType.DMA((2, cols, subs)),
        ]


class Gather:
    def __init__(self, cols, subs, spot, whole, sems, pair=True):
        self.cols, self.subs, self.spot, self.whole, self.pair = cols, subs, spot, whole, pair
        self.send, self.recv, self.pair_send, self.pair_recv = sems
        self.r, self.c = lax.axis_index("row"), lax.axis_index("col")

    def hop(self, way, source, s):
        where = self.whole.at[self.spot(self.r, source, s)]
        return send(
            where,
            where,
            self.send.at[way, source, s],
            self.recv.at[way, source, s],
            col=self.c + 1 if way == 0 else self.c - 1,
        )

    def across(self, r, source, s):
        where = self.whole.at[self.spot(r, source, s)]
        return send(
            where, where, self.pair_send.at[source, s], self.pair_recv.at[source, s], row=1 - self.r
        )

    def start(self, s):
        @pl.when(self.c < self.cols - 1)
        def _():
            self.hop(0, self.c, s).start()

        @pl.when(self.c > 0)
        def _():
            self.hop(1, self.c, s).start()

        if self.pair:
            self.across(self.r, self.c, s).start()

    def relay(self, s, k):
        @pl.when(self.c >= k)
        def _():
            self.hop(0, self.c - k, s).wait_recv()

            @pl.when(self.c < self.cols - 1)
            def _():
                self.hop(0, self.c - k, s).start()

            if self.pair:
                self.across(self.r, self.c - k, s).start()

        @pl.when(self.c + k < self.cols)
        def _():
            self.hop(1, self.c + k, s).wait_recv()

            @pl.when(self.c > 0)
            def _():
                self.hop(1, self.c + k, s).start()

            if self.pair:
                self.across(self.r, self.c + k, s).start()

    def slot(self, t, begin, step):
        for k in range(1, self.cols):
            after = t - begin - LAG * k

            @pl.when((after >= 0) & (lax.rem(after + step * LAG * self.cols * 8, step) == 0))
            def _():
                s = lax.div(after, step)

                @pl.when(s < self.subs)
                def _():
                    self.relay(s, k)

    def finish(self):
        @pl.loop(0, self.subs)
        def _(s):
            for source in range(self.cols):
                if self.pair:
                    self.across(1 - self.r, source, s).wait_recv()
                    self.across(self.r, source, s).wait_send()

                @pl.when((self.c >= source) & (self.c < self.cols - 1))
                def _():
                    self.hop(0, source, s).wait_send()

                @pl.when((self.c <= source) & (self.c > 0))
                def _():
                    self.hop(1, source, s).wait_send()

    @staticmethod
    def scratch(cols, subs):
        return [
            pltpu.SemaphoreType.DMA((2, cols, subs)),
            pltpu.SemaphoreType.DMA((2, cols, subs)),
            pltpu.SemaphoreType.DMA((cols, subs)),
            pltpu.SemaphoreType.DMA((cols, subs)),
        ]


def moments(rows):
    mean = jnp.mean(rows, axis=1, keepdims=True)
    centered = rows - mean
    return centered, lax.rsqrt(jnp.mean(centered * centered, axis=1, keepdims=True) + EPSILON)


def cost(us):
    return pl.CostEstimate(flops=us * 10**9, bytes_accessed=10**7, transcendentals=0)


def params(number):
    return pltpu.CompilerParams(
        collective_id=number, has_side_effects=True, vmem_limit_bytes=VMEM_LIMIT
    )


VM = pl.BlockSpec(memory_space=pltpu.VMEM)


def row_spot(own, step, half, width):
    def spot(r, source, s):
        return pl.ds(pl.multiple_of(r * half + source * own + s * step, 16), step), pl.ds(0, width)

    return spot


def norm_two_kernel(cols, part, tokens_own, vectors, normed, middle, *scratch):
    half, width = part.shape[0] // 2, part.shape[1]
    own = half // cols
    step = own // SUBS
    total = scratch[11]
    enter(cols)
    summing = Reduce(
        cols, SUBS, lambda d, s: (d * own + s * step, step, 0, width), part, *scratch[:3], scratch[3:7]
    )
    spread = Gather(cols, SUBS, row_spot(own, step, half, width), normed, scratch[7:11])
    summing.start()

    def land(s):
        summing.land(s, total)
        rows = pl.ds(pl.multiple_of(s * step, step), step)
        state = tokens_own[rows, :].astype(F32) + total[...]
        middle[rows, :] = state
        centered, rstd = moments(state)
        result = centered * rstd * vectors[2:3, :] + vectors[3:4, :]
        normed[spread.spot(spread.r, spread.c, s)] = result.astype(BF16)
        spread.start(s)

    @pl.loop(0, summing.slots + LAG * (cols - 1))
    def _(t):
        summing.slot(t)
        summing.landed(t, land)
        spread.slot(t, summing.landing, summing.per_sub)

    spread.finish()
    summing.finish()


def norm_two(cols, part, tokens_own, vectors):
    group, width = part.shape
    return pl.pallas_call(
        functools.partial(norm_two_kernel, cols),
        out_shape=(
            jax.ShapeDtypeStruct((group, width), BF16),
            jax.ShapeDtypeStruct(tokens_own.shape, F32),
        ),
        in_specs=[VM] * 3,
        out_specs=(VM, VM),
        scratch_shapes=Reduce.scratch(cols, SUBS, group // 2, width)
        + Gather.scratch(cols, SUBS)
        + [pltpu.VMEM((group // 2 // cols // SUBS, width), F32)],
        compiler_params=params(2),
        cost_estimate=cost(60),
        name="out_sum_norm_gather",
    )(part, tokens_own, vectors)


def norm_two_back_kernel(cols, part, middle, cotan_own, vectors, grads, sums, *scratch):
    half, width = part.shape[0] // 2, part.shape[1]
    own = half // cols
    step = own // SUBS
    total = scratch[11]
    enter(cols)
    summing = Reduce(
        cols, SUBS, lambda d, s: (d * own + s * step, step, 0, width), part, *scratch[:3], scratch[3:7]
    )
    spread = Gather(cols, SUBS, row_spot(own, step, half, width), grads, scratch[7:11])
    summing.start()
    sums[...] = jnp.zeros_like(sums)

    def land(s):
        summing.land(s, total)
        rows = pl.ds(pl.multiple_of(s * step, step), step)
        centered, rstd = moments(middle[rows, :])
        xhat = centered * rstd
        grad = total[...]
        sums[0:1, :] += jnp.sum(grad * xhat, axis=0, keepdims=True)
        sums[1:2, :] += jnp.sum(grad, axis=0, keepdims=True)
        scaled = grad * vectors[2:3, :]
        inner = (
            scaled
            - jnp.mean(scaled, axis=1, keepdims=True)
            - xhat * jnp.mean(scaled * xhat, axis=1, keepdims=True)
        )
        result = cotan_own[rows, :].astype(F32) + rstd * inner
        grads[spread.spot(spread.r, spread.c, s)] = result.astype(BF16)
        spread.start(s)

    @pl.loop(0, summing.slots + LAG * (cols - 1))
    def _(t):
        summing.slot(t)
        summing.landed(t, land)
        spread.slot(t, summing.landing, summing.per_sub)

    spread.finish()
    summing.finish()


def norm_two_back(cols, part, middle, cotan_own, vectors):
    group, width = part.shape
    return pl.pallas_call(
        functools.partial(norm_two_back_kernel, cols),
        out_shape=(
            jax.ShapeDtypeStruct((group, width), BF16),
            jax.ShapeDtypeStruct((8, width), F32),
        ),
        in_specs=[VM] * 4,
        out_specs=(VM, VM),
        scratch_shapes=Reduce.scratch(cols, SUBS, group // 2, width)
        + Gather.scratch(cols, SUBS)
        + [pltpu.VMEM((group // 2 // cols // SUBS, width), F32)],
        compiler_params=params(3),
        cost_estimate=cost(60),
        name="grad_sum_norm_gather",
    )(part, middle, cotan_own, vectors)


def mixed_sum(cols, part, middle, scratch):
    half, width = part.shape[0] // 2, part.shape[1]
    step, depth, own = half // SUBS, width // cols, half // cols
    c = lax.axis_index("col")

    def add(d, s):
        inside = s * step - c * own
        rows = pl.ds(pl.multiple_of(lax.rem(s * step, own), step), step)
        mine = middle[rows, pl.ds(pl.multiple_of(d * depth, 128), depth)]
        return jnp.where((inside >= 0) & (inside < own), mine, 0.0)

    return Reduce(
        cols,
        SUBS,
        lambda d, s: (s * step, step, d * depth, depth),
        part,
        *scratch[:3],
        scratch[3:7],
        add=add,
    )


def first_kernel(cols, part, xhat, rstd, gain, grad_middle, result, sums, *scratch):
    half, width = part.shape[0] // 2, part.shape[1]
    step, depth = half // SUBS, width // cols
    total, grad, mine, theirs, out_sem, in_sem = scratch[7:]
    enter(cols, everyone=True)
    c = lax.axis_index("col")
    summing = Reduce(
        cols,
        SUBS,
        lambda d, s: (s * step, step, d * depth, depth),
        part,
        *scratch[:3],
        scratch[3:7],
    )
    summing.start()
    sums[...] = jnp.zeros_like(sums)

    def land(s):
        summing.land(s, total)
        rows = pl.ds(pl.multiple_of(s * step, step), step)
        grad[rows, :] = total[...]
        standard = xhat[rows, :]
        sums[0:1, :] += jnp.sum(total[...] * standard, axis=0, keepdims=True)
        sums[1:2, :] += jnp.sum(total[...], axis=0, keepdims=True)

    @pl.loop(0, summing.slots)
    def _(t):
        summing.slot(t)
        summing.landed(t, land)

    lanes = lax.broadcasted_iota(jnp.int32, (128, 128), 1)
    for s in range(half // 128):
        rows = slice(s * 128, (s + 1) * 128)
        scaled = grad[rows, :] * gain[0:1, :]
        one = jnp.sum(scaled, axis=1, keepdims=True)
        two = jnp.sum(scaled * xhat[rows, :], axis=1, keepdims=True)
        both = jnp.where(lanes == 0, one, jnp.where(lanes == 1, two, 0.0))
        mine[:, rows] = both.T[0:8, :]

    def exchange(k):
        return send(
            mine, theirs.at[k - 1], out_sem.at[k - 1], in_sem.at[k - 1], col=lax.rem(c + k, cols)
        )

    for k in range(1, cols):
        exchange(k).start()
    for k in range(1, cols):
        exchange(k).wait_recv()
    for s in range(half // 128):
        rows = slice(s * 128, (s + 1) * 128)
        both = mine[:, rows]
        for k in range(1, cols):
            both = both + theirs[k - 1, :, rows]
        both = jnp.concatenate([both, jnp.zeros((120, 128), F32)], axis=0).T / (depth * cols)
        scaled = grad[rows, :] * gain[0:1, :]
        inner = scaled - both[:, 0:1] - xhat[rows, :] * both[:, 1:2]
        result[rows, :] = grad_middle[rows, :].astype(F32) + rstd[rows, 0:1] * inner
    for k in range(1, cols):
        exchange(k).wait_send()
    summing.finish()


def sum_first(cols, part, xhat, rstd, gain, grad_middle):
    group, width = part.shape
    half, depth = group // 2, width // cols
    return pl.pallas_call(
        functools.partial(first_kernel, cols),
        out_shape=(
            jax.ShapeDtypeStruct((half, depth), F32),
            jax.ShapeDtypeStruct((8, depth), F32),
        ),
        in_specs=[VM] * 5,
        out_specs=(VM, VM),
        scratch_shapes=Reduce.scratch(cols, SUBS, half, width)
        + [
            pltpu.VMEM((half // SUBS, depth), F32),
            pltpu.VMEM((half, depth), F32),
            pltpu.VMEM((8, half), F32),
            pltpu.VMEM((cols - 1, 8, half), F32),
            pltpu.SemaphoreType.DMA((cols - 1,)),
            pltpu.SemaphoreType.DMA((cols - 1,)),
        ],
        compiler_params=params(5),
        cost_estimate=cost(45),
        name="input_grad_sum",
    )(part, xhat, rstd, gain, grad_middle)


def norm_one_kernel(cols, tokens, vector, normed, tokens_own, xhat, rstd, vectors, *scratch):
    half, depth = tokens.shape
    width = depth * cols
    step = half // cols
    full = scratch[0]
    enter(cols)
    r, c = lax.axis_index("row"), lax.axis_index("col")

    def columns(source):
        return pl.ds(pl.multiple_of(source * depth, 128), depth)

    names = Gather(
        cols, 1, lambda r, source, s: (pl.ds(0, 8), columns(source)), vectors, scratch[1:5], pair=False
    )
    spread = Gather(
        cols,
        cols,
        lambda r, source, s: (pl.ds(s * step, step), columns(source)),
        full,
        scratch[5:9],
        pair=False,
    )
    pair_send, pair_recv = scratch[9:11]
    vectors[:, columns(c)] = vector[...]
    names.start(0)
    for s in range(cols):
        rows = pl.ds(s * step, step)
        full[rows, columns(c)] = tokens[rows, :]
        spread.start(s)

    def across(r, s):
        where = normed.at[pl.ds(pl.multiple_of(r * half + s * step, 16), step), :]
        return send(
            where,
            where,
            pair_send.at[s],
            pair_recv.at[s],
            row=1 - lax.axis_index("row"),
        )

    for k in range(1, cols):
        names.relay(0, k)
        for s in range(cols):
            if k < cols - 1:
                spread.relay(s, k)
    for s in range(cols):
        spread.relay(s, cols - 1)
        rows = slice(s * step, (s + 1) * step)
        state = full[rows, :].astype(F32)
        centered, inverse = moments(state)
        standard = centered * inverse
        out = standard * vectors[0:1, :] + vectors[1:2, :]
        normed[pl.ds(pl.multiple_of(r * half + s * step, 16), step), :] = out.astype(BF16)
        across(r, s).start()
        rstd[rows, :] = jnp.broadcast_to(inverse, (step, 128))
        mean = jnp.mean(state, axis=1, keepdims=True)
        xhat[rows, :] = (tokens[rows, :].astype(F32) - mean) * inverse

        @pl.when(c == s)
        def _():
            tokens_own[...] = full[rows, :]

    for s in range(cols):
        across(1 - r, s).wait_recv()
        across(r, s).wait_send()
    names.finish()
    spread.finish()


def norm_one(cols, tokens, vector):
    half, depth = tokens.shape
    width = depth * cols
    return pl.pallas_call(
        functools.partial(norm_one_kernel, cols),
        out_shape=(
            jax.ShapeDtypeStruct((2 * half, width), BF16),
            jax.ShapeDtypeStruct((half // cols, width), BF16),
            jax.ShapeDtypeStruct((half, depth), F32),
            jax.ShapeDtypeStruct((half, 128), F32),
            jax.ShapeDtypeStruct((8, width), F32),
        ),
        in_specs=[VM] * 2,
        out_specs=(VM,) * 5,
        scratch_shapes=[pltpu.VMEM((half, width), BF16)]
        + Gather.scratch(cols, 1)
        + Gather.scratch(cols, cols)
        + [pltpu.SemaphoreType.DMA((cols,)), pltpu.SemaphoreType.DMA((cols,))],
        compiler_params=params(1),
        cost_estimate=cost(40),
        name="gather_norm_one",
    )(tokens, vector)


def rope_tables(length):
    half_rot = ROT // 2
    lane = jnp.arange(2 * HD) % HD
    inverse = ROPE_BASE ** (-2.0 * (lane % half_rot).astype(F32) / ROT)
    angles = jnp.arange(length).astype(F32)[:, None] * inverse[None, :]
    turning = lane < ROT
    cosine = jnp.where(turning, jnp.cos(angles), 1.0)
    sine = jnp.where(turning, jnp.sin(angles), 0.0)
    lower = jnp.where(lane < half_rot, -sine, 0.0)
    upper = jnp.where(lane >= half_rot, sine, 0.0)
    return jnp.stack([cosine, lower, upper])


def turn(x, tables, back=False):
    half_rot = ROT // 2
    width = x.shape[1]
    sines = pltpu.roll(x, width - half_rot, 1) * tables[1] + pltpu.roll(x, half_rot, 1) * tables[2]
    return x * tables[0] - sines if back else x * tables[0] + sines


def dot_nt(a, b):
    return lax.dot_general(a, b, (((1,), (1,)), ((), ())), preferred_element_type=F32)


def dot_tn(a, b):
    return lax.dot_general(a, b, (((0,), (0,)), ((), ())), preferred_element_type=F32)


def dot_nn(a, b):
    return jnp.dot(a, b, preferred_element_type=F32)


BLOCK = 256
PACE = 2


def causal(rows):
    return lax.broadcasted_iota(jnp.int32, (rows, rows), 0) >= lax.broadcasted_iota(
        jnp.int32, (rows, rows), 1
    )


def attend_kernel(cols, qkv, bias, tables, cotan, heads_in, attn, logs, cotan_rows, *sems):
    length, wide = attn.shape
    two = 2 * HD
    half, depth = cotan.shape
    subs = 2 * (wide // two)
    step = half // subs

    def spot(r, source, s):
        rows = pl.ds(pl.multiple_of(r * half + s * step, 16), step)
        return rows, pl.ds(pl.multiple_of(source * depth, 128), depth)

    enter(cols)
    spread = Gather(cols, subs, spot, cotan_rows, sems)
    for s in range(subs):
        cotan_rows[spot(spread.r, spread.c, s)] = cotan[s * step : (s + 1) * step, :]
        spread.start(s)
    first_head = lax.broadcasted_iota(jnp.int32, (BLOCK, two), 1) < HD

    @pl.loop(0, wide // two)
    def _(pair):
        def lanes(k):
            return pl.ds(pl.multiple_of(k * wide + pair * two, two), two)

        for k in range(3):
            x = qkv[:, lanes(k)] + bias[0:1, lanes(k)]
            if k < 2:
                x = turn(x, tables)
            if k == 0:
                x = x * HD ** (-0.5)
            heads_in[:, lanes(k)] = x.astype(BF16)
        for i in range(length // BLOCK):
            keep = (i + 1) * BLOCK
            rows = slice(i * BLOCK, keep)
            query = heads_in[rows, lanes(0)]
            keys = heads_in[0:keep, lanes(1)]
            values = heads_in[0:keep, lanes(2)]
            outs = []
            for h in range(2):
                mine = first_head if h == 0 else ~first_head
                scores = dot_nt(jnp.where(mine, query, jnp.zeros_like(query)), keys)
                last = jnp.where(causal(BLOCK), scores[:, i * BLOCK :], NEG_LARGE)
                scores = last if i == 0 else jnp.concatenate([scores[:, : i * BLOCK], last], axis=1)
                top = jnp.max(scores, axis=1, keepdims=True)
                expo = jnp.exp(scores - top)
                total = jnp.sum(expo, axis=1, keepdims=True)
                probs = (expo * (1.0 / total)).astype(BF16)
                outs.append(dot_nn(probs, values))
                logs[pair, h, rows, :] = jnp.broadcast_to(top + jnp.log(total), (BLOCK, 128))
            attn[rows, pl.ds(pl.multiple_of(pair * two, two), two)] = jnp.where(
                first_head, outs[0], outs[1]
            ).astype(BF16)
            if i % 2 == 1:
                spread.relay(2 * pair + i // 2, 1)

    for k in range(2, cols):

        @pl.loop(0, subs)
        def _(s):
            spread.relay(s, k)

    spread.finish()


def attend(cols, qkv, bias, tables, cotan):
    length, wide = qkv.shape[0], qkv.shape[1] // 3
    subs = wide // HD
    return pl.pallas_call(
        functools.partial(attend_kernel, cols),
        out_shape=(
            jax.ShapeDtypeStruct(qkv.shape, BF16),
            jax.ShapeDtypeStruct((length, wide), BF16),
            jax.ShapeDtypeStruct((wide // (2 * HD), 2, length, 128), F32),
            jax.ShapeDtypeStruct((2 * cotan.shape[0], cols * cotan.shape[1]), BF16),
        ),
        in_specs=[VM] * 4,
        out_specs=(VM,) * 4,
        scratch_shapes=Gather.scratch(cols, subs),
        compiler_params=params(6),
        cost_estimate=cost(40),
        name="attention_cotangent_gather",
    )(qkv, bias, tables, cotan)


def attend_back_kernel(
    cols, heads_in, logs, grad, tables, part, middle, result, sums, mixed, *scratch
):
    length, wide = grad.shape
    two = 2 * HD
    queries_grad, keys_grad, values_grad, total = scratch[:4]
    step = part.shape[0] // 2 // SUBS
    enter(cols)
    summing = mixed_sum(cols, part, middle, scratch[4:])
    summing.start()

    def land(s):
        summing.land(s, total)
        mixed[pl.ds(pl.multiple_of(s * step, step), step), :] = total[...].astype(BF16)

    def slot(t):
        summing.slot(t)
        summing.landed(t, land)

    blocks = length // BLOCK
    done = wide // two * blocks * PACE
    first_head = lax.broadcasted_iota(jnp.int32, (BLOCK, two), 1) < HD

    @pl.loop(0, wide // two)
    def _(pair):
        def lanes(k):
            return pl.ds(pl.multiple_of(k * wide + pair * two, two), two)

        keys_grad[...] = jnp.zeros_like(keys_grad)
        values_grad[...] = jnp.zeros_like(values_grad)
        for i in range(length // BLOCK):
            keep = (i + 1) * BLOCK
            rows = slice(i * BLOCK, keep)
            query = heads_in[rows, lanes(0)]
            keys = heads_in[0:keep, lanes(1)]
            values = heads_in[0:keep, lanes(2)]
            out_grad = grad[rows, lanes(0)]
            outs = []
            for h in range(2):
                mine = first_head if h == 0 else ~first_head
                query_h = jnp.where(mine, query, jnp.zeros_like(query))
                grad_h = jnp.where(mine, out_grad, jnp.zeros_like(out_grad))
                scores = dot_nt(query_h, keys)
                probs = jnp.exp(scores - logs[pair, h, rows, 0:1])
                last = jnp.where(causal(BLOCK), probs[:, i * BLOCK :], 0.0)
                probs = last if i == 0 else jnp.concatenate([probs[:, : i * BLOCK], last], axis=1)
                probs_grad = dot_nt(grad_h, values)
                delta = jnp.sum(probs * probs_grad, axis=1, keepdims=True)
                scores_grad = (probs * (probs_grad - delta)).astype(BF16)
                outs.append(dot_nn(scores_grad, keys))
                keys_grad[0:keep, :] += dot_tn(scores_grad, query_h)
                values_grad[0:keep, :] += dot_tn(probs.astype(BF16), grad_h)
            queries_grad[rows, :] = jnp.where(first_head, outs[0], outs[1]) * HD ** (-0.5)

            @pl.loop(0, PACE)
            def _(u):
                slot((pair * blocks + i) * PACE + u)

        grads = (
            turn(queries_grad[...], tables, back=True),
            turn(keys_grad[...], tables, back=True),
            values_grad[...],
        )
        for k in range(3):
            low = grads[k].astype(BF16)
            result[:, lanes(k)] = low
            column_sum = jnp.sum(low.astype(F32), axis=0, keepdims=True)
            sums[:, lanes(k)] = jnp.broadcast_to(column_sum, (8, two))

    @pl.loop(done, max(done, summing.slots))
    def _(t):
        slot(t)

    summing.finish()


def attend_back(cols, heads_in, logs, grad, tables, part, middle):
    length, wide = grad.shape
    group, width = part.shape
    return pl.pallas_call(
        functools.partial(attend_back_kernel, cols),
        out_shape=(
            jax.ShapeDtypeStruct(heads_in.shape, BF16),
            jax.ShapeDtypeStruct((8, 3 * wide), F32),
            jax.ShapeDtypeStruct((group // 2, width // cols), BF16),
        ),
        in_specs=[VM] * 6,
        out_specs=(VM,) * 3,
        scratch_shapes=[pltpu.VMEM((length, 2 * HD), F32)] * 3
        + [pltpu.VMEM((group // 2 // SUBS, width // cols), F32)]
        + Reduce.scratch(cols, SUBS, group // 2, width),
        compiler_params=params(4),
        cost_estimate=cost(45),
        name="attention_back_mixed_sum",
    )(heads_in, logs, grad, tables, part, middle)


def dot(spec, a, b):
    return jnp.einsum(spec, a, b, preferred_element_type=F32)


def columns_piece(block, sizes):
    dp, col = sizes["dp"], sizes["col"]
    depth, k, wide = block.shape
    part = depth // dp
    piece = lax.dynamic_slice_in_dim(block, lax.axis_index("dp") * part, part, 0)
    piece = piece.reshape(part, k, col, wide // col).transpose(2, 0, 1, 3)
    return piece.reshape(col, part, k * wide // col)


def columns_whole(piece, sizes):
    whole = lax.all_gather(piece, "dp", axis=0)
    return whole.transpose(1, 0, 2, 3).reshape(-1, piece.shape[-1])


def rows_piece(block, sizes):
    dp, col = sizes["dp"], sizes["col"]
    tall, depth = block.shape
    return lax.dynamic_index_in_dim(
        block.reshape(col, dp, tall // col // dp, depth), lax.axis_index("dp"), 1, False
    )


def rows_whole(piece, sizes):
    col, part, depth = piece.shape
    return lax.all_gather(
        piece.transpose(1, 0, 2).reshape(part, col * depth), "dp", axis=0, tiled=True
    )


def exchange(pieces):
    return lax.all_to_all(pieces, "col", 0, 0, tiled=True)


def columns_sum(grad, sizes):
    dp, col = sizes["dp"], sizes["col"]
    width, narrow = grad.shape
    part = width // col // dp
    pieces = grad.astype(BF16).reshape(col, dp, part, narrow).transpose(1, 0, 2, 3)
    piece = lax.psum_scatter(
        pieces.reshape(width, narrow), "dp", scatter_dimension=0, tiled=True
    )
    return piece.reshape(col, part, narrow)


def columns_return(piece, k):
    col, part, narrow = piece.shape
    piece = piece.reshape(col, part, k, narrow // k).transpose(1, 2, 0, 3)
    piece = piece.reshape(part, k, col * narrow // k)
    return lax.all_gather(piece, "dp", axis=0, tiled=True).astype(F32)


def rows_sum(grad, sizes):
    dp, col = sizes["dp"], sizes["col"]
    short, width = grad.shape
    piece = lax.psum_scatter(grad.astype(BF16), "dp", scatter_dimension=0, tiled=True)
    return piece.reshape(short // dp, col, width // col).transpose(1, 0, 2)


def rows_return(piece):
    col, part, depth = piece.shape
    whole = lax.all_gather(piece, "dp", axis=0)
    return whole.transpose(1, 0, 2, 3).reshape(-1, depth).astype(F32)


def make_body(sizes):
    cols = sizes["col"]

    def body(
        tokens,
        attention_norm_gain,
        attention_norm_bias,
        qkv_weight,
        qkv_bias,
        out_weight,
        feedforward_norm_gain,
        feedforward_norm_bias,
        gate_up_weight,
        down_weight,
        cotangent,
    ):
        my_row, my_col, my_dp = (lax.axis_index(name) for name in ("row", "col", "dp"))
        half, depth = tokens.shape
        own = half // cols
        heads_wide = qkv_bias.shape[1]
        tables = rope_tables(SEQ)
        vector = jnp.stack(
            [attention_norm_gain, attention_norm_bias, feedforward_norm_gain, feedforward_norm_bias]
        )
        vector = jnp.concatenate([vector, jnp.zeros_like(vector)])
        qkv_piece = exchange(columns_piece(qkv_weight, sizes))
        out_piece = exchange(rows_piece(out_weight, sizes))
        tokens, qkv_piece, out_piece = lax.optimization_barrier((tokens, qkv_piece, out_piece))
        qkv_w = columns_whole(qkv_piece, sizes)
        out_w = rows_whole(out_piece, sizes)
        gate_up_piece = columns_piece(gate_up_weight, sizes)
        down_piece = rows_piece(down_weight, sizes)
        gate_up_piece, down_piece, qkv_piece = lax.optimization_barrier(
            (gate_up_piece, down_piece, qkv_piece)
        )
        gate_up_w = columns_whole(exchange(gate_up_piece), sizes)
        down_w = rows_whole(exchange(down_piece), sizes)
        normed_one, tokens_own, xhat_one, rstd_one, vectors = norm_one(cols, tokens, vector)

        qkv = dot_nn(normed_one, qkv_w)
        heads_in, attn, logs, cotan_rows = attend(
            cols, qkv, qkv_bias.reshape(1, -1), tables, cotangent
        )
        cotan_own = lax.dynamic_slice_in_dim(cotan_rows, my_row * half + my_col * own, own, 0)
        normed_two, middle = norm_two(cols, dot_nn(attn, out_w).astype(BF16), tokens_own, vectors)

        gate_up = dot_nn(normed_two, gate_up_w)
        wide = gate_up.shape[1] // 2
        gate, up = gate_up[:, :wide], gate_up[:, wide:]
        sig = jax.nn.sigmoid(gate)
        hidden = (gate * sig * up).astype(BF16)
        grad_down = dot_tn(hidden, cotan_rows).astype(BF16)
        cotan_rows, grad_down = lax.optimization_barrier((cotan_rows, grad_down))
        down_piece = exchange(rows_sum(grad_down, sizes))
        grad_hidden = dot_nt(cotan_rows, down_w)
        grad_gu = jnp.concatenate(
            [grad_hidden * up * sig * (1.0 + gate * (1.0 - sig)), grad_hidden * gate * sig], axis=1
        ).astype(BF16)
        grad_gate_up = dot_tn(normed_two, grad_gu).astype(BF16)
        grad_gu, grad_gate_up = lax.optimization_barrier((grad_gu, grad_gate_up))
        gate_up_piece = exchange(columns_sum(grad_gate_up, sizes))
        grad_middle, second = norm_two_back(
            cols, dot_nt(grad_gu, gate_up_w).astype(BF16), middle, cotan_own, vectors
        )
        grad_attn = dot_nt(grad_middle, out_w).astype(BF16)
        grad_out = dot_tn(attn, grad_middle).astype(BF16)
        grad_qkv, bias_part, mixed = attend_back(
            cols, heads_in, logs, grad_attn, tables, dot_nn(hidden, down_w).astype(BF16), middle
        )
        grad_qkv_weight = dot_tn(normed_one, grad_qkv).astype(BF16)
        grad_qkv, grad_qkv_weight = lax.optimization_barrier((grad_qkv, grad_qkv_weight))
        out_piece = exchange(rows_sum(grad_out, sizes))
        qkv_piece = exchange(columns_sum(grad_qkv_weight, sizes))
        grad_block = lax.dynamic_slice(grad_middle, (my_row * half, my_col * depth), (half, depth))
        input_grad, first = sum_first(
            cols,
            dot_nt(grad_qkv, qkv_w).astype(BF16),
            xhat_one,
            rstd_one,
            attention_norm_gain.reshape(1, -1),
            grad_block,
        )
        mine = jnp.zeros((4, cols * depth), F32)
        mine = lax.dynamic_update_slice(mine, first[:2], (0, my_col * depth))
        mine = lax.dynamic_update_slice(mine, second[:2], (2, 0))
        biases = jnp.zeros((sizes["row"] * cols, 3 * heads_wide), F32)
        biases = lax.dynamic_update_slice(biases, bias_part[:1], (my_row * cols + my_col, 0))
        small = lax.psum(
            jnp.concatenate([mine.reshape(-1), biases.reshape(-1)]), ("dp", "row", "col")
        )
        norms = lax.dynamic_slice_in_dim(
            small[: mine.size].reshape(mine.shape), my_col * depth, depth, 1
        )
        bias = lax.dynamic_index_in_dim(
            small[mine.size :].reshape(biases.shape), my_row * cols + my_col, 0, False
        ).reshape(3, heads_wide)
        return (
            mixed,
            input_grad,
            norms[0],
            norms[1],
            columns_return(qkv_piece, 3),
            bias,
            rows_return(out_piece),
            norms[2],
            norms[3],
            columns_return(gate_up_piece, 2),
            rows_return(down_piece),
        )

    return body


def solution(mesh):
    specs = (
        P(("dp", "row"), "col"),
        P("col"),
        P("col"),
        P("col", None, "row"),
        P(None, ("row", "col")),
        P("row", "col"),
        P("col"),
        P("col"),
        P("col", None, "row"),
        P("row", "col"),
    )
    return jax.shard_map(
        make_body(dict(mesh.shape)),
        mesh=mesh,
        in_specs=specs + (P(("dp", "row"), "col"),),
        out_specs=(P(("dp", "row"), "col"),) + specs,
        check_vma=False,
    )
```

```python
import functools

import jax
import jax.numpy as jnp
import numpy as np
from jax import lax
from jax.experimental import pallas as pl
from jax.experimental.pallas import tpu as pltpu
from jax.sharding import PartitionSpec as P

MODEL_WIDTH = 2048
HD = 64
ROT = 16
SEQ = 1024
EPSILON = 1e-05
ROPE_BASE = 10000.0
NEG_LARGE = -1e30
F32 = jnp.float32
BF16 = jnp.bfloat16
MESH = pl.DeviceIdType.MESH
VMEM_LIMIT = 56 * 1024 * 1024
SUBS = 8


def send(src, dst, send_sem, recv_sem, **where):
    return pltpu.make_async_remote_copy(
        src_ref=src,
        dst_ref=dst,
        send_sem=send_sem,
        recv_sem=recv_sem,
        device_id=where,
        device_id_type=MESH,
    )


def enter(cols, everyone=False, dp=1):
    r, c = lax.axis_index("row"), lax.axis_index("col")
    barrier = pltpu.get_barrier_semaphore()
    pl.semaphore_signal(barrier, inc=1, device_id={"row": 1 - r}, device_id_type=MESH)
    if everyone:
        for k in range(1, cols):
            pl.semaphore_signal(
                barrier, inc=1, device_id={"col": lax.rem(c + k, cols)}, device_id_type=MESH
            )
        for k in range(1, dp):
            pl.semaphore_signal(
                barrier,
                inc=1,
                device_id={"dp": lax.rem(lax.axis_index("dp") + k, dp)},
                device_id_type=MESH,
            )
        pl.semaphore_wait(barrier, cols + dp - 1)
        return

    @pl.when(c > 0)
    def _():
        pl.semaphore_signal(barrier, inc=1, device_id={"col": c - 1}, device_id_type=MESH)

    @pl.when(c < cols - 1)
    def _():
        pl.semaphore_signal(barrier, inc=1, device_id={"col": c + 1}, device_id_type=MESH)

    inner = (c > 0) & (c < cols - 1)

    @pl.when(inner)
    def _():
        pl.semaphore_wait(barrier, 3)

    @pl.when(jnp.logical_not(inner))
    def _():
        pl.semaphore_wait(barrier, 2)


LAG = 3
BLOCK = 256
PACE = 6


class Reduce:
    def __init__(self, cols, subs, spot, part, twin, going, coming, sems, add=None):
        self.cols, self.subs, self.spot, self.add = cols, subs, spot, add
        self.part, self.twin, self.going, self.coming = part, twin, going, coming
        self.twin_send, self.twin_recv, self.send, self.recv = sems
        self.r, self.c = lax.axis_index("row"), lax.axis_index("col")
        self.half = part.shape[0] // 2
        self.per_sub = cols - 1
        self.landing = LAG * (cols - 1)
        self.slots = self.per_sub * (subs - 1) + self.landing + 1

    def place(self, d, s, base=0):
        row, rows, column, columns = self.spot(d, s)
        if not isinstance(column, int):
            column = pl.multiple_of(column, 128)
        return pl.ds(pl.multiple_of(base + row, 16), rows), pl.ds(column, columns)

    def twin_copy(self, d, s):
        return send(
            self.part.at[self.place(d, s, (1 - self.r) * self.half)],
            self.twin.at[self.place(d, s)],
            self.twin_send.at[d, s],
            self.twin_recv.at[d, s],
            row=1 - self.r,
        )

    def start(self):
        @pl.loop(0, self.subs)
        def _(s):
            for j in range(self.cols):
                self.twin_copy(self.cols - 1 - j // 2 if j % 2 == 0 else j // 2, s).start()

    def hop(self, way, d, s):
        place = self.place(d, s)
        return send(
            self.going.at[(way,) + place],
            self.coming.at[(way,) + place],
            self.send.at[way, d, s],
            self.recv.at[way, d, s],
            col=self.c + 1 if way == 0 else self.c - 1,
        )

    def own(self, d, s):
        self.twin_copy(d, s).wait_recv()
        value = self.part[self.place(d, s, self.r * self.half)].astype(F32)
        value = value + self.twin[self.place(d, s)].astype(F32)
        if self.add is not None:
            value = value + self.add(d, s)
        return value

    def pass_on(self, way, d, s):
        place = (way,) + self.place(d, s)
        first = 0 if way == 0 else self.cols - 1

        @pl.when(self.c == first)
        def _():
            self.going[place] = self.own(d, s).astype(BF16)

        @pl.when(self.c != first)
        def _():
            value = self.own(d, s)
            self.hop(way, d, s).wait_recv()
            self.going[place] = (value + self.coming[place].astype(F32)).astype(BF16)

        self.hop(way, d, s).start()

    def slot(self, t):
        for way in range(2):
            made = self.c if way == 0 else self.cols - 1 - self.c
            event = t - LAG * made

            @pl.when((event >= 0) & (event < self.per_sub * self.subs))
            def _():
                s, j = lax.div(event, self.per_sub), lax.rem(event, self.per_sub)
                d = self.cols - 1 - j if way == 0 else j

                @pl.when(self.c < d if way == 0 else self.c > d)
                def _():
                    self.pass_on(way, d, s)

    def landed(self, t, do):
        after = t - self.landing

        @pl.when((after >= 0) & (lax.rem(after + self.per_sub * self.cols, self.per_sub) == 0))
        def _():
            s = lax.div(after, self.per_sub)

            @pl.when(s < self.subs)
            def _():
                do(s)

    def land(self, s, total):
        place = self.place(self.c, s)
        total[...] = self.own(self.c, s)

        @pl.when(self.c > 0)
        def _():
            self.hop(0, self.c, s).wait_recv()
            total[...] += self.coming[(0,) + place].astype(F32)

        @pl.when(self.c < self.cols - 1)
        def _():
            self.hop(1, self.c, s).wait_recv()
            total[...] += self.coming[(1,) + place].astype(F32)

    def finish(self):
        @pl.loop(0, self.subs)
        def _(s):
            for d in range(self.cols):
                self.twin_copy(d, s).wait_send()

                @pl.when(self.c < d)
                def _():
                    self.hop(0, d, s).wait_send()

                @pl.when(self.c > d)
                def _():
                    self.hop(1, d, s).wait_send()

    @staticmethod
    def scratch(cols, subs, half, width):
        return [
            pltpu.VMEM((half, width), BF16),
            pltpu.VMEM((2, half, width), BF16),
            pltpu.VMEM((2, half, width), BF16),
            pltpu.SemaphoreType.DMA((cols, subs)),
            pltpu.SemaphoreType.DMA((cols, subs)),
            pltpu.SemaphoreType.DMA((2, cols, subs)),
            pltpu.SemaphoreType.DMA((2, cols, subs)),
        ]


class Gather:
    def __init__(self, cols, subs, spot, whole, sems, pair=True):
        self.cols, self.subs, self.spot, self.whole, self.pair = cols, subs, spot, whole, pair
        self.send, self.recv, self.pair_send, self.pair_recv = sems
        self.r, self.c = lax.axis_index("row"), lax.axis_index("col")

    def hop(self, way, source, s):
        where = self.whole.at[self.spot(self.r, source, s)]
        return send(
            where,
            where,
            self.send.at[way, source, s],
            self.recv.at[way, source, s],
            col=self.c + 1 if way == 0 else self.c - 1,
        )

    def across(self, r, source, s):
        where = self.whole.at[self.spot(r, source, s)]
        return send(
            where, where, self.pair_send.at[source, s], self.pair_recv.at[source, s], row=1 - self.r
        )

    def start(self, s):
        @pl.when(self.c < self.cols - 1)
        def _():
            self.hop(0, self.c, s).start()

        @pl.when(self.c > 0)
        def _():
            self.hop(1, self.c, s).start()

        if self.pair:
            self.across(self.r, self.c, s).start()

    def relay(self, s, k):
        @pl.when(self.c >= k)
        def _():
            self.hop(0, self.c - k, s).wait_recv()

            @pl.when(self.c < self.cols - 1)
            def _():
                self.hop(0, self.c - k, s).start()

            if self.pair:
                self.across(self.r, self.c - k, s).start()

        @pl.when(self.c + k < self.cols)
        def _():
            self.hop(1, self.c + k, s).wait_recv()

            @pl.when(self.c > 0)
            def _():
                self.hop(1, self.c + k, s).start()

            if self.pair:
                self.across(self.r, self.c + k, s).start()

    def slot(self, t, begin, step):
        for k in range(1, self.cols):
            after = t - begin - LAG * k

            @pl.when((after >= 0) & (lax.rem(after + step * LAG * self.cols * 8, step) == 0))
            def _():
                s = lax.div(after, step)

                @pl.when(s < self.subs)
                def _():
                    self.relay(s, k)

    def finish(self):
        @pl.loop(0, self.subs)
        def _(s):
            for source in range(self.cols):
                if self.pair:
                    self.across(1 - self.r, source, s).wait_recv()
                    self.across(self.r, source, s).wait_send()

                @pl.when((self.c >= source) & (self.c < self.cols - 1))
                def _():
                    self.hop(0, source, s).wait_send()

                @pl.when((self.c <= source) & (self.c > 0))
                def _():
                    self.hop(1, source, s).wait_send()

    @staticmethod
    def scratch(cols, subs):
        return [
            pltpu.SemaphoreType.DMA((2, cols, subs)),
            pltpu.SemaphoreType.DMA((2, cols, subs)),
            pltpu.SemaphoreType.DMA((cols, subs)),
            pltpu.SemaphoreType.DMA((cols, subs)),
        ]


class Exchange:
    def __init__(self, axis, size, source, target, sems):
        self.axis, self.size, self.source, self.target = axis, size, source, target
        self.send, self.recv, self.local = sems
        self.c = lax.axis_index(axis)

    def hop(self, k):
        to = lax.rem(self.c + k, self.size)
        return send(
            self.source.at[to],
            self.target.at[self.c],
            self.send.at[k - 1],
            self.recv.at[k - 1],
            **{self.axis: to},
        )

    def own(self):
        return pltpu.make_async_copy(
            self.source.at[self.c], self.target.at[self.c], self.local.at[0]
        )

    def start(self):
        for k in range(1, self.size):
            self.hop(k).start()
        self.own().start()

    def finish(self):
        self.own().wait()
        for k in range(1, self.size):
            self.hop(k).wait_recv()
        for k in range(1, self.size):
            self.hop(k).wait_send()

    @staticmethod
    def scratch(size):
        return [
            pltpu.SemaphoreType.DMA((size - 1,)),
            pltpu.SemaphoreType.DMA((size - 1,)),
            pltpu.SemaphoreType.DMA((1,)),
        ]


class Broadcast:
    def __init__(self, source, target, sems):
        self.dp, self.source, self.target = target.shape[0], source, target
        self.send, self.recv, self.local = sems
        self.me = lax.axis_index("dp")

    def hop(self, k):
        return send(
            self.source,
            self.target.at[self.me],
            self.send.at[k - 1],
            self.recv.at[k - 1],
            dp=lax.rem(self.me + k, self.dp),
        )

    def own(self):
        return pltpu.make_async_copy(self.source, self.target.at[self.me], self.local.at[0])

    def start(self):
        for k in range(1, self.dp):
            self.hop(k).start()
        self.own().start()

    def finish(self):
        self.own().wait()
        for k in range(1, self.dp):
            self.hop(k).wait()


ANY = pl.BlockSpec(memory_space=pl.ANY)


def exchange_kernel(cols, count, *refs):
    enter(cols, everyone=True)
    sems = refs[2 * count :]
    riders = [
        Exchange("col", cols, refs[i], refs[count + i], sems[3 * i : 3 * i + 3]) for i in range(count)
    ]
    for rider in riders:
        rider.start()
    for rider in riders:
        rider.finish()


def exchange(cols, number, *pieces):
    count = len(pieces)
    return pl.pallas_call(
        functools.partial(exchange_kernel, cols, count),
        out_shape=tuple(jax.ShapeDtypeStruct(p.shape, p.dtype) for p in pieces),
        in_specs=[ANY] * count,
        out_specs=(ANY,) * count,
        scratch_shapes=Exchange.scratch(cols) * count,
        compiler_params=params(number),
        cost_estimate=cost(25),
        name="exchange",
    )(*pieces)


def load_columns(weight, whole, sem):
    dp, cols, part, _ = weight.shape
    copies = [
        pltpu.make_async_copy(
            weight.at[p, j],
            whole.at[pl.ds((j * dp + p) * part, part), :],
            sem.at[p, j],
        )
        for p in range(dp)
        for j in range(cols)
    ]
    for copy in copies:
        copy.start()
    return copies


def dot_nt(a, b):
    return lax.dot_general(a, b, (((1,), (1,)), ((), ())), preferred_element_type=F32)


def dot_tn(a, b):
    return lax.dot_general(a, b, (((0,), (0,)), ((), ())), preferred_element_type=F32)


def dot_nn(a, b):
    return jnp.dot(a, b, preferred_element_type=F32)


def moments(rows):
    mean = jnp.mean(rows, axis=1, keepdims=True)
    centered = rows - mean
    return centered, lax.rsqrt(jnp.mean(centered * centered, axis=1, keepdims=True) + EPSILON)


def cost(us):
    return pl.CostEstimate(flops=us * 10**9, bytes_accessed=10**7, transcendentals=0)


def params(number):
    return pltpu.CompilerParams(
        collective_id=number, has_side_effects=True, vmem_limit_bytes=VMEM_LIMIT
    )


VM = pl.BlockSpec(memory_space=pltpu.VMEM)


def row_spot(own, step, half, width):
    def spot(r, source, s):
        return pl.ds(pl.multiple_of(r * half + source * own + s * step, 16), step), pl.ds(0, width)

    return spot


def norm_two_kernel(cols, part, tokens_own, vectors, normed, middle, *scratch):
    half, width = part.shape[0] // 2, part.shape[1]
    own = half // cols
    step = own // SUBS
    total = scratch[11]
    enter(cols)
    summing = Reduce(
        cols, SUBS, lambda d, s: (d * own + s * step, step, 0, width), part, *scratch[:3], scratch[3:7]
    )
    spread = Gather(cols, SUBS, row_spot(own, step, half, width), normed, scratch[7:11])
    summing.start()

    def land(s):
        summing.land(s, total)
        rows = pl.ds(pl.multiple_of(s * step, step), step)
        state = tokens_own[rows, :].astype(F32) + total[...]
        middle[rows, :] = state
        centered, rstd = moments(state)
        result = centered * rstd * vectors[2:3, :] + vectors[3:4, :]
        normed[spread.spot(spread.r, spread.c, s)] = result.astype(BF16)
        spread.start(s)

    @pl.loop(0, summing.slots + LAG * (cols - 1))
    def _(t):
        summing.slot(t)
        summing.landed(t, land)
        spread.slot(t, summing.landing, summing.per_sub)

    spread.finish()
    summing.finish()


def norm_two(cols, part, tokens_own, vectors):
    group, width = part.shape
    return pl.pallas_call(
        functools.partial(norm_two_kernel, cols),
        out_shape=(
            jax.ShapeDtypeStruct((group, width), BF16),
            jax.ShapeDtypeStruct(tokens_own.shape, F32),
        ),
        in_specs=[VM] * 3,
        out_specs=(VM, VM),
        scratch_shapes=Reduce.scratch(cols, SUBS, group // 2, width)
        + Gather.scratch(cols, SUBS)
        + [pltpu.VMEM((group // 2 // cols // SUBS, width), F32)],
        compiler_params=params(2),
        cost_estimate=cost(60),
        name="out_sum_norm_gather",
    )(part, tokens_own, vectors)


def norm_two_back_kernel(
    cols,
    part,
    middle,
    cotan_own,
    vectors,
    hidden,
    weight,
    grads,
    sums,
    mixed_part,
    down,
    sem,
    *scratch
):
    narrow = hidden.shape[1]
    copies = load_columns(weight, down, sem)
    half, width = part.shape[0] // 2, part.shape[1]
    own = half // cols
    step = own // SUBS
    total = scratch[11]
    enter(cols)
    summing = Reduce(
        cols, SUBS, lambda d, s: (d * own + s * step, step, 0, width), part, *scratch[:3], scratch[3:7]
    )
    spread = Gather(cols, SUBS, row_spot(own, step, half, width), grads, scratch[7:11])
    summing.start()
    blocks = part.shape[0] // BLOCK
    for copy in copies:
        copy.wait()
    sums[...] = jnp.zeros_like(sums)

    def land(s):
        summing.land(s, total)
        rows = pl.ds(pl.multiple_of(s * step, step), step)
        centered, rstd = moments(middle[rows, :])
        xhat = centered * rstd
        grad = total[...]
        sums[0:1, :] += jnp.sum(grad * xhat, axis=0, keepdims=True)
        sums[1:2, :] += jnp.sum(grad, axis=0, keepdims=True)
        scaled = grad * vectors[2:3, :]
        inner = (
            scaled
            - jnp.mean(scaled, axis=1, keepdims=True)
            - xhat * jnp.mean(scaled * xhat, axis=1, keepdims=True)
        )
        result = cotan_own[rows, :].astype(F32) + rstd * inner
        grads[spread.spot(spread.r, spread.c, s)] = result.astype(BF16)
        spread.start(s)

    @pl.loop(0, summing.slots + LAG * (cols - 1))
    def _(t):
        summing.slot(t)
        summing.landed(t, land)
        spread.slot(t, summing.landing, summing.per_sub)

        @pl.when((lax.rem(t, PACE) == PACE - 1) & (t < PACE * blocks))
        def _():
            rows = pl.ds(pl.multiple_of(lax.div(t, PACE) * BLOCK, BLOCK), BLOCK)
            result = dot_nt(hidden[rows, :], down[:, :narrow])
            mixed_part[rows, :] = result.astype(BF16)

    spread.finish()
    summing.finish()


def norm_two_back(cols, part, middle, cotan_own, vectors, hidden, weight):
    group, width = part.shape
    tall = weight.shape[3]
    return pl.pallas_call(
        functools.partial(norm_two_back_kernel, cols),
        out_shape=(
            jax.ShapeDtypeStruct((group, width), BF16),
            jax.ShapeDtypeStruct((8, width), F32),
            jax.ShapeDtypeStruct((group, width), BF16),
        ),
        in_specs=[VM] * 5 + [ANY],
        out_specs=(VM,) * 3,
        scratch_shapes=[pltpu.VMEM((width, tall), BF16), pltpu.SemaphoreType.DMA(weight.shape[:2])]
        + Reduce.scratch(cols, SUBS, group // 2, width)
        + Gather.scratch(cols, SUBS)
        + [pltpu.VMEM((group // 2 // cols // SUBS, width), F32)],
        compiler_params=params(3),
        cost_estimate=cost(60),
        name="grad_sum_norm_gather",
    )(part, middle, cotan_own, vectors, hidden, weight)


def mixed_sum(cols, part, middle, scratch):
    half, width = part.shape[0] // 2, part.shape[1]
    step, depth, own = half // SUBS, width // cols, half // cols
    c = lax.axis_index("col")

    def add(d, s):
        inside = s * step - c * own
        rows = pl.ds(pl.multiple_of(lax.rem(s * step, own), step), step)
        mine = middle[rows, pl.ds(pl.multiple_of(d * depth, 128), depth)]
        return jnp.where((inside >= 0) & (inside < own), mine, 0.0)

    return Reduce(
        cols,
        SUBS,
        lambda d, s: (s * step, step, d * depth, depth),
        part,
        *scratch[:3],
        scratch[3:7],
        add=add,
    )


def mixed_kernel(cols, part, middle, piece, mixed, pieces, *scratch):
    half = part.shape[0] // 2
    step = half // SUBS
    total = scratch[7]
    enter(cols, everyone=True, dp=pieces.shape[0])
    rider = Broadcast(piece, pieces, scratch[8:])
    rider.start()
    summing = mixed_sum(cols, part, middle, scratch[:7])
    summing.start()

    def land(s):
        summing.land(s, total)
        mixed[pl.ds(pl.multiple_of(s * step, step), step), :] = total[...].astype(BF16)

    @pl.loop(0, summing.slots)
    def _(t):
        summing.slot(t)
        summing.landed(t, land)

    summing.finish()
    rider.finish()


def sum_mixed(cols, part, middle, piece, dp):
    group, width = part.shape
    return pl.pallas_call(
        functools.partial(mixed_kernel, cols),
        out_shape=(
            jax.ShapeDtypeStruct((group // 2, width // cols), BF16),
            jax.ShapeDtypeStruct((dp,) + piece.shape, BF16),
        ),
        in_specs=[VM] * 2 + [ANY],
        out_specs=(VM, ANY),
        scratch_shapes=Reduce.scratch(cols, SUBS, group // 2, width)
        + [pltpu.VMEM((group // 2 // SUBS, width // cols), F32)]
        + Exchange.scratch(dp),
        compiler_params=params(4),
        cost_estimate=cost(45),
        name="mixed_sum",
    )(part, middle, piece)


def first_kernel(
    cols, part, xhat, rstd, gain, grad_middle, pieces_from, result, sums, pieces_to, *scratch
):
    dp = pieces_from.shape[0]
    half, width = part.shape[0] // 2, part.shape[1]
    step, depth = half // SUBS, width // cols
    total, grad, mine, theirs, out_sem, in_sem = scratch[7:13]
    enter(cols, everyone=True, dp=dp)
    rider = Exchange("dp", dp, pieces_from, pieces_to, scratch[13:])
    c = lax.axis_index("col")
    summing = Reduce(
        cols,
        SUBS,
        lambda d, s: (s * step, step, d * depth, depth),
        part,
        *scratch[:3],
        scratch[3:7],
    )
    summing.start()
    rider.start()
    sums[...] = jnp.zeros_like(sums)

    def land(s):
        summing.land(s, total)
        rows = pl.ds(pl.multiple_of(s * step, step), step)
        grad[rows, :] = total[...]
        standard = xhat[rows, :]
        sums[0:1, :] += jnp.sum(total[...] * standard, axis=0, keepdims=True)
        sums[1:2, :] += jnp.sum(total[...], axis=0, keepdims=True)

    @pl.loop(0, summing.slots)
    def _(t):
        summing.slot(t)
        summing.landed(t, land)

    lanes = lax.broadcasted_iota(jnp.int32, (128, 128), 1)
    for s in range(half // 128):
        rows = slice(s * 128, (s + 1) * 128)
        scaled = grad[rows, :] * gain[0:1, :]
        one = jnp.sum(scaled, axis=1, keepdims=True)
        two = jnp.sum(scaled * xhat[rows, :], axis=1, keepdims=True)
        both = jnp.where(lanes == 0, one, jnp.where(lanes == 1, two, 0.0))
        mine[:, rows] = both.T[0:8, :]

    def exchange(k):
        return send(
            mine, theirs.at[k - 1], out_sem.at[k - 1], in_sem.at[k - 1], col=lax.rem(c + k, cols)
        )

    for k in range(1, cols):
        exchange(k).start()
    for k in range(1, cols):
        exchange(k).wait_recv()
    for s in range(half // 128):
        rows = slice(s * 128, (s + 1) * 128)
        both = mine[:, rows]
        for k in range(1, cols):
            both = both + theirs[k - 1, :, rows]
        both = jnp.concatenate([both, jnp.zeros((120, 128), F32)], axis=0).T / (depth * cols)
        scaled = grad[rows, :] * gain[0:1, :]
        inner = scaled - both[:, 0:1] - xhat[rows, :] * both[:, 1:2]
        result[rows, :] = grad_middle[rows, :].astype(F32) + rstd[rows, 0:1] * inner
    for k in range(1, cols):
        exchange(k).wait_send()
    summing.finish()
    rider.finish()


def sum_first(cols, part, xhat, rstd, gain, grad_middle, pieces):
    group, width = part.shape
    half, depth = group // 2, width // cols
    return pl.pallas_call(
        functools.partial(first_kernel, cols),
        out_shape=(
            jax.ShapeDtypeStruct((half, depth), F32),
            jax.ShapeDtypeStruct((8, depth), F32),
            jax.ShapeDtypeStruct(pieces.shape, BF16),
        ),
        in_specs=[VM] * 5 + [ANY],
        out_specs=(VM, VM, ANY),
        scratch_shapes=Reduce.scratch(cols, SUBS, half, width)
        + [
            pltpu.VMEM((half // SUBS, depth), F32),
            pltpu.VMEM((half, depth), F32),
            pltpu.VMEM((8, half), F32),
            pltpu.VMEM((cols - 1, 8, half), F32),
            pltpu.SemaphoreType.DMA((cols - 1,)),
            pltpu.SemaphoreType.DMA((cols - 1,)),
        ]
        + Exchange.scratch(pieces.shape[0]),
        compiler_params=params(5),
        cost_estimate=cost(45),
        name="input_grad_sum",
    )(part, xhat, rstd, gain, grad_middle, pieces)


def norm_one_kernel(cols, tokens, vector, normed, tokens_own, xhat, rstd, vectors, *scratch):
    half, depth = tokens.shape
    width = depth * cols
    step = half // cols
    full = scratch[0]
    enter(cols)
    r, c = lax.axis_index("row"), lax.axis_index("col")

    def columns(source):
        return pl.ds(pl.multiple_of(source * depth, 128), depth)

    names = Gather(
        cols, 1, lambda r, source, s: (pl.ds(0, 8), columns(source)), vectors, scratch[1:5], pair=False
    )
    spread = Gather(
        cols,
        cols,
        lambda r, source, s: (pl.ds(s * step, step), columns(source)),
        full,
        scratch[5:9],
        pair=False,
    )
    pair_send, pair_recv = scratch[9:11]
    vectors[:, columns(c)] = vector[...]
    names.start(0)
    for s in range(cols):
        rows = pl.ds(s * step, step)
        full[rows, columns(c)] = tokens[rows, :]
        spread.start(s)

    def across(r, s):
        where = normed.at[pl.ds(pl.multiple_of(r * half + s * step, 16), step), :]
        return send(
            where,
            where,
            pair_send.at[s],
            pair_recv.at[s],
            row=1 - lax.axis_index("row"),
        )

    for k in range(1, cols):
        names.relay(0, k)
        for s in range(cols):
            if k < cols - 1:
                spread.relay(s, k)
    for s in range(cols):
        spread.relay(s, cols - 1)
        rows = slice(s * step, (s + 1) * step)
        state = full[rows, :].astype(F32)
        centered, inverse = moments(state)
        standard = centered * inverse
        out = standard * vectors[0:1, :] + vectors[1:2, :]
        normed[pl.ds(pl.multiple_of(r * half + s * step, 16), step), :] = out.astype(BF16)
        across(r, s).start()
        rstd[rows, :] = jnp.broadcast_to(inverse, (step, 128))
        mean = jnp.mean(state, axis=1, keepdims=True)
        xhat[rows, :] = (tokens[rows, :].astype(F32) - mean) * inverse

        @pl.when(c == s)
        def _():
            tokens_own[...] = full[rows, :]

    for s in range(cols):
        across(1 - r, s).wait_recv()
        across(r, s).wait_send()
    names.finish()
    spread.finish()


def norm_one(cols, tokens, vector):
    half, depth = tokens.shape
    width = depth * cols
    return pl.pallas_call(
        functools.partial(norm_one_kernel, cols),
        out_shape=(
            jax.ShapeDtypeStruct((2 * half, width), BF16),
            jax.ShapeDtypeStruct((half // cols, width), BF16),
            jax.ShapeDtypeStruct((half, depth), F32),
            jax.ShapeDtypeStruct((half, 128), F32),
            jax.ShapeDtypeStruct((8, width), F32),
        ),
        in_specs=[VM] * 2,
        out_specs=(VM,) * 5,
        scratch_shapes=[pltpu.VMEM((half, width), BF16)]
        + Gather.scratch(cols, 1)
        + Gather.scratch(cols, cols)
        + [pltpu.SemaphoreType.DMA((cols,)), pltpu.SemaphoreType.DMA((cols,))],
        compiler_params=params(1),
        cost_estimate=cost(40),
        name="gather_norm_one",
    )(tokens, vector)


def finish_kernel(
    cols, pieces, second, first, bias, arranged, small, sums, landed, slices, mine, both, pair, all_dp, *sems
):
    dp, _, _, wide = pieces.shape
    depth = first.shape[1]
    narrow = wide // 4
    enter(cols, everyone=True, dp=dp)
    r, c, me = (lax.axis_index(name) for name in ("row", "col", "dp"))
    names = Exchange("col", cols, second, slices, sems[:3])
    names.start()
    rider = Exchange("col", cols, sums, landed, sems[3:6])

    def total(to):
        value = pieces[0, to].astype(F32)
        for p in range(1, dp):
            value = value + pieces[p, to].astype(F32)
        return value.astype(BF16)

    for k in range(1, cols):
        to = lax.rem(c + k, cols)
        sums[to] = total(to)
        rider.hop(k).start()
    landed[c] = total(c)
    names.finish()
    mine[...] = jnp.zeros_like(mine)
    mine[0:2, :depth] = first[0:2, :]
    shift = slices[0]
    for j in range(1, cols):
        shift = shift + slices[j]
    mine[2:4, :depth] = shift[0:2, :]
    mine[0:1, depth:] = bias[0:1, :]
    across = send(mine, pair, sems[6].at[0], sems[6].at[1], row=1 - r)
    across.start()
    across.wait()
    both[:, depth:] = mine[:, depth:]
    both[:, :depth] = mine[:, :depth] + pair[:, :depth]

    def hop(k):
        to = lax.rem(me + k, dp)
        return send(both, all_dp.at[me], sems[7].at[k - 1], sems[8].at[k - 1], dp=to)

    for k in range(1, dp):
        hop(k).start()
    all_dp[me] = both[...]
    for k in range(1, dp):
        hop(k).wait()
    value = all_dp[0]
    for p in range(1, dp):
        value = value + all_dp[p]
    small[...] = value
    for k in range(1, cols):
        rider.hop(k).wait()
    for k in range(4):
        for j in range(cols):
            arranged[k, :, j * narrow : (j + 1) * narrow] = landed[
                j, :, k * narrow : (k + 1) * narrow
            ]


def finish(cols, pieces, second, first, bias):
    dp, _, part, wide = pieces.shape
    depth, biases = first.shape[1], bias.shape[1]
    dma = pltpu.SemaphoreType.DMA
    return pl.pallas_call(
        functools.partial(finish_kernel, cols),
        out_shape=(
            jax.ShapeDtypeStruct((4, part, cols * wide // 4), BF16),
            jax.ShapeDtypeStruct((8, depth + biases), F32),
        ),
        in_specs=[VM] * 4,
        out_specs=(VM,) * 2,
        scratch_shapes=[
            pltpu.VMEM((cols, part, wide), BF16),
            pltpu.VMEM((cols, part, wide), BF16),
            pltpu.VMEM((cols, 8, depth), F32),
            pltpu.VMEM((8, depth + biases), F32),
            pltpu.VMEM((8, depth + biases), F32),
            pltpu.VMEM((8, depth + biases), F32),
            pltpu.VMEM((dp, 8, depth + biases), F32),
        ]
        + Exchange.scratch(cols) * 2
        + [dma((2,)), dma((max(dp - 1, 1),)), dma((max(dp - 1, 1),))],
        compiler_params=params(10),
        cost_estimate=cost(25),
        name="attention_grad_exchange",
    )(pieces, second, first, bias)


def rope_tables(length):
    half_rot = ROT // 2
    lane = np.arange(2 * HD) % HD
    inverse = (ROPE_BASE ** (-2.0 * (lane % half_rot) / ROT)).astype(np.float32)
    angles = np.arange(length).astype(np.float32)[:, None] * inverse[None, :]
    turning = lane < ROT
    cosine = np.where(turning, np.cos(angles), 1.0)
    sine = np.where(turning, np.sin(angles), 0.0)
    lower = np.where(lane < half_rot, -sine, 0.0)
    upper = np.where(lane >= half_rot, sine, 0.0)
    return np.stack([cosine, lower, upper]).astype(np.float32)


def turn(x, tables, back=False):
    half_rot = ROT // 2
    width = x.shape[1]
    sines = pltpu.roll(x, width - half_rot, 1) * tables[1] + pltpu.roll(x, half_rot, 1) * tables[2]
    return x * tables[0] - sines if back else x * tables[0] + sines


def causal(rows):
    return lax.broadcasted_iota(jnp.int32, (rows, rows), 0) >= lax.broadcasted_iota(
        jnp.int32, (rows, rows), 1
    )


def attend_kernel(
    cols,
    normed,
    weight,
    bias,
    tables,
    one_from,
    two_from,
    heads_in,
    attn,
    logs,
    part,
    one_to,
    two_to,
    whole,
    sem,
    qkv,
    *sems
):
    length, wide = attn.shape
    two = 2 * HD
    copies = load_columns(weight, whole, sem)
    enter(cols, everyone=True)
    riders = (
        Exchange("col", cols, one_from, one_to, sems[:3]),
        Exchange("col", cols, two_from, two_to, sems[3:]),
    )
    for rider in riders:
        rider.start()
    for copy in copies:
        copy.wait()
    first_head = lax.broadcasted_iota(jnp.int32, (BLOCK, two), 1) < HD

    @pl.loop(0, length // BLOCK)
    def _(m):
        rows = pl.ds(pl.multiple_of(m * BLOCK, BLOCK), BLOCK)
        qkv[rows, :] = dot_nn(normed[rows, :], whole[:, : 3 * wide]) + bias[0:1, :]

    @pl.loop(0, wide // two)
    def _(pair):
        def lanes(k):
            return pl.ds(pl.multiple_of(k * wide + pair * two, two), two)

        for k in range(3):
            x = qkv[:, lanes(k)]
            if k < 2:
                x = turn(x, tables)
            if k == 0:
                x = x * HD ** (-0.5)
            heads_in[:, lanes(k)] = x.astype(BF16)
        for i in range(length // BLOCK):
            keep = (i + 1) * BLOCK
            rows = slice(i * BLOCK, keep)
            query = heads_in[rows, lanes(0)]
            keys = heads_in[0:keep, lanes(1)]
            values = heads_in[0:keep, lanes(2)]
            outs = []
            for h in range(2):
                mine = first_head if h == 0 else ~first_head
                scores = dot_nt(jnp.where(mine, query, jnp.zeros_like(query)), keys)
                last = jnp.where(causal(BLOCK), scores[:, i * BLOCK :], NEG_LARGE)
                scores = last if i == 0 else jnp.concatenate([scores[:, : i * BLOCK], last], axis=1)
                top = jnp.max(scores, axis=1, keepdims=True)
                expo = jnp.exp(scores - top)
                total = jnp.sum(expo, axis=1, keepdims=True)
                probs = (expo * (1.0 / total)).astype(BF16)
                outs.append(dot_nn(probs, values))
                logs[pair, h, rows, :] = jnp.broadcast_to(top + jnp.log(total), (BLOCK, 128))
            attn[rows, pl.ds(pl.multiple_of(pair * two, two), two)] = jnp.where(
                first_head, outs[0], outs[1]
            ).astype(BF16)

    @pl.loop(0, length // BLOCK)
    def _(m):
        rows = pl.ds(pl.multiple_of(m * BLOCK, BLOCK), BLOCK)
        part[rows, :] = dot_nt(attn[rows, :], whole[:, 3 * wide :]).astype(BF16)

    for rider in riders:
        rider.finish()


def attend(cols, normed, weight, bias, tables, one, two):
    length, width = normed.shape
    dp = weight.shape[0]
    wide = weight.shape[3] // 4
    return pl.pallas_call(
        functools.partial(attend_kernel, cols),
        out_shape=(
            jax.ShapeDtypeStruct((length, 3 * wide), BF16),
            jax.ShapeDtypeStruct((length, wide), BF16),
            jax.ShapeDtypeStruct((wide // (2 * HD), 2, length, 128), F32),
            jax.ShapeDtypeStruct((length, width), BF16),
            jax.ShapeDtypeStruct(one.shape, BF16),
            jax.ShapeDtypeStruct(two.shape, BF16),
        ),
        in_specs=[VM, ANY, VM, VM, ANY, ANY],
        out_specs=(VM,) * 4 + (ANY,) * 2,
        scratch_shapes=[
            pltpu.VMEM((width, 4 * wide), BF16),
            pltpu.SemaphoreType.DMA((dp, cols)),
            pltpu.VMEM((length, 3 * wide), F32),
        ]
        + Exchange.scratch(cols) * 2,
        compiler_params=params(6),
        cost_estimate=cost(50),
        name="attention_weight_exchange",
    )(normed, weight, bias, tables, one, two)


def attend_back_kernel(
    cols,
    heads_in,
    logs,
    grad_middle,
    tables,
    weight,
    normed,
    attn,
    pieces_from,
    weight_grad,
    normed_grad,
    sums,
    arranged,
    queries_grad,
    keys_grad,
    values_grad,
    whole,
    sem,
    grad,
    result,
    pieces_to,
    *sems
):
    length, wide = attn.shape
    two = 2 * HD
    dp, _, part_rows, _ = weight.shape
    copies = load_columns(weight, whole, sem)
    enter(cols, everyone=True)
    rider = Exchange("col", cols, pieces_from, pieces_to, sems)
    rider.start()
    for copy in copies:
        copy.wait()
    first_head = lax.broadcasted_iota(jnp.int32, (BLOCK, two), 1) < HD

    @pl.loop(0, length // BLOCK)
    def _(m):
        rows = pl.ds(pl.multiple_of(m * BLOCK, BLOCK), BLOCK)
        grad[rows, :] = dot_nn(grad_middle[rows, :], whole[:, 3 * wide :]).astype(BF16)

    @pl.loop(0, wide // two)
    def _(pair):
        def lanes(k):
            return pl.ds(pl.multiple_of(k * wide + pair * two, two), two)

        keys_grad[...] = jnp.zeros_like(keys_grad)
        values_grad[...] = jnp.zeros_like(values_grad)
        for i in range(length // BLOCK):
            keep = (i + 1) * BLOCK
            rows = slice(i * BLOCK, keep)
            query = heads_in[rows, lanes(0)]
            keys = heads_in[0:keep, lanes(1)]
            values = heads_in[0:keep, lanes(2)]
            out_grad = grad[rows, lanes(0)]
            outs = []
            for h in range(2):
                mine = first_head if h == 0 else ~first_head
                query_h = jnp.where(mine, query, jnp.zeros_like(query))
                grad_h = jnp.where(mine, out_grad, jnp.zeros_like(out_grad))
                scores = dot_nt(query_h, keys)
                probs = jnp.exp(scores - logs[pair, h, rows, 0:1])
                last = jnp.where(causal(BLOCK), probs[:, i * BLOCK :], 0.0)
                probs = last if i == 0 else jnp.concatenate([probs[:, : i * BLOCK], last], axis=1)
                probs_grad = dot_nt(grad_h, values)
                delta = jnp.sum(probs * probs_grad, axis=1, keepdims=True)
                scores_grad = (probs * (probs_grad - delta)).astype(BF16)
                outs.append(dot_nn(scores_grad, keys))
                keys_grad[0:keep, :] += dot_tn(scores_grad, query_h)
                values_grad[0:keep, :] += dot_tn(probs.astype(BF16), grad_h)
            queries_grad[rows, :] = jnp.where(first_head, outs[0], outs[1]) * HD ** (-0.5)
        grads = (
            turn(queries_grad[...], tables, back=True),
            turn(keys_grad[...], tables, back=True),
            values_grad[...],
        )
        for k in range(3):
            low = grads[k].astype(BF16)
            result[:, lanes(k)] = low
            column_sum = jnp.sum(low.astype(F32), axis=0, keepdims=True)
            sums[:, lanes(k)] = jnp.broadcast_to(column_sum, (8, two))

    depth = normed.shape[1] // cols

    @pl.loop(0, cols)
    def _(j):
        columns = pl.ds(pl.multiple_of(j * depth, depth), depth)
        heads_grad = dot_tn(normed[:, columns], result[...]).astype(BF16)
        out_grad = dot_tn(grad_middle[:, columns], attn[...]).astype(BF16)
        for p in range(dp):
            rows = slice(p * part_rows, (p + 1) * part_rows)
            weight_grad[p, j, :, : 3 * wide] = heads_grad[rows, :]
            weight_grad[p, j, :, 3 * wide :] = out_grad[rows, :]

    @pl.loop(0, length // BLOCK)
    def _(m):
        rows = pl.ds(pl.multiple_of(m * BLOCK, BLOCK), BLOCK)
        normed_grad[rows, :] = dot_nt(result[rows, :], whole[:, : 3 * wide]).astype(BF16)

    rider.finish()
    share = arranged.shape[2] // cols
    for k in range(arranged.shape[0]):
        arranged[k] = jnp.concatenate(
            [pieces_to[j, :, k * share : (k + 1) * share] for j in range(cols)], axis=1
        )


def attend_back(cols, heads_in, logs, grad_middle, tables, weight, normed, attn, pieces, share):
    length, wide = attn.shape
    width = normed.shape[1]
    return pl.pallas_call(
        functools.partial(attend_back_kernel, cols),
        out_shape=(
            jax.ShapeDtypeStruct(weight.shape, BF16),
            jax.ShapeDtypeStruct((length, width), BF16),
            jax.ShapeDtypeStruct((8, 3 * wide), F32),
            jax.ShapeDtypeStruct((3, pieces.shape[1], cols * share), BF16),
        ),
        in_specs=[VM] * 4 + [ANY, VM, VM, ANY],
        out_specs=(VM,) * 4,
        scratch_shapes=[pltpu.VMEM((length, 2 * HD), F32)] * 3
        + [
            pltpu.VMEM((width, 4 * wide), BF16),
            pltpu.SemaphoreType.DMA(weight.shape[:2]),
            pltpu.VMEM((length, wide), BF16),
            pltpu.VMEM((length, 3 * wide), BF16),
            pltpu.VMEM(pieces.shape, BF16),
        ]
        + Exchange.scratch(cols),
        compiler_params=params(8),
        cost_estimate=cost(50),
        name="attention_back_exchange",
    )(heads_in, logs, grad_middle, tables, weight, normed, attn, pieces)


def gate_up_kernel(cols, normed, weight, cotan, hidden, gate_part, up_part, cotan_rows, *scratch):
    group, narrow = hidden.shape
    half, depth = cotan.shape
    step = half // SUBS
    whole, sem = scratch[:2]
    copies = load_columns(weight, whole, sem)
    enter(cols)

    def spot(r, source, s):
        rows = pl.ds(pl.multiple_of(r * half + s * step, 16), step)
        return rows, pl.ds(pl.multiple_of(source * depth, 128), depth)

    spread = Gather(cols, SUBS, spot, cotan_rows, scratch[2:])
    for s in range(SUBS):
        cotan_rows[spot(spread.r, spread.c, s)] = cotan[s * step : (s + 1) * step, :]
        spread.start(s)
    for copy in copies:
        copy.wait()
    blocks = group // BLOCK
    each = SUBS // blocks

    @pl.loop(0, blocks)
    def _(m):
        rows = pl.ds(pl.multiple_of(m * BLOCK, BLOCK), BLOCK)
        both = dot_nn(normed[rows, :], whole[...])
        gate, up = both[:, :narrow], both[:, narrow:]
        sig = 1.0 / (1.0 + jnp.exp(-gate))
        active = gate * sig
        hidden[rows, :] = (active * up).astype(BF16)
        up_part[rows, :] = active
        gate_part[rows, :] = up * sig * (1.0 + gate * (1.0 - sig))
        for u in range(each):
            spread.relay(m * each + u, 1)

    for k in range(2, cols):

        @pl.loop(0, SUBS)
        def _(s):
            spread.relay(s, k)

    spread.finish()


def gate_up(cols, normed, weight, cotan):
    group, width = normed.shape
    dp = weight.shape[0]
    narrow = weight.shape[3] // 2
    return pl.pallas_call(
        functools.partial(gate_up_kernel, cols),
        out_shape=(
            jax.ShapeDtypeStruct((group, narrow), BF16),
            jax.ShapeDtypeStruct((group, narrow), F32),
            jax.ShapeDtypeStruct((group, narrow), F32),
            jax.ShapeDtypeStruct((group, width), BF16),
        ),
        in_specs=[VM, ANY, VM],
        out_specs=(VM,) * 4,
        scratch_shapes=[
            pltpu.VMEM((width, weight.shape[3]), BF16),
            pltpu.SemaphoreType.DMA((dp, cols)),
        ]
        + Gather.scratch(cols, SUBS),
        compiler_params=params(7),
        cost_estimate=cost(35),
        name="gate_up_cotangent_gather",
    )(normed, weight, cotan)


def hidden_back_kernel(
    hidden_from,
    gate_from,
    up_from,
    cotan_from,
    gate_up_from,
    down_from,
    normed_from,
    weight_to,
    normed_to,
    hidden,
    gate_part,
    up_part,
    cotan,
    gate_up,
    down,
    normed,
    grads,
    weight_grad,
    normed_grad,
    gate_up_sem,
    down_sem,
    block_sem,
    whole_sem,
    out_sem,
    grad_sem,
):
    group, narrow = hidden.shape
    dp, cols, part_rows, _ = gate_up_from.shape
    wide = weight_grad.shape[3]
    blocks = group // BLOCK
    depth = normed.shape[1] // cols

    def rows_of(m):
        return pl.ds(pl.multiple_of(m * BLOCK, BLOCK), BLOCK)

    def block_copies(m):
        rows = rows_of(m)
        pairs = ((cotan_from, cotan), (gate_from, gate_part), (up_from, up_part))
        return [
            pltpu.make_async_copy(a.at[rows, :], b.at[rows, :], block_sem.at[i, m])
            for i, (a, b) in enumerate(pairs)
        ]

    down_copies = load_columns(down_from, down, down_sem)
    for copy in block_copies(0):
        copy.start()
    gate_up_copies = load_columns(gate_up_from, gate_up, gate_up_sem)
    for m in range(1, blocks):
        for copy in block_copies(m):
            copy.start()
    whole_copies = [
        pltpu.make_async_copy(hidden_from, hidden, whole_sem.at[0]),
        pltpu.make_async_copy(normed_from, normed, whole_sem.at[1]),
    ]
    for copy in whole_copies:
        copy.start()
    for copy in down_copies:
        copy.wait()

    def normed_out(m):
        rows = rows_of(m)
        return pltpu.make_async_copy(normed_grad.at[rows, :], normed_to.at[rows, :], out_sem.at[m])

    def weight_out(p, j):
        return pltpu.make_async_copy(weight_grad.at[p, j], weight_to.at[p, j], grad_sem.at[p, j])

    @pl.loop(0, blocks)
    def _(m):
        rows = rows_of(m)
        for copy in block_copies(m):
            copy.wait()
        grad = dot_nn(cotan[rows, :], down[:, :narrow])
        both = jnp.concatenate([grad * gate_part[rows, :], grad * up_part[rows, :]], axis=1)
        grads[rows, :] = both.astype(BF16)

    for copy in gate_up_copies:
        copy.wait()

    @pl.loop(0, blocks)
    def _(m):
        rows = rows_of(m)
        normed_grad[rows, :] = dot_nt(grads[rows, :], gate_up[...]).astype(BF16)
        normed_out(m).start()

    for copy in whole_copies:
        copy.wait()

    @pl.loop(0, cols)
    def _(j):
        columns = pl.ds(pl.multiple_of(j * depth, depth), depth)
        gate_up_grad = dot_tn(normed[:, columns], grads[...]).astype(BF16)
        down_grad = dot_tn(cotan[:, columns], hidden[...]).astype(BF16)
        for p in range(dp):
            rows = slice(p * part_rows, (p + 1) * part_rows)
            weight_grad[p, j, :, : 2 * narrow] = gate_up_grad[rows, :]
            weight_grad[p, j, :, 2 * narrow : 3 * narrow] = down_grad[rows, :]
            if wide > 3 * narrow:
                weight_grad[p, j, :, 3 * narrow :] = jnp.zeros((part_rows, wide - 3 * narrow), BF16)
            weight_out(p, j).start()

    for m in range(blocks):
        normed_out(m).wait()
    for p in range(dp):
        for j in range(cols):
            weight_out(p, j).wait()


def hidden_back(hidden, gate_part, up_part, cotan, gate_up, down, normed):
    group, width = normed.shape
    dp, cols, part, double = gate_up.shape
    grad_shape = (dp, cols, part, double + down.shape[3])
    blocks = group // BLOCK
    dma = pltpu.SemaphoreType.DMA
    return pl.pallas_call(
        hidden_back_kernel,
        out_shape=(
            jax.ShapeDtypeStruct(grad_shape, BF16),
            jax.ShapeDtypeStruct((group, width), BF16),
        ),
        in_specs=[ANY] * 7,
        out_specs=(ANY,) * 2,
        scratch_shapes=[
            pltpu.VMEM(hidden.shape, BF16),
            pltpu.VMEM(gate_part.shape, F32),
            pltpu.VMEM(up_part.shape, F32),
            pltpu.VMEM(cotan.shape, BF16),
            pltpu.VMEM((width, double), BF16),
            pltpu.VMEM((width, down.shape[3]), BF16),
            pltpu.VMEM(normed.shape, BF16),
            pltpu.VMEM((group, double), BF16),
            pltpu.VMEM(grad_shape, BF16),
            pltpu.VMEM((group, width), BF16),
            dma((dp, cols)),
            dma((dp, cols)),
            dma((3, blocks)),
            dma((2,)),
            dma((blocks,)),
            dma((dp, cols)),
        ],
        compiler_params=pltpu.CompilerParams(vmem_limit_bytes=VMEM_LIMIT),
        cost_estimate=cost(30),
        name="hidden_back",
    )(hidden, gate_part, up_part, cotan, gate_up, down, normed)


def split_kernel(whole, first, last):
    count, rows = whole.shape[1] - 1, whole.shape[0] * whole.shape[2]
    inner = first.shape[1] == count

    def part(k):
        return whole[:, k].reshape(rows, whole.shape[3]).astype(F32)

    for k in range(count):
        if inner:
            first[:, k, :] = part(k)
        else:
            first[k] = part(k)
    last[...] = part(count).T


def weights_split(whole, inner):
    dp, count, part, wide = whole.shape
    rows = min(part, 128)
    per = 128 // rows
    depth = dp * part
    count = count - 1
    if inner:
        shape, block, place = (depth, count, wide), (128, count, wide), lambda b: (b, 0, 0)
    else:
        shape, block, place = (count, depth, wide), (count, 128, wide), lambda b: (0, b, 0)
    return pl.pallas_call(
        split_kernel,
        grid=(depth // 128,),
        out_shape=(jax.ShapeDtypeStruct(shape, F32), jax.ShapeDtypeStruct((wide, depth), F32)),
        in_specs=[
            pl.BlockSpec(
                (per, count + 1, rows, wide),
                lambda b: (b * 128 // (per * part), 0, lax.rem(b, max(part // 128, 1)), 0),
            )
        ],
        out_specs=(pl.BlockSpec(block, place), pl.BlockSpec((wide, 128), lambda b: (0, b))),
        compiler_params=pltpu.CompilerParams(vmem_limit_bytes=VMEM_LIMIT),
        cost_estimate=cost(8),
        name="weight_gradients",
    )(whole)


def columns_piece(block, sizes):
    dp, cols = sizes["dp"], sizes["col"]
    depth, k, wide = block.shape
    part = depth // dp
    piece = lax.dynamic_slice_in_dim(block, lax.axis_index("dp") * part, part, 0)
    piece = piece.reshape(part, k, cols, wide // cols).transpose(2, 0, 1, 3)
    return piece.reshape(cols, part, k * wide // cols)


def rows_piece(block, sizes):
    dp, cols = sizes["dp"], sizes["col"]
    wide, depth = block.shape
    part, narrow = depth // dp, wide // cols
    piece = lax.dynamic_slice_in_dim(block, lax.axis_index("dp") * part, part, 1)
    piece = piece.reshape(cols, narrow, part).transpose(0, 2, 1)
    return jnp.pad(piece, ((0, 0), (0, 0), (0, -narrow % 128)))


def weights_whole(piece):
    return lax.all_gather(piece, "dp", axis=0)


def weights_sum(pieces):
    dp, cols, part, wide = pieces.shape
    piece = lax.psum_scatter(
        pieces.reshape(dp * cols * part, wide), "dp", scatter_dimension=0, tiled=True
    )
    return piece.reshape(cols, part, wide)


def make_body(sizes):
    cols = sizes["col"]

    def body(
        tokens,
        attention_norm_gain,
        attention_norm_bias,
        qkv_weight,
        qkv_bias,
        out_weight,
        feedforward_norm_gain,
        feedforward_norm_bias,
        gate_up_weight,
        down_weight,
        cotangent,
    ):
        my_row, my_col, my_dp = (lax.axis_index(name) for name in ("row", "col", "dp"))
        half, depth = tokens.shape
        own = half // cols
        tables = rope_tables(SEQ)
        vector = jnp.stack(
            [attention_norm_gain, attention_norm_bias, feedforward_norm_gain, feedforward_norm_bias]
        )
        vector = jnp.concatenate([vector, jnp.zeros_like(vector)])
        attention_piece = jnp.concatenate(
            [columns_piece(qkv_weight, sizes), rows_piece(out_weight, sizes)], axis=2
        )
        (attention_piece,) = exchange(cols, 9, attention_piece)
        tokens, attention_piece = lax.optimization_barrier((tokens, attention_piece))
        attention_w = weights_whole(attention_piece)
        gate_up_piece = columns_piece(gate_up_weight, sizes)
        down_piece = rows_piece(down_weight, sizes)
        normed_one, tokens_own, xhat_one, rstd_one, vectors = norm_one(cols, tokens, vector)
        heads_in, attn, logs, branch_part, gate_up_piece, down_piece = attend(
            cols,
            normed_one,
            attention_w,
            qkv_bias.reshape(1, -1),
            tables,
            gate_up_piece,
            down_piece,
        )
        gate_up_w = weights_whole(gate_up_piece)
        narrow = down_weight.shape[0] // cols
        normed_two, middle = norm_two(cols, branch_part, tokens_own, vectors)
        down_piece, normed_two = lax.optimization_barrier((down_piece, normed_two))
        down_w = weights_whole(down_piece)
        hidden, gate_part, up_part, cotan_rows = gate_up(cols, normed_two, gate_up_w, cotangent)
        cotan_own = lax.dynamic_slice_in_dim(cotan_rows, my_row * half + my_col * own, own, 0)
        hidden_grad, normed_part = hidden_back(
            hidden, gate_part, up_part, cotan_rows, gate_up_w, down_w, normed_two
        )
        hidden_sum = weights_sum(hidden_grad)
        grad_middle, second, mixed_part = norm_two_back(
            cols, normed_part, middle, cotan_own, vectors, hidden, down_w
        )
        second = second.reshape(8, cols, depth).transpose(1, 0, 2)
        grad_block = lax.dynamic_slice(grad_middle, (my_row * half, my_col * depth), (half, depth))
        attention_grad, normed_part, bias_part, hidden_sum = attend_back(
            cols,
            heads_in,
            logs,
            grad_middle,
            tables,
            attention_w,
            normed_one,
            attn,
            hidden_sum,
            narrow,
        )
        hidden_sum = lax.all_gather(hidden_sum, "dp", axis=0)
        input_grad, first, attention_grad = sum_first(
            cols,
            normed_part,
            xhat_one,
            rstd_one,
            attention_norm_gain.reshape(1, -1),
            grad_block,
            attention_grad,
        )
        attention_sum, small = finish(cols, attention_grad, second, first, bias_part)
        mixed, attention_sum = sum_mixed(cols, mixed_part, middle, attention_sum, sizes["dp"])
        grad_gate_up, grad_down = weights_split(hidden_sum, True)
        grad_qkv_weight, grad_out = weights_split(attention_sum, False)
        grad_qkv_weight = grad_qkv_weight.transpose(1, 0, 2)
        return (
            mixed,
            input_grad,
            small[0, :depth],
            small[1, :depth],
            grad_qkv_weight,
            small[0, depth:].reshape(3, -1),
            grad_out,
            small[2, :depth],
            small[3, :depth],
            grad_gate_up,
            grad_down,
        )

    return body


def solution(mesh):
    specs = (
        P(("dp", "row"), "col"),
        P("col"),
        P("col"),
        P("col", None, "row"),
        P(None, ("row", "col")),
        P("row", "col"),
        P("col"),
        P("col"),
        P("col", None, "row"),
        P("row", "col"),
    )
    return jax.shard_map(
        make_body(dict(mesh.shape)),
        mesh=mesh,
        in_specs=specs + (P(("dp", "row"), "col"),),
        out_specs=(P(("dp", "row"), "col"),) + specs,
        check_vma=False,
    )
```

```python
import functools

import jax
import jax.numpy as jnp
import numpy as np
from jax import lax
from jax.experimental import pallas as pl
from jax.experimental.pallas import tpu as pltpu
from jax.sharding import PartitionSpec as P

MODEL_WIDTH = 2048
HD = 64
ROT = 16
SEQ = 1024
EPSILON = 1e-05
ROPE_BASE = 10000.0
NEG_LARGE = -1e30
F32 = jnp.float32
BF16 = jnp.bfloat16
MESH = pl.DeviceIdType.MESH
VMEM_LIMIT = 56 * 1024 * 1024
SUBS = 8


def send(src, dst, send_sem, recv_sem, **where):
    return pltpu.make_async_remote_copy(
        src_ref=src,
        dst_ref=dst,
        send_sem=send_sem,
        recv_sem=recv_sem,
        device_id=where,
        device_id_type=MESH,
    )


def enter(cols, everyone=False, dp=1):
    r, c = lax.axis_index("row"), lax.axis_index("col")
    barrier = pltpu.get_barrier_semaphore()
    pl.semaphore_signal(barrier, inc=1, device_id={"row": 1 - r}, device_id_type=MESH)
    if everyone:
        for k in range(1, cols):
            pl.semaphore_signal(
                barrier, inc=1, device_id={"col": lax.rem(c + k, cols)}, device_id_type=MESH
            )
        for k in range(1, dp):
            pl.semaphore_signal(
                barrier,
                inc=1,
                device_id={"dp": lax.rem(lax.axis_index("dp") + k, dp)},
                device_id_type=MESH,
            )
        pl.semaphore_wait(barrier, cols + dp - 1)
        return

    @pl.when(c > 0)
    def _():
        pl.semaphore_signal(barrier, inc=1, device_id={"col": c - 1}, device_id_type=MESH)

    @pl.when(c < cols - 1)
    def _():
        pl.semaphore_signal(barrier, inc=1, device_id={"col": c + 1}, device_id_type=MESH)

    inner = (c > 0) & (c < cols - 1)

    @pl.when(inner)
    def _():
        pl.semaphore_wait(barrier, 3)

    @pl.when(jnp.logical_not(inner))
    def _():
        pl.semaphore_wait(barrier, 2)


LAG = 3
BLOCK = 256
PACE = 6


class Reduce:
    def __init__(self, cols, subs, spot, part, twin, going, coming, sems, add=None):
        self.cols, self.subs, self.spot, self.add = cols, subs, spot, add
        self.part, self.twin, self.going, self.coming = part, twin, going, coming
        self.twin_send, self.twin_recv, self.send, self.recv = sems
        self.r, self.c = lax.axis_index("row"), lax.axis_index("col")
        self.half = part.shape[0] // 2
        self.per_sub = cols - 1
        self.landing = LAG * (cols - 1)
        self.slots = self.per_sub * (subs - 1) + self.landing + 1

    def place(self, d, s, base=0):
        row, rows, column, columns = self.spot(d, s)
        if not isinstance(column, int):
            column = pl.multiple_of(column, 128)
        return pl.ds(pl.multiple_of(base + row, 16), rows), pl.ds(column, columns)

    def twin_copy(self, d, s):
        return send(
            self.part.at[self.place(d, s, (1 - self.r) * self.half)],
            self.twin.at[self.place(d, s)],
            self.twin_send.at[d, s],
            self.twin_recv.at[d, s],
            row=1 - self.r,
        )

    def start(self):
        @pl.loop(0, self.subs)
        def _(s):
            for j in range(self.cols):
                self.twin_copy(self.cols - 1 - j // 2 if j % 2 == 0 else j // 2, s).start()

    def hop(self, way, d, s):
        place = self.place(d, s)
        return send(
            self.going.at[(way,) + place],
            self.coming.at[(way,) + place],
            self.send.at[way, d, s],
            self.recv.at[way, d, s],
            col=self.c + 1 if way == 0 else self.c - 1,
        )

    def own(self, d, s):
        self.twin_copy(d, s).wait_recv()
        value = self.part[self.place(d, s, self.r * self.half)].astype(F32)
        value = value + self.twin[self.place(d, s)].astype(F32)
        if self.add is not None:
            value = value + self.add(d, s)
        return value

    def pass_on(self, way, d, s):
        place = (way,) + self.place(d, s)
        first = 0 if way == 0 else self.cols - 1

        @pl.when(self.c == first)
        def _():
            self.going[place] = self.own(d, s).astype(BF16)

        @pl.when(self.c != first)
        def _():
            value = self.own(d, s)
            self.hop(way, d, s).wait_recv()
            self.going[place] = (value + self.coming[place].astype(F32)).astype(BF16)

        self.hop(way, d, s).start()

    def slot(self, t):
        for way in range(2):
            made = self.c if way == 0 else self.cols - 1 - self.c
            event = t - LAG * made

            @pl.when((event >= 0) & (event < self.per_sub * self.subs))
            def _():
                s, j = lax.div(event, self.per_sub), lax.rem(event, self.per_sub)
                d = self.cols - 1 - j if way == 0 else j

                @pl.when(self.c < d if way == 0 else self.c > d)
                def _():
                    self.pass_on(way, d, s)

    def landed(self, t, do):
        after = t - self.landing

        @pl.when((after >= 0) & (lax.rem(after + self.per_sub * self.cols, self.per_sub) == 0))
        def _():
            s = lax.div(after, self.per_sub)

            @pl.when(s < self.subs)
            def _():
                do(s)

    def land(self, s, total):
        place = self.place(self.c, s)
        total[...] = self.own(self.c, s)

        @pl.when(self.c > 0)
        def _():
            self.hop(0, self.c, s).wait_recv()
            total[...] += self.coming[(0,) + place].astype(F32)

        @pl.when(self.c < self.cols - 1)
        def _():
            self.hop(1, self.c, s).wait_recv()
            total[...] += self.coming[(1,) + place].astype(F32)

    def finish(self):
        @pl.loop(0, self.subs)
        def _(s):
            for d in range(self.cols):
                self.twin_copy(d, s).wait_send()

                @pl.when(self.c < d)
                def _():
                    self.hop(0, d, s).wait_send()

                @pl.when(self.c > d)
                def _():
                    self.hop(1, d, s).wait_send()

    @staticmethod
    def scratch(cols, subs, half, width):
        return [
            pltpu.VMEM((half, width), BF16),
            pltpu.VMEM((2, half, width), BF16),
            pltpu.VMEM((2, half, width), BF16),
            pltpu.SemaphoreType.DMA((cols, subs)),
            pltpu.SemaphoreType.DMA((cols, subs)),
            pltpu.SemaphoreType.DMA((2, cols, subs)),
            pltpu.SemaphoreType.DMA((2, cols, subs)),
        ]


class Gather:
    def __init__(self, cols, subs, spot, whole, sems, pair=True):
        self.cols, self.subs, self.spot, self.whole, self.pair = cols, subs, spot, whole, pair
        self.send, self.recv, self.pair_send, self.pair_recv = sems
        self.r, self.c = lax.axis_index("row"), lax.axis_index("col")

    def hop(self, way, source, s):
        where = self.whole.at[self.spot(self.r, source, s)]
        return send(
            where,
            where,
            self.send.at[way, source, s],
            self.recv.at[way, source, s],
            col=self.c + 1 if way == 0 else self.c - 1,
        )

    def across(self, r, source, s):
        where = self.whole.at[self.spot(r, source, s)]
        return send(
            where, where, self.pair_send.at[source, s], self.pair_recv.at[source, s], row=1 - self.r
        )

    def start(self, s):
        @pl.when(self.c < self.cols - 1)
        def _():
            self.hop(0, self.c, s).start()

        @pl.when(self.c > 0)
        def _():
            self.hop(1, self.c, s).start()

        if self.pair:
            self.across(self.r, self.c, s).start()

    def relay(self, s, k):
        @pl.when(self.c >= k)
        def _():
            self.hop(0, self.c - k, s).wait_recv()

            @pl.when(self.c < self.cols - 1)
            def _():
                self.hop(0, self.c - k, s).start()

            if self.pair:
                self.across(self.r, self.c - k, s).start()

        @pl.when(self.c + k < self.cols)
        def _():
            self.hop(1, self.c + k, s).wait_recv()

            @pl.when(self.c > 0)
            def _():
                self.hop(1, self.c + k, s).start()

            if self.pair:
                self.across(self.r, self.c + k, s).start()

    def slot(self, t, begin, step):
        for k in range(1, self.cols):
            after = t - begin - LAG * k

            @pl.when((after >= 0) & (lax.rem(after + step * LAG * self.cols * 8, step) == 0))
            def _():
                s = lax.div(after, step)

                @pl.when(s < self.subs)
                def _():
                    self.relay(s, k)

    def finish(self):
        @pl.loop(0, self.subs)
        def _(s):
            for source in range(self.cols):
                if self.pair:
                    self.across(1 - self.r, source, s).wait_recv()
                    self.across(self.r, source, s).wait_send()

                @pl.when((self.c >= source) & (self.c < self.cols - 1))
                def _():
                    self.hop(0, source, s).wait_send()

                @pl.when((self.c <= source) & (self.c > 0))
                def _():
                    self.hop(1, source, s).wait_send()

    @staticmethod
    def scratch(cols, subs):
        return [
            pltpu.SemaphoreType.DMA((2, cols, subs)),
            pltpu.SemaphoreType.DMA((2, cols, subs)),
            pltpu.SemaphoreType.DMA((cols, subs)),
            pltpu.SemaphoreType.DMA((cols, subs)),
        ]


class Exchange:
    def __init__(self, axis, size, source, target, sems):
        self.axis, self.size, self.source, self.target = axis, size, source, target
        self.send, self.recv, self.local = sems
        self.c = lax.axis_index(axis)

    def peer(self, k):
        if self.size == 4 and k != 2:
            return self.c + 1 - 2 * lax.rem(self.c, 2) if k == 1 else 3 - self.c
        return lax.rem(self.c + k, self.size)

    def hop(self, k):
        to = self.peer(k)
        return send(
            self.source.at[to],
            self.target.at[self.c],
            self.send.at[k - 1],
            self.recv.at[k - 1],
            **{self.axis: to},
        )

    def own(self):
        return pltpu.make_async_copy(
            self.source.at[self.c], self.target.at[self.c], self.local.at[0]
        )

    def start(self):
        for k in range(1, self.size):
            self.hop(k).start()
        self.own().start()

    def finish(self):
        self.own().wait()
        for k in range(1, self.size):
            self.hop(k).wait_recv()
        for k in range(1, self.size):
            self.hop(k).wait_send()

    @staticmethod
    def scratch(size):
        return [
            pltpu.SemaphoreType.DMA((size - 1,)),
            pltpu.SemaphoreType.DMA((size - 1,)),
            pltpu.SemaphoreType.DMA((1,)),
        ]


class Broadcast:
    def __init__(self, dp, units, source, target, sems):
        self.dp, self.units, self.source, self.target = dp, units, source, target
        self.send, self.recv = sems
        self.me = lax.axis_index("dp")
        self.near = self.me + 1 - 2 * lax.rem(self.me, 2)
        self.far = lax.rem(self.me + 2, dp)
        self.square = dp == 4

    def hop(self, i, u):
        if self.square:
            to = self.near if i == 0 else self.far
        else:
            to = lax.rem(self.me + i + 1, self.dp)
        return send(
            self.source(u), self.target(self.me, u), self.send.at[i, u], self.recv.at[i, u], dp=to
        )

    def across(self, u):
        low = u < self.units // 2
        where = self.target(self.near if low else self.far, u)
        return send(
            where,
            where,
            self.send.at[2, u],
            self.recv.at[2, u],
            dp=self.far if low else self.near,
        )

    def hops(self):
        return 2 if self.square else self.dp - 1

    def start(self, units=None):
        half = self.units // 2
        for n in range(self.units) if units is None else units:
            for i in range(self.hops()):
                u = (n + half) % self.units if self.square and i == 1 and units is None else n
                self.hop(i, u).start()

    def forward(self, u):
        if self.square:
            self.hop(0 if u < self.units // 2 else 1, u).wait_recv()
            self.across(u).start()

    def finish(self):
        for u in range(self.units):
            for i in range(self.hops()):
                if not self.square or (i == 0) != (u < self.units // 2):
                    self.hop(i, u).wait_recv()
                self.hop(i, u).wait_send()
            if self.square:
                self.across(u).wait()

    @staticmethod
    def scratch(dp, units):
        return [
            pltpu.SemaphoreType.DMA((max(dp - 1, 1), units)),
            pltpu.SemaphoreType.DMA((max(dp - 1, 1), units)),
        ]


ANY = pl.BlockSpec(memory_space=pl.ANY)


def load_columns(weight, whole, sem):
    dp, cols, part, _ = weight.shape
    copies = [
        pltpu.make_async_copy(
            weight.at[p, j],
            whole.at[pl.ds((j * dp + p) * part, part), :],
            sem.at[p, j],
        )
        for p in range(dp)
        for j in range(cols)
    ]
    for copy in copies:
        copy.start()
    return copies


def dot_nt(a, b):
    return lax.dot_general(a, b, (((1,), (1,)), ((), ())), preferred_element_type=F32)


def dot_tn(a, b):
    return lax.dot_general(a, b, (((0,), (0,)), ((), ())), preferred_element_type=F32)


def dot_nn(a, b):
    return jnp.dot(a, b, preferred_element_type=F32)


def moments(rows):
    mean = jnp.mean(rows, axis=1, keepdims=True)
    centered = rows - mean
    return centered, lax.rsqrt(jnp.mean(centered * centered, axis=1, keepdims=True) + EPSILON)


def cost(us):
    return pl.CostEstimate(flops=us * 10**9, bytes_accessed=10**7, transcendentals=0)


def params(number):
    return pltpu.CompilerParams(
        collective_id=number, has_side_effects=True, vmem_limit_bytes=VMEM_LIMIT
    )


VM = pl.BlockSpec(memory_space=pltpu.VMEM)


def row_spot(own, step, half, width):
    def spot(r, source, s):
        return pl.ds(pl.multiple_of(r * half + source * own + s * step, 16), step), pl.ds(0, width)

    return spot


COTANGENT_SLOT = 14


def middle_kernel(
    cols,
    part,
    tokens_own,
    vectors,
    piece,
    cotan,
    normed_to,
    middle_to,
    hidden_to,
    gate_to,
    up_to,
    weight_to,
    cotan_to,
    normed,
    middle,
    hidden,
    gate_part,
    up_part,
    weight,
    cotan_rows,
    total,
    own_sem,
    out_sem,
    block_sem,
    *scratch
):
    group, width = part.shape
    half = group // 2
    own = half // cols
    step = own // SUBS
    depth = cotan.shape[1]
    rows_each = half // SUBS
    _, part_rows, double = piece.shape
    narrow = double // 2
    dp = weight.shape[0] // cols // part_rows
    me = lax.axis_index("dp")
    enter(cols, everyone=True, dp=dp)
    summing = Reduce(
        cols, SUBS, lambda d, s: (d * own + s * step, step, 0, width), part, *scratch[:3], scratch[3:7]
    )
    summing.start()
    spread = Gather(cols, SUBS, row_spot(own, step, half, width), normed, scratch[7:11])

    def cotan_spot(r, source, s):
        rows = pl.ds(pl.multiple_of(r * half + s * rows_each, 16), rows_each)
        return rows, pl.ds(pl.multiple_of(source * depth, 128), depth)

    cotan_spread = Gather(cols, SUBS, cotan_spot, cotan_rows, scratch[11:15])

    def weight_rows(p, j):
        return weight.at[pl.ds(pl.multiple_of((j * dp + p) * part_rows, 16), part_rows), :]

    rider = Broadcast(dp, cols, lambda u: piece.at[u], weight_rows, scratch[15:17])
    rider.start()
    own_copies = [
        pltpu.make_async_copy(piece.at[j], weight_rows(me, j), own_sem.at[j]) for j in range(cols)
    ]
    for copy in own_copies:
        copy.start()

    def land(s):
        summing.land(s, total)
        rows = pl.ds(pl.multiple_of(s * step, step), step)
        state = tokens_own[rows, :].astype(F32) + total[...]
        middle[rows, :] = state
        centered, rstd = moments(state)
        result = centered * rstd * vectors[2:3, :] + vectors[3:4, :]
        normed[spread.spot(spread.r, spread.c, s)] = result.astype(BF16)
        spread.start(s)

    def cotan_slot(t):
        after = t - COTANGENT_SLOT

        @pl.when((after >= 0) & (lax.rem(after + 60, 3) == 0) & (after < 3 * SUBS))
        def _():
            s = lax.div(after, 3)
            rows = pl.ds(pl.multiple_of(s * rows_each, 16), rows_each)
            cotan_rows[cotan_spot(spread.r, spread.c, s)] = cotan[rows, :]
            cotan_spread.start(s)

        cotan_spread.slot(t, COTANGENT_SLOT, 3)

    first = summing.slots + LAG * (cols - 1)
    last = COTANGENT_SLOT + 3 * (SUBS - 1) + LAG * (cols - 1) + 1
    blocks = group // BLOCK

    @pl.loop(0, first)
    def _(t):
        summing.slot(t)
        summing.landed(t, land)
        spread.slot(t, summing.landing, summing.per_sub)
        cotan_slot(t)
        for u in range(cols):

            @pl.when(t == 8 + 6 * (u % 2))
            def _():
                rider.forward(u)

    spread.finish()
    normed_out = pltpu.make_async_copy(normed, normed_to, out_sem.at[0])
    normed_out.start()
    middle_out = pltpu.make_async_copy(middle, middle_to, out_sem.at[1])
    middle_out.start()
    for copy in own_copies:
        copy.wait()
    rider.finish()
    weight_out = pltpu.make_async_copy(weight, weight_to, out_sem.at[2])
    weight_out.start()

    def block_out(m):
        rows = pl.ds(pl.multiple_of(m * BLOCK, BLOCK), BLOCK)
        pairs = ((hidden, hidden_to), (gate_part, gate_to), (up_part, up_to))
        return [
            pltpu.make_async_copy(a.at[rows, :], b.at[rows, :], block_sem.at[i, m])
            for i, (a, b) in enumerate(pairs)
        ]

    @pl.loop(0, max(last - first, blocks))
    def _(m):
        @pl.when(m < blocks)
        def _():
            rows = pl.ds(pl.multiple_of(m * BLOCK, BLOCK), BLOCK)
            both = dot_nn(normed[rows, :], weight[...])
            gate, up = both[:, :narrow], both[:, narrow:]
            sig = 1.0 / (1.0 + jnp.exp(-gate))
            active = gate * sig
            hidden[rows, :] = (active * up).astype(BF16)
            up_part[rows, :] = active
            gate_part[rows, :] = up * sig * (1.0 + gate * (1.0 - sig))
            for copy in block_out(m):
                copy.start()

        cotan_slot(first + m)

    cotan_spread.finish()
    cotan_out = pltpu.make_async_copy(cotan_rows, cotan_to, out_sem.at[3])
    cotan_out.start()
    summing.finish()
    for m in range(blocks):
        for copy in block_out(m):
            copy.wait()
    for copy in (normed_out, middle_out, weight_out, cotan_out):
        copy.wait()


def middle_part(cols, part, tokens_own, vectors, piece, cotan, dp):
    group, width = part.shape
    _, part_rows, double = piece.shape
    narrow = double // 2
    blocks = group // BLOCK
    dma = pltpu.SemaphoreType.DMA
    outs = (
        ((group, width), BF16),
        (tokens_own.shape, F32),
        ((group, narrow), BF16),
        ((group, narrow), F32),
        ((group, narrow), F32),
        ((dp * cols * part_rows, double), BF16),
        ((group, width), BF16),
    )
    return pl.pallas_call(
        functools.partial(middle_kernel, cols),
        out_shape=tuple(jax.ShapeDtypeStruct(*out) for out in outs),
        in_specs=[VM] * 3 + [ANY, VM],
        out_specs=(ANY,) * len(outs),
        scratch_shapes=[pltpu.VMEM(*out) for out in outs]
        + [
            pltpu.VMEM((group // 2 // cols // SUBS, width), F32),
            dma((cols,)),
            dma((4,)),
            dma((3, blocks)),
        ]
        + Reduce.scratch(cols, SUBS, group // 2, width)
        + Gather.scratch(cols, SUBS) * 2
        + Broadcast.scratch(dp, cols),
        compiler_params=params(2),
        cost_estimate=cost(95),
        name="middle_gate_up",
    )(part, tokens_own, vectors, piece, cotan)


def norm_two_back_kernel(
    cols,
    part,
    middle,
    cotan_own,
    vectors,
    hidden,
    weight,
    grads,
    sums,
    mixed_part,
    down,
    sem,
    *scratch
):
    narrow = hidden.shape[1]
    copies = load_columns(weight, down, sem)
    half, width = part.shape[0] // 2, part.shape[1]
    own = half // cols
    step = own // SUBS
    total = scratch[11]
    enter(cols)
    summing = Reduce(
        cols, SUBS, lambda d, s: (d * own + s * step, step, 0, width), part, *scratch[:3], scratch[3:7]
    )
    spread = Gather(cols, SUBS, row_spot(own, step, half, width), grads, scratch[7:11])
    summing.start()
    blocks = part.shape[0] // BLOCK
    for copy in copies:
        copy.wait()
    sums[...] = jnp.zeros_like(sums)

    def land(s):
        summing.land(s, total)
        rows = pl.ds(pl.multiple_of(s * step, step), step)
        centered, rstd = moments(middle[rows, :])
        xhat = centered * rstd
        grad = total[...]
        sums[0:1, :] += jnp.sum(grad * xhat, axis=0, keepdims=True)
        sums[1:2, :] += jnp.sum(grad, axis=0, keepdims=True)
        scaled = grad * vectors[2:3, :]
        inner = (
            scaled
            - jnp.mean(scaled, axis=1, keepdims=True)
            - xhat * jnp.mean(scaled * xhat, axis=1, keepdims=True)
        )
        result = cotan_own[rows, :].astype(F32) + rstd * inner
        grads[spread.spot(spread.r, spread.c, s)] = result.astype(BF16)
        spread.start(s)

    @pl.loop(0, summing.slots + LAG * (cols - 1))
    def _(t):
        summing.slot(t)
        summing.landed(t, land)
        spread.slot(t, summing.landing, summing.per_sub)

        @pl.when((lax.rem(t, PACE) == PACE - 1) & (t < PACE * blocks))
        def _():
            rows = pl.ds(pl.multiple_of(lax.div(t, PACE) * BLOCK, BLOCK), BLOCK)
            result = dot_nt(hidden[rows, :], down[:, :narrow])
            mixed_part[rows, :] = result.astype(BF16)

    spread.finish()
    summing.finish()


def norm_two_back(cols, part, middle, cotan_own, vectors, hidden, weight):
    group, width = part.shape
    tall = weight.shape[3]
    return pl.pallas_call(
        functools.partial(norm_two_back_kernel, cols),
        out_shape=(
            jax.ShapeDtypeStruct((group, width), BF16),
            jax.ShapeDtypeStruct((8, width), F32),
            jax.ShapeDtypeStruct((group, width), BF16),
        ),
        in_specs=[VM] * 5 + [ANY],
        out_specs=(VM,) * 3,
        scratch_shapes=[pltpu.VMEM((width, tall), BF16), pltpu.SemaphoreType.DMA(weight.shape[:2])]
        + Reduce.scratch(cols, SUBS, group // 2, width)
        + Gather.scratch(cols, SUBS)
        + [pltpu.VMEM((group // 2 // cols // SUBS, width), F32)],
        compiler_params=params(3),
        cost_estimate=cost(60),
        name="grad_sum_norm_gather",
    )(part, middle, cotan_own, vectors, hidden, weight)


def mixed_sum(cols, part, middle, scratch):
    half, width = part.shape[0] // 2, part.shape[1]
    step, depth, own = half // SUBS, width // cols, half // cols
    c = lax.axis_index("col")

    def add(d, s):
        inside = s * step - c * own
        rows = pl.ds(pl.multiple_of(lax.rem(s * step, own), step), step)
        mine = middle[rows, pl.ds(pl.multiple_of(d * depth, 128), depth)]
        return jnp.where((inside >= 0) & (inside < own), mine, 0.0)

    return Reduce(
        cols,
        SUBS,
        lambda d, s: (s * step, step, d * depth, depth),
        part,
        *scratch[:3],
        scratch[3:7],
        add=add,
    )


def mixed_kernel(
    cols, part, middle, piece, norms, bias, mixed, pieces, small, total, mine, all_dp, *sems
):
    half = part.shape[0] // 2
    step = half // SUBS
    dp = pieces.shape[0]
    depth = norms.shape[1]
    me = lax.axis_index("dp")
    enter(cols, everyone=True, dp=dp)
    summing = mixed_sum(cols, part, middle, sems[:7])
    summing.start()
    mine[:, :depth] = norms[...]
    mine[:, depth:] = bias[...]
    all_dp[me] = mine[...]

    def hop(k):
        to = lax.rem(me + k, dp)
        return send(mine, all_dp.at[me], sems[7].at[k - 1], sems[8].at[k - 1], dp=to)

    for k in range(1, dp):
        hop(k).start()
    rider = Broadcast(
        dp, piece.shape[0], lambda u: piece.at[u], lambda p, u: pieces.at[p, u], sems[9:11]
    )
    rider.start()
    own = pltpu.make_async_copy(piece, pieces.at[me], sems[11].at[0])
    own.start()

    def land(s):
        summing.land(s, total)
        mixed[pl.ds(pl.multiple_of(s * step, step), step), :] = total[...].astype(BF16)

    @pl.loop(0, summing.slots)
    def _(t):
        summing.slot(t)
        summing.landed(t, land)
        for u in range(rider.units):

            @pl.when(t == 14 + 7 * (u % 2))
            def _():
                rider.forward(u)

    for k in range(1, dp):
        hop(k).wait()
    value = all_dp[0]
    for p in range(1, dp):
        value = value + all_dp[p]
    small[...] = value
    summing.finish()
    own.wait()
    rider.finish()


def sum_mixed(cols, part, middle, piece, norms, bias, dp):
    group, width = part.shape
    small = (8, norms.shape[1] + bias.shape[1])
    hops = max(dp - 1, 1)
    return pl.pallas_call(
        functools.partial(mixed_kernel, cols),
        out_shape=(
            jax.ShapeDtypeStruct((group // 2, width // cols), BF16),
            jax.ShapeDtypeStruct((dp,) + piece.shape, BF16),
            jax.ShapeDtypeStruct(small, F32),
        ),
        in_specs=[VM] * 2 + [ANY] + [VM] * 2,
        out_specs=(VM, ANY, VM),
        scratch_shapes=[
            pltpu.VMEM((group // 2 // SUBS, width // cols), F32),
            pltpu.VMEM(small, F32),
            pltpu.VMEM((dp,) + small, F32),
        ]
        + Reduce.scratch(cols, SUBS, group // 2, width)
        + [pltpu.SemaphoreType.DMA((hops,)), pltpu.SemaphoreType.DMA((hops,))]
        + Broadcast.scratch(dp, piece.shape[0])
        + [pltpu.SemaphoreType.DMA((1,))],
        compiler_params=params(4),
        cost_estimate=cost(45),
        name="mixed_sum",
    )(part, middle, piece, norms, bias)


def first_kernel(
    cols,
    part,
    xhat,
    rstd,
    gain,
    grad_middle,
    heads_grad,
    out_grad,
    second,
    result,
    norms,
    arranged,
    total,
    grad,
    mine,
    theirs,
    sums,
    landed,
    slices,
    own_norms,
    pair_norms,
    *sems
):
    half, width = part.shape[0] // 2, part.shape[1]
    step, depth = half // SUBS, width // cols
    pairs, dp = heads_grad.shape[:2]
    two = heads_grad.shape[4] // 3
    narrow = sums.shape[2] // 4
    enter(cols, everyone=True)
    r, c = lax.axis_index("row"), lax.axis_index("col")
    summing = Reduce(
        cols,
        SUBS,
        lambda d, s: (s * step, step, d * depth, depth),
        part,
        *sems[:3],
        sems[3:7],
    )
    summing.start()
    out_sem, in_sem, pair_sem = sems[7:10]
    rider = Exchange("col", cols, sums, landed, sems[10:13])
    names = Exchange("col", cols, second, slices, sems[13:16])
    names.start()

    def over_dp(ref, to):
        value = ref[0, to].astype(F32)
        for p in range(1, dp):
            value = value + ref[p, to].astype(F32)
        return value.astype(BF16)

    def fill(to, target):
        for pair in range(pairs):
            value = over_dp(heads_grad.at[pair], to)
            for k in range(3):
                first = k * narrow + pair * two
                target[:, first : first + two] = value[:, k * two : (k + 1) * two]
        target[:, 3 * narrow :] = over_dp(out_grad, to)

    for k in range(1, cols):
        to = rider.peer(k)
        fill(to, sums.at[to])
        rider.hop(k).start()
    fill(c, landed.at[c])
    own_norms[...] = jnp.zeros_like(own_norms)

    def land(s):
        summing.land(s, total)
        rows = pl.ds(pl.multiple_of(s * step, step), step)
        grad[rows, :] = total[...]
        standard = xhat[rows, :]
        own_norms[0:1, :] += jnp.sum(total[...] * standard, axis=0, keepdims=True)
        own_norms[1:2, :] += jnp.sum(total[...], axis=0, keepdims=True)

    @pl.loop(0, summing.slots)
    def _(t):
        summing.slot(t)
        summing.landed(t, land)

    lanes = lax.broadcasted_iota(jnp.int32, (128, 128), 1)
    for s in range(half // 128):
        rows = slice(s * 128, (s + 1) * 128)
        scaled = grad[rows, :] * gain[0:1, :]
        one = jnp.sum(scaled, axis=1, keepdims=True)
        two_sum = jnp.sum(scaled * xhat[rows, :], axis=1, keepdims=True)
        both = jnp.where(lanes == 0, one, jnp.where(lanes == 1, two_sum, 0.0))
        mine[:, rows] = both.T[0:8, :]

    def exchange_sums(k):
        return send(
            mine, theirs.at[k - 1], out_sem.at[k - 1], in_sem.at[k - 1], col=lax.rem(c + k, cols)
        )

    for k in range(1, cols):
        exchange_sums(k).start()
    names.finish()
    shift = slices[0]
    for j in range(1, cols):
        shift = shift + slices[j]
    own_norms[2:4, :] = shift[0:2, :]
    across = send(own_norms, pair_norms, pair_sem.at[0], pair_sem.at[1], row=1 - r)
    across.start()
    for k in range(1, cols):
        exchange_sums(k).wait_recv()
    for s in range(half // 128):
        rows = slice(s * 128, (s + 1) * 128)
        both = mine[:, rows]
        for k in range(1, cols):
            both = both + theirs[k - 1, :, rows]
        both = jnp.concatenate([both, jnp.zeros((120, 128), F32)], axis=0).T / (depth * cols)
        scaled = grad[rows, :] * gain[0:1, :]
        inner = scaled - both[:, 0:1] - xhat[rows, :] * both[:, 1:2]
        result[rows, :] = grad_middle[rows, :].astype(F32) + rstd[rows, 0:1] * inner
    for k in range(1, cols):
        exchange_sums(k).wait_send()
    across.wait()
    norms[...] = own_norms[...] + pair_norms[...]
    summing.finish()
    for k in range(1, cols):
        rider.hop(k).wait()
    for k in range(4):
        for j in range(cols):
            arranged[k, :, j * narrow : (j + 1) * narrow] = landed[
                j, :, k * narrow : (k + 1) * narrow
            ]


def sum_first(cols, part, xhat, rstd, gain, grad_middle, heads_grad, out_grad, second):
    group, width = part.shape
    half, depth = group // 2, width // cols
    rows, narrow = out_grad.shape[2:]
    dma = pltpu.SemaphoreType.DMA
    return pl.pallas_call(
        functools.partial(first_kernel, cols),
        out_shape=(
            jax.ShapeDtypeStruct((half, depth), F32),
            jax.ShapeDtypeStruct((8, depth), F32),
            jax.ShapeDtypeStruct((4, rows, cols * narrow), BF16),
        ),
        in_specs=[VM] * 8,
        out_specs=(VM,) * 3,
        scratch_shapes=[
            pltpu.VMEM((half // SUBS, depth), F32),
            pltpu.VMEM((half, depth), F32),
            pltpu.VMEM((8, half), F32),
            pltpu.VMEM((cols - 1, 8, half), F32),
            pltpu.VMEM((cols, rows, 4 * narrow), BF16),
            pltpu.VMEM((cols, rows, 4 * narrow), BF16),
            pltpu.VMEM((cols, 8, depth), F32),
            pltpu.VMEM((8, depth), F32),
            pltpu.VMEM((8, depth), F32),
        ]
        + Reduce.scratch(cols, SUBS, half, width)
        + [dma((cols - 1,)), dma((cols - 1,)), dma((2,))]
        + Exchange.scratch(cols) * 2,
        compiler_params=params(5),
        cost_estimate=cost(60),
        name="input_grad_sum",
    )(part, xhat, rstd, gain, grad_middle, heads_grad, out_grad, second)


def start_kernel(
    cols,
    tokens,
    vector,
    heads_from,
    out_from,
    gate_up_from,
    down_from,
    normed,
    tokens_own,
    xhat,
    rstd,
    vectors,
    gate_up_piece,
    down_piece,
    attention_w,
    heads,
    out,
    gate_up,
    down,
    pieces,
    landed,
    full,
    in_sem,
    own_sem,
    pair_send,
    pair_recv,
    *sems
):
    half, depth = tokens.shape
    width = depth * cols
    step = half // cols
    dp, _, part, wide = attention_w.shape
    narrow = wide // 4
    tall = down.shape[0] // cols
    r, c, me = (lax.axis_index(name) for name in ("row", "col", "dp"))
    begin = pl.multiple_of(me * part, part)
    rows_in = pl.ds(begin, part)

    def share_of(ref):
        return ref if ref.shape[1] == part else ref.at[:, rows_in]

    loads = [
        pltpu.make_async_copy(heads_from.at[:, rows_in], heads, in_sem.at[0]),
        pltpu.make_async_copy(share_of(out_from), out, in_sem.at[1]),
        pltpu.make_async_copy(gate_up_from.at[rows_in], gate_up, in_sem.at[2]),
        pltpu.make_async_copy(share_of(down_from), down, in_sem.at[3]),
    ]
    for load in loads:
        load.start()
    enter(cols, everyone=True, dp=dp)
    loads[0].wait()
    loads[1].wait()
    for j in range(cols):
        share = slice(j * narrow, (j + 1) * narrow)
        for k in range(3):
            pieces[j, :, k * narrow : (k + 1) * narrow] = heads[k, :, share]
        pieces[j, :, 3 * narrow :] = out[share, :].T
    rider = Exchange("col", cols, pieces, landed, sems[:3])
    assert cols == 4
    landed[c] = pieces[c]
    units = [c] + [rider.peer(k) for k in range(1, cols)]
    cast = Broadcast(
        dp, cols, lambda k: landed.at[units[k]], lambda p, k: attention_w.at[p, units[k]], sems[11:13]
    )
    cast.start((0,))
    for k in range(1, cols):
        rider.hop(k).start()

    def columns(source):
        return pl.ds(pl.multiple_of(source * depth, 128), depth)

    names = Gather(
        cols, 1, lambda r, source, s: (pl.ds(0, 8), columns(source)), vectors, sems[3:7], pair=False
    )
    spread = Gather(
        cols,
        cols,
        lambda r, source, s: (pl.ds(s * step, step), columns(source)),
        full,
        sems[7:11],
        pair=False,
    )
    vectors[:, columns(c)] = vector[...]
    names.start(0)
    for s in range(cols):
        rows = pl.ds(s * step, step)
        full[rows, columns(c)] = tokens[rows, :]
        spread.start(s)
    loads[2].wait()
    for i in range(2):
        values = gate_up[:, i, :]
        for j in range(cols):
            gate_up_piece[j, :, i * tall : (i + 1) * tall] = values[:, j * tall : (j + 1) * tall]
    loads[3].wait()
    for j in range(cols):
        down_piece[j, :, :tall] = down[j * tall : (j + 1) * tall, :].T
        if down_piece.shape[2] > tall:
            down_piece[j, :, tall:] = jnp.zeros((part, down_piece.shape[2] - tall), BF16)

    def across(r, s):
        where = normed.at[pl.ds(pl.multiple_of(r * half + s * step, 16), step), :]
        return send(where, where, pair_send.at[s], pair_recv.at[s], row=1 - lax.axis_index("row"))

    def own(k):
        u = units[k]
        return pltpu.make_async_copy(landed.at[u], attention_w.at[me, u], own_sem.at[k])

    def take(k):
        rider.hop(k).wait_recv()
        cast.start((k,))
        own(k).start()

    def norm(s):
        rows = slice(s * step, (s + 1) * step)
        state = full[rows, :].astype(F32)
        centered, inverse = moments(state)
        result = centered * inverse * vectors[0:1, :] + vectors[1:2, :]
        normed[pl.ds(pl.multiple_of(r * half + s * step, 16), step), :] = result.astype(BF16)
        across(r, s).start()
        rstd[rows, :] = jnp.broadcast_to(inverse, (step, 128))
        mean = jnp.mean(state, axis=1, keepdims=True)
        xhat[rows, :] = (tokens[rows, :].astype(F32) - mean) * inverse

        @pl.when(c == s)
        def _():
            tokens_own[...] = full[rows, :]

    own(0).start()
    take(1)
    for k in range(1, cols):
        names.relay(0, k)
    for s in range(cols):
        spread.relay(s, 1)
    cast.forward(0)
    take(2)
    take(3)
    for s in range(cols):
        spread.relay(s, 2)
    cast.forward(1)
    cast.forward(2)
    for s in range(cols):
        spread.relay(s, 3)
        norm(s)
        if s == 1:
            cast.forward(3)

    for s in range(cols):
        across(1 - r, s).wait_recv()
        across(r, s).wait_send()
    for u in range(cols):
        own(u).wait()
    cast.finish()
    for k in range(1, cols):
        rider.hop(k).wait_send()
    names.finish()
    spread.finish()


def start_part(tokens, vector, heads, out, gate_up, down, sizes):
    dp, cols = sizes["dp"], sizes["col"]
    half, depth = tokens.shape
    width = depth * cols
    part, wide, tall = depth // dp, heads.shape[2], down.shape[0]
    each = tall // cols
    dma = pltpu.SemaphoreType.DMA
    return pl.pallas_call(
        functools.partial(start_kernel, cols),
        out_shape=(
            jax.ShapeDtypeStruct((2 * half, width), BF16),
            jax.ShapeDtypeStruct((half // cols, width), BF16),
            jax.ShapeDtypeStruct((half, depth), F32),
            jax.ShapeDtypeStruct((half, 128), F32),
            jax.ShapeDtypeStruct((8, width), F32),
            jax.ShapeDtypeStruct((cols, part, 2 * each), BF16),
            jax.ShapeDtypeStruct((cols, part, each + -each % 128), BF16),
            jax.ShapeDtypeStruct((dp, cols, part, 4 * wide // cols), BF16),
        ),
        in_specs=[VM] * 2 + [ANY] * 4,
        out_specs=(VM,) * 7 + (ANY,),
        scratch_shapes=[
            pltpu.VMEM((3, part, wide), BF16),
            pltpu.VMEM((wide, part), BF16),
            pltpu.VMEM((part, 2, tall), BF16),
            pltpu.VMEM((tall, part), BF16),
            pltpu.VMEM((cols, part, 4 * wide // cols), BF16),
            pltpu.VMEM((cols, part, 4 * wide // cols), BF16),
            pltpu.VMEM((half, width), BF16),
            dma((4,)),
            dma((cols,)),
            dma((cols,)),
            dma((cols,)),
        ]
        + Exchange.scratch(cols)
        + Gather.scratch(cols, 1)
        + Gather.scratch(cols, cols)
        + Broadcast.scratch(dp, cols),
        compiler_params=params(1),
        cost_estimate=cost(60),
        name="tokens_norm_weights",
    )(tokens, vector, heads, out, gate_up, down)


def rope_tables(length):
    half_rot = ROT // 2
    lane = np.arange(2 * HD) % HD
    inverse = (ROPE_BASE ** (-2.0 * (lane % half_rot) / ROT)).astype(np.float32)
    angles = np.arange(length).astype(np.float32)[:, None] * inverse[None, :]
    turning = lane < ROT
    cosine = np.where(turning, np.cos(angles), 1.0)
    sine = np.where(turning, np.sin(angles), 0.0)
    lower = np.where(lane < half_rot, -sine, 0.0)
    upper = np.where(lane >= half_rot, sine, 0.0)
    return np.stack([cosine, lower, upper]).astype(np.float32)


def turn(x, tables, back=False):
    half_rot = ROT // 2
    width = x.shape[1]
    sines = pltpu.roll(x, width - half_rot, 1) * tables[1] + pltpu.roll(x, half_rot, 1) * tables[2]
    return x * tables[0] - sines if back else x * tables[0] + sines


def causal(rows):
    return lax.broadcasted_iota(jnp.int32, (rows, rows), 0) >= lax.broadcasted_iota(
        jnp.int32, (rows, rows), 1
    )


def attend_kernel(
    cols,
    normed,
    weight,
    bias,
    tables,
    one_from,
    two_from,
    heads_in,
    attn,
    logs,
    part,
    one_to,
    two_to,
    whole,
    sem,
    qkv,
    *sems
):
    length, wide = attn.shape
    two = 2 * HD
    copies = load_columns(weight, whole, sem)
    enter(cols, everyone=True)
    riders = (
        Exchange("col", cols, one_from, one_to, sems[:3]),
        Exchange("col", cols, two_from, two_to, sems[3:]),
    )
    for rider in riders:
        rider.start()
    for copy in copies:
        copy.wait()
    first_head = lax.broadcasted_iota(jnp.int32, (BLOCK, two), 1) < HD

    @pl.loop(0, length // BLOCK)
    def _(m):
        rows = pl.ds(pl.multiple_of(m * BLOCK, BLOCK), BLOCK)
        qkv[rows, :] = dot_nn(normed[rows, :], whole[:, : 3 * wide]) + bias[0:1, :]

    @pl.loop(0, wide // two)
    def _(pair):
        def lanes(k):
            return pl.ds(pl.multiple_of(k * wide + pair * two, two), two)

        for k in range(3):
            x = qkv[:, lanes(k)]
            if k < 2:
                x = turn(x, tables)
            if k == 0:
                x = x * HD ** (-0.5)
            heads_in[:, lanes(k)] = x.astype(BF16)
        for i in range(length // BLOCK):
            keep = (i + 1) * BLOCK
            rows = slice(i * BLOCK, keep)
            query = heads_in[rows, lanes(0)]
            keys = heads_in[0:keep, lanes(1)]
            values = heads_in[0:keep, lanes(2)]
            outs = []
            for h in range(2):
                mine = first_head if h == 0 else ~first_head
                scores = dot_nt(jnp.where(mine, query, jnp.zeros_like(query)), keys)
                last = jnp.where(causal(BLOCK), scores[:, i * BLOCK :], NEG_LARGE)
                scores = last if i == 0 else jnp.concatenate([scores[:, : i * BLOCK], last], axis=1)
                top = jnp.max(scores, axis=1, keepdims=True)
                expo = jnp.exp(scores - top)
                total = jnp.sum(expo, axis=1, keepdims=True)
                probs = (expo * (1.0 / total)).astype(BF16)
                outs.append(dot_nn(probs, values))
                logs[pair, h, rows, :] = jnp.broadcast_to(top + jnp.log(total), (BLOCK, 128))
            attn[rows, pl.ds(pl.multiple_of(pair * two, two), two)] = jnp.where(
                first_head, outs[0], outs[1]
            ).astype(BF16)

    @pl.loop(0, length // BLOCK)
    def _(m):
        rows = pl.ds(pl.multiple_of(m * BLOCK, BLOCK), BLOCK)
        part[rows, :] = dot_nt(attn[rows, :], whole[:, 3 * wide :]).astype(BF16)

    for rider in riders:
        rider.finish()


def attend(cols, normed, weight, bias, tables, one, two):
    length, width = normed.shape
    dp = weight.shape[0]
    wide = weight.shape[3] // 4
    return pl.pallas_call(
        functools.partial(attend_kernel, cols),
        out_shape=(
            jax.ShapeDtypeStruct((length, 3 * wide), BF16),
            jax.ShapeDtypeStruct((length, wide), BF16),
            jax.ShapeDtypeStruct((wide // (2 * HD), 2, length, 128), F32),
            jax.ShapeDtypeStruct((length, width), BF16),
            jax.ShapeDtypeStruct(one.shape, BF16),
            jax.ShapeDtypeStruct(two.shape, BF16),
        ),
        in_specs=[VM, ANY, VM, VM, ANY, ANY],
        out_specs=(VM,) * 4 + (ANY,) * 2,
        scratch_shapes=[
            pltpu.VMEM((width, 4 * wide), BF16),
            pltpu.SemaphoreType.DMA((dp, cols)),
            pltpu.VMEM((length, 3 * wide), F32),
        ]
        + Exchange.scratch(cols) * 2,
        compiler_params=params(6),
        cost_estimate=cost(50),
        name="attention_weight_exchange",
    )(normed, weight, bias, tables, one, two)


def attend_back_kernel(
    cols,
    heads_in,
    logs,
    grad_middle,
    tables,
    weight,
    normed,
    attn,
    pieces_from,
    heads_to,
    out_to,
    normed_grad,
    sums,
    arranged,
    queries_grad,
    keys_grad,
    values_grad,
    whole,
    sem,
    grad,
    result,
    own,
    pieces_to,
    heads_from,
    out_from,
    *sems
):
    length, wide = attn.shape
    two = 2 * HD
    dp, _, part_rows, _ = weight.shape
    copies = load_columns(weight, whole, sem)
    enter(cols, everyone=True, dp=dp)
    rider = Exchange("col", cols, pieces_from, pieces_to, sems[:3])
    rider.start()
    out_rider = Exchange("dp", dp, out_from, out_to, sems[3:6])
    depth = normed.shape[1] // cols

    def heads_rider(pair):
        return Exchange(
            "dp", dp, heads_from.at[pair], heads_to.at[pair], [sem.at[pair] for sem in sems[6:]]
        )

    def parts(j):
        return pl.ds(pl.multiple_of(j * depth, depth), depth)

    @pl.loop(0, cols)
    def _(j):
        out_grad = dot_tn(grad_middle[:, parts(j)], attn[...]).astype(BF16)
        for p in range(dp):
            out_from[p, j] = out_grad[p * part_rows : (p + 1) * part_rows, :]

    out_rider.start()
    for copy in copies:
        copy.wait()
    sums[...] = jnp.zeros_like(sums)
    first_head = lax.broadcasted_iota(jnp.int32, (BLOCK, two), 1) < HD

    @pl.loop(0, length // BLOCK)
    def _(m):
        rows = pl.ds(pl.multiple_of(m * BLOCK, BLOCK), BLOCK)
        grad[rows, :] = dot_nn(grad_middle[rows, :], whole[:, 3 * wide :]).astype(BF16)

    @pl.loop(0, wide // two)
    def _(pair):
        def lanes(k):
            return pl.ds(pl.multiple_of(k * wide + pair * two, two), two)

        keys_grad[...] = jnp.zeros_like(keys_grad)
        values_grad[...] = jnp.zeros_like(values_grad)
        for i in range(length // BLOCK):
            keep = (i + 1) * BLOCK
            rows = slice(i * BLOCK, keep)
            query = heads_in[rows, lanes(0)]
            keys = heads_in[0:keep, lanes(1)]
            values = heads_in[0:keep, lanes(2)]
            out_grad = grad[rows, lanes(0)]
            outs = []
            for h in range(2):
                mine = first_head if h == 0 else ~first_head
                query_h = jnp.where(mine, query, jnp.zeros_like(query))
                grad_h = jnp.where(mine, out_grad, jnp.zeros_like(out_grad))
                scores = dot_nt(query_h, keys)
                probs = jnp.exp(scores - logs[pair, h, rows, 0:1])
                last = jnp.where(causal(BLOCK), probs[:, i * BLOCK :], 0.0)
                probs = last if i == 0 else jnp.concatenate([probs[:, : i * BLOCK], last], axis=1)
                probs_grad = dot_nt(grad_h, values)
                delta = jnp.sum(probs * probs_grad, axis=1, keepdims=True)
                scores_grad = (probs * (probs_grad - delta)).astype(BF16)
                outs.append(dot_nn(scores_grad, keys))
                keys_grad[0:keep, :] += dot_tn(scores_grad, query_h)
                values_grad[0:keep, :] += dot_tn(probs.astype(BF16), grad_h)
            queries_grad[rows, :] = jnp.where(first_head, outs[0], outs[1]) * HD ** (-0.5)
        grads = (
            turn(queries_grad[...], tables, back=True),
            turn(keys_grad[...], tables, back=True),
            values_grad[...],
        )
        for k in range(3):
            low = grads[k].astype(BF16)
            result[:, lanes(k)] = low
            own[:, k * two : (k + 1) * two] = low
            column_sum = jnp.sum(low.astype(F32), axis=0, keepdims=True)
            sums[0:1, lanes(k)] = column_sum

        @pl.loop(0, cols)
        def _(j):
            heads_grad = dot_tn(normed[:, parts(j)], own[...]).astype(BF16)
            for p in range(dp):
                heads_from[pair, p, j] = heads_grad[p * part_rows : (p + 1) * part_rows, :]

        heads_rider(pair).start()

    @pl.loop(0, length // BLOCK)
    def _(m):
        rows = pl.ds(pl.multiple_of(m * BLOCK, BLOCK), BLOCK)
        normed_grad[rows, :] = dot_nt(result[rows, :], whole[:, : 3 * wide]).astype(BF16)

    out_rider.finish()
    for pair in range(wide // two):
        heads_rider(pair).finish()
    rider.finish()
    share = arranged.shape[2] // cols
    for k in range(arranged.shape[0]):
        arranged[k] = jnp.concatenate(
            [pieces_to[j, :, k * share : (k + 1) * share] for j in range(cols)], axis=1
        )


def attend_back(cols, heads_in, logs, grad_middle, tables, weight, normed, attn, pieces, share):
    length, wide = attn.shape
    width = normed.shape[1]
    dp, _, part, _ = weight.shape
    pairs = wide // (2 * HD)
    heads = (pairs, dp, cols, part, 6 * HD)
    out = (dp, cols, part, wide)
    hops = max(dp - 1, 1)
    dma = pltpu.SemaphoreType.DMA
    return pl.pallas_call(
        functools.partial(attend_back_kernel, cols),
        out_shape=(
            jax.ShapeDtypeStruct(heads, BF16),
            jax.ShapeDtypeStruct(out, BF16),
            jax.ShapeDtypeStruct((length, width), BF16),
            jax.ShapeDtypeStruct((8, 3 * wide), F32),
            jax.ShapeDtypeStruct((3, pieces.shape[1], cols * share), BF16),
        ),
        in_specs=[VM] * 4 + [ANY, VM, VM, ANY],
        out_specs=(ANY,) * 2 + (VM,) * 3,
        scratch_shapes=[pltpu.VMEM((length, 2 * HD), F32)] * 3
        + [
            pltpu.VMEM((width, 4 * wide), BF16),
            pltpu.SemaphoreType.DMA(weight.shape[:2]),
            pltpu.VMEM((length, wide), BF16),
            pltpu.VMEM((length, 3 * wide), BF16),
            pltpu.VMEM((length, 6 * HD), BF16),
            pltpu.VMEM(pieces.shape, BF16),
            pltpu.VMEM(heads, BF16),
            pltpu.VMEM(out, BF16),
        ]
        + Exchange.scratch(cols)
        + Exchange.scratch(dp)
        + [dma((pairs, hops)), dma((pairs, hops)), dma((pairs, 1))],
        compiler_params=params(8),
        cost_estimate=cost(50),
        name="attention_back_exchange",
    )(heads_in, logs, grad_middle, tables, weight, normed, attn, pieces)


def hidden_back_kernel(
    hidden_from,
    gate_from,
    up_from,
    cotan_from,
    gate_up_from,
    down_from,
    normed_from,
    weight_to,
    normed_to,
    hidden,
    gate_part,
    up_part,
    cotan,
    gate_up,
    down,
    normed,
    grads,
    weight_grad,
    normed_grad,
    gate_up_sem,
    down_sem,
    block_sem,
    whole_sem,
    out_sem,
    grad_sem,
):
    group, narrow = hidden.shape
    dp, cols, part_rows, _ = down_from.shape
    wide = weight_grad.shape[3]
    blocks = group // BLOCK
    depth = normed.shape[1] // cols

    def rows_of(m):
        return pl.ds(pl.multiple_of(m * BLOCK, BLOCK), BLOCK)

    def block_copies(m):
        rows = rows_of(m)
        pairs = ((cotan_from, cotan), (gate_from, gate_part), (up_from, up_part))
        return [
            pltpu.make_async_copy(a.at[rows, :], b.at[rows, :], block_sem.at[i, m])
            for i, (a, b) in enumerate(pairs)
        ]

    down_copies = load_columns(down_from, down, down_sem)
    for copy in block_copies(0):
        copy.start()
    gate_up_copy = pltpu.make_async_copy(gate_up_from, gate_up, gate_up_sem.at[0])
    gate_up_copy.start()
    for m in range(1, blocks):
        for copy in block_copies(m):
            copy.start()
    whole_copies = [
        pltpu.make_async_copy(hidden_from, hidden, whole_sem.at[0]),
        pltpu.make_async_copy(normed_from, normed, whole_sem.at[1]),
    ]
    for copy in whole_copies:
        copy.start()
    for copy in down_copies:
        copy.wait()

    def normed_out(m):
        rows = rows_of(m)
        return pltpu.make_async_copy(normed_grad.at[rows, :], normed_to.at[rows, :], out_sem.at[m])

    def weight_out(p, j):
        return pltpu.make_async_copy(weight_grad.at[p, j], weight_to.at[p, j], grad_sem.at[p, j])

    @pl.loop(0, blocks)
    def _(m):
        rows = rows_of(m)
        for copy in block_copies(m):
            copy.wait()
        grad = dot_nn(cotan[rows, :], down[:, :narrow])
        both = jnp.concatenate([grad * gate_part[rows, :], grad * up_part[rows, :]], axis=1)
        grads[rows, :] = both.astype(BF16)

    gate_up_copy.wait()

    @pl.loop(0, blocks)
    def _(m):
        rows = rows_of(m)
        normed_grad[rows, :] = dot_nt(grads[rows, :], gate_up[...]).astype(BF16)
        normed_out(m).start()

    for copy in whole_copies:
        copy.wait()

    @pl.loop(0, cols)
    def _(j):
        columns = pl.ds(pl.multiple_of(j * depth, depth), depth)
        gate_up_grad = dot_tn(normed[:, columns], grads[...]).astype(BF16)
        down_grad = dot_tn(cotan[:, columns], hidden[...]).astype(BF16)
        for p in range(dp):
            rows = slice(p * part_rows, (p + 1) * part_rows)
            weight_grad[p, j, :, : 2 * narrow] = gate_up_grad[rows, :]
            weight_grad[p, j, :, 2 * narrow : 3 * narrow] = down_grad[rows, :]
            if wide > 3 * narrow:
                weight_grad[p, j, :, 3 * narrow :] = jnp.zeros((part_rows, wide - 3 * narrow), BF16)
            weight_out(p, j).start()

    for m in range(blocks):
        normed_out(m).wait()
    for p in range(dp):
        for j in range(cols):
            weight_out(p, j).wait()


def hidden_back(hidden, gate_part, up_part, cotan, gate_up, down, normed):
    group, width = normed.shape
    dp, cols, part, _ = down.shape
    double = gate_up.shape[1]
    grad_shape = (dp, cols, part, double + down.shape[3])
    blocks = group // BLOCK
    dma = pltpu.SemaphoreType.DMA
    return pl.pallas_call(
        hidden_back_kernel,
        out_shape=(
            jax.ShapeDtypeStruct(grad_shape, BF16),
            jax.ShapeDtypeStruct((group, width), BF16),
        ),
        in_specs=[ANY] * 7,
        out_specs=(ANY,) * 2,
        scratch_shapes=[
            pltpu.VMEM(hidden.shape, BF16),
            pltpu.VMEM(gate_part.shape, F32),
            pltpu.VMEM(up_part.shape, F32),
            pltpu.VMEM(cotan.shape, BF16),
            pltpu.VMEM((width, double), BF16),
            pltpu.VMEM((width, down.shape[3]), BF16),
            pltpu.VMEM(normed.shape, BF16),
            pltpu.VMEM((group, double), BF16),
            pltpu.VMEM(grad_shape, BF16),
            pltpu.VMEM((group, width), BF16),
            dma((1,)),
            dma((dp, cols)),
            dma((3, blocks)),
            dma((2,)),
            dma((blocks,)),
            dma((dp, cols)),
        ],
        compiler_params=pltpu.CompilerParams(vmem_limit_bytes=VMEM_LIMIT),
        cost_estimate=cost(30),
        name="hidden_back",
    )(hidden, gate_part, up_part, cotan, gate_up, down, normed)


def split_kernel(whole, first, last):
    count, rows = whole.shape[1] - 1, whole.shape[0] * whole.shape[2]
    inner = first.shape[1] == count

    def part(k):
        return whole[:, k].reshape(rows, whole.shape[3]).astype(F32)

    for k in range(count):
        if inner:
            first[:, k, :] = part(k)
        else:
            first[k] = part(k)
    last[...] = part(count).T


def weights_split(whole, inner):
    dp, count, part, wide = whole.shape
    rows = min(part, 128)
    per = 128 // rows
    depth = dp * part
    count = count - 1
    if inner:
        shape, block, place = (depth, count, wide), (128, count, wide), lambda b: (b, 0, 0)
    else:
        shape, block, place = (count, depth, wide), (count, 128, wide), lambda b: (0, b, 0)
    return pl.pallas_call(
        split_kernel,
        grid=(depth // 128,),
        out_shape=(jax.ShapeDtypeStruct(shape, F32), jax.ShapeDtypeStruct((wide, depth), F32)),
        in_specs=[
            pl.BlockSpec(
                (per, count + 1, rows, wide),
                lambda b: (b * 128 // (per * part), 0, lax.rem(b, max(part // 128, 1)), 0),
            )
        ],
        out_specs=(pl.BlockSpec(block, place), pl.BlockSpec((wide, 128), lambda b: (0, b))),
        compiler_params=pltpu.CompilerParams(vmem_limit_bytes=VMEM_LIMIT),
        cost_estimate=cost(8),
        name="weight_gradients",
    )(whole)


def weights_whole(piece):
    return lax.all_gather(piece, "dp", axis=0)


def weights_sum(pieces):
    dp, cols, part, wide = pieces.shape
    piece = lax.psum_scatter(
        pieces.reshape(dp * cols * part, wide), "dp", scatter_dimension=0, tiled=True
    )
    return piece.reshape(cols, part, wide)


def make_body(sizes):
    cols = sizes["col"]

    def body(
        tokens,
        attention_norm_gain,
        attention_norm_bias,
        qkv_weight,
        qkv_bias,
        out_weight,
        feedforward_norm_gain,
        feedforward_norm_bias,
        gate_up_weight,
        down_weight,
        cotangent,
    ):
        my_row, my_col, my_dp = (lax.axis_index(name) for name in ("row", "col", "dp"))
        half, depth = tokens.shape
        own = half // cols
        tables = rope_tables(SEQ)
        vector = jnp.stack(
            [attention_norm_gain, attention_norm_bias, feedforward_norm_gain, feedforward_norm_bias]
        )
        vector = jnp.concatenate([vector, jnp.zeros_like(vector)])
        part = depth // sizes["dp"]

        def share_of(rows):
            return rows if part % 128 == 0 else lax.dynamic_slice_in_dim(rows, my_dp * part, part, 1)

        (
            normed_one,
            tokens_own,
            xhat_one,
            rstd_one,
            vectors,
            gate_up_piece,
            down_piece,
            attention_w,
        ) = start_part(
            tokens,
            vector,
            qkv_weight.transpose(1, 0, 2),
            share_of(out_weight),
            gate_up_weight,
            share_of(down_weight),
            sizes,
        )
        heads_in, attn, logs, branch_part, gate_up_piece, down_piece = attend(
            cols,
            normed_one,
            attention_w,
            qkv_bias.reshape(1, -1),
            tables,
            gate_up_piece,
            down_piece,
        )
        down_w = weights_whole(down_piece)
        narrow = down_weight.shape[0] // cols
        normed_two, middle, hidden, gate_part, up_part, gate_up_w, cotan_rows = middle_part(
            cols, branch_part, tokens_own, vectors, gate_up_piece, cotangent, sizes["dp"]
        )
        cotan_own = lax.dynamic_slice_in_dim(cotan_rows, my_row * half + my_col * own, own, 0)
        hidden_grad, normed_part = hidden_back(
            hidden, gate_part, up_part, cotan_rows, gate_up_w, down_w, normed_two
        )
        hidden_sum = weights_sum(hidden_grad)
        grad_middle, second, mixed_part = norm_two_back(
            cols, normed_part, middle, cotan_own, vectors, hidden, down_w
        )
        second = second.reshape(8, cols, depth).transpose(1, 0, 2)
        grad_block = lax.dynamic_slice(grad_middle, (my_row * half, my_col * depth), (half, depth))
        heads_grad, out_grad, normed_part, bias_part, hidden_sum = attend_back(
            cols,
            heads_in,
            logs,
            grad_middle,
            tables,
            attention_w,
            normed_one,
            attn,
            hidden_sum,
            narrow,
        )
        hidden_sum = lax.all_gather(hidden_sum, "dp", axis=0)
        input_grad, norms, attention_sum = sum_first(
            cols,
            normed_part,
            xhat_one,
            rstd_one,
            attention_norm_gain.reshape(1, -1),
            grad_block,
            heads_grad,
            out_grad,
            second,
        )
        mixed, attention_sum, small = sum_mixed(
            cols, mixed_part, middle, attention_sum, norms, bias_part, sizes["dp"]
        )
        grad_gate_up, grad_down = weights_split(hidden_sum, True)
        grad_qkv_weight, grad_out = weights_split(attention_sum, False)
        grad_qkv_weight = grad_qkv_weight.transpose(1, 0, 2)
        return (
            mixed,
            input_grad,
            small[0, :depth],
            small[1, :depth],
            grad_qkv_weight,
            small[0, depth:].reshape(3, -1),
            grad_out,
            small[2, :depth],
            small[3, :depth],
            grad_gate_up,
            grad_down,
        )

    return body


def solution(mesh):
    specs = (
        P(("dp", "row"), "col"),
        P("col"),
        P("col"),
        P("col", None, "row"),
        P(None, ("row", "col")),
        P("row", "col"),
        P("col"),
        P("col"),
        P("col", None, "row"),
        P("row", "col"),
    )
    return jax.shard_map(
        make_body(dict(mesh.shape)),
        mesh=mesh,
        in_specs=specs + (P(("dp", "row"), "col"),),
        out_specs=(P(("dp", "row"), "col"),) + specs,
        check_vma=False,
    )
```

```python
import functools

import jax
import jax.numpy as jnp
import numpy as np
from jax import lax
from jax.experimental import pallas as pl
from jax.experimental.pallas import tpu as pltpu
from jax.sharding import PartitionSpec as P

MODEL_WIDTH = 2048
HD = 64
ROT = 16
SEQ = 1024
EPSILON = 1e-05
ROPE_BASE = 10000.0
NEG_LARGE = -1e30
F32 = jnp.float32
BF16 = jnp.bfloat16
MESH = pl.DeviceIdType.MESH
VMEM_LIMIT = 56 * 1024 * 1024
SUBS = 8


def send(src, dst, send_sem, recv_sem, **where):
    return pltpu.make_async_remote_copy(
        src_ref=src,
        dst_ref=dst,
        send_sem=send_sem,
        recv_sem=recv_sem,
        device_id=where,
        device_id_type=MESH,
    )


def enter(cols, everyone=False, dp=1):
    r, c = lax.axis_index("row"), lax.axis_index("col")
    barrier = pltpu.get_barrier_semaphore()
    pl.semaphore_signal(barrier, inc=1, device_id={"row": 1 - r}, device_id_type=MESH)
    if everyone:
        for k in range(1, cols):
            pl.semaphore_signal(
                barrier, inc=1, device_id={"col": lax.rem(c + k, cols)}, device_id_type=MESH
            )
        for k in range(1, dp):
            pl.semaphore_signal(
                barrier,
                inc=1,
                device_id={"dp": lax.rem(lax.axis_index("dp") + k, dp)},
                device_id_type=MESH,
            )
        pl.semaphore_wait(barrier, cols + dp - 1)
        return

    @pl.when(c > 0)
    def _():
        pl.semaphore_signal(barrier, inc=1, device_id={"col": c - 1}, device_id_type=MESH)

    @pl.when(c < cols - 1)
    def _():
        pl.semaphore_signal(barrier, inc=1, device_id={"col": c + 1}, device_id_type=MESH)

    inner = (c > 0) & (c < cols - 1)

    @pl.when(inner)
    def _():
        pl.semaphore_wait(barrier, 3)

    @pl.when(jnp.logical_not(inner))
    def _():
        pl.semaphore_wait(barrier, 2)


LAG = 3
BLOCK = 256
PACE = 6


class Reduce:
    def __init__(self, cols, subs, spot, part, twin, going, coming, sems, add=None):
        self.cols, self.subs, self.spot, self.add = cols, subs, spot, add
        self.part, self.twin, self.going, self.coming = part, twin, going, coming
        self.twin_send, self.twin_recv, self.send, self.recv = sems
        self.r, self.c = lax.axis_index("row"), lax.axis_index("col")
        self.half = part.shape[0] // 2
        self.per_sub = cols - 1
        self.landing = LAG * (cols - 1)
        self.slots = self.per_sub * (subs - 1) + self.landing + 1

    def place(self, d, s, base=0):
        row, rows, column, columns = self.spot(d, s)
        if not isinstance(column, int):
            column = pl.multiple_of(column, 128)
        return pl.ds(pl.multiple_of(base + row, 16), rows), pl.ds(column, columns)

    def twin_copy(self, d, s):
        return send(
            self.part.at[self.place(d, s, (1 - self.r) * self.half)],
            self.twin.at[self.place(d, s)],
            self.twin_send.at[d, s],
            self.twin_recv.at[d, s],
            row=1 - self.r,
        )

    def start(self):
        @pl.loop(0, self.subs)
        def _(s):
            for j in range(self.cols):
                self.twin_copy(self.cols - 1 - j // 2 if j % 2 == 0 else j // 2, s).start()

    def hop(self, way, d, s):
        place = self.place(d, s)
        return send(
            self.going.at[(way,) + place],
            self.coming.at[(way,) + place],
            self.send.at[way, d, s],
            self.recv.at[way, d, s],
            col=self.c + 1 if way == 0 else self.c - 1,
        )

    def own(self, d, s):
        self.twin_copy(d, s).wait_recv()
        value = self.part[self.place(d, s, self.r * self.half)].astype(F32)
        value = value + self.twin[self.place(d, s)].astype(F32)
        if self.add is not None:
            value = value + self.add(d, s)
        return value

    def pass_on(self, way, d, s):
        place = (way,) + self.place(d, s)
        first = 0 if way == 0 else self.cols - 1

        @pl.when(self.c == first)
        def _():
            self.going[place] = self.own(d, s).astype(BF16)

        @pl.when(self.c != first)
        def _():
            value = self.own(d, s)
            self.hop(way, d, s).wait_recv()
            self.going[place] = (value + self.coming[place].astype(F32)).astype(BF16)

        self.hop(way, d, s).start()

    def slot(self, t):
        for way in range(2):
            made = self.c if way == 0 else self.cols - 1 - self.c
            event = t - LAG * made

            @pl.when((event >= 0) & (event < self.per_sub * self.subs))
            def _():
                s, j = lax.div(event, self.per_sub), lax.rem(event, self.per_sub)
                d = self.cols - 1 - j if way == 0 else j

                @pl.when(self.c < d if way == 0 else self.c > d)
                def _():
                    self.pass_on(way, d, s)

    def landed(self, t, do):
        after = t - self.landing

        @pl.when((after >= 0) & (lax.rem(after + self.per_sub * self.cols, self.per_sub) == 0))
        def _():
            s = lax.div(after, self.per_sub)

            @pl.when(s < self.subs)
            def _():
                do(s)

    def land(self, s, total):
        place = self.place(self.c, s)
        total[...] = self.own(self.c, s)

        @pl.when(self.c > 0)
        def _():
            self.hop(0, self.c, s).wait_recv()
            total[...] += self.coming[(0,) + place].astype(F32)

        @pl.when(self.c < self.cols - 1)
        def _():
            self.hop(1, self.c, s).wait_recv()
            total[...] += self.coming[(1,) + place].astype(F32)

    def finish(self):
        @pl.loop(0, self.subs)
        def _(s):
            for d in range(self.cols):
                self.twin_copy(d, s).wait_send()

                @pl.when(self.c < d)
                def _():
                    self.hop(0, d, s).wait_send()

                @pl.when(self.c > d)
                def _():
                    self.hop(1, d, s).wait_send()

    @staticmethod
    def scratch(cols, subs, half, width):
        return [
            pltpu.VMEM((half, width), BF16),
            pltpu.VMEM((2, half, width), BF16),
            pltpu.VMEM((2, half, width), BF16),
            pltpu.SemaphoreType.DMA((cols, subs)),
            pltpu.SemaphoreType.DMA((cols, subs)),
            pltpu.SemaphoreType.DMA((2, cols, subs)),
            pltpu.SemaphoreType.DMA((2, cols, subs)),
        ]


class Gather:
    def __init__(self, cols, subs, spot, whole, sems, pair=True):
        self.cols, self.subs, self.spot, self.whole, self.pair = cols, subs, spot, whole, pair
        self.send, self.recv, self.pair_send, self.pair_recv = sems
        self.r, self.c = lax.axis_index("row"), lax.axis_index("col")

    def hop(self, way, source, s):
        where = self.whole.at[self.spot(self.r, source, s)]
        return send(
            where,
            where,
            self.send.at[way, source, s],
            self.recv.at[way, source, s],
            col=self.c + 1 if way == 0 else self.c - 1,
        )

    def across(self, r, source, s):
        where = self.whole.at[self.spot(r, source, s)]
        return send(
            where, where, self.pair_send.at[source, s], self.pair_recv.at[source, s], row=1 - self.r
        )

    def start(self, s):
        @pl.when(self.c < self.cols - 1)
        def _():
            self.hop(0, self.c, s).start()

        @pl.when(self.c > 0)
        def _():
            self.hop(1, self.c, s).start()

        if self.pair:
            self.across(self.r, self.c, s).start()

    def relay(self, s, k):
        @pl.when(self.c >= k)
        def _():
            self.hop(0, self.c - k, s).wait_recv()

            @pl.when(self.c < self.cols - 1)
            def _():
                self.hop(0, self.c - k, s).start()

            if self.pair:
                self.across(self.r, self.c - k, s).start()

        @pl.when(self.c + k < self.cols)
        def _():
            self.hop(1, self.c + k, s).wait_recv()

            @pl.when(self.c > 0)
            def _():
                self.hop(1, self.c + k, s).start()

            if self.pair:
                self.across(self.r, self.c + k, s).start()

    def slot(self, t, begin, step):
        for k in range(1, self.cols):
            after = t - begin - LAG * k

            @pl.when((after >= 0) & (lax.rem(after + step * LAG * self.cols * 8, step) == 0))
            def _():
                s = lax.div(after, step)

                @pl.when(s < self.subs)
                def _():
                    self.relay(s, k)

    def finish(self):
        @pl.loop(0, self.subs)
        def _(s):
            for source in range(self.cols):
                if self.pair:
                    self.across(1 - self.r, source, s).wait_recv()
                    self.across(self.r, source, s).wait_send()

                @pl.when((self.c >= source) & (self.c < self.cols - 1))
                def _():
                    self.hop(0, source, s).wait_send()

                @pl.when((self.c <= source) & (self.c > 0))
                def _():
                    self.hop(1, source, s).wait_send()

    @staticmethod
    def scratch(cols, subs):
        return [
            pltpu.SemaphoreType.DMA((2, cols, subs)),
            pltpu.SemaphoreType.DMA((2, cols, subs)),
            pltpu.SemaphoreType.DMA((cols, subs)),
            pltpu.SemaphoreType.DMA((cols, subs)),
        ]


class Exchange:
    def __init__(self, axis, size, source, target, sems):
        self.axis, self.size, self.source, self.target = axis, size, source, target
        self.send, self.recv, self.local = sems
        self.c = lax.axis_index(axis)

    def peer(self, k):
        if self.size == 4 and k != 2:
            return self.c + 1 - 2 * lax.rem(self.c, 2) if k == 1 else 3 - self.c
        return lax.rem(self.c + k, self.size)

    def hop(self, k):
        to = self.peer(k)
        return send(
            self.source.at[to],
            self.target.at[self.c],
            self.send.at[k - 1],
            self.recv.at[k - 1],
            **{self.axis: to},
        )

    def own(self):
        return pltpu.make_async_copy(
            self.source.at[self.c], self.target.at[self.c], self.local.at[0]
        )

    def start(self):
        for k in range(1, self.size):
            self.hop(k).start()
        self.own().start()

    def finish(self):
        self.own().wait()
        for k in range(1, self.size):
            self.hop(k).wait_recv()
        for k in range(1, self.size):
            self.hop(k).wait_send()

    @staticmethod
    def scratch(size):
        return [
            pltpu.SemaphoreType.DMA((size - 1,)),
            pltpu.SemaphoreType.DMA((size - 1,)),
            pltpu.SemaphoreType.DMA((1,)),
        ]


class Broadcast:
    def __init__(self, dp, units, source, target, sems):
        self.dp, self.units, self.source, self.target = dp, units, source, target
        self.send, self.recv = sems
        self.me = lax.axis_index("dp")
        self.near = self.me + 1 - 2 * lax.rem(self.me, 2)
        self.far = lax.rem(self.me + 2, dp)
        self.square = dp == 4

    def hop(self, i, u):
        if self.square:
            to = self.near if i == 0 else self.far
        else:
            to = lax.rem(self.me + i + 1, self.dp)
        return send(
            self.source(u), self.target(self.me, u), self.send.at[i, u], self.recv.at[i, u], dp=to
        )

    def across(self, u):
        low = u < self.units // 2
        where = self.target(self.near if low else self.far, u)
        return send(
            where,
            where,
            self.send.at[2, u],
            self.recv.at[2, u],
            dp=self.far if low else self.near,
        )

    def hops(self):
        return 2 if self.square else self.dp - 1

    def start(self, units=None):
        half = self.units // 2
        for n in range(self.units) if units is None else units:
            for i in range(self.hops()):
                u = (n + half) % self.units if self.square and i == 1 and units is None else n
                self.hop(i, u).start()

    def forward(self, u):
        if self.square:
            self.hop(0 if u < self.units // 2 else 1, u).wait_recv()
            self.across(u).start()

    def finish(self):
        for u in range(self.units):
            for i in range(self.hops()):
                if not self.square or (i == 0) != (u < self.units // 2):
                    self.hop(i, u).wait_recv()
                self.hop(i, u).wait_send()
            if self.square:
                self.across(u).wait()

    @staticmethod
    def scratch(dp, units):
        return [
            pltpu.SemaphoreType.DMA((max(dp - 1, 1), units)),
            pltpu.SemaphoreType.DMA((max(dp - 1, 1), units)),
        ]


ANY = pl.BlockSpec(memory_space=pl.ANY)


def staged_call(kernel, args, out_shape, in_specs, out_specs, scratch_shapes, loads, stores, **kinds):
    counts = len(args), len(out_shape)
    dma = pltpu.SemaphoreType.DMA
    buffers = [pltpu.VMEM(shape, args[i].dtype) for i, shape, _ in loads]
    buffers += [pltpu.VMEM(out_shape[j].shape, out_shape[j].dtype) for j in stores]
    in_specs, out_specs = list(in_specs), list(out_specs)
    for i, _, _ in loads:
        in_specs[i] = ANY
    for j in stores:
        out_specs[j] = ANY

    def run(*refs):
        ins, outs = list(refs[: counts[0]]), list(refs[counts[0] : sum(counts)])
        own = refs[len(refs) - len(buffers) - 2 :]
        in_sem, out_sem = own[-2:]
        coming, going = {}, {}
        for n, (i, _, part) in enumerate(loads):
            source = ins[i] if part is None else ins[i].at[part()]
            coming[i] = pltpu.make_async_copy(source, own[n], in_sem.at[n])
            ins[i] = own[n]
        for n, j in enumerate(stores):
            buffer = own[len(loads) + n]
            going[j] = pltpu.make_async_copy(buffer, outs[j], out_sem.at[n])
            outs[j] = buffer
        for copy in coming.values():
            copy.start()

        def load(*which):
            for i in which:
                coming[i].wait()

        def store(*which):
            for j in which:
                going[j].start()

        kernel(*ins, *outs, *refs[sum(counts) : len(refs) - len(own)], load=load, store=store)
        for copy in going.values():
            copy.wait()

    return pl.pallas_call(
        run,
        out_shape=tuple(out_shape),
        in_specs=in_specs,
        out_specs=tuple(out_specs),
        scratch_shapes=list(scratch_shapes)
        + buffers
        + [dma((max(len(loads), 1),)), dma((max(len(stores), 1),))],
        **kinds,
    )(*args)


def load_columns(weight, whole, sem):
    dp, cols, part, _ = weight.shape
    copies = [
        pltpu.make_async_copy(
            weight.at[p, j],
            whole.at[pl.ds((j * dp + p) * part, part), :],
            sem.at[p, j],
        )
        for p in range(dp)
        for j in range(cols)
    ]
    for copy in copies:
        copy.start()
    return copies


def dot_nt(a, b):
    return lax.dot_general(a, b, (((1,), (1,)), ((), ())), preferred_element_type=F32)


def dot_tn(a, b):
    return lax.dot_general(a, b, (((0,), (0,)), ((), ())), preferred_element_type=F32)


def dot_nn(a, b):
    return jnp.dot(a, b, preferred_element_type=F32)


def moments(rows):
    mean = jnp.mean(rows, axis=1, keepdims=True)
    centered = rows - mean
    return centered, lax.rsqrt(jnp.mean(centered * centered, axis=1, keepdims=True) + EPSILON)


def cost(us):
    return pl.CostEstimate(flops=us * 10**9, bytes_accessed=10**7, transcendentals=0)


def params(number):
    return pltpu.CompilerParams(
        collective_id=number, has_side_effects=True, vmem_limit_bytes=VMEM_LIMIT
    )


VM = pl.BlockSpec(memory_space=pltpu.VMEM)


def row_spot(own, step, half, width):
    def spot(r, source, s):
        return pl.ds(pl.multiple_of(r * half + source * own + s * step, 16), step), pl.ds(0, width)

    return spot


COTANGENT_SLOT = 14


def middle_kernel(
    cols,
    part,
    tokens_own,
    vectors,
    piece,
    cotan,
    normed_to,
    middle_to,
    hidden_to,
    gate_to,
    up_to,
    weight_to,
    cotan_to,
    normed,
    middle,
    hidden,
    gate_part,
    up_part,
    weight,
    cotan_rows,
    total,
    own_sem,
    out_sem,
    block_sem,
    *scratch,
    load,
    store
):
    group, width = part.shape
    half = group // 2
    own = half // cols
    step = own // SUBS
    depth = cotan.shape[1]
    rows_each = half // SUBS
    _, part_rows, double = piece.shape
    narrow = double // 2
    dp = weight.shape[0] // cols // part_rows
    me = lax.axis_index("dp")
    enter(cols, everyone=True, dp=dp)
    load(0)
    summing = Reduce(
        cols, SUBS, lambda d, s: (d * own + s * step, step, 0, width), part, *scratch[:3], scratch[3:7]
    )
    summing.start()
    spread = Gather(cols, SUBS, row_spot(own, step, half, width), normed, scratch[7:11])

    def cotan_spot(r, source, s):
        rows = pl.ds(pl.multiple_of(r * half + s * rows_each, 16), rows_each)
        return rows, pl.ds(pl.multiple_of(source * depth, 128), depth)

    cotan_spread = Gather(cols, SUBS, cotan_spot, cotan_rows, scratch[11:15])

    def weight_rows(p, j):
        return weight.at[pl.ds(pl.multiple_of((j * dp + p) * part_rows, 16), part_rows), :]

    rider = Broadcast(dp, cols, lambda u: piece.at[u], weight_rows, scratch[15:17])
    rider.start()
    own_copies = [
        pltpu.make_async_copy(piece.at[j], weight_rows(me, j), own_sem.at[j]) for j in range(cols)
    ]
    for copy in own_copies:
        copy.start()
    load(1, 2, 4)

    def land(s):
        summing.land(s, total)
        rows = pl.ds(pl.multiple_of(s * step, step), step)
        state = tokens_own[rows, :].astype(F32) + total[...]
        middle[rows, :] = state
        centered, rstd = moments(state)
        result = centered * rstd * vectors[2:3, :] + vectors[3:4, :]
        normed[spread.spot(spread.r, spread.c, s)] = result.astype(BF16)
        spread.start(s)

    def cotan_slot(t):
        after = t - COTANGENT_SLOT

        @pl.when((after >= 0) & (lax.rem(after + 60, 3) == 0) & (after < 3 * SUBS))
        def _():
            s = lax.div(after, 3)
            rows = pl.ds(pl.multiple_of(s * rows_each, 16), rows_each)
            cotan_rows[cotan_spot(spread.r, spread.c, s)] = cotan[rows, :]
            cotan_spread.start(s)

        cotan_spread.slot(t, COTANGENT_SLOT, 3)

    first = summing.slots + LAG * (cols - 1)
    last = COTANGENT_SLOT + 3 * (SUBS - 1) + LAG * (cols - 1) + 1
    blocks = group // BLOCK

    @pl.loop(0, first)
    def _(t):
        summing.slot(t)
        summing.landed(t, land)
        spread.slot(t, summing.landing, summing.per_sub)
        cotan_slot(t)
        for u in range(cols):

            @pl.when(t == 8 + 6 * (u % 2))
            def _():
                rider.forward(u)

    spread.finish()
    normed_out = pltpu.make_async_copy(normed, normed_to, out_sem.at[0])
    normed_out.start()
    middle_out = pltpu.make_async_copy(middle, middle_to, out_sem.at[1])
    middle_out.start()
    for copy in own_copies:
        copy.wait()
    rider.finish()
    weight_out = pltpu.make_async_copy(weight, weight_to, out_sem.at[2])
    weight_out.start()

    def block_out(m):
        rows = pl.ds(pl.multiple_of(m * BLOCK, BLOCK), BLOCK)
        pairs = ((hidden, hidden_to), (gate_part, gate_to), (up_part, up_to))
        return [
            pltpu.make_async_copy(a.at[rows, :], b.at[rows, :], block_sem.at[i, m])
            for i, (a, b) in enumerate(pairs)
        ]

    @pl.loop(0, max(last - first, blocks))
    def _(m):
        @pl.when(m < blocks)
        def _():
            rows = pl.ds(pl.multiple_of(m * BLOCK, BLOCK), BLOCK)
            both = dot_nn(normed[rows, :], weight[...])
            gate, up = both[:, :narrow], both[:, narrow:]
            sig = 1.0 / (1.0 + jnp.exp(-gate))
            active = gate * sig
            hidden[rows, :] = (active * up).astype(BF16)
            up_part[rows, :] = active
            gate_part[rows, :] = up * sig * (1.0 + gate * (1.0 - sig))
            for copy in block_out(m):
                copy.start()

        cotan_slot(first + m)

    cotan_spread.finish()
    cotan_out = pltpu.make_async_copy(cotan_rows, cotan_to, out_sem.at[3])
    cotan_out.start()
    summing.finish()
    for m in range(blocks):
        for copy in block_out(m):
            copy.wait()
    for copy in (normed_out, middle_out, weight_out, cotan_out):
        copy.wait()


def middle_part(cols, part, tokens_own, vectors, piece, cotan, dp):
    group, width = part.shape
    _, part_rows, double = piece.shape
    narrow = double // 2
    blocks = group // BLOCK
    dma = pltpu.SemaphoreType.DMA
    outs = (
        ((group, width), BF16),
        (tokens_own.shape, F32),
        ((group, narrow), BF16),
        ((group, narrow), F32),
        ((group, narrow), F32),
        ((dp * cols * part_rows, double), BF16),
        ((group, width), BF16),
    )
    args = (part, tokens_own, vectors, piece, cotan)
    return staged_call(
        functools.partial(middle_kernel, cols),
        args,
        out_shape=tuple(jax.ShapeDtypeStruct(*out) for out in outs),
        in_specs=[VM] * 3 + [ANY, VM],
        out_specs=[ANY] * len(outs),
        loads=[(i, args[i].shape, None) for i in (0, 1, 2, 4)],
        stores=(),
        scratch_shapes=[pltpu.VMEM(*out) for out in outs]
        + [
            pltpu.VMEM((group // 2 // cols // SUBS, width), F32),
            dma((cols,)),
            dma((4,)),
            dma((3, blocks)),
        ]
        + Reduce.scratch(cols, SUBS, group // 2, width)
        + Gather.scratch(cols, SUBS) * 2
        + Broadcast.scratch(dp, cols),
        compiler_params=params(2),
        cost_estimate=cost(95),
        name="middle_gate_up",
    )


def norm_two_back_kernel(
    cols,
    part,
    middle,
    cotan_own,
    vectors,
    hidden,
    weight,
    grads,
    sums,
    mixed_part,
    down,
    sem,
    *scratch,
    load,
    store
):
    narrow = hidden.shape[1]
    copies = load_columns(weight, down, sem)
    half, width = part.shape[0] // 2, part.shape[1]
    own = half // cols
    step = own // SUBS
    total = scratch[11]
    enter(cols)
    load(0)
    summing = Reduce(
        cols, SUBS, lambda d, s: (d * own + s * step, step, 0, width), part, *scratch[:3], scratch[3:7]
    )
    spread = Gather(cols, SUBS, row_spot(own, step, half, width), grads, scratch[7:11])
    summing.start()
    blocks = part.shape[0] // BLOCK
    for copy in copies:
        copy.wait()
    load(1, 2, 3, 4)
    sums[...] = jnp.zeros_like(sums)

    def land(s):
        summing.land(s, total)
        rows = pl.ds(pl.multiple_of(s * step, step), step)
        centered, rstd = moments(middle[rows, :])
        xhat = centered * rstd
        grad = total[...]
        sums[0:1, :] += jnp.sum(grad * xhat, axis=0, keepdims=True)
        sums[1:2, :] += jnp.sum(grad, axis=0, keepdims=True)
        scaled = grad * vectors[2:3, :]
        inner = (
            scaled
            - jnp.mean(scaled, axis=1, keepdims=True)
            - xhat * jnp.mean(scaled * xhat, axis=1, keepdims=True)
        )
        result = cotan_own[rows, :].astype(F32) + rstd * inner
        grads[spread.spot(spread.r, spread.c, s)] = result.astype(BF16)
        spread.start(s)

    @pl.loop(0, summing.slots + LAG * (cols - 1))
    def _(t):
        summing.slot(t)
        summing.landed(t, land)
        spread.slot(t, summing.landing, summing.per_sub)

        @pl.when((lax.rem(t, PACE) == PACE - 1) & (t < PACE * blocks))
        def _():
            rows = pl.ds(pl.multiple_of(lax.div(t, PACE) * BLOCK, BLOCK), BLOCK)
            result = dot_nt(hidden[rows, :], down[:, :narrow])
            mixed_part[rows, :] = result.astype(BF16)

    store(2)
    spread.finish()
    store(0)
    summing.finish()


def norm_two_back(cols, part, middle, cotan, vectors, hidden, weight):
    group, width = part.shape
    tall = weight.shape[3]
    own = group // 2 // cols

    def own_rows():
        row = lax.axis_index("row") * (group // 2) + lax.axis_index("col") * own
        return pl.ds(pl.multiple_of(row, own), own)

    args = (part, middle, cotan, vectors, hidden, weight)
    return staged_call(
        functools.partial(norm_two_back_kernel, cols),
        args,
        out_shape=(
            jax.ShapeDtypeStruct((group, width), BF16),
            jax.ShapeDtypeStruct((8, width), F32),
            jax.ShapeDtypeStruct((group, width), BF16),
        ),
        in_specs=[VM] * 5 + [ANY],
        out_specs=[VM] * 3,
        loads=[(i, args[i].shape, None) for i in (0, 1)]
        + [(2, (own, width), own_rows)]
        + [(i, args[i].shape, None) for i in (3, 4)],
        stores=(0, 2),
        scratch_shapes=[pltpu.VMEM((width, tall), BF16), pltpu.SemaphoreType.DMA(weight.shape[:2])]
        + Reduce.scratch(cols, SUBS, group // 2, width)
        + Gather.scratch(cols, SUBS)
        + [pltpu.VMEM((group // 2 // cols // SUBS, width), F32)],
        compiler_params=params(3),
        cost_estimate=cost(60),
        name="grad_sum_norm_gather",
    )


def mixed_sum(cols, part, middle, scratch):
    half, width = part.shape[0] // 2, part.shape[1]
    step, depth, own = half // SUBS, width // cols, half // cols
    c = lax.axis_index("col")

    def add(d, s):
        inside = s * step - c * own
        rows = pl.ds(pl.multiple_of(lax.rem(s * step, own), step), step)
        mine = middle[rows, pl.ds(pl.multiple_of(d * depth, 128), depth)]
        return jnp.where((inside >= 0) & (inside < own), mine, 0.0)

    return Reduce(
        cols,
        SUBS,
        lambda d, s: (s * step, step, d * depth, depth),
        part,
        *scratch[:3],
        scratch[3:7],
        add=add,
    )


MIXED_SLOT = 22
ARRANGE_SLOT = 24


def last_kernel(
    cols,
    part,
    xhat,
    rstd,
    gain,
    grad_middle,
    heads_grad,
    out_grad,
    second,
    mixed_part,
    middle,
    hidden_piece,
    bias,
    result,
    mixed,
    small,
    attention_all,
    hidden_all,
    total,
    grad,
    mine,
    theirs,
    sums,
    landed,
    slices,
    own_norms,
    pair_norms,
    arranged,
    own_small,
    all_small,
    out_sem,
    in_sem,
    pair_sem,
    small_send,
    small_recv,
    own_sem,
    *sems,
    load,
    store
):
    half, width = part.shape[0] // 2, part.shape[1]
    step, depth = half // SUBS, width // cols
    pairs, dp = heads_grad.shape[:2]
    two = heads_grad.shape[4] // 3
    narrow = sums.shape[2] // 4
    rows_each = hidden_piece.shape[1] // 2
    weights = hidden_piece.shape[0]
    enter(cols, everyone=True, dp=dp)
    r, c, me = (lax.axis_index(name) for name in ("row", "col", "dp"))
    load(0)
    summing = Reduce(
        cols, SUBS, lambda d, s: (s * step, step, d * depth, depth), part, *sems[:3], sems[3:7]
    )
    summing.start()
    rider = Exchange("col", cols, sums, landed, sems[14:17])
    names = Exchange("col", cols, second, slices, sems[17:20])
    names.start()

    def hidden_rows(u):
        return u % weights, pl.ds(u // weights * rows_each, rows_each)

    hidden_cast = Broadcast(
        dp,
        2 * weights,
        lambda u: hidden_piece.at[hidden_rows(u)],
        lambda p, u: hidden_all.at[(p,) + hidden_rows(u)],
        sems[20:22],
    )
    attention_cast = Broadcast(
        dp, 4, lambda u: arranged.at[u], lambda p, u: attention_all.at[p, u], sems[22:24]
    )
    hidden_own = pltpu.make_async_copy(hidden_piece, hidden_all.at[me], own_sem.at[0])
    attention_own = pltpu.make_async_copy(arranged, attention_all.at[me], own_sem.at[1])
    hidden_cast.start()
    hidden_own.start()
    load(5, 6)

    def over_dp(ref, to):
        value = ref[0, to].astype(F32)
        for p in range(1, dp):
            value = value + ref[p, to].astype(F32)
        return value.astype(BF16)

    def fill(to, target):
        for pair in range(pairs):
            value = over_dp(heads_grad.at[pair], to)
            for k in range(3):
                first = k * narrow + pair * two
                target[:, first : first + two] = value[:, k * two : (k + 1) * two]
        target[:, 3 * narrow :] = over_dp(out_grad, to)

    for k in range(1, cols):
        to = rider.peer(k)
        fill(to, sums.at[to])
        rider.hop(k).start()
    fill(c, landed.at[c])
    own_norms[...] = jnp.zeros_like(own_norms)
    load(8, 9)
    mixing = mixed_sum(cols, mixed_part, middle, sems[7:14])
    mixing.start()
    load(1, 2, 4)

    def land(s):
        summing.land(s, total)
        rows = pl.ds(pl.multiple_of(s * step, step), step)
        grad[rows, :] = total[...]
        standard = xhat[rows, :]
        own_norms[0:1, :] += jnp.sum(total[...] * standard, axis=0, keepdims=True)
        own_norms[1:2, :] += jnp.sum(total[...], axis=0, keepdims=True)

    def land_mixed(s):
        mixing.land(s, total)
        mixed[pl.ds(pl.multiple_of(s * step, step), step), :] = total[...].astype(BF16)

    def arrange():
        for k in range(1, cols):
            rider.hop(k).wait_recv()
        for k in range(4):
            for j in range(cols):
                arranged[k, :, j * narrow : (j + 1) * narrow] = landed[
                    j, :, k * narrow : (k + 1) * narrow
                ]
        attention_cast.start()
        attention_own.start()

    @pl.loop(0, summing.slots)
    def _(t):
        summing.slot(t)
        summing.landed(t, land)
        mixing.slot(t - MIXED_SLOT)
        mixing.landed(t - MIXED_SLOT, land_mixed)
        for u in range(weights):

            @pl.when(t == 8 + 6 * u)
            def _():
                hidden_cast.forward(u)
                hidden_cast.forward(weights + u)

        @pl.when(t == ARRANGE_SLOT)
        def _():
            arrange()

    lanes = lax.broadcasted_iota(jnp.int32, (128, 128), 1)
    for s in range(half // 128):
        rows = slice(s * 128, (s + 1) * 128)
        scaled = grad[rows, :] * gain[0:1, :]
        one = jnp.sum(scaled, axis=1, keepdims=True)
        two_sum = jnp.sum(scaled * xhat[rows, :], axis=1, keepdims=True)
        both = jnp.where(lanes == 0, one, jnp.where(lanes == 1, two_sum, 0.0))
        mine[:, rows] = both.T[0:8, :]

    def exchange_sums(k):
        return send(
            mine, theirs.at[k - 1], out_sem.at[k - 1], in_sem.at[k - 1], col=lax.rem(c + k, cols)
        )

    for k in range(1, cols):
        exchange_sums(k).start()
    names.finish()
    shift = slices[0]
    for j in range(1, cols):
        shift = shift + slices[j]
    own_norms[2:4, :] = shift[0:2, :]
    across = send(own_norms, pair_norms, pair_sem.at[0], pair_sem.at[1], row=1 - r)
    across.start()

    @pl.loop(summing.slots, MIXED_SLOT + mixing.slots)
    def _(t):
        mixing.slot(t - MIXED_SLOT)
        mixing.landed(t - MIXED_SLOT, land_mixed)
        for u in range(2):

            @pl.when(t == summing.slots + 6 + 8 * u)
            def _():
                attention_cast.forward(u)
                attention_cast.forward(2 + u)

    across.wait()
    own_small[:, :depth] = own_norms[...] + pair_norms[...]
    own_small[:, depth:] = bias[...]
    all_small[me] = own_small[...]

    def hop(k):
        to = lax.rem(me + k, dp)
        return send(
            own_small, all_small.at[me], small_send.at[k - 1], small_recv.at[k - 1], dp=to
        )

    for k in range(1, dp):
        hop(k).start()
    for k in range(1, cols):
        exchange_sums(k).wait_recv()
    for s in range(half // 128):
        rows = slice(s * 128, (s + 1) * 128)
        both = mine[:, rows]
        for k in range(1, cols):
            both = both + theirs[k - 1, :, rows]
        both = jnp.concatenate([both, jnp.zeros((120, 128), F32)], axis=0).T / (depth * cols)
        scaled = grad[rows, :] * gain[0:1, :]
        inner = scaled - both[:, 0:1] - xhat[rows, :] * both[:, 1:2]
        result[rows, :] = grad_middle[rows, :].astype(F32) + rstd[rows, 0:1] * inner
    store(0, 1)
    for k in range(1, dp):
        hop(k).wait()
    value = all_small[0]
    for p in range(1, dp):
        value = value + all_small[p]
    small[...] = value
    for k in range(1, cols):
        exchange_sums(k).wait_send()
        rider.hop(k).wait_send()
    summing.finish()
    mixing.finish()
    hidden_own.wait()
    attention_own.wait()
    hidden_cast.finish()
    attention_cast.finish()


def last_part(
    cols, part, xhat, rstd, gain, grad_middle, heads_grad, out_grad, second, mixed_part, middle, piece, bias
):
    group, width = part.shape
    half, depth = group // 2, width // cols
    dp, _, rows, narrow = out_grad.shape
    small = (8, depth + bias.shape[1])
    hops = max(dp - 1, 1)
    dma = pltpu.SemaphoreType.DMA

    def own_block():
        row = lax.axis_index("row") * half
        column = lax.axis_index("col") * depth
        return pl.ds(pl.multiple_of(row, half), half), pl.ds(pl.multiple_of(column, 128), depth)

    args = (
        part,
        xhat,
        rstd,
        gain,
        grad_middle,
        heads_grad,
        out_grad,
        second,
        mixed_part,
        middle,
        piece,
        bias,
    )
    return staged_call(
        functools.partial(last_kernel, cols),
        args,
        out_shape=(
            jax.ShapeDtypeStruct((half, depth), F32),
            jax.ShapeDtypeStruct((half, depth), BF16),
            jax.ShapeDtypeStruct(small, F32),
            jax.ShapeDtypeStruct((dp, 4, rows, cols * narrow), BF16),
            jax.ShapeDtypeStruct((dp,) + piece.shape, BF16),
        ),
        in_specs=[VM] * 10 + [ANY, VM],
        out_specs=[VM] * 3 + [ANY] * 2,
        loads=[(i, args[i].shape, None) for i in (0, 5, 6, 8, 9, 1, 2)]
        + [(4, (half, depth), own_block)],
        stores=(0, 1),
        scratch_shapes=[
            pltpu.VMEM((half // SUBS, depth), F32),
            pltpu.VMEM((half, depth), F32),
            pltpu.VMEM((8, half), F32),
            pltpu.VMEM((cols - 1, 8, half), F32),
            pltpu.VMEM((cols, rows, 4 * narrow), BF16),
            pltpu.VMEM((cols, rows, 4 * narrow), BF16),
            pltpu.VMEM((cols, 8, depth), F32),
            pltpu.VMEM((8, depth), F32),
            pltpu.VMEM((8, depth), F32),
            pltpu.VMEM((4, rows, cols * narrow), BF16),
            pltpu.VMEM(small, F32),
            pltpu.VMEM((dp,) + small, F32),
            dma((cols - 1,)),
            dma((cols - 1,)),
            dma((2,)),
            dma((hops,)),
            dma((hops,)),
            dma((2,)),
        ]
        + Reduce.scratch(cols, SUBS, half, width) * 2
        + Exchange.scratch(cols) * 2
        + Broadcast.scratch(dp, 2 * piece.shape[0])
        + Broadcast.scratch(dp, 4),
        compiler_params=params(5),
        cost_estimate=cost(110),
        name="input_grad_mixed_sum",
    )


def start_kernel(
    cols,
    tokens,
    vector,
    heads_from,
    out_from,
    gate_up_from,
    down_from,
    normed,
    tokens_own,
    xhat,
    rstd,
    vectors,
    gate_up_piece,
    down_piece,
    attention_w,
    heads,
    out,
    gate_up,
    down,
    pieces,
    landed,
    full,
    in_sem,
    own_sem,
    pair_send,
    pair_recv,
    *sems
):
    half, depth = tokens.shape
    width = depth * cols
    step = half // cols
    dp, _, part, wide = attention_w.shape
    narrow = wide // 4
    tall = down.shape[0] // cols
    r, c, me = (lax.axis_index(name) for name in ("row", "col", "dp"))
    begin = pl.multiple_of(me * part, part)
    rows_in = pl.ds(begin, part)

    def share_of(ref):
        return ref if ref.shape[1] == part else ref.at[:, rows_in]

    loads = [
        pltpu.make_async_copy(heads_from.at[:, rows_in], heads, in_sem.at[0]),
        pltpu.make_async_copy(share_of(out_from), out, in_sem.at[1]),
        pltpu.make_async_copy(gate_up_from.at[rows_in], gate_up, in_sem.at[2]),
        pltpu.make_async_copy(share_of(down_from), down, in_sem.at[3]),
    ]
    for load in loads:
        load.start()
    enter(cols, everyone=True, dp=dp)
    loads[0].wait()
    loads[1].wait()
    for j in range(cols):
        share = slice(j * narrow, (j + 1) * narrow)
        for k in range(3):
            pieces[j, :, k * narrow : (k + 1) * narrow] = heads[k, :, share]
        pieces[j, :, 3 * narrow :] = out[share, :].T
    rider = Exchange("col", cols, pieces, landed, sems[:3])
    assert cols == 4
    landed[c] = pieces[c]
    units = [c] + [rider.peer(k) for k in range(1, cols)]
    cast = Broadcast(
        dp, cols, lambda k: landed.at[units[k]], lambda p, k: attention_w.at[p, units[k]], sems[11:13]
    )
    cast.start((0,))
    for k in range(1, cols):
        rider.hop(k).start()

    def columns(source):
        return pl.ds(pl.multiple_of(source * depth, 128), depth)

    names = Gather(
        cols, 1, lambda r, source, s: (pl.ds(0, 8), columns(source)), vectors, sems[3:7], pair=False
    )
    spread = Gather(
        cols,
        cols,
        lambda r, source, s: (pl.ds(s * step, step), columns(source)),
        full,
        sems[7:11],
        pair=False,
    )
    vectors[:, columns(c)] = vector[...]
    names.start(0)
    for s in range(cols):
        rows = pl.ds(s * step, step)
        full[rows, columns(c)] = tokens[rows, :]
        spread.start(s)
    loads[2].wait()
    for i in range(2):
        values = gate_up[:, i, :]
        for j in range(cols):
            gate_up_piece[j, :, i * tall : (i + 1) * tall] = values[:, j * tall : (j + 1) * tall]
    loads[3].wait()
    for j in range(cols):
        down_piece[j, :, :tall] = down[j * tall : (j + 1) * tall, :].T
        if down_piece.shape[2] > tall:
            down_piece[j, :, tall:] = jnp.zeros((part, down_piece.shape[2] - tall), BF16)

    def across(r, s):
        where = normed.at[pl.ds(pl.multiple_of(r * half + s * step, 16), step), :]
        return send(where, where, pair_send.at[s], pair_recv.at[s], row=1 - lax.axis_index("row"))

    def own(k):
        u = units[k]
        return pltpu.make_async_copy(landed.at[u], attention_w.at[me, u], own_sem.at[k])

    def take(k):
        rider.hop(k).wait_recv()
        cast.start((k,))
        own(k).start()

    def norm(s):
        rows = slice(s * step, (s + 1) * step)
        state = full[rows, :].astype(F32)
        centered, inverse = moments(state)
        result = centered * inverse * vectors[0:1, :] + vectors[1:2, :]
        normed[pl.ds(pl.multiple_of(r * half + s * step, 16), step), :] = result.astype(BF16)
        across(r, s).start()
        rstd[rows, :] = jnp.broadcast_to(inverse, (step, 128))
        mean = jnp.mean(state, axis=1, keepdims=True)
        xhat[rows, :] = (tokens[rows, :].astype(F32) - mean) * inverse

        @pl.when(c == s)
        def _():
            tokens_own[...] = full[rows, :]

    own(0).start()
    take(1)
    for k in range(1, cols):
        names.relay(0, k)
    for s in range(cols):
        spread.relay(s, 1)
    cast.forward(0)
    take(2)
    take(3)
    for s in range(cols):
        spread.relay(s, 2)
    cast.forward(1)
    cast.forward(2)
    for s in range(cols):
        spread.relay(s, 3)
        norm(s)
        if s == 1:
            cast.forward(3)

    for s in range(cols):
        across(1 - r, s).wait_recv()
        across(r, s).wait_send()
    for u in range(cols):
        own(u).wait()
    cast.finish()
    for k in range(1, cols):
        rider.hop(k).wait_send()
    names.finish()
    spread.finish()


def start_part(tokens, vector, heads, out, gate_up, down, sizes):
    dp, cols = sizes["dp"], sizes["col"]
    half, depth = tokens.shape
    width = depth * cols
    part, wide, tall = depth // dp, heads.shape[2], down.shape[0]
    each = tall // cols
    dma = pltpu.SemaphoreType.DMA
    return pl.pallas_call(
        functools.partial(start_kernel, cols),
        out_shape=(
            jax.ShapeDtypeStruct((2 * half, width), BF16),
            jax.ShapeDtypeStruct((half // cols, width), BF16),
            jax.ShapeDtypeStruct((half, depth), F32),
            jax.ShapeDtypeStruct((half, 128), F32),
            jax.ShapeDtypeStruct((8, width), F32),
            jax.ShapeDtypeStruct((cols, part, 2 * each), BF16),
            jax.ShapeDtypeStruct((cols, part, each + -each % 128), BF16),
            jax.ShapeDtypeStruct((dp, cols, part, 4 * wide // cols), BF16),
        ),
        in_specs=[VM] * 2 + [ANY] * 4,
        out_specs=(VM,) * 7 + (ANY,),
        scratch_shapes=[
            pltpu.VMEM((3, part, wide), BF16),
            pltpu.VMEM((wide, part), BF16),
            pltpu.VMEM((part, 2, tall), BF16),
            pltpu.VMEM((tall, part), BF16),
            pltpu.VMEM((cols, part, 4 * wide // cols), BF16),
            pltpu.VMEM((cols, part, 4 * wide // cols), BF16),
            pltpu.VMEM((half, width), BF16),
            dma((4,)),
            dma((cols,)),
            dma((cols,)),
            dma((cols,)),
        ]
        + Exchange.scratch(cols)
        + Gather.scratch(cols, 1)
        + Gather.scratch(cols, cols)
        + Broadcast.scratch(dp, cols),
        compiler_params=params(1),
        cost_estimate=cost(60),
        name="tokens_norm_weights",
    )(tokens, vector, heads, out, gate_up, down)


def rope_tables(length):
    half_rot = ROT // 2
    lane = np.arange(2 * HD) % HD
    inverse = (ROPE_BASE ** (-2.0 * (lane % half_rot) / ROT)).astype(np.float32)
    angles = np.arange(length).astype(np.float32)[:, None] * inverse[None, :]
    turning = lane < ROT
    cosine = np.where(turning, np.cos(angles), 1.0)
    sine = np.where(turning, np.sin(angles), 0.0)
    lower = np.where(lane < half_rot, -sine, 0.0)
    upper = np.where(lane >= half_rot, sine, 0.0)
    return np.stack([cosine, lower, upper]).astype(np.float32)


def turn(x, tables, back=False):
    half_rot = ROT // 2
    width = x.shape[1]
    sines = pltpu.roll(x, width - half_rot, 1) * tables[1] + pltpu.roll(x, half_rot, 1) * tables[2]
    return x * tables[0] - sines if back else x * tables[0] + sines


def causal(rows):
    return lax.broadcasted_iota(jnp.int32, (rows, rows), 0) >= lax.broadcasted_iota(
        jnp.int32, (rows, rows), 1
    )


def attend_kernel(
    cols,
    normed,
    weight,
    bias,
    tables,
    one_from,
    two_from,
    heads_in,
    attn,
    logs,
    part,
    one_to,
    two_to,
    whole,
    sem,
    qkv,
    *sems,
    load,
    store
):
    length, wide = attn.shape
    two = 2 * HD
    copies = load_columns(weight, whole, sem)
    enter(cols, everyone=True)
    riders = (
        Exchange("col", cols, one_from, one_to, sems[:3]),
        Exchange("col", cols, two_from, two_to, sems[3:]),
    )
    for rider in riders:
        rider.start()
    for copy in copies:
        copy.wait()
    load(0, 3)
    first_head = lax.broadcasted_iota(jnp.int32, (BLOCK, two), 1) < HD

    @pl.loop(0, length // BLOCK)
    def _(m):
        rows = pl.ds(pl.multiple_of(m * BLOCK, BLOCK), BLOCK)
        qkv[rows, :] = dot_nn(normed[rows, :], whole[:, : 3 * wide]) + bias[0:1, :]

    @pl.loop(0, wide // two)
    def _(pair):
        def lanes(k):
            return pl.ds(pl.multiple_of(k * wide + pair * two, two), two)

        for k in range(3):
            x = qkv[:, lanes(k)]
            if k < 2:
                x = turn(x, tables)
            if k == 0:
                x = x * HD ** (-0.5)
            heads_in[:, lanes(k)] = x.astype(BF16)
        for i in range(length // BLOCK):
            keep = (i + 1) * BLOCK
            rows = slice(i * BLOCK, keep)
            query = heads_in[rows, lanes(0)]
            keys = heads_in[0:keep, lanes(1)]
            values = heads_in[0:keep, lanes(2)]
            outs = []
            for h in range(2):
                mine = first_head if h == 0 else ~first_head
                scores = dot_nt(jnp.where(mine, query, jnp.zeros_like(query)), keys)
                last = jnp.where(causal(BLOCK), scores[:, i * BLOCK :], NEG_LARGE)
                scores = last if i == 0 else jnp.concatenate([scores[:, : i * BLOCK], last], axis=1)
                top = jnp.max(scores, axis=1, keepdims=True)
                expo = jnp.exp(scores - top)
                total = jnp.sum(expo, axis=1, keepdims=True)
                probs = (expo * (1.0 / total)).astype(BF16)
                outs.append(dot_nn(probs, values))
                logs[pair, h, rows, :] = jnp.broadcast_to(top + jnp.log(total), (BLOCK, 128))
            attn[rows, pl.ds(pl.multiple_of(pair * two, two), two)] = jnp.where(
                first_head, outs[0], outs[1]
            ).astype(BF16)

    store(0, 1, 2)

    @pl.loop(0, length // BLOCK)
    def _(m):
        rows = pl.ds(pl.multiple_of(m * BLOCK, BLOCK), BLOCK)
        part[rows, :] = dot_nt(attn[rows, :], whole[:, 3 * wide :]).astype(BF16)

    store(3)
    for rider in riders:
        rider.finish()


def attend(cols, normed, weight, bias, tables, one, two):
    length, width = normed.shape
    dp = weight.shape[0]
    wide = weight.shape[3] // 4
    args = (normed, weight, bias, tables, one, two)
    return staged_call(
        functools.partial(attend_kernel, cols),
        args,
        out_shape=(
            jax.ShapeDtypeStruct((length, 3 * wide), BF16),
            jax.ShapeDtypeStruct((length, wide), BF16),
            jax.ShapeDtypeStruct((wide // (2 * HD), 2, length, 128), F32),
            jax.ShapeDtypeStruct((length, width), BF16),
            jax.ShapeDtypeStruct(one.shape, BF16),
            jax.ShapeDtypeStruct(two.shape, BF16),
        ),
        in_specs=[VM, ANY, VM, VM, ANY, ANY],
        out_specs=[VM] * 4 + [ANY] * 2,
        loads=[(i, args[i].shape, None) for i in (0, 3)],
        stores=(0, 1, 2, 3),
        scratch_shapes=[
            pltpu.VMEM((width, 4 * wide), BF16),
            pltpu.SemaphoreType.DMA((dp, cols)),
            pltpu.VMEM((length, 3 * wide), F32),
        ]
        + Exchange.scratch(cols) * 2,
        compiler_params=params(6),
        cost_estimate=cost(50),
        name="attention_weight_exchange",
    )


def attend_back_kernel(
    cols,
    heads_in,
    logs,
    grad_middle,
    tables,
    weight,
    normed,
    attn,
    pieces_from,
    heads_to,
    out_to,
    normed_grad,
    sums,
    arranged,
    queries_grad,
    keys_grad,
    values_grad,
    whole,
    sem,
    grad,
    result,
    own,
    pieces_to,
    heads_from,
    out_from,
    *sems,
    load,
    store
):
    length, wide = attn.shape
    two = 2 * HD
    dp, _, part_rows, _ = weight.shape
    copies = load_columns(weight, whole, sem)
    enter(cols, everyone=True, dp=dp)
    rider = Exchange("col", cols, pieces_from, pieces_to, sems[:3])
    rider.start()
    out_rider = Exchange("dp", dp, out_from, out_to, sems[3:6])
    depth = normed.shape[1] // cols
    load(2, 6)

    def heads_rider(pair):
        return Exchange(
            "dp", dp, heads_from.at[pair], heads_to.at[pair], [sem.at[pair] for sem in sems[6:]]
        )

    def parts(j):
        return pl.ds(pl.multiple_of(j * depth, depth), depth)

    @pl.loop(0, cols)
    def _(j):
        out_grad = dot_tn(grad_middle[:, parts(j)], attn[...]).astype(BF16)
        for p in range(dp):
            out_from[p, j] = out_grad[p * part_rows : (p + 1) * part_rows, :]

    out_rider.start()
    for copy in copies:
        copy.wait()
    load(0, 1, 3, 5)
    sums[...] = jnp.zeros_like(sums)
    first_head = lax.broadcasted_iota(jnp.int32, (BLOCK, two), 1) < HD

    @pl.loop(0, length // BLOCK)
    def _(m):
        rows = pl.ds(pl.multiple_of(m * BLOCK, BLOCK), BLOCK)
        grad[rows, :] = dot_nn(grad_middle[rows, :], whole[:, 3 * wide :]).astype(BF16)

    @pl.loop(0, wide // two)
    def _(pair):
        def lanes(k):
            return pl.ds(pl.multiple_of(k * wide + pair * two, two), two)

        keys_grad[...] = jnp.zeros_like(keys_grad)
        values_grad[...] = jnp.zeros_like(values_grad)
        for i in range(length // BLOCK):
            keep = (i + 1) * BLOCK
            rows = slice(i * BLOCK, keep)
            query = heads_in[rows, lanes(0)]
            keys = heads_in[0:keep, lanes(1)]
            values = heads_in[0:keep, lanes(2)]
            out_grad = grad[rows, lanes(0)]
            outs = []
            for h in range(2):
                mine = first_head if h == 0 else ~first_head
                query_h = jnp.where(mine, query, jnp.zeros_like(query))
                grad_h = jnp.where(mine, out_grad, jnp.zeros_like(out_grad))
                scores = dot_nt(query_h, keys)
                probs = jnp.exp(scores - logs[pair, h, rows, 0:1])
                last = jnp.where(causal(BLOCK), probs[:, i * BLOCK :], 0.0)
                probs = last if i == 0 else jnp.concatenate([probs[:, : i * BLOCK], last], axis=1)
                probs_grad = dot_nt(grad_h, values)
                delta = jnp.sum(probs * probs_grad, axis=1, keepdims=True)
                scores_grad = (probs * (probs_grad - delta)).astype(BF16)
                outs.append(dot_nn(scores_grad, keys))
                keys_grad[0:keep, :] += dot_tn(scores_grad, query_h)
                values_grad[0:keep, :] += dot_tn(probs.astype(BF16), grad_h)
            queries_grad[rows, :] = jnp.where(first_head, outs[0], outs[1]) * HD ** (-0.5)
        grads = (
            turn(queries_grad[...], tables, back=True),
            turn(keys_grad[...], tables, back=True),
            values_grad[...],
        )
        for k in range(3):
            low = grads[k].astype(BF16)
            result[:, lanes(k)] = low
            own[:, k * two : (k + 1) * two] = low
            column_sum = jnp.sum(low.astype(F32), axis=0, keepdims=True)
            sums[0:1, lanes(k)] = column_sum

        @pl.loop(0, cols)
        def _(j):
            heads_grad = dot_tn(normed[:, parts(j)], own[...]).astype(BF16)
            for p in range(dp):
                heads_from[pair, p, j] = heads_grad[p * part_rows : (p + 1) * part_rows, :]

        heads_rider(pair).start()

    @pl.loop(0, length // BLOCK)
    def _(m):
        rows = pl.ds(pl.multiple_of(m * BLOCK, BLOCK), BLOCK)
        normed_grad[rows, :] = dot_nt(result[rows, :], whole[:, : 3 * wide]).astype(BF16)

    store(2)
    out_rider.finish()
    for pair in range(wide // two):
        heads_rider(pair).finish()
    rider.finish()
    share = arranged.shape[2] // cols
    for k in range(arranged.shape[0]):
        arranged[k] = jnp.concatenate(
            [pieces_to[j, :, k * share : (k + 1) * share] for j in range(cols)], axis=1
        )


def attend_back(cols, heads_in, logs, grad_middle, tables, weight, normed, attn, pieces, share):
    length, wide = attn.shape
    width = normed.shape[1]
    dp, _, part, _ = weight.shape
    pairs = wide // (2 * HD)
    heads = (pairs, dp, cols, part, 6 * HD)
    out = (dp, cols, part, wide)
    hops = max(dp - 1, 1)
    dma = pltpu.SemaphoreType.DMA
    args = (heads_in, logs, grad_middle, tables, weight, normed, attn, pieces)
    return staged_call(
        functools.partial(attend_back_kernel, cols),
        args,
        out_shape=(
            jax.ShapeDtypeStruct(heads, BF16),
            jax.ShapeDtypeStruct(out, BF16),
            jax.ShapeDtypeStruct((length, width), BF16),
            jax.ShapeDtypeStruct((8, 3 * wide), F32),
            jax.ShapeDtypeStruct((3, pieces.shape[1], cols * share), BF16),
        ),
        in_specs=[VM] * 4 + [ANY, VM, VM, ANY],
        out_specs=[ANY] * 2 + [VM] * 3,
        loads=[(i, args[i].shape, None) for i in (2, 6, 0, 1, 3, 5)],
        stores=(2,),
        scratch_shapes=[pltpu.VMEM((length, 2 * HD), F32)] * 3
        + [
            pltpu.VMEM((width, 4 * wide), BF16),
            pltpu.SemaphoreType.DMA(weight.shape[:2]),
            pltpu.VMEM((length, wide), BF16),
            pltpu.VMEM((length, 3 * wide), BF16),
            pltpu.VMEM((length, 6 * HD), BF16),
            pltpu.VMEM(pieces.shape, BF16),
            pltpu.VMEM(heads, BF16),
            pltpu.VMEM(out, BF16),
        ]
        + Exchange.scratch(cols)
        + Exchange.scratch(dp)
        + [dma((pairs, hops)), dma((pairs, hops)), dma((pairs, 1))],
        compiler_params=params(8),
        cost_estimate=cost(50),
        name="attention_back_exchange",
    )


def hidden_back_kernel(
    hidden_from,
    gate_from,
    up_from,
    cotan_from,
    gate_up_from,
    down_from,
    normed_from,
    weight_to,
    normed_to,
    hidden,
    gate_part,
    up_part,
    cotan,
    gate_up,
    down,
    normed,
    grads,
    weight_grad,
    normed_grad,
    gate_up_sem,
    down_sem,
    block_sem,
    whole_sem,
    out_sem,
    grad_sem,
):
    group, narrow = hidden.shape
    dp, cols, part_rows, _ = down_from.shape
    wide = weight_grad.shape[3]
    blocks = group // BLOCK
    depth = normed.shape[1] // cols

    def rows_of(m):
        return pl.ds(pl.multiple_of(m * BLOCK, BLOCK), BLOCK)

    def block_copies(m):
        rows = rows_of(m)
        pairs = ((cotan_from, cotan), (gate_from, gate_part), (up_from, up_part))
        return [
            pltpu.make_async_copy(a.at[rows, :], b.at[rows, :], block_sem.at[i, m])
            for i, (a, b) in enumerate(pairs)
        ]

    down_copies = load_columns(down_from, down, down_sem)
    for copy in block_copies(0):
        copy.start()
    gate_up_copy = pltpu.make_async_copy(gate_up_from, gate_up, gate_up_sem.at[0])
    gate_up_copy.start()
    for m in range(1, blocks):
        for copy in block_copies(m):
            copy.start()
    whole_copies = [
        pltpu.make_async_copy(hidden_from, hidden, whole_sem.at[0]),
        pltpu.make_async_copy(normed_from, normed, whole_sem.at[1]),
    ]
    for copy in whole_copies:
        copy.start()
    for copy in down_copies:
        copy.wait()

    def normed_out(m):
        rows = rows_of(m)
        return pltpu.make_async_copy(normed_grad.at[rows, :], normed_to.at[rows, :], out_sem.at[m])

    def weight_out(p, j):
        return pltpu.make_async_copy(weight_grad.at[p, j], weight_to.at[p, j], grad_sem.at[p, j])

    @pl.loop(0, blocks)
    def _(m):
        rows = rows_of(m)
        for copy in block_copies(m):
            copy.wait()
        grad = dot_nn(cotan[rows, :], down[:, :narrow])
        both = jnp.concatenate([grad * gate_part[rows, :], grad * up_part[rows, :]], axis=1)
        grads[rows, :] = both.astype(BF16)

    gate_up_copy.wait()

    @pl.loop(0, blocks)
    def _(m):
        rows = rows_of(m)
        normed_grad[rows, :] = dot_nt(grads[rows, :], gate_up[...]).astype(BF16)
        normed_out(m).start()

    for copy in whole_copies:
        copy.wait()

    @pl.loop(0, cols)
    def _(j):
        columns = pl.ds(pl.multiple_of(j * depth, depth), depth)
        gate_up_grad = dot_tn(normed[:, columns], grads[...]).astype(BF16)
        down_grad = dot_tn(cotan[:, columns], hidden[...]).astype(BF16)
        for p in range(dp):
            rows = slice(p * part_rows, (p + 1) * part_rows)
            weight_grad[p, j, :, : 2 * narrow] = gate_up_grad[rows, :]
            weight_grad[p, j, :, 2 * narrow : 3 * narrow] = down_grad[rows, :]
            if wide > 3 * narrow:
                weight_grad[p, j, :, 3 * narrow :] = jnp.zeros((part_rows, wide - 3 * narrow), BF16)
            weight_out(p, j).start()

    for m in range(blocks):
        normed_out(m).wait()
    for p in range(dp):
        for j in range(cols):
            weight_out(p, j).wait()


def hidden_back(hidden, gate_part, up_part, cotan, gate_up, down, normed):
    group, width = normed.shape
    dp, cols, part, _ = down.shape
    double = gate_up.shape[1]
    grad_shape = (dp, cols, part, double + down.shape[3])
    blocks = group // BLOCK
    dma = pltpu.SemaphoreType.DMA
    return pl.pallas_call(
        hidden_back_kernel,
        out_shape=(
            jax.ShapeDtypeStruct(grad_shape, BF16),
            jax.ShapeDtypeStruct((group, width), BF16),
        ),
        in_specs=[ANY] * 7,
        out_specs=(ANY,) * 2,
        scratch_shapes=[
            pltpu.VMEM(hidden.shape, BF16),
            pltpu.VMEM(gate_part.shape, F32),
            pltpu.VMEM(up_part.shape, F32),
            pltpu.VMEM(cotan.shape, BF16),
            pltpu.VMEM((width, double), BF16),
            pltpu.VMEM((width, down.shape[3]), BF16),
            pltpu.VMEM(normed.shape, BF16),
            pltpu.VMEM((group, double), BF16),
            pltpu.VMEM(grad_shape, BF16),
            pltpu.VMEM((group, width), BF16),
            dma((1,)),
            dma((dp, cols)),
            dma((3, blocks)),
            dma((2,)),
            dma((blocks,)),
            dma((dp, cols)),
        ],
        compiler_params=pltpu.CompilerParams(vmem_limit_bytes=VMEM_LIMIT),
        cost_estimate=cost(30),
        name="hidden_back",
    )(hidden, gate_part, up_part, cotan, gate_up, down, normed)


def split_kernel(whole, first, last):
    count, rows = whole.shape[1] - 1, whole.shape[0] * whole.shape[2]
    inner = first.shape[1] == count

    def part(k):
        return whole[:, k].reshape(rows, whole.shape[3]).astype(F32)

    for k in range(count):
        if inner:
            first[:, k, :] = part(k)
        else:
            first[k] = part(k)
    last[...] = part(count).T


def weights_split(whole, inner):
    dp, count, part, wide = whole.shape
    rows = min(part, 128)
    per = 128 // rows
    depth = dp * part
    count = count - 1
    if inner:
        shape, block, place = (depth, count, wide), (128, count, wide), lambda b: (b, 0, 0)
    else:
        shape, block, place = (count, depth, wide), (count, 128, wide), lambda b: (0, b, 0)
    return pl.pallas_call(
        split_kernel,
        grid=(depth // 128,),
        out_shape=(jax.ShapeDtypeStruct(shape, F32), jax.ShapeDtypeStruct((wide, depth), F32)),
        in_specs=[
            pl.BlockSpec(
                (per, count + 1, rows, wide),
                lambda b: (b * 128 // (per * part), 0, lax.rem(b, max(part // 128, 1)), 0),
            )
        ],
        out_specs=(pl.BlockSpec(block, place), pl.BlockSpec((wide, 128), lambda b: (0, b))),
        compiler_params=pltpu.CompilerParams(vmem_limit_bytes=VMEM_LIMIT),
        cost_estimate=cost(8),
        name="weight_gradients",
    )(whole)


def weights_whole(piece):
    return lax.all_gather(piece, "dp", axis=0)


def weights_sum(pieces):
    dp, cols, part, wide = pieces.shape
    piece = lax.psum_scatter(
        pieces.reshape(dp * cols * part, wide), "dp", scatter_dimension=0, tiled=True
    )
    return piece.reshape(cols, part, wide)


def make_body(sizes):
    cols = sizes["col"]

    def body(
        tokens,
        attention_norm_gain,
        attention_norm_bias,
        qkv_weight,
        qkv_bias,
        out_weight,
        feedforward_norm_gain,
        feedforward_norm_bias,
        gate_up_weight,
        down_weight,
        cotangent,
    ):
        my_dp = lax.axis_index("dp")
        depth = tokens.shape[1]
        tables = rope_tables(SEQ)
        vector = jnp.stack(
            [attention_norm_gain, attention_norm_bias, feedforward_norm_gain, feedforward_norm_bias]
        )
        vector = jnp.concatenate([vector, jnp.zeros_like(vector)])
        part = depth // sizes["dp"]

        def share_of(rows):
            return rows if part % 128 == 0 else lax.dynamic_slice_in_dim(rows, my_dp * part, part, 1)

        (
            normed_one,
            tokens_own,
            xhat_one,
            rstd_one,
            vectors,
            gate_up_piece,
            down_piece,
            attention_w,
        ) = start_part(
            tokens,
            vector,
            qkv_weight.transpose(1, 0, 2),
            share_of(out_weight),
            gate_up_weight,
            share_of(down_weight),
            sizes,
        )
        heads_in, attn, logs, branch_part, gate_up_piece, down_piece = attend(
            cols,
            normed_one,
            attention_w,
            qkv_bias.reshape(1, -1),
            tables,
            gate_up_piece,
            down_piece,
        )
        down_w = weights_whole(down_piece)
        narrow = down_weight.shape[0] // cols
        normed_two, middle, hidden, gate_part, up_part, gate_up_w, cotan_rows = middle_part(
            cols, branch_part, tokens_own, vectors, gate_up_piece, cotangent, sizes["dp"]
        )
        hidden_grad, normed_part = hidden_back(
            hidden, gate_part, up_part, cotan_rows, gate_up_w, down_w, normed_two
        )
        hidden_sum = weights_sum(hidden_grad)
        grad_middle, second, mixed_part = norm_two_back(
            cols, normed_part, middle, cotan_rows, vectors, hidden, down_w
        )
        second = second.reshape(8, cols, depth).transpose(1, 0, 2)
        heads_grad, out_grad, normed_part, bias_part, hidden_sum = attend_back(
            cols,
            heads_in,
            logs,
            grad_middle,
            tables,
            attention_w,
            normed_one,
            attn,
            hidden_sum,
            narrow,
        )
        input_grad, mixed, small, attention_sum, hidden_sum = last_part(
            cols,
            normed_part,
            xhat_one,
            rstd_one,
            attention_norm_gain.reshape(1, -1),
            grad_middle,
            heads_grad,
            out_grad,
            second,
            mixed_part,
            middle,
            hidden_sum,
            bias_part,
        )
        grad_gate_up, grad_down = weights_split(hidden_sum, True)
        grad_qkv_weight, grad_out = weights_split(attention_sum, False)
        grad_qkv_weight = grad_qkv_weight.transpose(1, 0, 2)
        return (
            mixed,
            input_grad,
            small[0, :depth],
            small[1, :depth],
            grad_qkv_weight,
            small[0, depth:].reshape(3, -1),
            grad_out,
            small[2, :depth],
            small[3, :depth],
            grad_gate_up,
            grad_down,
        )

    return body


def solution(mesh):
    specs = (
        P(("dp", "row"), "col"),
        P("col"),
        P("col"),
        P("col", None, "row"),
        P(None, ("row", "col")),
        P("row", "col"),
        P("col"),
        P("col"),
        P("col", None, "row"),
        P("row", "col"),
    )
    return jax.shard_map(
        make_body(dict(mesh.shape)),
        mesh=mesh,
        in_specs=specs + (P(("dp", "row"), "col"),),
        out_specs=(P(("dp", "row"), "col"),) + specs,
        check_vma=False,
    )
```

```python
import functools

import jax
import jax.numpy as jnp
import numpy as np
from jax import lax
from jax.experimental import pallas as pl
from jax.experimental.pallas import tpu as pltpu
from jax.sharding import PartitionSpec as P

MODEL_WIDTH = 2048
HD = 64
ROT = 16
SEQ = 1024
EPSILON = 1e-05
ROPE_BASE = 10000.0
NEG_LARGE = -1e30
F32 = jnp.float32
BF16 = jnp.bfloat16
MESH = pl.DeviceIdType.MESH
VMEM_LIMIT = 56 * 1024 * 1024
SUBS = 8


def send(src, dst, send_sem, recv_sem, **where):
    return pltpu.make_async_remote_copy(
        src_ref=src,
        dst_ref=dst,
        send_sem=send_sem,
        recv_sem=recv_sem,
        device_id=where,
        device_id_type=MESH,
    )


def enter(cols, everyone=False, dp=1):
    r, c = lax.axis_index("row"), lax.axis_index("col")
    barrier = pltpu.get_barrier_semaphore()
    pl.semaphore_signal(barrier, inc=1, device_id={"row": 1 - r}, device_id_type=MESH)
    if everyone:
        for k in range(1, cols):
            pl.semaphore_signal(
                barrier, inc=1, device_id={"col": lax.rem(c + k, cols)}, device_id_type=MESH
            )
        for k in range(1, dp):
            pl.semaphore_signal(
                barrier,
                inc=1,
                device_id={"dp": lax.rem(lax.axis_index("dp") + k, dp)},
                device_id_type=MESH,
            )
        pl.semaphore_wait(barrier, cols + dp - 1)
        return

    @pl.when(c > 0)
    def _():
        pl.semaphore_signal(barrier, inc=1, device_id={"col": c - 1}, device_id_type=MESH)

    @pl.when(c < cols - 1)
    def _():
        pl.semaphore_signal(barrier, inc=1, device_id={"col": c + 1}, device_id_type=MESH)

    inner = (c > 0) & (c < cols - 1)

    @pl.when(inner)
    def _():
        pl.semaphore_wait(barrier, 3)

    @pl.when(jnp.logical_not(inner))
    def _():
        pl.semaphore_wait(barrier, 2)


LAG = 3
BLOCK = 256
PACE = 6


class Reduce:
    def __init__(self, cols, subs, spot, part, twin, going, coming, sems, add=None):
        self.cols, self.subs, self.spot, self.add = cols, subs, spot, add
        self.part, self.twin, self.going, self.coming = part, twin, going, coming
        self.twin_send, self.twin_recv, self.send, self.recv = sems
        self.r, self.c = lax.axis_index("row"), lax.axis_index("col")
        self.half = part.shape[0] // 2
        self.per_sub = cols - 1
        self.landing = LAG * (cols - 1)
        self.slots = self.per_sub * (subs - 1) + self.landing + 1

    def place(self, d, s, base=0):
        row, rows, column, columns = self.spot(d, s)
        if not isinstance(column, int):
            column = pl.multiple_of(column, 128)
        return pl.ds(pl.multiple_of(base + row, 16), rows), pl.ds(column, columns)

    def twin_copy(self, d, s):
        return send(
            self.part.at[self.place(d, s, (1 - self.r) * self.half)],
            self.twin.at[self.place(d, s)],
            self.twin_send.at[d, s],
            self.twin_recv.at[d, s],
            row=1 - self.r,
        )

    def start(self):
        @pl.loop(0, self.subs)
        def _(s):
            for j in range(self.cols):
                self.twin_copy(self.cols - 1 - j // 2 if j % 2 == 0 else j // 2, s).start()

    def hop(self, way, d, s):
        place = self.place(d, s)
        return send(
            self.going.at[(way,) + place],
            self.coming.at[(way,) + place],
            self.send.at[way, d, s],
            self.recv.at[way, d, s],
            col=self.c + 1 if way == 0 else self.c - 1,
        )

    def own(self, d, s):
        self.twin_copy(d, s).wait_recv()
        value = self.part[self.place(d, s, self.r * self.half)].astype(F32)
        value = value + self.twin[self.place(d, s)].astype(F32)
        if self.add is not None:
            value = value + self.add(d, s)
        return value

    def pass_on(self, way, d, s):
        place = (way,) + self.place(d, s)
        first = 0 if way == 0 else self.cols - 1

        @pl.when(self.c == first)
        def _():
            self.going[place] = self.own(d, s).astype(BF16)

        @pl.when(self.c != first)
        def _():
            value = self.own(d, s)
            self.hop(way, d, s).wait_recv()
            self.going[place] = (value + self.coming[place].astype(F32)).astype(BF16)

        self.hop(way, d, s).start()

    def slot(self, t):
        for way in range(2):
            made = self.c if way == 0 else self.cols - 1 - self.c
            event = t - LAG * made

            @pl.when((event >= 0) & (event < self.per_sub * self.subs))
            def _():
                s, j = lax.div(event, self.per_sub), lax.rem(event, self.per_sub)
                d = self.cols - 1 - j if way == 0 else j

                @pl.when(self.c < d if way == 0 else self.c > d)
                def _():
                    self.pass_on(way, d, s)

    def landed(self, t, do):
        after = t - self.landing

        @pl.when((after >= 0) & (lax.rem(after + self.per_sub * self.cols, self.per_sub) == 0))
        def _():
            s = lax.div(after, self.per_sub)

            @pl.when(s < self.subs)
            def _():
                do(s)

    def land(self, s, total):
        place = self.place(self.c, s)
        total[...] = self.own(self.c, s)

        @pl.when(self.c > 0)
        def _():
            self.hop(0, self.c, s).wait_recv()
            total[...] += self.coming[(0,) + place].astype(F32)

        @pl.when(self.c < self.cols - 1)
        def _():
            self.hop(1, self.c, s).wait_recv()
            total[...] += self.coming[(1,) + place].astype(F32)

    def finish(self):
        @pl.loop(0, self.subs)
        def _(s):
            for d in range(self.cols):
                self.twin_copy(d, s).wait_send()

                @pl.when(self.c < d)
                def _():
                    self.hop(0, d, s).wait_send()

                @pl.when(self.c > d)
                def _():
                    self.hop(1, d, s).wait_send()

    @staticmethod
    def scratch(cols, subs, half, width):
        return [
            pltpu.VMEM((half, width), BF16),
            pltpu.VMEM((2, half, width), BF16),
            pltpu.VMEM((2, half, width), BF16),
            pltpu.SemaphoreType.DMA((cols, subs)),
            pltpu.SemaphoreType.DMA((cols, subs)),
            pltpu.SemaphoreType.DMA((2, cols, subs)),
            pltpu.SemaphoreType.DMA((2, cols, subs)),
        ]


class Gather:
    def __init__(self, cols, subs, spot, whole, sems, pair=True):
        self.cols, self.subs, self.spot, self.whole, self.pair = cols, subs, spot, whole, pair
        self.send, self.recv, self.pair_send, self.pair_recv = sems
        self.r, self.c = lax.axis_index("row"), lax.axis_index("col")

    def hop(self, way, source, s):
        where = self.whole.at[self.spot(self.r, source, s)]
        return send(
            where,
            where,
            self.send.at[way, source, s],
            self.recv.at[way, source, s],
            col=self.c + 1 if way == 0 else self.c - 1,
        )

    def across(self, r, source, s):
        where = self.whole.at[self.spot(r, source, s)]
        return send(
            where, where, self.pair_send.at[source, s], self.pair_recv.at[source, s], row=1 - self.r
        )

    def start(self, s):
        @pl.when(self.c < self.cols - 1)
        def _():
            self.hop(0, self.c, s).start()

        @pl.when(self.c > 0)
        def _():
            self.hop(1, self.c, s).start()

        if self.pair:
            self.across(self.r, self.c, s).start()

    def relay(self, s, k):
        @pl.when(self.c >= k)
        def _():
            self.hop(0, self.c - k, s).wait_recv()

            @pl.when(self.c < self.cols - 1)
            def _():
                self.hop(0, self.c - k, s).start()

            if self.pair:
                self.across(self.r, self.c - k, s).start()

        @pl.when(self.c + k < self.cols)
        def _():
            self.hop(1, self.c + k, s).wait_recv()

            @pl.when(self.c > 0)
            def _():
                self.hop(1, self.c + k, s).start()

            if self.pair:
                self.across(self.r, self.c + k, s).start()

    def slot(self, t, begin, step):
        for k in range(1, self.cols):
            after = t - begin - LAG * k

            @pl.when((after >= 0) & (lax.rem(after + step * LAG * self.cols * 8, step) == 0))
            def _():
                s = lax.div(after, step)

                @pl.when(s < self.subs)
                def _():
                    self.relay(s, k)

    def finish(self):
        @pl.loop(0, self.subs)
        def _(s):
            for source in range(self.cols):
                if self.pair:
                    self.across(1 - self.r, source, s).wait_recv()
                    self.across(self.r, source, s).wait_send()

                @pl.when((self.c >= source) & (self.c < self.cols - 1))
                def _():
                    self.hop(0, source, s).wait_send()

                @pl.when((self.c <= source) & (self.c > 0))
                def _():
                    self.hop(1, source, s).wait_send()

    @staticmethod
    def scratch(cols, subs):
        return [
            pltpu.SemaphoreType.DMA((2, cols, subs)),
            pltpu.SemaphoreType.DMA((2, cols, subs)),
            pltpu.SemaphoreType.DMA((cols, subs)),
            pltpu.SemaphoreType.DMA((cols, subs)),
        ]


class Exchange:
    def __init__(self, axis, size, source, target, sems):
        self.axis, self.size, self.source, self.target = axis, size, source, target
        self.send, self.recv, self.local = sems
        self.c = lax.axis_index(axis)

    def peer(self, k):
        if self.size == 4 and k != 2:
            return self.c + 1 - 2 * lax.rem(self.c, 2) if k == 1 else 3 - self.c
        return lax.rem(self.c + k, self.size)

    def hop(self, k):
        to = self.peer(k)
        return send(
            self.source.at[to],
            self.target.at[self.c],
            self.send.at[k - 1],
            self.recv.at[k - 1],
            **{self.axis: to},
        )

    def own(self):
        return pltpu.make_async_copy(
            self.source.at[self.c], self.target.at[self.c], self.local.at[0]
        )

    def start(self):
        for k in range(1, self.size):
            self.hop(k).start()
        self.own().start()

    def finish(self):
        self.own().wait()
        for k in range(1, self.size):
            self.hop(k).wait_recv()
        for k in range(1, self.size):
            self.hop(k).wait_send()

    @staticmethod
    def scratch(size):
        return [
            pltpu.SemaphoreType.DMA((size - 1,)),
            pltpu.SemaphoreType.DMA((size - 1,)),
            pltpu.SemaphoreType.DMA((1,)),
        ]


class Broadcast:
    def __init__(self, dp, units, source, target, sems):
        self.dp, self.units, self.source, self.target = dp, units, source, target
        self.send, self.recv = sems
        self.me = lax.axis_index("dp")
        self.near = self.me + 1 - 2 * lax.rem(self.me, 2)
        self.far = lax.rem(self.me + 2, dp)
        self.square = dp == 4

    def hop(self, i, u):
        if self.square:
            to = self.near if i == 0 else self.far
        else:
            to = lax.rem(self.me + i + 1, self.dp)
        return send(
            self.source(u), self.target(self.me, u), self.send.at[i, u], self.recv.at[i, u], dp=to
        )

    def across(self, u):
        low = u < self.units // 2
        where = self.target(self.near if low else self.far, u)
        return send(
            where,
            where,
            self.send.at[2, u],
            self.recv.at[2, u],
            dp=self.far if low else self.near,
        )

    def hops(self):
        return 2 if self.square else self.dp - 1

    def start(self, units=None):
        half = self.units // 2
        for n in range(self.units) if units is None else units:
            for i in range(self.hops()):
                u = (n + half) % self.units if self.square and i == 1 and units is None else n
                self.hop(i, u).start()

    def forward(self, u):
        if self.square:
            self.hop(0 if u < self.units // 2 else 1, u).wait_recv()
            self.across(u).start()

    def finish(self):
        for u in range(self.units):
            for i in range(self.hops()):
                if not self.square or (i == 0) != (u < self.units // 2):
                    self.hop(i, u).wait_recv()
                self.hop(i, u).wait_send()
            if self.square:
                self.across(u).wait()

    @staticmethod
    def scratch(dp, units):
        return [
            pltpu.SemaphoreType.DMA((max(dp - 1, 1), units)),
            pltpu.SemaphoreType.DMA((max(dp - 1, 1), units)),
        ]


ANY = pl.BlockSpec(memory_space=pl.ANY)


def staged_call(kernel, args, out_shape, in_specs, out_specs, scratch_shapes, loads, stores, **kinds):
    counts = len(args), len(out_shape)
    dma = pltpu.SemaphoreType.DMA
    buffers = [pltpu.VMEM(shape, args[i].dtype) for i, shape, _ in loads]
    buffers += [pltpu.VMEM(out_shape[j].shape, out_shape[j].dtype) for j in stores]
    in_specs, out_specs = list(in_specs), list(out_specs)
    for i, _, _ in loads:
        in_specs[i] = ANY
    for j in stores:
        out_specs[j] = ANY

    def run(*refs):
        ins, outs = list(refs[: counts[0]]), list(refs[counts[0] : sum(counts)])
        own = refs[len(refs) - len(buffers) - 2 :]
        in_sem, out_sem = own[-2:]
        coming, going = {}, {}
        for n, (i, _, part) in enumerate(loads):
            source = ins[i] if part is None else ins[i].at[part()]
            coming[i] = pltpu.make_async_copy(source, own[n], in_sem.at[n])
            ins[i] = own[n]
        for n, j in enumerate(stores):
            buffer = own[len(loads) + n]
            going[j] = pltpu.make_async_copy(buffer, outs[j], out_sem.at[n])
            outs[j] = buffer
        for copy in coming.values():
            copy.start()

        def load(*which):
            for i in which:
                coming[i].wait()

        def store(*which):
            for j in which:
                going[j].start()

        kernel(*ins, *outs, *refs[sum(counts) : len(refs) - len(own)], load=load, store=store)
        for copy in going.values():
            copy.wait()

    return pl.pallas_call(
        run,
        out_shape=tuple(out_shape),
        in_specs=in_specs,
        out_specs=tuple(out_specs),
        scratch_shapes=list(scratch_shapes)
        + buffers
        + [dma((max(len(loads), 1),)), dma((max(len(stores), 1),))],
        **kinds,
    )(*args)


def load_columns(weight, whole, sem):
    dp, cols, part, _ = weight.shape
    copies = [
        pltpu.make_async_copy(
            weight.at[p, j],
            whole.at[pl.ds((j * dp + p) * part, part), :],
            sem.at[p, j],
        )
        for p in range(dp)
        for j in range(cols)
    ]
    for copy in copies:
        copy.start()
    return copies


def dot_nt(a, b):
    return lax.dot_general(a, b, (((1,), (1,)), ((), ())), preferred_element_type=F32)


def dot_tn(a, b):
    return lax.dot_general(a, b, (((0,), (0,)), ((), ())), preferred_element_type=F32)


def dot_nn(a, b):
    return jnp.dot(a, b, preferred_element_type=F32)


def moments(rows):
    mean = jnp.mean(rows, axis=1, keepdims=True)
    centered = rows - mean
    return centered, lax.rsqrt(jnp.mean(centered * centered, axis=1, keepdims=True) + EPSILON)


def cost(us):
    return pl.CostEstimate(flops=us * 10**9, bytes_accessed=10**7, transcendentals=0)


def params(number):
    return pltpu.CompilerParams(
        collective_id=number, has_side_effects=True, vmem_limit_bytes=VMEM_LIMIT
    )


VM = pl.BlockSpec(memory_space=pltpu.VMEM)


def row_spot(own, step, half, width):
    def spot(r, source, s):
        return pl.ds(pl.multiple_of(r * half + source * own + s * step, 16), step), pl.ds(0, width)

    return spot


COTANGENT_SLOT = 0


def middle_kernel(
    cols,
    part,
    tokens_own,
    vectors,
    piece,
    cotan,
    normed_to,
    middle_to,
    hidden_to,
    gate_to,
    up_to,
    weight_to,
    cotan_to,
    normed,
    middle,
    hidden,
    gate_part,
    up_part,
    weight,
    cotan_rows,
    total,
    own_sem,
    out_sem,
    block_sem,
    *scratch,
    load,
    store
):
    group, width = part.shape
    half = group // 2
    own = half // cols
    step = own // SUBS
    depth = cotan.shape[1]
    rows_each = half // SUBS
    _, part_rows, double = piece.shape
    narrow = double // 2
    dp = weight.shape[0] // cols // part_rows
    me = lax.axis_index("dp")
    enter(cols, everyone=True, dp=dp)
    load(0)
    summing = Reduce(
        cols, SUBS, lambda d, s: (d * own + s * step, step, 0, width), part, *scratch[:3], scratch[3:7]
    )
    summing.start()
    spread = Gather(cols, SUBS, row_spot(own, step, half, width), normed, scratch[7:11])

    def cotan_spot(r, source, s):
        rows = pl.ds(pl.multiple_of(r * half + s * rows_each, 16), rows_each)
        return rows, pl.ds(pl.multiple_of(source * depth, 128), depth)

    cotan_spread = Gather(cols, SUBS, cotan_spot, cotan_rows, scratch[11:15])

    def weight_rows(p, j):
        return weight.at[pl.ds(pl.multiple_of((j * dp + p) * part_rows, 16), part_rows), :]

    rider = Broadcast(dp, cols, lambda u: piece.at[u], weight_rows, scratch[15:17])
    rider.start()
    own_copies = [
        pltpu.make_async_copy(piece.at[j], weight_rows(me, j), own_sem.at[j]) for j in range(cols)
    ]
    for copy in own_copies:
        copy.start()
    load(1, 2, 4)

    def land(s):
        summing.land(s, total)
        rows = pl.ds(pl.multiple_of(s * step, step), step)
        state = tokens_own[rows, :].astype(F32) + total[...]
        middle[rows, :] = state
        centered, rstd = moments(state)
        result = centered * rstd * vectors[2:3, :] + vectors[3:4, :]
        normed[spread.spot(spread.r, spread.c, s)] = result.astype(BF16)
        spread.start(s)

    def cotan_slot(t):
        after = t - COTANGENT_SLOT

        @pl.when((after >= 0) & (lax.rem(after + 60, 3) == 0) & (after < 3 * SUBS))
        def _():
            s = lax.div(after, 3)
            rows = pl.ds(pl.multiple_of(s * rows_each, 16), rows_each)
            cotan_rows[cotan_spot(spread.r, spread.c, s)] = cotan[rows, :]
            cotan_spread.start(s)

        cotan_spread.slot(t, COTANGENT_SLOT, 3)

    first = summing.slots + LAG * (cols - 1)
    last = COTANGENT_SLOT + 3 * (SUBS - 1) + LAG * (cols - 1) + 1
    blocks = group // BLOCK

    @pl.loop(0, first)
    def _(t):
        summing.slot(t)
        summing.landed(t, land)
        spread.slot(t, summing.landing, summing.per_sub)
        cotan_slot(t)
        for u in range(cols):

            @pl.when(t == 14 + 8 * (u % 2))
            def _():
                rider.forward(u)

    spread.finish()
    normed_out = pltpu.make_async_copy(normed, normed_to, out_sem.at[0])
    normed_out.start()
    middle_out = pltpu.make_async_copy(middle, middle_to, out_sem.at[1])
    middle_out.start()
    for copy in own_copies:
        copy.wait()
    rider.finish()
    weight_out = pltpu.make_async_copy(weight, weight_to, out_sem.at[2])
    weight_out.start()

    def block_out(m):
        rows = pl.ds(pl.multiple_of(m * BLOCK, BLOCK), BLOCK)
        pairs = ((hidden, hidden_to), (gate_part, gate_to), (up_part, up_to))
        return [
            pltpu.make_async_copy(a.at[rows, :], b.at[rows, :], block_sem.at[i, m])
            for i, (a, b) in enumerate(pairs)
        ]

    @pl.loop(0, max(last - first, blocks))
    def _(m):
        @pl.when(m < blocks)
        def _():
            rows = pl.ds(pl.multiple_of(m * BLOCK, BLOCK), BLOCK)
            both = dot_nn(normed[rows, :], weight[...])
            gate, up = both[:, :narrow], both[:, narrow:]
            sig = 1.0 / (1.0 + jnp.exp(-gate))
            active = gate * sig
            hidden[rows, :] = (active * up).astype(BF16)
            up_part[rows, :] = active.astype(BF16)
            gate_part[rows, :] = (up * sig * (1.0 + gate * (1.0 - sig))).astype(BF16)
            for copy in block_out(m):
                copy.start()

        cotan_slot(first + m)

    cotan_spread.finish()
    cotan_out = pltpu.make_async_copy(cotan_rows, cotan_to, out_sem.at[3])
    cotan_out.start()
    summing.finish()
    for m in range(blocks):
        for copy in block_out(m):
            copy.wait()
    for copy in (normed_out, middle_out, weight_out, cotan_out):
        copy.wait()


def middle_part(cols, part, tokens_own, vectors, piece, cotan, dp):
    group, width = part.shape
    _, part_rows, double = piece.shape
    narrow = double // 2
    blocks = group // BLOCK
    dma = pltpu.SemaphoreType.DMA
    outs = (
        ((group, width), BF16),
        (tokens_own.shape, F32),
        ((group, narrow), BF16),
        ((group, narrow), BF16),
        ((group, narrow), BF16),
        ((dp * cols * part_rows, double), BF16),
        ((group, width), BF16),
    )
    args = (part, tokens_own, vectors, piece, cotan)
    return staged_call(
        functools.partial(middle_kernel, cols),
        args,
        out_shape=tuple(jax.ShapeDtypeStruct(*out) for out in outs),
        in_specs=[VM] * 3 + [ANY, VM],
        out_specs=[ANY] * len(outs),
        loads=[(i, args[i].shape, None) for i in (0, 1, 2, 4)],
        stores=(),
        scratch_shapes=[pltpu.VMEM(*out) for out in outs]
        + [
            pltpu.VMEM((group // 2 // cols // SUBS, width), F32),
            dma((cols,)),
            dma((4,)),
            dma((3, blocks)),
        ]
        + Reduce.scratch(cols, SUBS, group // 2, width)
        + Gather.scratch(cols, SUBS) * 2
        + Broadcast.scratch(dp, cols),
        compiler_params=params(2),
        cost_estimate=cost(95),
        name="middle_gate_up",
    )


def norm_two_back_kernel(
    cols,
    gate_up_grad,
    gate_up,
    middle,
    cotan_own,
    vectors,
    hidden,
    weight,
    grads,
    sums,
    mixed_part,
    part,
    down,
    sem,
    *scratch,
    load,
    store
):
    narrow = hidden.shape[1]
    copies = load_columns(weight, down, sem)
    half, width = part.shape[0] // 2, part.shape[1]
    own = half // cols
    step = own // SUBS
    total = scratch[11]
    enter(cols)
    load(0, 1)
    summing = Reduce(
        cols, SUBS, lambda d, s: (d * own + s * step, step, 0, width), part, *scratch[:3], scratch[3:7]
    )
    spread = Gather(cols, SUBS, row_spot(own, step, half, width), grads, scratch[7:11])
    blocks = part.shape[0] // BLOCK
    row = lax.axis_index("row")

    def product(r):
        @pl.loop(0, blocks // 2)
        def _(m):
            rows = pl.ds(pl.multiple_of(r * half + m * BLOCK, BLOCK), BLOCK)
            part[rows, :] = dot_nt(gate_up_grad[rows, :], gate_up[...]).astype(BF16)

    product(1 - row)
    summing.start()
    product(row)
    for copy in copies:
        copy.wait()
    load(2, 3, 4, 5)
    sums[...] = jnp.zeros_like(sums)

    def land(s):
        summing.land(s, total)
        rows = pl.ds(pl.multiple_of(s * step, step), step)
        centered, rstd = moments(middle[rows, :])
        xhat = centered * rstd
        grad = total[...]
        sums[0:1, :] += jnp.sum(grad * xhat, axis=0, keepdims=True)
        sums[1:2, :] += jnp.sum(grad, axis=0, keepdims=True)
        scaled = grad * vectors[2:3, :]
        inner = (
            scaled
            - jnp.mean(scaled, axis=1, keepdims=True)
            - xhat * jnp.mean(scaled * xhat, axis=1, keepdims=True)
        )
        result = cotan_own[rows, :].astype(F32) + rstd * inner
        grads[spread.spot(spread.r, spread.c, s)] = result.astype(BF16)
        spread.start(s)

    @pl.loop(0, summing.slots + LAG * (cols - 1))
    def _(t):
        summing.slot(t)
        summing.landed(t, land)
        spread.slot(t, summing.landing, summing.per_sub)

        @pl.when((lax.rem(t, PACE) == PACE - 1) & (t < PACE * blocks))
        def _():
            rows = pl.ds(pl.multiple_of(lax.div(t, PACE) * BLOCK, BLOCK), BLOCK)
            result = dot_nt(hidden[rows, :], down[:, :narrow])
            mixed_part[rows, :] = result.astype(BF16)

    store(2)
    spread.finish()
    store(0)
    summing.finish()


def norm_two_back(cols, gate_up_grad, gate_up, middle, cotan, vectors, hidden, weight):
    group, width = cotan.shape
    tall = weight.shape[3]
    own = group // 2 // cols

    def own_rows():
        row = lax.axis_index("row") * (group // 2) + lax.axis_index("col") * own
        return pl.ds(pl.multiple_of(row, own), own)

    args = (gate_up_grad, gate_up, middle, cotan, vectors, hidden, weight)
    return staged_call(
        functools.partial(norm_two_back_kernel, cols),
        args,
        out_shape=(
            jax.ShapeDtypeStruct((group, width), BF16),
            jax.ShapeDtypeStruct((8, width), F32),
            jax.ShapeDtypeStruct((group, width), BF16),
        ),
        in_specs=[VM] * 6 + [ANY],
        out_specs=[VM] * 3,
        loads=[(i, args[i].shape, None) for i in (0, 1, 2)]
        + [(3, (own, width), own_rows)]
        + [(i, args[i].shape, None) for i in (4, 5)],
        stores=(0, 2),
        scratch_shapes=[pltpu.VMEM((group, width), BF16), pltpu.VMEM((width, tall), BF16), pltpu.SemaphoreType.DMA(weight.shape[:2])]
        + Reduce.scratch(cols, SUBS, group // 2, width)
        + Gather.scratch(cols, SUBS)
        + [pltpu.VMEM((group // 2 // cols // SUBS, width), F32)],
        compiler_params=params(3),
        cost_estimate=cost(60),
        name="grad_sum_norm_gather",
    )


def mixed_sum(cols, part, middle, scratch):
    half, width = part.shape[0] // 2, part.shape[1]
    step, depth, own = half // SUBS, width // cols, half // cols
    c = lax.axis_index("col")

    def add(d, s):
        inside = s * step - c * own
        rows = pl.ds(pl.multiple_of(lax.rem(s * step, own), step), step)
        mine = middle[rows, pl.ds(pl.multiple_of(d * depth, 128), depth)]
        return jnp.where((inside >= 0) & (inside < own), mine, 0.0)

    return Reduce(
        cols,
        SUBS,
        lambda d, s: (s * step, step, d * depth, depth),
        part,
        *scratch[:3],
        scratch[3:7],
        add=add,
    )


MIXED_SLOT = 22
ARRANGE_SLOT = 24


def last_kernel(
    cols,
    part,
    xhat,
    rstd,
    gain,
    grad_middle,
    heads_grad,
    out_grad,
    second,
    mixed_part,
    middle,
    hidden_piece,
    bias,
    result,
    mixed,
    small,
    attention_all,
    hidden_all,
    total,
    grad,
    mine,
    theirs,
    sums,
    landed,
    slices,
    own_norms,
    pair_norms,
    arranged,
    own_small,
    all_small,
    out_sem,
    in_sem,
    pair_sem,
    small_send,
    small_recv,
    own_sem,
    *sems,
    load,
    store
):
    half, width = part.shape[0] // 2, part.shape[1]
    step, depth = half // SUBS, width // cols
    pairs, dp = heads_grad.shape[:2]
    two = heads_grad.shape[4] // 3
    narrow = sums.shape[2] // 4
    rows_each = hidden_piece.shape[1] // 2
    weights = hidden_piece.shape[0]
    enter(cols, everyone=True, dp=dp)
    r, c, me = (lax.axis_index(name) for name in ("row", "col", "dp"))
    load(0)
    summing = Reduce(
        cols, SUBS, lambda d, s: (s * step, step, d * depth, depth), part, *sems[:3], sems[3:7]
    )
    summing.start()
    rider = Exchange("col", cols, sums, landed, sems[14:17])
    names = Exchange("col", cols, second, slices, sems[17:20])
    names.start()

    def hidden_rows(u):
        return u % weights, pl.ds(u // weights * rows_each, rows_each)

    hidden_cast = Broadcast(
        dp,
        2 * weights,
        lambda u: hidden_piece.at[hidden_rows(u)],
        lambda p, u: hidden_all.at[(p,) + hidden_rows(u)],
        sems[20:22],
    )
    attention_cast = Broadcast(
        dp, 4, lambda u: arranged.at[u], lambda p, u: attention_all.at[p, u], sems[22:24]
    )
    hidden_own = pltpu.make_async_copy(hidden_piece, hidden_all.at[me], own_sem.at[0])
    attention_own = pltpu.make_async_copy(arranged, attention_all.at[me], own_sem.at[1])
    hidden_cast.start()
    hidden_own.start()
    load(5, 6)

    def over_dp(ref, to):
        value = ref[0, to].astype(F32)
        for p in range(1, dp):
            value = value + ref[p, to].astype(F32)
        return value.astype(BF16)

    def fill(to, target):
        for pair in range(pairs):
            value = over_dp(heads_grad.at[pair], to)
            for k in range(3):
                first = k * narrow + pair * two
                target[:, first : first + two] = value[:, k * two : (k + 1) * two]
        target[:, 3 * narrow :] = over_dp(out_grad, to)

    for k in range(1, cols):
        to = rider.peer(k)
        fill(to, sums.at[to])
        rider.hop(k).start()
    fill(c, landed.at[c])
    own_norms[...] = jnp.zeros_like(own_norms)
    load(8, 9)
    mixing = mixed_sum(cols, mixed_part, middle, sems[7:14])
    mixing.start()
    load(1, 2, 4)

    def land(s):
        summing.land(s, total)
        rows = pl.ds(pl.multiple_of(s * step, step), step)
        grad[rows, :] = total[...]
        standard = xhat[rows, :]
        own_norms[0:1, :] += jnp.sum(total[...] * standard, axis=0, keepdims=True)
        own_norms[1:2, :] += jnp.sum(total[...], axis=0, keepdims=True)

    def land_mixed(s):
        mixing.land(s, total)
        mixed[pl.ds(pl.multiple_of(s * step, step), step), :] = total[...].astype(BF16)

    def arrange():
        for k in range(1, cols):
            rider.hop(k).wait_recv()
        for k in range(4):
            for j in range(cols):
                arranged[k, :, j * narrow : (j + 1) * narrow] = landed[
                    j, :, k * narrow : (k + 1) * narrow
                ]
        attention_cast.start()
        attention_own.start()

    @pl.loop(0, summing.slots)
    def _(t):
        summing.slot(t)
        summing.landed(t, land)
        mixing.slot(t - MIXED_SLOT)
        mixing.landed(t - MIXED_SLOT, land_mixed)
        for u in range(weights):

            @pl.when(t == 8 + 6 * u)
            def _():
                hidden_cast.forward(u)
                hidden_cast.forward(weights + u)

        @pl.when(t == ARRANGE_SLOT)
        def _():
            arrange()

    lanes = lax.broadcasted_iota(jnp.int32, (128, 128), 1)
    for s in range(half // 128):
        rows = slice(s * 128, (s + 1) * 128)
        scaled = grad[rows, :] * gain[0:1, :]
        one = jnp.sum(scaled, axis=1, keepdims=True)
        two_sum = jnp.sum(scaled * xhat[rows, :], axis=1, keepdims=True)
        both = jnp.where(lanes == 0, one, jnp.where(lanes == 1, two_sum, 0.0))
        mine[:, rows] = both.T[0:8, :]

    def exchange_sums(k):
        return send(
            mine, theirs.at[k - 1], out_sem.at[k - 1], in_sem.at[k - 1], col=lax.rem(c + k, cols)
        )

    for k in range(1, cols):
        exchange_sums(k).start()
    names.finish()
    shift = slices[0]
    for j in range(1, cols):
        shift = shift + slices[j]
    own_norms[2:4, :] = shift[0:2, :]
    across = send(own_norms, pair_norms, pair_sem.at[0], pair_sem.at[1], row=1 - r)
    across.start()

    @pl.loop(summing.slots, MIXED_SLOT + mixing.slots)
    def _(t):
        mixing.slot(t - MIXED_SLOT)
        mixing.landed(t - MIXED_SLOT, land_mixed)
        for u in range(2):

            @pl.when(t == summing.slots + 6 + 8 * u)
            def _():
                attention_cast.forward(u)
                attention_cast.forward(2 + u)

    across.wait()
    own_small[:, :depth] = own_norms[...] + pair_norms[...]
    own_small[:, depth:] = bias[...]
    all_small[me] = own_small[...]

    def hop(k):
        to = lax.rem(me + k, dp)
        return send(
            own_small, all_small.at[me], small_send.at[k - 1], small_recv.at[k - 1], dp=to
        )

    for k in range(1, dp):
        hop(k).start()
    for k in range(1, cols):
        exchange_sums(k).wait_recv()
    for s in range(half // 128):
        rows = slice(s * 128, (s + 1) * 128)
        both = mine[:, rows]
        for k in range(1, cols):
            both = both + theirs[k - 1, :, rows]
        both = jnp.concatenate([both, jnp.zeros((120, 128), F32)], axis=0).T / (depth * cols)
        scaled = grad[rows, :] * gain[0:1, :]
        inner = scaled - both[:, 0:1] - xhat[rows, :] * both[:, 1:2]
        result[rows, :] = grad_middle[rows, :].astype(F32) + rstd[rows, 0:1] * inner
    store(0, 1)
    for k in range(1, dp):
        hop(k).wait()
    value = all_small[0]
    for p in range(1, dp):
        value = value + all_small[p]
    small[...] = value
    for k in range(1, cols):
        exchange_sums(k).wait_send()
        rider.hop(k).wait_send()
    summing.finish()
    mixing.finish()
    hidden_own.wait()
    attention_own.wait()
    hidden_cast.finish()
    attention_cast.finish()


def last_part(
    cols, part, xhat, rstd, gain, grad_middle, heads_grad, out_grad, second, mixed_part, middle, piece, bias
):
    group, width = part.shape
    half, depth = group // 2, width // cols
    dp, _, rows, narrow = out_grad.shape
    small = (8, depth + bias.shape[1])
    hops = max(dp - 1, 1)
    dma = pltpu.SemaphoreType.DMA

    def own_block():
        row = lax.axis_index("row") * half
        column = lax.axis_index("col") * depth
        return pl.ds(pl.multiple_of(row, half), half), pl.ds(pl.multiple_of(column, 128), depth)

    args = (
        part,
        xhat,
        rstd,
        gain,
        grad_middle,
        heads_grad,
        out_grad,
        second,
        mixed_part,
        middle,
        piece,
        bias,
    )
    return staged_call(
        functools.partial(last_kernel, cols),
        args,
        out_shape=(
            jax.ShapeDtypeStruct((half, depth), F32),
            jax.ShapeDtypeStruct((half, depth), BF16),
            jax.ShapeDtypeStruct(small, F32),
            jax.ShapeDtypeStruct((dp, 4, rows, cols * narrow), BF16),
            jax.ShapeDtypeStruct((dp,) + piece.shape, BF16),
        ),
        in_specs=[VM] * 10 + [ANY, VM],
        out_specs=[VM] * 3 + [ANY] * 2,
        loads=[(i, args[i].shape, None) for i in (0, 5, 6, 8, 9, 1, 2)]
        + [(4, (half, depth), own_block)],
        stores=(0, 1),
        scratch_shapes=[
            pltpu.VMEM((half // SUBS, depth), F32),
            pltpu.VMEM((half, depth), F32),
            pltpu.VMEM((8, half), F32),
            pltpu.VMEM((cols - 1, 8, half), F32),
            pltpu.VMEM((cols, rows, 4 * narrow), BF16),
            pltpu.VMEM((cols, rows, 4 * narrow), BF16),
            pltpu.VMEM((cols, 8, depth), F32),
            pltpu.VMEM((8, depth), F32),
            pltpu.VMEM((8, depth), F32),
            pltpu.VMEM((4, rows, cols * narrow), BF16),
            pltpu.VMEM(small, F32),
            pltpu.VMEM((dp,) + small, F32),
            dma((cols - 1,)),
            dma((cols - 1,)),
            dma((2,)),
            dma((hops,)),
            dma((hops,)),
            dma((2,)),
        ]
        + Reduce.scratch(cols, SUBS, half, width) * 2
        + Exchange.scratch(cols) * 2
        + Broadcast.scratch(dp, 2 * piece.shape[0])
        + Broadcast.scratch(dp, 4),
        compiler_params=params(5),
        cost_estimate=cost(110),
        name="input_grad_mixed_sum",
    )


def start_kernel(
    cols,
    tokens,
    vector,
    heads_from,
    out_from,
    gate_up_from,
    down_from,
    normed,
    tokens_own,
    xhat,
    rstd,
    vectors,
    gate_up_piece,
    down_piece,
    attention_w,
    heads,
    out,
    gate_up,
    down,
    pieces,
    landed,
    full,
    in_sem,
    own_sem,
    pair_send,
    pair_recv,
    *sems,
    load,
    store
):
    half, depth = tokens.shape
    width = depth * cols
    step = half // cols
    dp, _, part, wide = attention_w.shape
    narrow = wide // 4
    tall = down.shape[0] // cols
    r, c, me = (lax.axis_index(name) for name in ("row", "col", "dp"))
    begin = pl.multiple_of(me * part, part)
    rows_in = pl.ds(begin, part)

    def share_of(ref):
        return ref if ref.shape[1] == part else ref.at[:, rows_in]

    loads = [
        pltpu.make_async_copy(heads_from.at[:, rows_in], heads, in_sem.at[0]),
        pltpu.make_async_copy(share_of(out_from), out, in_sem.at[1]),
        pltpu.make_async_copy(gate_up_from.at[rows_in], gate_up, in_sem.at[2]),
        pltpu.make_async_copy(share_of(down_from), down, in_sem.at[3]),
    ]
    for load in loads:
        load.start()
    enter(cols, everyone=True, dp=dp)
    loads[0].wait()
    loads[1].wait()
    for j in range(cols):
        share = slice(j * narrow, (j + 1) * narrow)
        for k in range(3):
            pieces[j, :, k * narrow : (k + 1) * narrow] = heads[k, :, share]
        pieces[j, :, 3 * narrow :] = out[share, :].T
    rider = Exchange("col", cols, pieces, landed, sems[:3])
    assert cols == 4
    landed[c] = pieces[c]
    units = [c] + [rider.peer(k) for k in range(1, cols)]
    cast = Broadcast(
        dp, cols, lambda k: landed.at[units[k]], lambda p, k: attention_w.at[p, units[k]], sems[11:13]
    )
    cast.start((0,))
    for k in range(1, cols):
        rider.hop(k).start()

    def columns(source):
        return pl.ds(pl.multiple_of(source * depth, 128), depth)

    names = Gather(
        cols, 1, lambda r, source, s: (pl.ds(0, 8), columns(source)), vectors, sems[3:7], pair=False
    )
    spread = Gather(
        cols,
        cols,
        lambda r, source, s: (pl.ds(s * step, step), columns(source)),
        full,
        sems[7:11],
        pair=False,
    )
    vectors[:, columns(c)] = vector[...]
    names.start(0)
    for s in range(cols):
        rows = pl.ds(s * step, step)
        full[rows, columns(c)] = tokens[rows, :]
        spread.start(s)
    loads[2].wait()
    for i in range(2):
        values = gate_up[:, i, :]
        for j in range(cols):
            gate_up_piece[j, :, i * tall : (i + 1) * tall] = values[:, j * tall : (j + 1) * tall]
    loads[3].wait()
    for j in range(cols):
        down_piece[j, :, :tall] = down[j * tall : (j + 1) * tall, :].T
        if down_piece.shape[2] > tall:
            down_piece[j, :, tall:] = jnp.zeros((part, down_piece.shape[2] - tall), BF16)

    store(5, 6)

    def across(r, s):
        where = normed.at[pl.ds(pl.multiple_of(r * half + s * step, 16), step), :]
        return send(where, where, pair_send.at[s], pair_recv.at[s], row=1 - lax.axis_index("row"))

    def own(k):
        u = units[k]
        return pltpu.make_async_copy(landed.at[u], attention_w.at[me, u], own_sem.at[k])

    def take(k):
        rider.hop(k).wait_recv()
        cast.start((k,))
        own(k).start()

    def norm(s):
        rows = slice(s * step, (s + 1) * step)
        state = full[rows, :].astype(F32)
        centered, inverse = moments(state)
        result = centered * inverse * vectors[0:1, :] + vectors[1:2, :]
        normed[pl.ds(pl.multiple_of(r * half + s * step, 16), step), :] = result.astype(BF16)
        across(r, s).start()
        rstd[rows, :] = jnp.broadcast_to(inverse, (step, 128))
        mean = jnp.mean(state, axis=1, keepdims=True)
        xhat[rows, :] = (tokens[rows, :].astype(F32) - mean) * inverse

        @pl.when(c == s)
        def _():
            tokens_own[...] = full[rows, :]

    own(0).start()
    take(1)
    for k in range(1, cols):
        names.relay(0, k)
    for s in range(cols):
        spread.relay(s, 1)
    cast.forward(0)
    take(2)
    take(3)
    for s in range(cols):
        spread.relay(s, 2)
    cast.forward(1)
    cast.forward(2)
    for s in range(cols):
        spread.relay(s, 3)
        norm(s)
        if s == 1:
            cast.forward(3)

    for s in range(cols):
        across(1 - r, s).wait_recv()
    store(0, 1, 2, 3)
    for s in range(cols):
        across(r, s).wait_send()
    for u in range(cols):
        own(u).wait()
    cast.finish()
    for k in range(1, cols):
        rider.hop(k).wait_send()
    names.finish()
    spread.finish()


def start_part(tokens, vector, heads, out, gate_up, down, sizes):
    dp, cols = sizes["dp"], sizes["col"]
    half, depth = tokens.shape
    width = depth * cols
    part, wide, tall = depth // dp, heads.shape[2], down.shape[0]
    each = tall // cols
    dma = pltpu.SemaphoreType.DMA
    return staged_call(
        functools.partial(start_kernel, cols),
        (tokens, vector, heads, out, gate_up, down),
        out_shape=(
            jax.ShapeDtypeStruct((2 * half, width), BF16),
            jax.ShapeDtypeStruct((half // cols, width), BF16),
            jax.ShapeDtypeStruct((half, depth), F32),
            jax.ShapeDtypeStruct((half, 128), F32),
            jax.ShapeDtypeStruct((8, width), F32),
            jax.ShapeDtypeStruct((cols, part, 2 * each), BF16),
            jax.ShapeDtypeStruct((cols, part, each + -each % 128), BF16),
            jax.ShapeDtypeStruct((dp, cols, part, 4 * wide // cols), BF16),
        ),
        in_specs=[VM] * 2 + [ANY] * 4,
        out_specs=[VM] * 7 + [ANY],
        loads=(),
        stores=(0, 1, 2, 3, 5, 6),
        scratch_shapes=[
            pltpu.VMEM((3, part, wide), BF16),
            pltpu.VMEM((wide, part), BF16),
            pltpu.VMEM((part, 2, tall), BF16),
            pltpu.VMEM((tall, part), BF16),
            pltpu.VMEM((cols, part, 4 * wide // cols), BF16),
            pltpu.VMEM((cols, part, 4 * wide // cols), BF16),
            pltpu.VMEM((half, width), BF16),
            dma((4,)),
            dma((cols,)),
            dma((cols,)),
            dma((cols,)),
        ]
        + Exchange.scratch(cols)
        + Gather.scratch(cols, 1)
        + Gather.scratch(cols, cols)
        + Broadcast.scratch(dp, cols),
        compiler_params=params(1),
        cost_estimate=cost(60),
        name="tokens_norm_weights",
    )


def rope_tables(length):
    half_rot = ROT // 2
    lane = np.arange(2 * HD) % HD
    inverse = (ROPE_BASE ** (-2.0 * (lane % half_rot) / ROT)).astype(np.float32)
    angles = np.arange(length).astype(np.float32)[:, None] * inverse[None, :]
    turning = lane < ROT
    cosine = np.where(turning, np.cos(angles), 1.0)
    sine = np.where(turning, np.sin(angles), 0.0)
    lower = np.where(lane < half_rot, -sine, 0.0)
    upper = np.where(lane >= half_rot, sine, 0.0)
    return np.stack([cosine, lower, upper]).astype(np.float32)


def turn(x, tables, back=False):
    half_rot = ROT // 2
    width = x.shape[1]
    sines = pltpu.roll(x, width - half_rot, 1) * tables[1] + pltpu.roll(x, half_rot, 1) * tables[2]
    return x * tables[0] - sines if back else x * tables[0] + sines


def causal(rows):
    return lax.broadcasted_iota(jnp.int32, (rows, rows), 0) >= lax.broadcasted_iota(
        jnp.int32, (rows, rows), 1
    )


def attend_kernel(
    cols,
    normed,
    weight,
    bias,
    tables,
    one_from,
    two_from,
    heads_in,
    attn,
    logs,
    part,
    one_to,
    two_to,
    whole,
    sem,
    qkv,
    *sems,
    load,
    store
):
    length, wide = attn.shape
    two = 2 * HD
    copies = load_columns(weight, whole, sem)
    enter(cols, everyone=True)
    riders = (
        Exchange("col", cols, one_from, one_to, sems[:3]),
        Exchange("col", cols, two_from, two_to, sems[3:]),
    )
    for rider in riders:
        rider.start()
    for copy in copies:
        copy.wait()
    load(0, 3)
    first_head = lax.broadcasted_iota(jnp.int32, (BLOCK, two), 1) < HD

    @pl.loop(0, length // BLOCK)
    def _(m):
        rows = pl.ds(pl.multiple_of(m * BLOCK, BLOCK), BLOCK)
        qkv[rows, :] = dot_nn(normed[rows, :], whole[:, : 3 * wide]) + bias[0:1, :]

    @pl.loop(0, wide // two)
    def _(pair):
        def lanes(k):
            return pl.ds(pl.multiple_of(k * wide + pair * two, two), two)

        for k in range(3):
            x = qkv[:, lanes(k)]
            if k < 2:
                x = turn(x, tables)
            if k == 0:
                x = x * HD ** (-0.5)
            heads_in[:, lanes(k)] = x.astype(BF16)
        for i in range(length // BLOCK):
            keep = (i + 1) * BLOCK
            rows = slice(i * BLOCK, keep)
            query = heads_in[rows, lanes(0)]
            keys = heads_in[0:keep, lanes(1)]
            values = heads_in[0:keep, lanes(2)]
            outs = []
            for h in range(2):
                mine = first_head if h == 0 else ~first_head
                scores = dot_nt(jnp.where(mine, query, jnp.zeros_like(query)), keys)
                last = jnp.where(causal(BLOCK), scores[:, i * BLOCK :], NEG_LARGE)
                scores = last if i == 0 else jnp.concatenate([scores[:, : i * BLOCK], last], axis=1)
                top = jnp.max(scores, axis=1, keepdims=True)
                expo = jnp.exp(scores - top)
                total = jnp.sum(expo, axis=1, keepdims=True)
                probs = (expo * (1.0 / total)).astype(BF16)
                outs.append(dot_nn(probs, values))
                logs[pair, h, rows, :] = jnp.broadcast_to(top + jnp.log(total), (BLOCK, 128))
            attn[rows, pl.ds(pl.multiple_of(pair * two, two), two)] = jnp.where(
                first_head, outs[0], outs[1]
            ).astype(BF16)

    store(0, 1, 2)

    @pl.loop(0, length // BLOCK)
    def _(m):
        rows = pl.ds(pl.multiple_of(m * BLOCK, BLOCK), BLOCK)
        part[rows, :] = dot_nt(attn[rows, :], whole[:, 3 * wide :]).astype(BF16)

    store(3)
    for rider in riders:
        rider.finish()


def attend(cols, normed, weight, bias, tables, one, two):
    length, width = normed.shape
    dp = weight.shape[0]
    wide = weight.shape[3] // 4
    args = (normed, weight, bias, tables, one, two)
    return staged_call(
        functools.partial(attend_kernel, cols),
        args,
        out_shape=(
            jax.ShapeDtypeStruct((length, 3 * wide), BF16),
            jax.ShapeDtypeStruct((length, wide), BF16),
            jax.ShapeDtypeStruct((wide // (2 * HD), 2, length, 128), F32),
            jax.ShapeDtypeStruct((length, width), BF16),
            jax.ShapeDtypeStruct(one.shape, BF16),
            jax.ShapeDtypeStruct(two.shape, BF16),
        ),
        in_specs=[VM, ANY, VM, VM, ANY, ANY],
        out_specs=[VM] * 4 + [ANY] * 2,
        loads=[(i, args[i].shape, None) for i in (0, 3)],
        stores=(0, 1, 2, 3),
        scratch_shapes=[
            pltpu.VMEM((width, 4 * wide), BF16),
            pltpu.SemaphoreType.DMA((dp, cols)),
            pltpu.VMEM((length, 3 * wide), F32),
        ]
        + Exchange.scratch(cols) * 2,
        compiler_params=params(6),
        cost_estimate=cost(50),
        name="attention_weight_exchange",
    )


def attend_back_kernel(
    cols,
    heads_in,
    logs,
    grad_middle,
    tables,
    weight,
    normed,
    attn,
    pieces_from,
    heads_to,
    out_to,
    normed_grad,
    sums,
    arranged,
    queries_grad,
    keys_grad,
    values_grad,
    whole,
    sem,
    grad,
    result,
    own,
    pieces_to,
    heads_from,
    out_from,
    *sems,
    load,
    store
):
    length, wide = attn.shape
    two = 2 * HD
    dp, _, part_rows, _ = weight.shape
    copies = load_columns(weight, whole, sem)
    enter(cols, everyone=True, dp=dp)
    rider = Exchange("col", cols, pieces_from, pieces_to, sems[:3])
    rider.start()
    out_rider = Exchange("dp", dp, out_from, out_to, sems[3:6])
    depth = normed.shape[1] // cols
    load(2, 6)

    def heads_rider(pair):
        return Exchange(
            "dp", dp, heads_from.at[pair], heads_to.at[pair], [sem.at[pair] for sem in sems[6:]]
        )

    def parts(j):
        return pl.ds(pl.multiple_of(j * depth, depth), depth)

    @pl.loop(0, cols)
    def _(j):
        out_grad = dot_tn(grad_middle[:, parts(j)], attn[...]).astype(BF16)
        for p in range(dp):
            out_from[p, j] = out_grad[p * part_rows : (p + 1) * part_rows, :]

    out_rider.start()
    for copy in copies:
        copy.wait()
    load(0, 1, 3, 5)
    sums[...] = jnp.zeros_like(sums)
    first_head = lax.broadcasted_iota(jnp.int32, (BLOCK, two), 1) < HD

    @pl.loop(0, length // BLOCK)
    def _(m):
        rows = pl.ds(pl.multiple_of(m * BLOCK, BLOCK), BLOCK)
        grad[rows, :] = dot_nn(grad_middle[rows, :], whole[:, 3 * wide :]).astype(BF16)

    @pl.loop(0, wide // two)
    def _(pair):
        def lanes(k):
            return pl.ds(pl.multiple_of(k * wide + pair * two, two), two)

        keys_grad[...] = jnp.zeros_like(keys_grad)
        values_grad[...] = jnp.zeros_like(values_grad)
        for i in range(length // BLOCK):
            keep = (i + 1) * BLOCK
            rows = slice(i * BLOCK, keep)
            query = heads_in[rows, lanes(0)]
            keys = heads_in[0:keep, lanes(1)]
            values = heads_in[0:keep, lanes(2)]
            out_grad = grad[rows, lanes(0)]
            outs = []
            for h in range(2):
                mine = first_head if h == 0 else ~first_head
                query_h = jnp.where(mine, query, jnp.zeros_like(query))
                grad_h = jnp.where(mine, out_grad, jnp.zeros_like(out_grad))
                scores = dot_nt(query_h, keys)
                probs = jnp.exp(scores - logs[pair, h, rows, 0:1])
                last = jnp.where(causal(BLOCK), probs[:, i * BLOCK :], 0.0)
                probs = last if i == 0 else jnp.concatenate([probs[:, : i * BLOCK], last], axis=1)
                probs_grad = dot_nt(grad_h, values)
                delta = jnp.sum(probs * probs_grad, axis=1, keepdims=True)
                scores_grad = (probs * (probs_grad - delta)).astype(BF16)
                outs.append(dot_nn(scores_grad, keys))
                keys_grad[0:keep, :] += dot_tn(scores_grad, query_h)
                values_grad[0:keep, :] += dot_tn(probs.astype(BF16), grad_h)
            queries_grad[rows, :] = jnp.where(first_head, outs[0], outs[1]) * HD ** (-0.5)
        grads = (
            turn(queries_grad[...], tables, back=True),
            turn(keys_grad[...], tables, back=True),
            values_grad[...],
        )
        for k in range(3):
            low = grads[k].astype(BF16)
            result[:, lanes(k)] = low
            own[:, k * two : (k + 1) * two] = low
            column_sum = jnp.sum(low.astype(F32), axis=0, keepdims=True)
            sums[0:1, lanes(k)] = column_sum

        @pl.loop(0, cols)
        def _(j):
            heads_grad = dot_tn(normed[:, parts(j)], own[...]).astype(BF16)
            for p in range(dp):
                heads_from[pair, p, j] = heads_grad[p * part_rows : (p + 1) * part_rows, :]

        heads_rider(pair).start()

    @pl.loop(0, length // BLOCK)
    def _(m):
        rows = pl.ds(pl.multiple_of(m * BLOCK, BLOCK), BLOCK)
        normed_grad[rows, :] = dot_nt(result[rows, :], whole[:, : 3 * wide]).astype(BF16)

    store(2)
    out_rider.finish()
    for pair in range(wide // two):
        heads_rider(pair).finish()
    rider.finish()
    share = arranged.shape[2] // cols
    for k in range(arranged.shape[0]):
        arranged[k] = jnp.concatenate(
            [pieces_to[j, :, k * share : (k + 1) * share] for j in range(cols)], axis=1
        )


def attend_back(cols, heads_in, logs, grad_middle, tables, weight, normed, attn, pieces, share):
    length, wide = attn.shape
    width = normed.shape[1]
    dp, _, part, _ = weight.shape
    pairs = wide // (2 * HD)
    heads = (pairs, dp, cols, part, 6 * HD)
    out = (dp, cols, part, wide)
    hops = max(dp - 1, 1)
    dma = pltpu.SemaphoreType.DMA
    args = (heads_in, logs, grad_middle, tables, weight, normed, attn, pieces)
    return staged_call(
        functools.partial(attend_back_kernel, cols),
        args,
        out_shape=(
            jax.ShapeDtypeStruct(heads, BF16),
            jax.ShapeDtypeStruct(out, BF16),
            jax.ShapeDtypeStruct((length, width), BF16),
            jax.ShapeDtypeStruct((8, 3 * wide), F32),
            jax.ShapeDtypeStruct((3, pieces.shape[1], cols * share), BF16),
        ),
        in_specs=[VM] * 4 + [ANY, VM, VM, ANY],
        out_specs=[ANY] * 2 + [VM] * 3,
        loads=[(i, args[i].shape, None) for i in (2, 6, 0, 1, 3, 5)],
        stores=(2,),
        scratch_shapes=[pltpu.VMEM((length, 2 * HD), F32)] * 3
        + [
            pltpu.VMEM((width, 4 * wide), BF16),
            pltpu.SemaphoreType.DMA(weight.shape[:2]),
            pltpu.VMEM((length, wide), BF16),
            pltpu.VMEM((length, 3 * wide), BF16),
            pltpu.VMEM((length, 6 * HD), BF16),
            pltpu.VMEM(pieces.shape, BF16),
            pltpu.VMEM(heads, BF16),
            pltpu.VMEM(out, BF16),
        ]
        + Exchange.scratch(cols)
        + Exchange.scratch(dp)
        + [dma((pairs, hops)), dma((pairs, hops)), dma((pairs, 1))],
        compiler_params=params(8),
        cost_estimate=cost(50),
        name="attention_back_exchange",
    )


def hidden_back_kernel(
    hidden_from,
    gate_from,
    up_from,
    cotan_from,
    down_from,
    normed_from,
    weight_to,
    grads_to,
    hidden,
    gate_part,
    up_part,
    cotan,
    down,
    normed,
    grads,
    weight_grad,
    down_sem,
    block_sem,
    whole_sem,
    out_sem,
    grad_sem,
):
    group, narrow = hidden.shape
    dp, cols, part_rows, _ = down_from.shape
    wide = weight_grad.shape[3]
    blocks = group // BLOCK
    depth = normed.shape[1] // cols

    def rows_of(m):
        return pl.ds(pl.multiple_of(m * BLOCK, BLOCK), BLOCK)

    def block_copies(m):
        rows = rows_of(m)
        pairs = ((cotan_from, cotan), (gate_from, gate_part), (up_from, up_part))
        return [
            pltpu.make_async_copy(a.at[rows, :], b.at[rows, :], block_sem.at[i, m])
            for i, (a, b) in enumerate(pairs)
        ]

    down_copies = load_columns(down_from, down, down_sem)
    for copy in block_copies(0):
        copy.start()
    for m in range(1, blocks):
        for copy in block_copies(m):
            copy.start()
    whole_copies = [
        pltpu.make_async_copy(hidden_from, hidden, whole_sem.at[0]),
        pltpu.make_async_copy(normed_from, normed, whole_sem.at[1]),
    ]
    for copy in whole_copies:
        copy.start()
    for copy in down_copies:
        copy.wait()

    def grads_out(m):
        rows = rows_of(m)
        return pltpu.make_async_copy(grads.at[rows, :], grads_to.at[rows, :], out_sem.at[m])

    def weight_out(p, j):
        return pltpu.make_async_copy(weight_grad.at[p, j], weight_to.at[p, j], grad_sem.at[p, j])

    @pl.loop(0, blocks)
    def _(m):
        rows = rows_of(m)
        for copy in block_copies(m):
            copy.wait()
        grad = dot_nn(cotan[rows, :], down[:, :narrow])
        both = jnp.concatenate(
            [grad * gate_part[rows, :].astype(F32), grad * up_part[rows, :].astype(F32)], axis=1
        )
        grads[rows, :] = both.astype(BF16)
        grads_out(m).start()

    for copy in whole_copies:
        copy.wait()

    @pl.loop(0, cols)
    def _(j):
        columns = pl.ds(pl.multiple_of(j * depth, depth), depth)
        gate_up_grad = dot_tn(normed[:, columns], grads[...]).astype(BF16)
        down_grad = dot_tn(cotan[:, columns], hidden[...]).astype(BF16)
        for p in range(dp):
            rows = slice(p * part_rows, (p + 1) * part_rows)
            weight_grad[p, j, :, : 2 * narrow] = gate_up_grad[rows, :]
            weight_grad[p, j, :, 2 * narrow : 3 * narrow] = down_grad[rows, :]
            if wide > 3 * narrow:
                weight_grad[p, j, :, 3 * narrow :] = jnp.zeros((part_rows, wide - 3 * narrow), BF16)
            weight_out(p, j).start()

    for m in range(blocks):
        grads_out(m).wait()
    for p in range(dp):
        for j in range(cols):
            weight_out(p, j).wait()


def hidden_back(hidden, gate_part, up_part, cotan, down, normed):
    group, width = normed.shape
    dp, cols, part, _ = down.shape
    double = 2 * hidden.shape[1]
    grad_shape = (dp, cols, part, double + down.shape[3])
    blocks = group // BLOCK
    dma = pltpu.SemaphoreType.DMA
    return pl.pallas_call(
        hidden_back_kernel,
        out_shape=(
            jax.ShapeDtypeStruct(grad_shape, BF16),
            jax.ShapeDtypeStruct((group, double), BF16),
        ),
        in_specs=[ANY] * 6,
        out_specs=(ANY,) * 2,
        scratch_shapes=[
            pltpu.VMEM(hidden.shape, BF16),
            pltpu.VMEM(gate_part.shape, BF16),
            pltpu.VMEM(up_part.shape, BF16),
            pltpu.VMEM(cotan.shape, BF16),
            pltpu.VMEM((width, down.shape[3]), BF16),
            pltpu.VMEM(normed.shape, BF16),
            pltpu.VMEM((group, double), BF16),
            pltpu.VMEM(grad_shape, BF16),
            dma((dp, cols)),
            dma((3, blocks)),
            dma((2,)),
            dma((blocks,)),
            dma((dp, cols)),
        ],
        compiler_params=pltpu.CompilerParams(vmem_limit_bytes=VMEM_LIMIT),
        cost_estimate=cost(30),
        name="hidden_back",
    )(hidden, gate_part, up_part, cotan, down, normed)


def split_kernel(hidden, attention, gate_up, down, heads, out):
    def part(whole, k):
        return whole[:, k].reshape(whole.shape[0] * whole.shape[2], whole.shape[3]).astype(F32)

    for k in range(2):
        gate_up[:, k, :] = part(hidden, k)
    down[...] = part(hidden, 2).T
    for k in range(3):
        heads[k] = part(attention, k)
    out[...] = part(attention, 3).T


def weights_split(hidden, attention):
    dp, _, part, _ = hidden.shape
    rows = min(part, 128)
    per = 128 // rows
    depth = dp * part
    tall, wide = hidden.shape[3], attention.shape[3]

    def source(count, lanes):
        return pl.BlockSpec(
            (per, count, rows, lanes),
            lambda b: (b * 128 // (per * part), 0, lax.rem(b, max(part // 128, 1)), 0),
        )

    return pl.pallas_call(
        split_kernel,
        grid=(depth // 128,),
        out_shape=(
            jax.ShapeDtypeStruct((depth, 2, tall), F32),
            jax.ShapeDtypeStruct((tall, depth), F32),
            jax.ShapeDtypeStruct((3, depth, wide), F32),
            jax.ShapeDtypeStruct((wide, depth), F32),
        ),
        in_specs=[source(3, tall), source(4, wide)],
        out_specs=(
            pl.BlockSpec((128, 2, tall), lambda b: (b, 0, 0)),
            pl.BlockSpec((tall, 128), lambda b: (0, b)),
            pl.BlockSpec((3, 128, wide), lambda b: (0, b, 0)),
            pl.BlockSpec((wide, 128), lambda b: (0, b)),
        ),
        compiler_params=pltpu.CompilerParams(vmem_limit_bytes=VMEM_LIMIT),
        cost_estimate=cost(15),
        name="weight_gradients",
    )(hidden, attention)


def weights_whole(piece):
    return lax.all_gather(piece, "dp", axis=0)


def weights_sum(pieces):
    dp, cols, part, wide = pieces.shape
    piece = lax.psum_scatter(
        pieces.reshape(dp * cols * part, wide), "dp", scatter_dimension=0, tiled=True
    )
    return piece.reshape(cols, part, wide)


def make_body(sizes):
    cols = sizes["col"]

    def body(
        tokens,
        attention_norm_gain,
        attention_norm_bias,
        qkv_weight,
        qkv_bias,
        out_weight,
        feedforward_norm_gain,
        feedforward_norm_bias,
        gate_up_weight,
        down_weight,
        cotangent,
    ):
        my_dp = lax.axis_index("dp")
        depth = tokens.shape[1]
        tables = rope_tables(SEQ)
        vector = jnp.stack(
            [attention_norm_gain, attention_norm_bias, feedforward_norm_gain, feedforward_norm_bias]
        )
        vector = jnp.concatenate([vector, jnp.zeros_like(vector)])
        part = depth // sizes["dp"]

        def share_of(rows):
            return rows if part % 128 == 0 else lax.dynamic_slice_in_dim(rows, my_dp * part, part, 1)

        (
            normed_one,
            tokens_own,
            xhat_one,
            rstd_one,
            vectors,
            gate_up_piece,
            down_piece,
            attention_w,
        ) = start_part(
            tokens,
            vector,
            qkv_weight.transpose(1, 0, 2),
            share_of(out_weight),
            gate_up_weight,
            share_of(down_weight),
            sizes,
        )
        heads_in, attn, logs, branch_part, gate_up_piece, down_piece = attend(
            cols,
            normed_one,
            attention_w,
            qkv_bias.reshape(1, -1),
            tables,
            gate_up_piece,
            down_piece,
        )
        down_w = weights_whole(down_piece)
        narrow = down_weight.shape[0] // cols
        normed_two, middle, hidden, gate_part, up_part, gate_up_w, cotan_rows = middle_part(
            cols, branch_part, tokens_own, vectors, gate_up_piece, cotangent, sizes["dp"]
        )
        hidden_grad, gate_up_grad = hidden_back(
            hidden, gate_part, up_part, cotan_rows, down_w, normed_two
        )
        hidden_sum = weights_sum(hidden_grad)
        grad_middle, second, mixed_part = norm_two_back(
            cols, gate_up_grad, gate_up_w, middle, cotan_rows, vectors, hidden, down_w
        )
        second = second.reshape(8, cols, depth).transpose(1, 0, 2)
        heads_grad, out_grad, normed_part, bias_part, hidden_sum = attend_back(
            cols,
            heads_in,
            logs,
            grad_middle,
            tables,
            attention_w,
            normed_one,
            attn,
            hidden_sum,
            narrow,
        )
        input_grad, mixed, small, attention_sum, hidden_sum = last_part(
            cols,
            normed_part,
            xhat_one,
            rstd_one,
            attention_norm_gain.reshape(1, -1),
            grad_middle,
            heads_grad,
            out_grad,
            second,
            mixed_part,
            middle,
            hidden_sum,
            bias_part,
        )
        grad_gate_up, grad_down, grad_qkv_weight, grad_out = weights_split(hidden_sum, attention_sum)
        grad_qkv_weight = grad_qkv_weight.transpose(1, 0, 2)
        return (
            mixed,
            input_grad,
            small[0, :depth],
            small[1, :depth],
            grad_qkv_weight,
            small[0, depth:].reshape(3, -1),
            grad_out,
            small[2, :depth],
            small[3, :depth],
            grad_gate_up,
            grad_down,
        )

    return body


def solution(mesh):
    specs = (
        P(("dp", "row"), "col"),
        P("col"),
        P("col"),
        P("col", None, "row"),
        P(None, ("row", "col")),
        P("row", "col"),
        P("col"),
        P("col"),
        P("col", None, "row"),
        P("row", "col"),
    )
    return jax.shard_map(
        make_body(dict(mesh.shape)),
        mesh=mesh,
        in_specs=specs + (P(("dp", "row"), "col"),),
        out_specs=(P(("dp", "row"), "col"),) + specs,
        check_vma=False,
    )
```

```python
import functools

import jax
import jax.numpy as jnp
import numpy as np
from jax import lax
from jax.experimental import pallas as pl
from jax.experimental.pallas import tpu as pltpu
from jax.sharding import PartitionSpec as P

MODEL_WIDTH = 2048
HD = 64
ROT = 16
SEQ = 1024
EPSILON = 1e-05
ROPE_BASE = 10000.0
NEG_LARGE = -1e30
F32 = jnp.float32
BF16 = jnp.bfloat16
MESH = pl.DeviceIdType.MESH
VMEM_LIMIT = 56 * 1024 * 1024
SUBS = 8


def send(src, dst, send_sem, recv_sem, **where):
    return pltpu.make_async_remote_copy(
        src_ref=src,
        dst_ref=dst,
        send_sem=send_sem,
        recv_sem=recv_sem,
        device_id=where,
        device_id_type=MESH,
    )


def enter(cols, everyone=False, dp=1):
    r, c = lax.axis_index("row"), lax.axis_index("col")
    barrier = pltpu.get_barrier_semaphore()
    pl.semaphore_signal(barrier, inc=1, device_id={"row": 1 - r}, device_id_type=MESH)
    if everyone:
        for k in range(1, cols):
            pl.semaphore_signal(
                barrier, inc=1, device_id={"col": lax.rem(c + k, cols)}, device_id_type=MESH
            )
        for k in range(1, dp):
            pl.semaphore_signal(
                barrier,
                inc=1,
                device_id={"dp": lax.rem(lax.axis_index("dp") + k, dp)},
                device_id_type=MESH,
            )
        pl.semaphore_wait(barrier, cols + dp - 1)
        return

    @pl.when(c > 0)
    def _():
        pl.semaphore_signal(barrier, inc=1, device_id={"col": c - 1}, device_id_type=MESH)

    @pl.when(c < cols - 1)
    def _():
        pl.semaphore_signal(barrier, inc=1, device_id={"col": c + 1}, device_id_type=MESH)

    inner = (c > 0) & (c < cols - 1)

    @pl.when(inner)
    def _():
        pl.semaphore_wait(barrier, 3)

    @pl.when(jnp.logical_not(inner))
    def _():
        pl.semaphore_wait(barrier, 2)


LAG = 3
BLOCK = 256
PACE = 6


class Reduce:
    def __init__(self, cols, subs, spot, part, twin, going, coming, sems, add=None):
        self.cols, self.subs, self.spot, self.add = cols, subs, spot, add
        self.part, self.twin, self.going, self.coming = part, twin, going, coming
        self.twin_send, self.twin_recv, self.send, self.recv = sems
        self.r, self.c = lax.axis_index("row"), lax.axis_index("col")
        self.half = part.shape[0] // 2
        self.per_sub = cols - 1
        self.landing = LAG * (cols - 1)
        self.slots = self.per_sub * (subs - 1) + self.landing + 1

    def place(self, d, s, base=0):
        row, rows, column, columns = self.spot(d, s)
        if not isinstance(column, int):
            column = pl.multiple_of(column, 128)
        return pl.ds(pl.multiple_of(base + row, 16), rows), pl.ds(column, columns)

    def twin_copy(self, d, s):
        return send(
            self.part.at[self.place(d, s, (1 - self.r) * self.half)],
            self.twin.at[self.place(d, s)],
            self.twin_send.at[d, s],
            self.twin_recv.at[d, s],
            row=1 - self.r,
        )

    def start(self):
        @pl.loop(0, self.subs)
        def _(s):
            for j in range(self.cols):
                self.twin_copy(self.cols - 1 - j // 2 if j % 2 == 0 else j // 2, s).start()

    def hop(self, way, d, s):
        place = self.place(d, s)
        return send(
            self.going.at[(way,) + place],
            self.coming.at[(way,) + place],
            self.send.at[way, d, s],
            self.recv.at[way, d, s],
            col=self.c + 1 if way == 0 else self.c - 1,
        )

    def own(self, d, s):
        self.twin_copy(d, s).wait_recv()
        value = self.part[self.place(d, s, self.r * self.half)].astype(F32)
        value = value + self.twin[self.place(d, s)].astype(F32)
        if self.add is not None:
            value = value + self.add(d, s)
        return value

    def pass_on(self, way, d, s):
        place = (way,) + self.place(d, s)
        first = 0 if way == 0 else self.cols - 1

        @pl.when(self.c == first)
        def _():
            self.going[place] = self.own(d, s).astype(BF16)

        @pl.when(self.c != first)
        def _():
            value = self.own(d, s)
            self.hop(way, d, s).wait_recv()
            self.going[place] = (value + self.coming[place].astype(F32)).astype(BF16)

        self.hop(way, d, s).start()

    def slot(self, t):
        for way in range(2):
            made = self.c if way == 0 else self.cols - 1 - self.c
            event = t - LAG * made

            @pl.when((event >= 0) & (event < self.per_sub * self.subs))
            def _():
                s, j = lax.div(event, self.per_sub), lax.rem(event, self.per_sub)
                d = self.cols - 1 - j if way == 0 else j

                @pl.when(self.c < d if way == 0 else self.c > d)
                def _():
                    self.pass_on(way, d, s)

    def landed(self, t, do):
        after = t - self.landing

        @pl.when((after >= 0) & (lax.rem(after + self.per_sub * self.cols, self.per_sub) == 0))
        def _():
            s = lax.div(after, self.per_sub)

            @pl.when(s < self.subs)
            def _():
                do(s)

    def land(self, s, total):
        place = self.place(self.c, s)
        total[...] = self.own(self.c, s)

        @pl.when(self.c > 0)
        def _():
            self.hop(0, self.c, s).wait_recv()
            total[...] += self.coming[(0,) + place].astype(F32)

        @pl.when(self.c < self.cols - 1)
        def _():
            self.hop(1, self.c, s).wait_recv()
            total[...] += self.coming[(1,) + place].astype(F32)

    def finish(self):
        @pl.loop(0, self.subs)
        def _(s):
            for d in range(self.cols):
                self.twin_copy(d, s).wait_send()

                @pl.when(self.c < d)
                def _():
                    self.hop(0, d, s).wait_send()

                @pl.when(self.c > d)
                def _():
                    self.hop(1, d, s).wait_send()

    @staticmethod
    def scratch(cols, subs, half, width):
        return [
            pltpu.VMEM((half, width), BF16),
            pltpu.VMEM((2, half, width), BF16),
            pltpu.VMEM((2, half, width), BF16),
            pltpu.SemaphoreType.DMA((cols, subs)),
            pltpu.SemaphoreType.DMA((cols, subs)),
            pltpu.SemaphoreType.DMA((2, cols, subs)),
            pltpu.SemaphoreType.DMA((2, cols, subs)),
        ]


class Gather:
    def __init__(self, cols, subs, spot, whole, sems, pair=True):
        self.cols, self.subs, self.spot, self.whole, self.pair = cols, subs, spot, whole, pair
        self.send, self.recv, self.pair_send, self.pair_recv = sems
        self.r, self.c = lax.axis_index("row"), lax.axis_index("col")

    def hop(self, way, source, s):
        where = self.whole.at[self.spot(self.r, source, s)]
        return send(
            where,
            where,
            self.send.at[way, source, s],
            self.recv.at[way, source, s],
            col=self.c + 1 if way == 0 else self.c - 1,
        )

    def across(self, r, source, s):
        where = self.whole.at[self.spot(r, source, s)]
        return send(
            where, where, self.pair_send.at[source, s], self.pair_recv.at[source, s], row=1 - self.r
        )

    def start(self, s):
        @pl.when(self.c < self.cols - 1)
        def _():
            self.hop(0, self.c, s).start()

        @pl.when(self.c > 0)
        def _():
            self.hop(1, self.c, s).start()

        if self.pair:
            self.across(self.r, self.c, s).start()

    def relay(self, s, k):
        @pl.when(self.c >= k)
        def _():
            self.hop(0, self.c - k, s).wait_recv()

            @pl.when(self.c < self.cols - 1)
            def _():
                self.hop(0, self.c - k, s).start()

            if self.pair:
                self.across(self.r, self.c - k, s).start()

        @pl.when(self.c + k < self.cols)
        def _():
            self.hop(1, self.c + k, s).wait_recv()

            @pl.when(self.c > 0)
            def _():
                self.hop(1, self.c + k, s).start()

            if self.pair:
                self.across(self.r, self.c + k, s).start()

    def slot(self, t, begin, step, first=0, count=None):
        count = self.subs if count is None else count
        for k in range(1, self.cols):
            after = t - begin - LAG * k

            @pl.when((after >= 0) & (lax.rem(after + step * LAG * self.cols * 8, step) == 0))
            def _():
                s = lax.div(after, step)

                @pl.when(s < count)
                def _():
                    self.relay(first + s, k)

    def finish(self):
        @pl.loop(0, self.subs)
        def _(s):
            for source in range(self.cols):
                if self.pair:
                    self.across(1 - self.r, source, s).wait_recv()
                    self.across(self.r, source, s).wait_send()

                @pl.when((self.c >= source) & (self.c < self.cols - 1))
                def _():
                    self.hop(0, source, s).wait_send()

                @pl.when((self.c <= source) & (self.c > 0))
                def _():
                    self.hop(1, source, s).wait_send()

    @staticmethod
    def scratch(cols, subs):
        return [
            pltpu.SemaphoreType.DMA((2, cols, subs)),
            pltpu.SemaphoreType.DMA((2, cols, subs)),
            pltpu.SemaphoreType.DMA((cols, subs)),
            pltpu.SemaphoreType.DMA((cols, subs)),
        ]


class Exchange:
    def __init__(self, axis, size, source, target, sems):
        self.axis, self.size, self.source, self.target = axis, size, source, target
        self.send, self.recv, self.local = sems
        self.c = lax.axis_index(axis)

    def peer(self, k):
        if self.size == 4 and k != 2:
            return self.c + 1 - 2 * lax.rem(self.c, 2) if k == 1 else 3 - self.c
        return lax.rem(self.c + k, self.size)

    def hop(self, k):
        to = self.peer(k)
        return send(
            self.source.at[to],
            self.target.at[self.c],
            self.send.at[k - 1],
            self.recv.at[k - 1],
            **{self.axis: to},
        )

    def own(self):
        return pltpu.make_async_copy(
            self.source.at[self.c], self.target.at[self.c], self.local.at[0]
        )

    def start(self):
        for k in range(1, self.size):
            self.hop(k).start()
        self.own().start()

    def finish(self):
        self.own().wait()
        for k in range(1, self.size):
            self.hop(k).wait_recv()
        for k in range(1, self.size):
            self.hop(k).wait_send()

    @staticmethod
    def scratch(size):
        return [
            pltpu.SemaphoreType.DMA((size - 1,)),
            pltpu.SemaphoreType.DMA((size - 1,)),
            pltpu.SemaphoreType.DMA((1,)),
        ]


class Broadcast:
    def __init__(self, dp, units, source, target, sems):
        self.dp, self.units, self.source, self.target = dp, units, source, target
        self.send, self.recv = sems
        self.me = lax.axis_index("dp")
        self.near = self.me + 1 - 2 * lax.rem(self.me, 2)
        self.far = lax.rem(self.me + 2, dp)
        self.square = dp == 4

    def hop(self, i, u):
        if self.square:
            to = self.near if i == 0 else self.far
        else:
            to = lax.rem(self.me + i + 1, self.dp)
        return send(
            self.source(u), self.target(self.me, u), self.send.at[i, u], self.recv.at[i, u], dp=to
        )

    def across(self, u):
        low = u < self.units // 2
        where = self.target(self.near if low else self.far, u)
        return send(
            where,
            where,
            self.send.at[2, u],
            self.recv.at[2, u],
            dp=self.far if low else self.near,
        )

    def hops(self):
        return 2 if self.square else self.dp - 1

    def start(self, units=None):
        half = self.units // 2
        for n in range(self.units) if units is None else units:
            for i in range(self.hops()):
                u = (n + half) % self.units if self.square and i == 1 and units is None else n
                self.hop(i, u).start()

    def forward(self, u):
        if self.square:
            self.hop(0 if u < self.units // 2 else 1, u).wait_recv()
            self.across(u).start()

    def finish(self):
        for u in range(self.units):
            for i in range(self.hops()):
                if not self.square or (i == 0) != (u < self.units // 2):
                    self.hop(i, u).wait_recv()
                self.hop(i, u).wait_send()
            if self.square:
                self.across(u).wait()

    @staticmethod
    def scratch(dp, units):
        return [
            pltpu.SemaphoreType.DMA((max(dp - 1, 1), units)),
            pltpu.SemaphoreType.DMA((max(dp - 1, 1), units)),
        ]


ANY = pl.BlockSpec(memory_space=pl.ANY)


def staged_call(kernel, args, out_shape, in_specs, out_specs, scratch_shapes, loads, stores, **kinds):
    counts = len(args), len(out_shape)
    dma = pltpu.SemaphoreType.DMA
    buffers = [pltpu.VMEM(shape, args[i].dtype) for i, shape, _ in loads]
    buffers += [pltpu.VMEM(out_shape[j].shape, out_shape[j].dtype) for j in stores]
    in_specs, out_specs = list(in_specs), list(out_specs)
    for i, _, _ in loads:
        in_specs[i] = ANY
    for j in stores:
        out_specs[j] = ANY

    def run(*refs):
        ins, outs = list(refs[: counts[0]]), list(refs[counts[0] : sum(counts)])
        own = refs[len(refs) - len(buffers) - 2 :]
        in_sem, out_sem = own[-2:]
        coming, going = {}, {}
        for n, (i, _, part) in enumerate(loads):
            source = ins[i] if part is None else ins[i].at[part()]
            coming[i] = pltpu.make_async_copy(source, own[n], in_sem.at[n])
            ins[i] = own[n]
        for n, j in enumerate(stores):
            buffer = own[len(loads) + n]
            going[j] = pltpu.make_async_copy(buffer, outs[j], out_sem.at[n])
            outs[j] = buffer
        for copy in coming.values():
            copy.start()

        def load(*which):
            for i in which:
                coming[i].wait()

        def store(*which):
            for j in which:
                going[j].start()

        kernel(*ins, *outs, *refs[sum(counts) : len(refs) - len(own)], load=load, store=store)
        for copy in going.values():
            copy.wait()

    return pl.pallas_call(
        run,
        out_shape=tuple(out_shape),
        in_specs=in_specs,
        out_specs=tuple(out_specs),
        scratch_shapes=list(scratch_shapes)
        + buffers
        + [dma((max(len(loads), 1),)), dma((max(len(stores), 1),))],
        **kinds,
    )(*args)


def load_columns(weight, whole, sem):
    dp, cols, part, _ = weight.shape
    copies = [
        pltpu.make_async_copy(
            weight.at[p, j],
            whole.at[pl.ds((j * dp + p) * part, part), :],
            sem.at[p, j],
        )
        for p in range(dp)
        for j in range(cols)
    ]
    for copy in copies:
        copy.start()
    return copies


def dot_nt(a, b):
    return lax.dot_general(a, b, (((1,), (1,)), ((), ())), preferred_element_type=F32)


def dot_tn(a, b):
    return lax.dot_general(a, b, (((0,), (0,)), ((), ())), preferred_element_type=F32)


def dot_nn(a, b):
    return jnp.dot(a, b, preferred_element_type=F32)


def moments(rows):
    mean = jnp.mean(rows, axis=1, keepdims=True)
    centered = rows - mean
    return centered, lax.rsqrt(jnp.mean(centered * centered, axis=1, keepdims=True) + EPSILON)


def cost(us):
    return pl.CostEstimate(flops=us * 10**9, bytes_accessed=10**7, transcendentals=0)


def params(number):
    return pltpu.CompilerParams(
        collective_id=number, has_side_effects=True, vmem_limit_bytes=VMEM_LIMIT
    )


VM = pl.BlockSpec(memory_space=pltpu.VMEM)


def row_spot(own, step, half, width):
    def spot(r, source, s):
        return pl.ds(pl.multiple_of(r * half + source * own + s * step, 16), step), pl.ds(0, width)

    return spot


COTANGENT_SLOTS = (0, 28)


def middle_kernel(
    cols,
    part,
    tokens_own,
    vectors,
    piece,
    cotan,
    normed_to,
    middle_to,
    hidden_to,
    gate_to,
    up_to,
    weight_to,
    cotan_to,
    normed,
    middle,
    hidden,
    gate_part,
    up_part,
    weight,
    cotan_rows,
    total,
    own_sem,
    out_sem,
    block_sem,
    *scratch,
    load,
    store
):
    group, width = part.shape
    half = group // 2
    own = half // cols
    step = own // SUBS
    depth = cotan.shape[1]
    rows_each = half // SUBS
    _, part_rows, double = piece.shape
    narrow = double // 2
    dp = weight.shape[0] // cols // part_rows
    me = lax.axis_index("dp")
    enter(cols, everyone=True, dp=dp)
    load(0)
    summing = Reduce(
        cols, SUBS, lambda d, s: (d * own + s * step, step, 0, width), part, *scratch[:3], scratch[3:7]
    )
    summing.start()
    spread = Gather(cols, SUBS, row_spot(own, step, half, width), normed, scratch[7:11])

    def cotan_spot(r, source, s):
        rows = pl.ds(pl.multiple_of(r * half + s * rows_each, 16), rows_each)
        return rows, pl.ds(pl.multiple_of(source * depth, 128), depth)

    cotan_spread = Gather(cols, SUBS, cotan_spot, cotan_rows, scratch[11:15])

    def weight_rows(p, j):
        return weight.at[pl.ds(pl.multiple_of((j * dp + p) * part_rows, 16), part_rows), :]

    rider = Broadcast(dp, cols, lambda u: piece.at[u], weight_rows, scratch[15:17])
    rider.start()
    own_copies = [
        pltpu.make_async_copy(piece.at[j], weight_rows(me, j), own_sem.at[j]) for j in range(cols)
    ]
    for copy in own_copies:
        copy.start()
    load(1, 2, 4)

    def land(s):
        summing.land(s, total)
        rows = pl.ds(pl.multiple_of(s * step, step), step)
        state = tokens_own[rows, :].astype(F32) + total[...]
        middle[rows, :] = state
        centered, rstd = moments(state)
        result = centered * rstd * vectors[2:3, :] + vectors[3:4, :]
        normed[spread.spot(spread.r, spread.c, s)] = result.astype(BF16)
        spread.start(s)

    batch = SUBS // len(COTANGENT_SLOTS)

    def cotan_slot(t):
        for i, begin in enumerate(COTANGENT_SLOTS):
            after = t - begin

            @pl.when((after >= 0) & (lax.rem(after + 60, 3) == 0) & (after < 3 * batch))
            def _():
                s = i * batch + lax.div(after, 3)
                rows = pl.ds(pl.multiple_of(s * rows_each, 16), rows_each)
                cotan_rows[cotan_spot(spread.r, spread.c, s)] = cotan[rows, :]
                cotan_spread.start(s)

            cotan_spread.slot(t, begin, 3, i * batch, batch)

    first = summing.slots + LAG * (cols - 1)
    last = COTANGENT_SLOTS[-1] + 3 * (batch - 1) + LAG * (cols - 1) + 1
    blocks = group // BLOCK

    @pl.loop(0, first)
    def _(t):
        summing.slot(t)
        summing.landed(t, land)
        spread.slot(t, summing.landing, summing.per_sub)
        cotan_slot(t)
        for u in range(cols):

            @pl.when(t == 14 + 8 * (u % 2))
            def _():
                rider.forward(u)

    spread.finish()
    normed_out = pltpu.make_async_copy(normed, normed_to, out_sem.at[0])
    normed_out.start()
    middle_out = pltpu.make_async_copy(middle, middle_to, out_sem.at[1])
    middle_out.start()
    for copy in own_copies:
        copy.wait()
    rider.finish()
    weight_out = pltpu.make_async_copy(weight, weight_to, out_sem.at[2])
    weight_out.start()

    def block_out(m):
        rows = pl.ds(pl.multiple_of(m * BLOCK, BLOCK), BLOCK)
        pairs = ((hidden, hidden_to), (gate_part, gate_to), (up_part, up_to))
        return [
            pltpu.make_async_copy(a.at[rows, :], b.at[rows, :], block_sem.at[i, m])
            for i, (a, b) in enumerate(pairs)
        ]

    @pl.loop(0, max(last - first, blocks))
    def _(m):
        @pl.when(m < blocks)
        def _():
            rows = pl.ds(pl.multiple_of(m * BLOCK, BLOCK), BLOCK)
            both = dot_nn(normed[rows, :], weight[...])
            gate, up = both[:, :narrow], both[:, narrow:]
            sig = 1.0 / (1.0 + jnp.exp(-gate))
            active = gate * sig
            hidden[rows, :] = (active * up).astype(BF16)
            up_part[rows, :] = active.astype(BF16)
            gate_part[rows, :] = (up * sig * (1.0 + gate * (1.0 - sig))).astype(BF16)
            for copy in block_out(m):
                copy.start()

        cotan_slot(first + m)

    cotan_spread.finish()
    cotan_out = pltpu.make_async_copy(cotan_rows, cotan_to, out_sem.at[3])
    cotan_out.start()
    summing.finish()
    for m in range(blocks):
        for copy in block_out(m):
            copy.wait()
    for copy in (normed_out, middle_out, weight_out, cotan_out):
        copy.wait()


def middle_part(cols, part, tokens_own, vectors, piece, cotan, dp):
    group, width = part.shape
    _, part_rows, double = piece.shape
    narrow = double // 2
    blocks = group // BLOCK
    dma = pltpu.SemaphoreType.DMA
    outs = (
        ((group, width), BF16),
        (tokens_own.shape, F32),
        ((group, narrow), BF16),
        ((group, narrow), BF16),
        ((group, narrow), BF16),
        ((dp * cols * part_rows, double), BF16),
        ((group, width), BF16),
    )
    args = (part, tokens_own, vectors, piece, cotan)
    return staged_call(
        functools.partial(middle_kernel, cols),
        args,
        out_shape=tuple(jax.ShapeDtypeStruct(*out) for out in outs),
        in_specs=[VM] * 3 + [ANY, VM],
        out_specs=[ANY] * len(outs),
        loads=[(i, args[i].shape, None) for i in (0, 1, 2, 4)],
        stores=(),
        scratch_shapes=[pltpu.VMEM(*out) for out in outs]
        + [
            pltpu.VMEM((group // 2 // cols // SUBS, width), F32),
            dma((cols,)),
            dma((4,)),
            dma((3, blocks)),
        ]
        + Reduce.scratch(cols, SUBS, group // 2, width)
        + Gather.scratch(cols, SUBS) * 2
        + Broadcast.scratch(dp, cols),
        compiler_params=params(2),
        cost_estimate=cost(95),
        name="middle_gate_up",
    )


def norm_two_back_kernel(
    cols,
    gate_up_grad,
    gate_up,
    middle,
    cotan_own,
    vectors,
    hidden,
    weight,
    grads,
    sums,
    mixed_part,
    part,
    down,
    sem,
    *scratch,
    load,
    store
):
    narrow = hidden.shape[1]
    copies = load_columns(weight, down, sem)
    half, width = part.shape[0] // 2, part.shape[1]
    own = half // cols
    step = own // SUBS
    total = scratch[11]
    enter(cols)
    load(0, 1)
    summing = Reduce(
        cols, SUBS, lambda d, s: (d * own + s * step, step, 0, width), part, *scratch[:3], scratch[3:7]
    )
    spread = Gather(cols, SUBS, row_spot(own, step, half, width), grads, scratch[7:11])
    blocks = part.shape[0] // BLOCK
    row = lax.axis_index("row")

    def product(r):
        @pl.loop(0, blocks // 2)
        def _(m):
            rows = pl.ds(pl.multiple_of(r * half + m * BLOCK, BLOCK), BLOCK)
            part[rows, :] = dot_nt(gate_up_grad[rows, :], gate_up[...]).astype(BF16)

    product(1 - row)
    summing.start()
    product(row)
    for copy in copies:
        copy.wait()
    load(2, 3, 4, 5)
    sums[...] = jnp.zeros_like(sums)

    def land(s):
        summing.land(s, total)
        rows = pl.ds(pl.multiple_of(s * step, step), step)
        centered, rstd = moments(middle[rows, :])
        xhat = centered * rstd
        grad = total[...]
        sums[0:1, :] += jnp.sum(grad * xhat, axis=0, keepdims=True)
        sums[1:2, :] += jnp.sum(grad, axis=0, keepdims=True)
        scaled = grad * vectors[2:3, :]
        inner = (
            scaled
            - jnp.mean(scaled, axis=1, keepdims=True)
            - xhat * jnp.mean(scaled * xhat, axis=1, keepdims=True)
        )
        result = cotan_own[rows, :].astype(F32) + rstd * inner
        grads[spread.spot(spread.r, spread.c, s)] = result.astype(BF16)
        spread.start(s)

    @pl.loop(0, summing.slots + LAG * (cols - 1))
    def _(t):
        summing.slot(t)
        summing.landed(t, land)
        spread.slot(t, summing.landing, summing.per_sub)

        @pl.when((lax.rem(t, PACE) == PACE - 1) & (t < PACE * blocks))
        def _():
            rows = pl.ds(pl.multiple_of(lax.div(t, PACE) * BLOCK, BLOCK), BLOCK)
            result = dot_nt(hidden[rows, :], down[:, :narrow])
            mixed_part[rows, :] = result.astype(BF16)

    store(2)
    spread.finish()
    store(0)
    summing.finish()


def norm_two_back(cols, gate_up_grad, gate_up, middle, cotan, vectors, hidden, weight):
    group, width = cotan.shape
    tall = weight.shape[3]
    own = group // 2 // cols

    def own_rows():
        row = lax.axis_index("row") * (group // 2) + lax.axis_index("col") * own
        return pl.ds(pl.multiple_of(row, own), own)

    args = (gate_up_grad, gate_up, middle, cotan, vectors, hidden, weight)
    return staged_call(
        functools.partial(norm_two_back_kernel, cols),
        args,
        out_shape=(
            jax.ShapeDtypeStruct((group, width), BF16),
            jax.ShapeDtypeStruct((8, width), F32),
            jax.ShapeDtypeStruct((group, width), BF16),
        ),
        in_specs=[VM] * 6 + [ANY],
        out_specs=[VM] * 3,
        loads=[(i, args[i].shape, None) for i in (0, 1, 2)]
        + [(3, (own, width), own_rows)]
        + [(i, args[i].shape, None) for i in (4, 5)],
        stores=(0, 2),
        scratch_shapes=[pltpu.VMEM((group, width), BF16), pltpu.VMEM((width, tall), BF16), pltpu.SemaphoreType.DMA(weight.shape[:2])]
        + Reduce.scratch(cols, SUBS, group // 2, width)
        + Gather.scratch(cols, SUBS)
        + [pltpu.VMEM((group // 2 // cols // SUBS, width), F32)],
        compiler_params=params(3),
        cost_estimate=cost(60),
        name="grad_sum_norm_gather",
    )


def mixed_sum(cols, part, middle, scratch):
    half, width = part.shape[0] // 2, part.shape[1]
    step, depth, own = half // SUBS, width // cols, half // cols
    c = lax.axis_index("col")

    def add(d, s):
        inside = s * step - c * own
        rows = pl.ds(pl.multiple_of(lax.rem(s * step, own), step), step)
        mine = middle[rows, pl.ds(pl.multiple_of(d * depth, 128), depth)]
        return jnp.where((inside >= 0) & (inside < own), mine, 0.0)

    return Reduce(
        cols,
        SUBS,
        lambda d, s: (s * step, step, d * depth, depth),
        part,
        *scratch[:3],
        scratch[3:7],
        add=add,
    )


MIXED_SLOT = 22
ARRANGE_SLOT = 24


def last_kernel(
    cols,
    part,
    xhat,
    rstd,
    gain,
    grad_middle,
    heads_grad,
    out_grad,
    second,
    mixed_part,
    middle,
    hidden_piece,
    bias,
    result,
    mixed,
    small,
    attention_all,
    hidden_all,
    total,
    grad,
    mine,
    theirs,
    sums,
    landed,
    slices,
    own_norms,
    pair_norms,
    arranged,
    own_small,
    all_small,
    out_sem,
    in_sem,
    pair_sem,
    small_send,
    small_recv,
    own_sem,
    *sems,
    load,
    store
):
    half, width = part.shape[0] // 2, part.shape[1]
    step, depth = half // SUBS, width // cols
    pairs, dp = heads_grad.shape[:2]
    two = heads_grad.shape[4] // 3
    narrow = sums.shape[2] // 4
    rows_each = hidden_piece.shape[1] // 2
    weights = hidden_piece.shape[0]
    enter(cols, everyone=True, dp=dp)
    r, c, me = (lax.axis_index(name) for name in ("row", "col", "dp"))
    load(0)
    summing = Reduce(
        cols, SUBS, lambda d, s: (s * step, step, d * depth, depth), part, *sems[:3], sems[3:7]
    )
    summing.start()
    rider = Exchange("col", cols, sums, landed, sems[14:17])
    names = Exchange("col", cols, second, slices, sems[17:20])
    names.start()

    def hidden_rows(u):
        return u % weights, pl.ds(u // weights * rows_each, rows_each)

    hidden_cast = Broadcast(
        dp,
        2 * weights,
        lambda u: hidden_piece.at[hidden_rows(u)],
        lambda p, u: hidden_all.at[(p,) + hidden_rows(u)],
        sems[20:22],
    )
    attention_cast = Broadcast(
        dp, 4, lambda u: arranged.at[u], lambda p, u: attention_all.at[p, u], sems[22:24]
    )
    hidden_own = pltpu.make_async_copy(hidden_piece, hidden_all.at[me], own_sem.at[0])
    attention_own = pltpu.make_async_copy(arranged, attention_all.at[me], own_sem.at[1])
    hidden_cast.start()
    hidden_own.start()
    load(5, 6)

    def over_dp(ref, to):
        value = ref[0, to].astype(F32)
        for p in range(1, dp):
            value = value + ref[p, to].astype(F32)
        return value.astype(BF16)

    def fill(to, target):
        for pair in range(pairs):
            value = over_dp(heads_grad.at[pair], to)
            for k in range(3):
                first = k * narrow + pair * two
                target[:, first : first + two] = value[:, k * two : (k + 1) * two]
        target[:, 3 * narrow :] = over_dp(out_grad, to)

    for k in range(1, cols):
        to = rider.peer(k)
        fill(to, sums.at[to])
        rider.hop(k).start()
    fill(c, landed.at[c])
    own_norms[...] = jnp.zeros_like(own_norms)
    load(8, 9)
    mixing = mixed_sum(cols, mixed_part, middle, sems[7:14])
    mixing.start()
    load(1, 2, 4)

    def land(s):
        summing.land(s, total)
        rows = pl.ds(pl.multiple_of(s * step, step), step)
        grad[rows, :] = total[...]
        standard = xhat[rows, :]
        own_norms[0:1, :] += jnp.sum(total[...] * standard, axis=0, keepdims=True)
        own_norms[1:2, :] += jnp.sum(total[...], axis=0, keepdims=True)

    def land_mixed(s):
        mixing.land(s, total)
        mixed[pl.ds(pl.multiple_of(s * step, step), step), :] = total[...].astype(BF16)

    def arrange():
        for k in range(1, cols):
            rider.hop(k).wait_recv()
        for k in range(4):
            for j in range(cols):
                arranged[k, :, j * narrow : (j + 1) * narrow] = landed[
                    j, :, k * narrow : (k + 1) * narrow
                ]
        attention_cast.start()
        attention_own.start()

    @pl.loop(0, summing.slots)
    def _(t):
        summing.slot(t)
        summing.landed(t, land)
        mixing.slot(t - MIXED_SLOT)
        mixing.landed(t - MIXED_SLOT, land_mixed)
        for u in range(weights):

            @pl.when(t == 8 + 6 * u)
            def _():
                hidden_cast.forward(u)
                hidden_cast.forward(weights + u)

        @pl.when(t == ARRANGE_SLOT)
        def _():
            arrange()

    lanes = lax.broadcasted_iota(jnp.int32, (128, 128), 1)
    for s in range(half // 128):
        rows = slice(s * 128, (s + 1) * 128)
        scaled = grad[rows, :] * gain[0:1, :]
        one = jnp.sum(scaled, axis=1, keepdims=True)
        two_sum = jnp.sum(scaled * xhat[rows, :], axis=1, keepdims=True)
        both = jnp.where(lanes == 0, one, jnp.where(lanes == 1, two_sum, 0.0))
        mine[:, rows] = both.T[0:8, :]

    def exchange_sums(k):
        return send(
            mine, theirs.at[k - 1], out_sem.at[k - 1], in_sem.at[k - 1], col=lax.rem(c + k, cols)
        )

    for k in range(1, cols):
        exchange_sums(k).start()
    names.finish()
    shift = slices[0]
    for j in range(1, cols):
        shift = shift + slices[j]
    own_norms[2:4, :] = shift[0:2, :]
    across = send(own_norms, pair_norms, pair_sem.at[0], pair_sem.at[1], row=1 - r)
    across.start()

    @pl.loop(summing.slots, MIXED_SLOT + mixing.slots)
    def _(t):
        mixing.slot(t - MIXED_SLOT)
        mixing.landed(t - MIXED_SLOT, land_mixed)
        for u in range(2):

            @pl.when(t == summing.slots + 6 + 8 * u)
            def _():
                attention_cast.forward(u)
                attention_cast.forward(2 + u)

    across.wait()
    own_small[:, :depth] = own_norms[...] + pair_norms[...]
    own_small[:, depth:] = bias[...]
    all_small[me] = own_small[...]

    def hop(k):
        to = lax.rem(me + k, dp)
        return send(
            own_small, all_small.at[me], small_send.at[k - 1], small_recv.at[k - 1], dp=to
        )

    for k in range(1, dp):
        hop(k).start()
    for k in range(1, cols):
        exchange_sums(k).wait_recv()
    for s in range(half // 128):
        rows = slice(s * 128, (s + 1) * 128)
        both = mine[:, rows]
        for k in range(1, cols):
            both = both + theirs[k - 1, :, rows]
        both = jnp.concatenate([both, jnp.zeros((120, 128), F32)], axis=0).T / (depth * cols)
        scaled = grad[rows, :] * gain[0:1, :]
        inner = scaled - both[:, 0:1] - xhat[rows, :] * both[:, 1:2]
        result[rows, :] = grad_middle[rows, :].astype(F32) + rstd[rows, 0:1] * inner
    store(0, 1)
    for k in range(1, dp):
        hop(k).wait()
    value = all_small[0]
    for p in range(1, dp):
        value = value + all_small[p]
    small[...] = value
    for k in range(1, cols):
        exchange_sums(k).wait_send()
        rider.hop(k).wait_send()
    summing.finish()
    mixing.finish()
    hidden_own.wait()
    attention_own.wait()
    hidden_cast.finish()
    attention_cast.finish()


def last_part(
    cols, part, xhat, rstd, gain, grad_middle, heads_grad, out_grad, second, mixed_part, middle, piece, bias
):
    group, width = part.shape
    half, depth = group // 2, width // cols
    dp, _, rows, narrow = out_grad.shape
    small = (8, depth + bias.shape[1])
    hops = max(dp - 1, 1)
    dma = pltpu.SemaphoreType.DMA

    def own_block():
        row = lax.axis_index("row") * half
        column = lax.axis_index("col") * depth
        return pl.ds(pl.multiple_of(row, half), half), pl.ds(pl.multiple_of(column, 128), depth)

    args = (
        part,
        xhat,
        rstd,
        gain,
        grad_middle,
        heads_grad,
        out_grad,
        second,
        mixed_part,
        middle,
        piece,
        bias,
    )
    return staged_call(
        functools.partial(last_kernel, cols),
        args,
        out_shape=(
            jax.ShapeDtypeStruct((half, depth), F32),
            jax.ShapeDtypeStruct((half, depth), BF16),
            jax.ShapeDtypeStruct(small, F32),
            jax.ShapeDtypeStruct((dp, 4, rows, cols * narrow), BF16),
            jax.ShapeDtypeStruct((dp,) + piece.shape, BF16),
        ),
        in_specs=[VM] * 10 + [ANY, VM],
        out_specs=[VM] * 3 + [ANY] * 2,
        loads=[(i, args[i].shape, None) for i in (0, 5, 6, 8, 9, 1, 2)]
        + [(4, (half, depth), own_block)],
        stores=(0, 1),
        scratch_shapes=[
            pltpu.VMEM((half // SUBS, depth), F32),
            pltpu.VMEM((half, depth), F32),
            pltpu.VMEM((8, half), F32),
            pltpu.VMEM((cols - 1, 8, half), F32),
            pltpu.VMEM((cols, rows, 4 * narrow), BF16),
            pltpu.VMEM((cols, rows, 4 * narrow), BF16),
            pltpu.VMEM((cols, 8, depth), F32),
            pltpu.VMEM((8, depth), F32),
            pltpu.VMEM((8, depth), F32),
            pltpu.VMEM((4, rows, cols * narrow), BF16),
            pltpu.VMEM(small, F32),
            pltpu.VMEM((dp,) + small, F32),
            dma((cols - 1,)),
            dma((cols - 1,)),
            dma((2,)),
            dma((hops,)),
            dma((hops,)),
            dma((2,)),
        ]
        + Reduce.scratch(cols, SUBS, half, width) * 2
        + Exchange.scratch(cols) * 2
        + Broadcast.scratch(dp, 2 * piece.shape[0])
        + Broadcast.scratch(dp, 4),
        compiler_params=params(5),
        cost_estimate=cost(110),
        name="input_grad_mixed_sum",
    )


def start_kernel(
    cols,
    tokens,
    one_gain,
    one_bias,
    two_gain,
    two_bias,
    heads_from,
    out_from,
    gate_up_from,
    down_from,
    normed,
    tokens_own,
    xhat,
    rstd,
    vectors,
    gate_up_piece,
    down_piece,
    attention_w,
    heads,
    out,
    gate_up,
    down,
    pieces,
    landed,
    full,
    in_sem,
    own_sem,
    pair_send,
    pair_recv,
    *sems,
    load,
    store
):
    half, depth = tokens.shape
    width = depth * cols
    step = half // cols
    dp, _, part, wide = attention_w.shape
    narrow = wide // 4
    tall = down.shape[0] // cols
    r, c, me = (lax.axis_index(name) for name in ("row", "col", "dp"))
    begin = pl.multiple_of(me * part, part)
    rows_in = pl.ds(begin, part)

    def share_of(ref):
        return ref if ref.shape[1] == part else ref.at[:, rows_in]

    loads = [
        pltpu.make_async_copy(heads_from.at[:, rows_in], heads, in_sem.at[0]),
        pltpu.make_async_copy(share_of(out_from), out, in_sem.at[1]),
        pltpu.make_async_copy(gate_up_from.at[rows_in], gate_up, in_sem.at[2]),
        pltpu.make_async_copy(share_of(down_from), down, in_sem.at[3]),
    ]
    for load in loads:
        load.start()
    enter(cols, everyone=True, dp=dp)
    loads[0].wait()
    loads[1].wait()
    for j in range(cols):
        share = slice(j * narrow, (j + 1) * narrow)
        for k in range(3):
            pieces[j, :, k * narrow : (k + 1) * narrow] = heads[k, :, share]
        pieces[j, :, 3 * narrow :] = out[share, :].T
    rider = Exchange("col", cols, pieces, landed, sems[:3])
    assert cols == 4
    landed[c] = pieces[c]
    units = [c] + [rider.peer(k) for k in range(1, cols)]
    cast = Broadcast(
        dp, cols, lambda k: landed.at[units[k]], lambda p, k: attention_w.at[p, units[k]], sems[11:13]
    )
    cast.start((0,))
    for k in range(1, cols):
        rider.hop(k).start()

    def columns(source):
        return pl.ds(pl.multiple_of(source * depth, 128), depth)

    names = Gather(
        cols, 1, lambda r, source, s: (pl.ds(0, 8), columns(source)), vectors, sems[3:7], pair=False
    )
    spread = Gather(
        cols,
        cols,
        lambda r, source, s: (pl.ds(s * step, step), columns(source)),
        full,
        sems[7:11],
        pair=False,
    )
    vectors[:, columns(c)] = jnp.zeros((8, depth), F32)
    for i, values in enumerate((one_gain, one_bias, two_gain, two_bias)):
        vectors[i : i + 1, columns(c)] = values[...]
    names.start(0)
    for s in range(cols):
        rows = pl.ds(s * step, step)
        full[rows, columns(c)] = tokens[rows, :]
        spread.start(s)
    loads[2].wait()
    for i in range(2):
        values = gate_up[:, i, :]
        for j in range(cols):
            gate_up_piece[j, :, i * tall : (i + 1) * tall] = values[:, j * tall : (j + 1) * tall]
    loads[3].wait()
    for j in range(cols):
        down_piece[j, :, :tall] = down[j * tall : (j + 1) * tall, :].T
        if down_piece.shape[2] > tall:
            down_piece[j, :, tall:] = jnp.zeros((part, down_piece.shape[2] - tall), BF16)

    store(5, 6)

    def across(r, s):
        where = normed.at[pl.ds(pl.multiple_of(r * half + s * step, 16), step), :]
        return send(where, where, pair_send.at[s], pair_recv.at[s], row=1 - lax.axis_index("row"))

    def own(k):
        u = units[k]
        return pltpu.make_async_copy(landed.at[u], attention_w.at[me, u], own_sem.at[k])

    def take(k):
        rider.hop(k).wait_recv()
        cast.start((k,))
        own(k).start()

    def norm(s):
        rows = slice(s * step, (s + 1) * step)
        state = full[rows, :].astype(F32)
        centered, inverse = moments(state)
        result = centered * inverse * vectors[0:1, :] + vectors[1:2, :]
        normed[pl.ds(pl.multiple_of(r * half + s * step, 16), step), :] = result.astype(BF16)
        across(r, s).start()
        rstd[rows, :] = jnp.broadcast_to(inverse, (step, 128))
        mean = jnp.mean(state, axis=1, keepdims=True)
        xhat[rows, :] = (tokens[rows, :].astype(F32) - mean) * inverse

        @pl.when(c == s)
        def _():
            tokens_own[...] = full[rows, :]

    own(0).start()
    take(1)
    for k in range(1, cols):
        names.relay(0, k)
    for s in range(cols):
        spread.relay(s, 1)
    cast.forward(0)
    take(2)
    take(3)
    for s in range(cols):
        spread.relay(s, 2)
    cast.forward(1)
    cast.forward(2)
    for s in range(cols):
        spread.relay(s, 3)
        norm(s)
        if s == 1:
            cast.forward(3)

    for s in range(cols):
        across(1 - r, s).wait_recv()
    store(0, 1, 2, 3)
    for s in range(cols):
        across(r, s).wait_send()
    for u in range(cols):
        own(u).wait()
    cast.finish()
    for k in range(1, cols):
        rider.hop(k).wait_send()
    names.finish()
    spread.finish()


def start_part(tokens, vectors, heads, out, gate_up, down, sizes):
    dp, cols = sizes["dp"], sizes["col"]
    half, depth = tokens.shape
    width = depth * cols
    part, wide, tall = depth // dp, heads.shape[2], down.shape[0]
    each = tall // cols
    dma = pltpu.SemaphoreType.DMA
    return staged_call(
        functools.partial(start_kernel, cols),
        (tokens, *vectors, heads, out, gate_up, down),
        out_shape=(
            jax.ShapeDtypeStruct((2 * half, width), BF16),
            jax.ShapeDtypeStruct((half // cols, width), BF16),
            jax.ShapeDtypeStruct((half, depth), F32),
            jax.ShapeDtypeStruct((half, 128), F32),
            jax.ShapeDtypeStruct((8, width), F32),
            jax.ShapeDtypeStruct((cols, part, 2 * each), BF16),
            jax.ShapeDtypeStruct((cols, part, each + -each % 128), BF16),
            jax.ShapeDtypeStruct((dp, cols, part, 4 * wide // cols), BF16),
        ),
        in_specs=[VM] * 5 + [ANY] * 4,
        out_specs=[VM] * 7 + [ANY],
        loads=(),
        stores=(0, 1, 2, 3, 5, 6),
        scratch_shapes=[
            pltpu.VMEM((3, part, wide), BF16),
            pltpu.VMEM((wide, part), BF16),
            pltpu.VMEM((part, 2, tall), BF16),
            pltpu.VMEM((tall, part), BF16),
            pltpu.VMEM((cols, part, 4 * wide // cols), BF16),
            pltpu.VMEM((cols, part, 4 * wide // cols), BF16),
            pltpu.VMEM((half, width), BF16),
            dma((4,)),
            dma((cols,)),
            dma((cols,)),
            dma((cols,)),
        ]
        + Exchange.scratch(cols)
        + Gather.scratch(cols, 1)
        + Gather.scratch(cols, cols)
        + Broadcast.scratch(dp, cols),
        compiler_params=params(1),
        cost_estimate=cost(60),
        name="tokens_norm_weights",
    )


def rope_tables(length):
    half_rot = ROT // 2
    lane = np.arange(2 * HD) % HD
    inverse = (ROPE_BASE ** (-2.0 * (lane % half_rot) / ROT)).astype(np.float32)
    angles = np.arange(length).astype(np.float32)[:, None] * inverse[None, :]
    turning = lane < ROT
    cosine = np.where(turning, np.cos(angles), 1.0)
    sine = np.where(turning, np.sin(angles), 0.0)
    lower = np.where(lane < half_rot, -sine, 0.0)
    upper = np.where(lane >= half_rot, sine, 0.0)
    return np.stack([cosine, lower, upper]).astype(np.float32)


def turn(x, tables, back=False):
    half_rot = ROT // 2
    width = x.shape[1]
    sines = pltpu.roll(x, width - half_rot, 1) * tables[1] + pltpu.roll(x, half_rot, 1) * tables[2]
    return x * tables[0] - sines if back else x * tables[0] + sines


def causal(rows):
    return lax.broadcasted_iota(jnp.int32, (rows, rows), 0) >= lax.broadcasted_iota(
        jnp.int32, (rows, rows), 1
    )


def attend_kernel(
    cols,
    normed,
    weight,
    bias,
    tables,
    one_from,
    two_from,
    heads_in,
    attn,
    logs,
    part,
    one_to,
    two_to,
    whole,
    sem,
    qkv,
    *sems,
    load,
    store
):
    length, wide = attn.shape
    two = 2 * HD
    copies = load_columns(weight, whole, sem)
    enter(cols, everyone=True)
    riders = (
        Exchange("col", cols, one_from, one_to, sems[:3]),
        Exchange("col", cols, two_from, two_to, sems[3:]),
    )
    for rider in riders:
        rider.start()
    for copy in copies:
        copy.wait()
    load(0, 3)
    first_head = lax.broadcasted_iota(jnp.int32, (BLOCK, two), 1) < HD

    @pl.loop(0, length // BLOCK)
    def _(m):
        rows = pl.ds(pl.multiple_of(m * BLOCK, BLOCK), BLOCK)
        qkv[rows, :] = dot_nn(normed[rows, :], whole[:, : 3 * wide])

    @pl.loop(0, wide // two)
    def _(pair):
        def lanes(k):
            return pl.ds(pl.multiple_of(k * wide + pair * two, two), two)

        for k in range(3):
            x = qkv[:, lanes(k)] + bias[k : k + 1, pl.ds(pl.multiple_of(pair * two, two), two)]
            if k < 2:
                x = turn(x, tables)
            if k == 0:
                x = x * HD ** (-0.5)
            heads_in[:, lanes(k)] = x.astype(BF16)
        for i in range(length // BLOCK):
            keep = (i + 1) * BLOCK
            rows = slice(i * BLOCK, keep)
            query = heads_in[rows, lanes(0)]
            keys = heads_in[0:keep, lanes(1)]
            values = heads_in[0:keep, lanes(2)]
            outs = []
            for h in range(2):
                mine = first_head if h == 0 else ~first_head
                scores = dot_nt(jnp.where(mine, query, jnp.zeros_like(query)), keys)
                last = jnp.where(causal(BLOCK), scores[:, i * BLOCK :], NEG_LARGE)
                scores = last if i == 0 else jnp.concatenate([scores[:, : i * BLOCK], last], axis=1)
                top = jnp.max(scores, axis=1, keepdims=True)
                expo = jnp.exp(scores - top)
                total = jnp.sum(expo, axis=1, keepdims=True)
                probs = (expo * (1.0 / total)).astype(BF16)
                outs.append(dot_nn(probs, values))
                logs[pair, h, rows, :] = jnp.broadcast_to(top + jnp.log(total), (BLOCK, 128))
            attn[rows, pl.ds(pl.multiple_of(pair * two, two), two)] = jnp.where(
                first_head, outs[0], outs[1]
            ).astype(BF16)

    store(0, 1, 2)

    @pl.loop(0, length // BLOCK)
    def _(m):
        rows = pl.ds(pl.multiple_of(m * BLOCK, BLOCK), BLOCK)
        part[rows, :] = dot_nt(attn[rows, :], whole[:, 3 * wide :]).astype(BF16)

    store(3)
    for rider in riders:
        rider.finish()


def attend(cols, normed, weight, bias, tables, one, two):
    length, width = normed.shape
    dp = weight.shape[0]
    wide = weight.shape[3] // 4
    args = (normed, weight, bias, tables, one, two)
    return staged_call(
        functools.partial(attend_kernel, cols),
        args,
        out_shape=(
            jax.ShapeDtypeStruct((length, 3 * wide), BF16),
            jax.ShapeDtypeStruct((length, wide), BF16),
            jax.ShapeDtypeStruct((wide // (2 * HD), 2, length, 128), F32),
            jax.ShapeDtypeStruct((length, width), BF16),
            jax.ShapeDtypeStruct(one.shape, BF16),
            jax.ShapeDtypeStruct(two.shape, BF16),
        ),
        in_specs=[VM, ANY, VM, VM, ANY, ANY],
        out_specs=[VM] * 4 + [ANY] * 2,
        loads=[(i, args[i].shape, None) for i in (0, 3)],
        stores=(0, 1, 2, 3),
        scratch_shapes=[
            pltpu.VMEM((width, 4 * wide), BF16),
            pltpu.SemaphoreType.DMA((dp, cols)),
            pltpu.VMEM((length, 3 * wide), F32),
        ]
        + Exchange.scratch(cols) * 2,
        compiler_params=params(6),
        cost_estimate=cost(50),
        name="attention_weight_exchange",
    )


def attend_back_kernel(
    cols,
    heads_in,
    logs,
    grad_middle,
    tables,
    weight,
    normed,
    attn,
    pieces_from,
    heads_to,
    out_to,
    normed_grad,
    sums,
    arranged,
    queries_grad,
    keys_grad,
    values_grad,
    whole,
    sem,
    grad,
    result,
    own,
    pieces_to,
    heads_from,
    out_from,
    *sems,
    load,
    store
):
    length, wide = attn.shape
    two = 2 * HD
    dp, _, part_rows, _ = weight.shape
    copies = load_columns(weight, whole, sem)
    enter(cols, everyone=True, dp=dp)
    rider = Exchange("col", cols, pieces_from, pieces_to, sems[:3])
    rider.start()
    out_rider = Exchange("dp", dp, out_from, out_to, sems[3:6])
    depth = normed.shape[1] // cols
    load(2, 6)

    def heads_rider(pair):
        return Exchange(
            "dp", dp, heads_from.at[pair], heads_to.at[pair], [sem.at[pair] for sem in sems[6:]]
        )

    def parts(j):
        return pl.ds(pl.multiple_of(j * depth, depth), depth)

    @pl.loop(0, cols)
    def _(j):
        out_grad = dot_tn(grad_middle[:, parts(j)], attn[...]).astype(BF16)
        for p in range(dp):
            out_from[p, j] = out_grad[p * part_rows : (p + 1) * part_rows, :]

    out_rider.start()
    for copy in copies:
        copy.wait()
    load(0, 1, 3, 5)
    sums[...] = jnp.zeros_like(sums)
    first_head = lax.broadcasted_iota(jnp.int32, (BLOCK, two), 1) < HD

    @pl.loop(0, length // BLOCK)
    def _(m):
        rows = pl.ds(pl.multiple_of(m * BLOCK, BLOCK), BLOCK)
        grad[rows, :] = dot_nn(grad_middle[rows, :], whole[:, 3 * wide :]).astype(BF16)

    @pl.loop(0, wide // two)
    def _(pair):
        def lanes(k):
            return pl.ds(pl.multiple_of(k * wide + pair * two, two), two)

        keys_grad[...] = jnp.zeros_like(keys_grad)
        values_grad[...] = jnp.zeros_like(values_grad)
        for i in range(length // BLOCK):
            keep = (i + 1) * BLOCK
            rows = slice(i * BLOCK, keep)
            query = heads_in[rows, lanes(0)]
            keys = heads_in[0:keep, lanes(1)]
            values = heads_in[0:keep, lanes(2)]
            out_grad = grad[rows, lanes(0)]
            outs = []
            for h in range(2):
                mine = first_head if h == 0 else ~first_head
                query_h = jnp.where(mine, query, jnp.zeros_like(query))
                grad_h = jnp.where(mine, out_grad, jnp.zeros_like(out_grad))
                scores = dot_nt(query_h, keys)
                probs = jnp.exp(scores - logs[pair, h, rows, 0:1])
                last = jnp.where(causal(BLOCK), probs[:, i * BLOCK :], 0.0)
                probs = last if i == 0 else jnp.concatenate([probs[:, : i * BLOCK], last], axis=1)
                probs_grad = dot_nt(grad_h, values)
                delta = jnp.sum(probs * probs_grad, axis=1, keepdims=True)
                scores_grad = (probs * (probs_grad - delta)).astype(BF16)
                outs.append(dot_nn(scores_grad, keys))
                keys_grad[0:keep, :] += dot_tn(scores_grad, query_h)
                values_grad[0:keep, :] += dot_tn(probs.astype(BF16), grad_h)
            queries_grad[rows, :] = jnp.where(first_head, outs[0], outs[1]) * HD ** (-0.5)
        grads = (
            turn(queries_grad[...], tables, back=True),
            turn(keys_grad[...], tables, back=True),
            values_grad[...],
        )
        for k in range(3):
            low = grads[k].astype(BF16)
            result[:, lanes(k)] = low
            own[:, k * two : (k + 1) * two] = low
            column_sum = jnp.sum(low.astype(F32), axis=0, keepdims=True)
            sums[0:1, lanes(k)] = column_sum

        @pl.loop(0, cols)
        def _(j):
            heads_grad = dot_tn(normed[:, parts(j)], own[...]).astype(BF16)
            for p in range(dp):
                heads_from[pair, p, j] = heads_grad[p * part_rows : (p + 1) * part_rows, :]

        heads_rider(pair).start()

    @pl.loop(0, length // BLOCK)
    def _(m):
        rows = pl.ds(pl.multiple_of(m * BLOCK, BLOCK), BLOCK)
        normed_grad[rows, :] = dot_nt(result[rows, :], whole[:, : 3 * wide]).astype(BF16)

    store(2)
    out_rider.finish()
    for pair in range(wide // two):
        heads_rider(pair).finish()
    rider.finish()
    share = arranged.shape[2] // cols
    for k in range(arranged.shape[0]):
        arranged[k] = jnp.concatenate(
            [pieces_to[j, :, k * share : (k + 1) * share] for j in range(cols)], axis=1
        )


def attend_back(cols, heads_in, logs, grad_middle, tables, weight, normed, attn, pieces, share):
    length, wide = attn.shape
    width = normed.shape[1]
    dp, _, part, _ = weight.shape
    pairs = wide // (2 * HD)
    heads = (pairs, dp, cols, part, 6 * HD)
    out = (dp, cols, part, wide)
    hops = max(dp - 1, 1)
    dma = pltpu.SemaphoreType.DMA
    args = (heads_in, logs, grad_middle, tables, weight, normed, attn, pieces)
    return staged_call(
        functools.partial(attend_back_kernel, cols),
        args,
        out_shape=(
            jax.ShapeDtypeStruct(heads, BF16),
            jax.ShapeDtypeStruct(out, BF16),
            jax.ShapeDtypeStruct((length, width), BF16),
            jax.ShapeDtypeStruct((8, 3 * wide), F32),
            jax.ShapeDtypeStruct((3, pieces.shape[1], cols * share), BF16),
        ),
        in_specs=[VM] * 4 + [ANY, VM, VM, ANY],
        out_specs=[ANY] * 2 + [VM] * 3,
        loads=[(i, args[i].shape, None) for i in (2, 6, 0, 1, 3, 5)],
        stores=(2,),
        scratch_shapes=[pltpu.VMEM((length, 2 * HD), F32)] * 3
        + [
            pltpu.VMEM((width, 4 * wide), BF16),
            pltpu.SemaphoreType.DMA(weight.shape[:2]),
            pltpu.VMEM((length, wide), BF16),
            pltpu.VMEM((length, 3 * wide), BF16),
            pltpu.VMEM((length, 6 * HD), BF16),
            pltpu.VMEM(pieces.shape, BF16),
            pltpu.VMEM(heads, BF16),
            pltpu.VMEM(out, BF16),
        ]
        + Exchange.scratch(cols)
        + Exchange.scratch(dp)
        + [dma((pairs, hops)), dma((pairs, hops)), dma((pairs, 1))],
        compiler_params=params(8),
        cost_estimate=cost(50),
        name="attention_back_exchange",
    )


def hidden_back_kernel(
    hidden_from,
    gate_from,
    up_from,
    cotan_from,
    down_from,
    normed_from,
    weight_to,
    grads_to,
    hidden,
    gate_part,
    up_part,
    cotan,
    down,
    normed,
    grads,
    weight_grad,
    down_sem,
    block_sem,
    whole_sem,
    out_sem,
    grad_sem,
):
    group, narrow = hidden.shape
    dp, cols, part_rows, _ = down_from.shape
    wide = weight_grad.shape[3]
    blocks = group // BLOCK
    depth = normed.shape[1] // cols

    def rows_of(m):
        return pl.ds(pl.multiple_of(m * BLOCK, BLOCK), BLOCK)

    def block_copies(m):
        rows = rows_of(m)
        pairs = ((cotan_from, cotan), (gate_from, gate_part), (up_from, up_part))
        return [
            pltpu.make_async_copy(a.at[rows, :], b.at[rows, :], block_sem.at[i, m])
            for i, (a, b) in enumerate(pairs)
        ]

    down_copies = load_columns(down_from, down, down_sem)
    for copy in block_copies(0):
        copy.start()
    for m in range(1, blocks):
        for copy in block_copies(m):
            copy.start()
    whole_copies = [
        pltpu.make_async_copy(hidden_from, hidden, whole_sem.at[0]),
        pltpu.make_async_copy(normed_from, normed, whole_sem.at[1]),
    ]
    for copy in whole_copies:
        copy.start()
    for copy in down_copies:
        copy.wait()

    def grads_out(m):
        rows = rows_of(m)
        return pltpu.make_async_copy(grads.at[rows, :], grads_to.at[rows, :], out_sem.at[m])

    def weight_out(p, j):
        return pltpu.make_async_copy(weight_grad.at[p, j], weight_to.at[p, j], grad_sem.at[p, j])

    @pl.loop(0, blocks)
    def _(m):
        rows = rows_of(m)
        for copy in block_copies(m):
            copy.wait()
        grad = dot_nn(cotan[rows, :], down[:, :narrow])
        both = jnp.concatenate(
            [grad * gate_part[rows, :].astype(F32), grad * up_part[rows, :].astype(F32)], axis=1
        )
        grads[rows, :] = both.astype(BF16)
        grads_out(m).start()

    for copy in whole_copies:
        copy.wait()

    @pl.loop(0, cols)
    def _(j):
        columns = pl.ds(pl.multiple_of(j * depth, depth), depth)
        gate_up_grad = dot_tn(normed[:, columns], grads[...]).astype(BF16)
        down_grad = dot_tn(cotan[:, columns], hidden[...]).astype(BF16)
        for p in range(dp):
            rows = slice(p * part_rows, (p + 1) * part_rows)
            weight_grad[p, j, :, : 2 * narrow] = gate_up_grad[rows, :]
            weight_grad[p, j, :, 2 * narrow : 3 * narrow] = down_grad[rows, :]
            if wide > 3 * narrow:
                weight_grad[p, j, :, 3 * narrow :] = jnp.zeros((part_rows, wide - 3 * narrow), BF16)
            weight_out(p, j).start()

    for m in range(blocks):
        grads_out(m).wait()
    for p in range(dp):
        for j in range(cols):
            weight_out(p, j).wait()


def hidden_back(hidden, gate_part, up_part, cotan, down, normed):
    group, width = normed.shape
    dp, cols, part, _ = down.shape
    double = 2 * hidden.shape[1]
    grad_shape = (dp, cols, part, double + down.shape[3])
    blocks = group // BLOCK
    dma = pltpu.SemaphoreType.DMA
    return pl.pallas_call(
        hidden_back_kernel,
        out_shape=(
            jax.ShapeDtypeStruct(grad_shape, BF16),
            jax.ShapeDtypeStruct((group, double), BF16),
        ),
        in_specs=[ANY] * 6,
        out_specs=(ANY,) * 2,
        scratch_shapes=[
            pltpu.VMEM(hidden.shape, BF16),
            pltpu.VMEM(gate_part.shape, BF16),
            pltpu.VMEM(up_part.shape, BF16),
            pltpu.VMEM(cotan.shape, BF16),
            pltpu.VMEM((width, down.shape[3]), BF16),
            pltpu.VMEM(normed.shape, BF16),
            pltpu.VMEM((group, double), BF16),
            pltpu.VMEM(grad_shape, BF16),
            dma((dp, cols)),
            dma((3, blocks)),
            dma((2,)),
            dma((blocks,)),
            dma((dp, cols)),
        ],
        compiler_params=pltpu.CompilerParams(vmem_limit_bytes=VMEM_LIMIT),
        cost_estimate=cost(30),
        name="hidden_back",
    )(hidden, gate_part, up_part, cotan, down, normed)


def split_kernel(hidden, attention, gate_up, down, heads, out):
    def part(whole, k):
        return whole[:, k].reshape(whole.shape[0] * whole.shape[2], whole.shape[3]).astype(F32)

    for k in range(2):
        gate_up[:, k, :] = part(hidden, k)
    down[...] = part(hidden, 2).T
    for k in range(3):
        heads[k] = part(attention, k)
    out[...] = part(attention, 3).T


def weights_split(hidden, attention):
    dp, _, part, _ = hidden.shape
    rows = min(part, 128)
    per = 128 // rows
    depth = dp * part
    tall, wide = hidden.shape[3], attention.shape[3]

    def source(count, lanes):
        return pl.BlockSpec(
            (per, count, rows, lanes),
            lambda b: (b * 128 // (per * part), 0, lax.rem(b, max(part // 128, 1)), 0),
        )

    return pl.pallas_call(
        split_kernel,
        grid=(depth // 128,),
        out_shape=(
            jax.ShapeDtypeStruct((depth, 2, tall), F32),
            jax.ShapeDtypeStruct((tall, depth), F32),
            jax.ShapeDtypeStruct((3, depth, wide), F32),
            jax.ShapeDtypeStruct((wide, depth), F32),
        ),
        in_specs=[source(3, tall), source(4, wide)],
        out_specs=(
            pl.BlockSpec((128, 2, tall), lambda b: (b, 0, 0)),
            pl.BlockSpec((tall, 128), lambda b: (0, b)),
            pl.BlockSpec((3, 128, wide), lambda b: (0, b, 0)),
            pl.BlockSpec((wide, 128), lambda b: (0, b)),
        ),
        compiler_params=pltpu.CompilerParams(vmem_limit_bytes=VMEM_LIMIT),
        cost_estimate=cost(15),
        name="weight_gradients",
    )(hidden, attention)


def weights_whole(piece):
    return lax.all_gather(piece, "dp", axis=0)


def weights_sum(pieces):
    dp, cols, part, wide = pieces.shape
    piece = lax.psum_scatter(
        pieces.reshape(dp * cols * part, wide), "dp", scatter_dimension=0, tiled=True
    )
    return piece.reshape(cols, part, wide)


def make_body(sizes):
    cols = sizes["col"]

    def body(
        tokens,
        attention_norm_gain,
        attention_norm_bias,
        qkv_weight,
        qkv_bias,
        out_weight,
        feedforward_norm_gain,
        feedforward_norm_bias,
        gate_up_weight,
        down_weight,
        cotangent,
    ):
        my_dp = lax.axis_index("dp")
        depth = tokens.shape[1]
        tables = rope_tables(SEQ)
        part = depth // sizes["dp"]

        def share_of(rows):
            return rows if part % 128 == 0 else lax.dynamic_slice_in_dim(rows, my_dp * part, part, 1)

        (
            normed_one,
            tokens_own,
            xhat_one,
            rstd_one,
            vectors,
            gate_up_piece,
            down_piece,
            attention_w,
        ) = start_part(
            tokens,
            [
                values.reshape(1, -1)
                for values in (
                    attention_norm_gain,
                    attention_norm_bias,
                    feedforward_norm_gain,
                    feedforward_norm_bias,
                )
            ],
            qkv_weight.transpose(1, 0, 2),
            share_of(out_weight),
            gate_up_weight,
            share_of(down_weight),
            sizes,
        )
        heads_in, attn, logs, branch_part, gate_up_piece, down_piece = attend(
            cols,
            normed_one,
            attention_w,
            qkv_bias,
            tables,
            gate_up_piece,
            down_piece,
        )
        down_w = weights_whole(down_piece)
        narrow = down_weight.shape[0] // cols
        normed_two, middle, hidden, gate_part, up_part, gate_up_w, cotan_rows = middle_part(
            cols, branch_part, tokens_own, vectors, gate_up_piece, cotangent, sizes["dp"]
        )
        hidden_grad, gate_up_grad = hidden_back(
            hidden, gate_part, up_part, cotan_rows, down_w, normed_two
        )
        hidden_sum = weights_sum(hidden_grad)
        grad_middle, second, mixed_part = norm_two_back(
            cols, gate_up_grad, gate_up_w, middle, cotan_rows, vectors, hidden, down_w
        )
        second = second.reshape(8, cols, depth).transpose(1, 0, 2)
        heads_grad, out_grad, normed_part, bias_part, hidden_sum = attend_back(
            cols,
            heads_in,
            logs,
            grad_middle,
            tables,
            attention_w,
            normed_one,
            attn,
            hidden_sum,
            narrow,
        )
        input_grad, mixed, small, attention_sum, hidden_sum = last_part(
            cols,
            normed_part,
            xhat_one,
            rstd_one,
            attention_norm_gain.reshape(1, -1),
            grad_middle,
            heads_grad,
            out_grad,
            second,
            mixed_part,
            middle,
            hidden_sum,
            bias_part,
        )
        grad_gate_up, grad_down, grad_qkv_weight, grad_out = weights_split(hidden_sum, attention_sum)
        grad_qkv_weight = grad_qkv_weight.transpose(1, 0, 2)
        return (
            mixed,
            input_grad,
            small[0, :depth],
            small[1, :depth],
            grad_qkv_weight,
            small[0, depth:].reshape(3, -1),
            grad_out,
            small[2, :depth],
            small[3, :depth],
            grad_gate_up,
            grad_down,
        )

    return body


def solution(mesh):
    specs = (
        P(("dp", "row"), "col"),
        P("col"),
        P("col"),
        P("col", None, "row"),
        P(None, ("row", "col")),
        P("row", "col"),
        P("col"),
        P("col"),
        P("col", None, "row"),
        P("row", "col"),
    )
    return jax.shard_map(
        make_body(dict(mesh.shape)),
        mesh=mesh,
        in_specs=specs + (P(("dp", "row"), "col"),),
        out_specs=(P(("dp", "row"), "col"),) + specs,
        check_vma=False,
    )
```

```python
import functools

import jax
import jax.numpy as jnp
import numpy as np
from jax import lax
from jax.experimental import pallas as pl
from jax.experimental.pallas import tpu as pltpu
from jax.sharding import PartitionSpec as P

MODEL_WIDTH = 2048
HD = 64
ROT = 16
SEQ = 1024
EPSILON = 1e-05
ROPE_BASE = 10000.0
NEG_LARGE = -1e30
F32 = jnp.float32
BF16 = jnp.bfloat16
MESH = pl.DeviceIdType.MESH
VMEM_LIMIT = 56 * 1024 * 1024
SUBS = 8


def send(src, dst, send_sem, recv_sem, **where):
    return pltpu.make_async_remote_copy(
        src_ref=src,
        dst_ref=dst,
        send_sem=send_sem,
        recv_sem=recv_sem,
        device_id=where,
        device_id_type=MESH,
    )


def enter(cols, everyone=False, dp=1):
    r, c = lax.axis_index("row"), lax.axis_index("col")
    barrier = pltpu.get_barrier_semaphore()
    pl.semaphore_signal(barrier, inc=1, device_id={"row": 1 - r}, device_id_type=MESH)
    if everyone:
        for k in range(1, cols):
            pl.semaphore_signal(
                barrier, inc=1, device_id={"col": lax.rem(c + k, cols)}, device_id_type=MESH
            )
        for k in range(1, dp):
            pl.semaphore_signal(
                barrier,
                inc=1,
                device_id={"dp": lax.rem(lax.axis_index("dp") + k, dp)},
                device_id_type=MESH,
            )
        pl.semaphore_wait(barrier, cols + dp - 1)
        return

    @pl.when(c > 0)
    def _():
        pl.semaphore_signal(barrier, inc=1, device_id={"col": c - 1}, device_id_type=MESH)

    @pl.when(c < cols - 1)
    def _():
        pl.semaphore_signal(barrier, inc=1, device_id={"col": c + 1}, device_id_type=MESH)

    inner = (c > 0) & (c < cols - 1)

    @pl.when(inner)
    def _():
        pl.semaphore_wait(barrier, 3)

    @pl.when(jnp.logical_not(inner))
    def _():
        pl.semaphore_wait(barrier, 2)


LAG = 4
BLOCK = 256
PACE = 6


class Reduce:
    def __init__(self, cols, subs, spot, part, twin, going, coming, sems, add=None):
        self.cols, self.subs, self.spot, self.add = cols, subs, spot, add
        self.part, self.twin, self.going, self.coming = part, twin, going, coming
        self.twin_send, self.twin_recv, self.send, self.recv = sems
        self.r, self.c = lax.axis_index("row"), lax.axis_index("col")
        self.half = part.shape[0] // 2
        self.per_sub = cols - 1
        self.landing = LAG * (cols - 1)
        self.slots = self.per_sub * (subs - 1) + self.landing + 1

    def place(self, d, s, base=0):
        row, rows, column, columns = self.spot(d, s)
        if not isinstance(column, int):
            column = pl.multiple_of(column, 128)
        return pl.ds(pl.multiple_of(base + row, 16), rows), pl.ds(column, columns)

    def twin_copy(self, d, s):
        return send(
            self.part.at[self.place(d, s, (1 - self.r) * self.half)],
            self.twin.at[self.place(d, s)],
            self.twin_send.at[d, s],
            self.twin_recv.at[d, s],
            row=1 - self.r,
        )

    def start(self):
        @pl.loop(0, self.subs)
        def _(s):
            for j in range(self.cols):
                self.twin_copy(self.cols - 1 - j // 2 if j % 2 == 0 else j // 2, s).start()

    def hop(self, way, d, s):
        place = self.place(d, s)
        return send(
            self.going.at[(way,) + place],
            self.coming.at[(way,) + place],
            self.send.at[way, d, s],
            self.recv.at[way, d, s],
            col=self.c + 1 if way == 0 else self.c - 1,
        )

    def own(self, d, s):
        self.twin_copy(d, s).wait_recv()
        value = self.part[self.place(d, s, self.r * self.half)].astype(F32)
        value = value + self.twin[self.place(d, s)].astype(F32)
        if self.add is not None:
            value = value + self.add(d, s)
        return value

    def pass_on(self, way, d, s):
        place = (way,) + self.place(d, s)
        first = 0 if way == 0 else self.cols - 1

        @pl.when(self.c == first)
        def _():
            self.going[place] = self.own(d, s).astype(BF16)

        @pl.when(self.c != first)
        def _():
            value = self.own(d, s)
            self.hop(way, d, s).wait_recv()
            self.going[place] = (value + self.coming[place].astype(F32)).astype(BF16)

        self.hop(way, d, s).start()

    def slot(self, t):
        for way in range(2):
            made = self.c if way == 0 else self.cols - 1 - self.c
            event = t - LAG * made

            @pl.when((event >= 0) & (event < self.per_sub * self.subs))
            def _():
                s, j = lax.div(event, self.per_sub), lax.rem(event, self.per_sub)
                d = self.cols - 1 - j if way == 0 else j

                @pl.when(self.c < d if way == 0 else self.c > d)
                def _():
                    self.pass_on(way, d, s)

    def landed(self, t, do):
        after = t - self.landing

        @pl.when((after >= 0) & (lax.rem(after + self.per_sub * self.cols, self.per_sub) == 0))
        def _():
            s = lax.div(after, self.per_sub)

            @pl.when(s < self.subs)
            def _():
                do(s)

    def land(self, s, total):
        place = self.place(self.c, s)
        total[...] = self.own(self.c, s)

        @pl.when(self.c > 0)
        def _():
            self.hop(0, self.c, s).wait_recv()
            total[...] += self.coming[(0,) + place].astype(F32)

        @pl.when(self.c < self.cols - 1)
        def _():
            self.hop(1, self.c, s).wait_recv()
            total[...] += self.coming[(1,) + place].astype(F32)

    def finish(self):
        @pl.loop(0, self.subs)
        def _(s):
            for d in range(self.cols):
                self.twin_copy(d, s).wait_send()

                @pl.when(self.c < d)
                def _():
                    self.hop(0, d, s).wait_send()

                @pl.when(self.c > d)
                def _():
                    self.hop(1, d, s).wait_send()

    @staticmethod
    def scratch(cols, subs, half, width):
        return [
            pltpu.VMEM((half, width), BF16),
            pltpu.VMEM((2, half, width), BF16),
            pltpu.VMEM((2, half, width), BF16),
            pltpu.SemaphoreType.DMA((cols, subs)),
            pltpu.SemaphoreType.DMA((cols, subs)),
            pltpu.SemaphoreType.DMA((2, cols, subs)),
            pltpu.SemaphoreType.DMA((2, cols, subs)),
        ]


class Gather:
    def __init__(self, cols, subs, spot, whole, sems, pair=True):
        self.cols, self.subs, self.spot, self.whole, self.pair = cols, subs, spot, whole, pair
        self.send, self.recv, self.pair_send, self.pair_recv = sems
        self.r, self.c = lax.axis_index("row"), lax.axis_index("col")

    def hop(self, way, source, s):
        where = self.whole.at[self.spot(self.r, source, s)]
        return send(
            where,
            where,
            self.send.at[way, source, s],
            self.recv.at[way, source, s],
            col=self.c + 1 if way == 0 else self.c - 1,
        )

    def across(self, r, source, s):
        where = self.whole.at[self.spot(r, source, s)]
        return send(
            where, where, self.pair_send.at[source, s], self.pair_recv.at[source, s], row=1 - self.r
        )

    def start(self, s):
        @pl.when(self.c < self.cols - 1)
        def _():
            self.hop(0, self.c, s).start()

        @pl.when(self.c > 0)
        def _():
            self.hop(1, self.c, s).start()

        if self.pair:
            self.across(self.r, self.c, s).start()

    def relay(self, s, k):
        @pl.when(self.c >= k)
        def _():
            self.hop(0, self.c - k, s).wait_recv()

            @pl.when(self.c < self.cols - 1)
            def _():
                self.hop(0, self.c - k, s).start()

            if self.pair:
                self.across(self.r, self.c - k, s).start()

        @pl.when(self.c + k < self.cols)
        def _():
            self.hop(1, self.c + k, s).wait_recv()

            @pl.when(self.c > 0)
            def _():
                self.hop(1, self.c + k, s).start()

            if self.pair:
                self.across(self.r, self.c + k, s).start()

    def slot(self, t, begin, step, first=0, count=None):
        count = self.subs if count is None else count
        for k in range(1, self.cols):
            after = t - begin - LAG * k

            @pl.when((after >= 0) & (lax.rem(after + step * LAG * self.cols * 8, step) == 0))
            def _():
                s = lax.div(after, step)

                @pl.when(s < count)
                def _():
                    self.relay(first + s, k)

    def finish(self):
        @pl.loop(0, self.subs)
        def _(s):
            for source in range(self.cols):
                if self.pair:
                    self.across(1 - self.r, source, s).wait_recv()
                    self.across(self.r, source, s).wait_send()

                @pl.when((self.c >= source) & (self.c < self.cols - 1))
                def _():
                    self.hop(0, source, s).wait_send()

                @pl.when((self.c <= source) & (self.c > 0))
                def _():
                    self.hop(1, source, s).wait_send()

    @staticmethod
    def scratch(cols, subs):
        return [
            pltpu.SemaphoreType.DMA((2, cols, subs)),
            pltpu.SemaphoreType.DMA((2, cols, subs)),
            pltpu.SemaphoreType.DMA((cols, subs)),
            pltpu.SemaphoreType.DMA((cols, subs)),
        ]


class Exchange:
    def __init__(self, axis, size, source, target, sems):
        self.axis, self.size, self.source, self.target = axis, size, source, target
        self.send, self.recv, self.local = sems
        self.c = lax.axis_index(axis)

    def peer(self, k):
        if self.size == 4 and k != 2:
            return self.c + 1 - 2 * lax.rem(self.c, 2) if k == 1 else 3 - self.c
        return lax.rem(self.c + k, self.size)

    def hop(self, k):
        to = self.peer(k)
        return send(
            self.source.at[to],
            self.target.at[self.c],
            self.send.at[k - 1],
            self.recv.at[k - 1],
            **{self.axis: to},
        )

    def own(self):
        return pltpu.make_async_copy(
            self.source.at[self.c], self.target.at[self.c], self.local.at[0]
        )

    def start(self):
        for k in range(1, self.size):
            self.hop(k).start()
        self.own().start()

    def finish(self):
        self.own().wait()
        for k in range(1, self.size):
            self.hop(k).wait_recv()
        for k in range(1, self.size):
            self.hop(k).wait_send()

    @staticmethod
    def scratch(size):
        return [
            pltpu.SemaphoreType.DMA((size - 1,)),
            pltpu.SemaphoreType.DMA((size - 1,)),
            pltpu.SemaphoreType.DMA((1,)),
        ]


class Broadcast:
    def __init__(self, dp, units, source, target, sems):
        self.dp, self.units, self.source, self.target = dp, units, source, target
        self.send, self.recv = sems
        self.me = lax.axis_index("dp")
        self.near = self.me + 1 - 2 * lax.rem(self.me, 2)
        self.far = lax.rem(self.me + 2, dp)
        self.square = dp == 4

    def hop(self, i, u):
        if self.square:
            to = self.near if i == 0 else self.far
        else:
            to = lax.rem(self.me + i + 1, self.dp)
        return send(
            self.source(u), self.target(self.me, u), self.send.at[i, u], self.recv.at[i, u], dp=to
        )

    def across(self, u):
        low = u < self.units // 2
        where = self.target(self.near if low else self.far, u)
        return send(
            where,
            where,
            self.send.at[2, u],
            self.recv.at[2, u],
            dp=self.far if low else self.near,
        )

    def hops(self):
        return 2 if self.square else self.dp - 1

    def start(self, units=None):
        half = self.units // 2
        for n in range(self.units) if units is None else units:
            for i in range(self.hops()):
                u = (n + half) % self.units if self.square and i == 1 and units is None else n
                self.hop(i, u).start()

    def forward(self, u):
        if self.square:
            self.hop(0 if u < self.units // 2 else 1, u).wait_recv()
            self.across(u).start()

    def finish(self):
        for u in range(self.units):
            for i in range(self.hops()):
                if not self.square or (i == 0) != (u < self.units // 2):
                    self.hop(i, u).wait_recv()
                self.hop(i, u).wait_send()
            if self.square:
                self.across(u).wait()

    @staticmethod
    def scratch(dp, units):
        return [
            pltpu.SemaphoreType.DMA((max(dp - 1, 1), units)),
            pltpu.SemaphoreType.DMA((max(dp - 1, 1), units)),
        ]


ANY = pl.BlockSpec(memory_space=pl.ANY)


def staged_call(kernel, args, out_shape, in_specs, out_specs, scratch_shapes, loads, stores, **kinds):
    counts = len(args), len(out_shape)
    dma = pltpu.SemaphoreType.DMA
    buffers = [pltpu.VMEM(shape, args[i].dtype) for i, shape, _ in loads]
    buffers += [pltpu.VMEM(out_shape[j].shape, out_shape[j].dtype) for j in stores]
    in_specs, out_specs = list(in_specs), list(out_specs)
    for i, _, _ in loads:
        in_specs[i] = ANY
    for j in stores:
        out_specs[j] = ANY

    def run(*refs):
        ins, outs = list(refs[: counts[0]]), list(refs[counts[0] : sum(counts)])
        own = refs[len(refs) - len(buffers) - 2 :]
        in_sem, out_sem = own[-2:]
        coming, going = {}, {}
        for n, (i, _, part) in enumerate(loads):
            source = ins[i] if part is None else ins[i].at[part()]
            coming[i] = pltpu.make_async_copy(source, own[n], in_sem.at[n])
            ins[i] = own[n]
        for n, j in enumerate(stores):
            buffer = own[len(loads) + n]
            going[j] = pltpu.make_async_copy(buffer, outs[j], out_sem.at[n])
            outs[j] = buffer
        for copy in coming.values():
            copy.start()

        def load(*which):
            for i in which:
                coming[i].wait()

        def store(*which):
            for j in which:
                going[j].start()

        kernel(*ins, *outs, *refs[sum(counts) : len(refs) - len(own)], load=load, store=store)
        for copy in going.values():
            copy.wait()

    return pl.pallas_call(
        run,
        out_shape=tuple(out_shape),
        in_specs=in_specs,
        out_specs=tuple(out_specs),
        scratch_shapes=list(scratch_shapes)
        + buffers
        + [dma((max(len(loads), 1),)), dma((max(len(stores), 1),))],
        **kinds,
    )(*args)


def load_columns(weight, whole, sem):
    dp, cols, part, _ = weight.shape
    copies = [
        pltpu.make_async_copy(
            weight.at[p, j],
            whole.at[pl.ds((j * dp + p) * part, part), :],
            sem.at[p, j],
        )
        for p in range(dp)
        for j in range(cols)
    ]
    for copy in copies:
        copy.start()
    return copies


def dot_nt(a, b):
    return lax.dot_general(a, b, (((1,), (1,)), ((), ())), preferred_element_type=F32)


def dot_tn(a, b):
    return lax.dot_general(a, b, (((0,), (0,)), ((), ())), preferred_element_type=F32)


def dot_nn(a, b):
    return jnp.dot(a, b, preferred_element_type=F32)


def moments(rows):
    mean = jnp.mean(rows, axis=1, keepdims=True)
    centered = rows - mean
    return centered, lax.rsqrt(jnp.mean(centered * centered, axis=1, keepdims=True) + EPSILON)


def cost(us):
    return pl.CostEstimate(flops=us * 10**9, bytes_accessed=10**7, transcendentals=0)


def params(number):
    return pltpu.CompilerParams(
        collective_id=number, has_side_effects=True, vmem_limit_bytes=VMEM_LIMIT
    )


VM = pl.BlockSpec(memory_space=pltpu.VMEM)


def row_spot(own, step, half, width):
    def spot(r, source, s):
        return pl.ds(pl.multiple_of(r * half + source * own + s * step, 16), step), pl.ds(0, width)

    return spot


COTANGENT_SLOTS = (0, 34)


def middle_kernel(
    cols,
    part,
    tokens_own,
    vectors,
    piece,
    cotan,
    normed_to,
    middle_to,
    hidden_to,
    gate_to,
    up_to,
    weight_to,
    cotan_to,
    normed,
    middle,
    hidden,
    gate_part,
    up_part,
    weight,
    cotan_rows,
    total,
    own_sem,
    out_sem,
    block_sem,
    *scratch,
    load,
    store
):
    group, width = part.shape
    half = group // 2
    own = half // cols
    step = own // SUBS
    depth = cotan.shape[1]
    rows_each = half // SUBS
    _, part_rows, double = piece.shape
    narrow = double // 2
    dp = weight.shape[0] // cols // part_rows
    me = lax.axis_index("dp")
    enter(cols, everyone=True, dp=dp)
    load(0)
    summing = Reduce(
        cols, SUBS, lambda d, s: (d * own + s * step, step, 0, width), part, *scratch[:3], scratch[3:7]
    )
    summing.start()
    spread = Gather(cols, SUBS, row_spot(own, step, half, width), normed, scratch[7:11])

    def cotan_spot(r, source, s):
        rows = pl.ds(pl.multiple_of(r * half + s * rows_each, 16), rows_each)
        return rows, pl.ds(pl.multiple_of(source * depth, 128), depth)

    cotan_spread = Gather(cols, SUBS, cotan_spot, cotan_rows, scratch[11:15])

    def weight_rows(p, j):
        return weight.at[pl.ds(pl.multiple_of((j * dp + p) * part_rows, 16), part_rows), :]

    rider = Broadcast(dp, cols, lambda u: piece.at[u], weight_rows, scratch[15:17])
    rider.start()
    own_copies = [
        pltpu.make_async_copy(piece.at[j], weight_rows(me, j), own_sem.at[j]) for j in range(cols)
    ]
    for copy in own_copies:
        copy.start()
    load(1, 2, 4)

    def land(s):
        summing.land(s, total)
        rows = pl.ds(pl.multiple_of(s * step, step), step)
        state = tokens_own[rows, :].astype(F32) + total[...]
        middle[rows, :] = state
        centered, rstd = moments(state)
        result = centered * rstd * vectors[2:3, :] + vectors[3:4, :]
        normed[spread.spot(spread.r, spread.c, s)] = result.astype(BF16)
        spread.start(s)

    batch = SUBS // len(COTANGENT_SLOTS)

    def cotan_slot(t):
        for i, begin in enumerate(COTANGENT_SLOTS):
            after = t - begin

            @pl.when((after >= 0) & (lax.rem(after + 60, 3) == 0) & (after < 3 * batch))
            def _():
                s = i * batch + lax.div(after, 3)
                rows = pl.ds(pl.multiple_of(s * rows_each, 16), rows_each)
                cotan_rows[cotan_spot(spread.r, spread.c, s)] = cotan[rows, :]
                cotan_spread.start(s)

            cotan_spread.slot(t, begin, 3, i * batch, batch)

    first = summing.slots + LAG * (cols - 1)
    last = COTANGENT_SLOTS[-1] + 3 * (batch - 1) + LAG * (cols - 1) + 1
    blocks = group // BLOCK

    @pl.loop(0, first)
    def _(t):
        summing.slot(t)
        summing.landed(t, land)
        spread.slot(t, summing.landing, summing.per_sub)
        cotan_slot(t)
        for u in range(cols):

            @pl.when(t == 14 + 8 * (u % 2))
            def _():
                rider.forward(u)

    spread.finish()
    normed_out = pltpu.make_async_copy(normed, normed_to, out_sem.at[0])
    normed_out.start()
    middle_out = pltpu.make_async_copy(middle, middle_to, out_sem.at[1])
    middle_out.start()
    for copy in own_copies:
        copy.wait()
    rider.finish()
    weight_out = pltpu.make_async_copy(weight, weight_to, out_sem.at[2])
    weight_out.start()

    def block_out(m):
        rows = pl.ds(pl.multiple_of(m * BLOCK, BLOCK), BLOCK)
        pairs = ((hidden, hidden_to), (gate_part, gate_to), (up_part, up_to))
        return [
            pltpu.make_async_copy(a.at[rows, :], b.at[rows, :], block_sem.at[i, m])
            for i, (a, b) in enumerate(pairs)
        ]

    @pl.loop(0, max(last - first, blocks))
    def _(m):
        @pl.when(m < blocks)
        def _():
            rows = pl.ds(pl.multiple_of(m * BLOCK, BLOCK), BLOCK)
            both = dot_nn(normed[rows, :], weight[...])
            gate, up = both[:, :narrow], both[:, narrow:]
            sig = 1.0 / (1.0 + jnp.exp(-gate))
            active = gate * sig
            hidden[rows, :] = (active * up).astype(BF16)
            up_part[rows, :] = active.astype(BF16)
            gate_part[rows, :] = (up * sig * (1.0 + gate * (1.0 - sig))).astype(BF16)
            for copy in block_out(m):
                copy.start()

        cotan_slot(first + m)

    cotan_spread.finish()
    cotan_out = pltpu.make_async_copy(cotan_rows, cotan_to, out_sem.at[3])
    cotan_out.start()
    summing.finish()
    for m in range(blocks):
        for copy in block_out(m):
            copy.wait()
    for copy in (normed_out, middle_out, weight_out, cotan_out):
        copy.wait()


def middle_part(cols, part, tokens_own, vectors, piece, cotan, dp):
    group, width = part.shape
    _, part_rows, double = piece.shape
    narrow = double // 2
    blocks = group // BLOCK
    dma = pltpu.SemaphoreType.DMA
    outs = (
        ((group, width), BF16),
        (tokens_own.shape, F32),
        ((group, narrow), BF16),
        ((group, narrow), BF16),
        ((group, narrow), BF16),
        ((dp * cols * part_rows, double), BF16),
        ((group, width), BF16),
    )
    args = (part, tokens_own, vectors, piece, cotan)
    return staged_call(
        functools.partial(middle_kernel, cols),
        args,
        out_shape=tuple(jax.ShapeDtypeStruct(*out) for out in outs),
        in_specs=[VM] * 3 + [ANY, VM],
        out_specs=[ANY] * len(outs),
        loads=[(i, args[i].shape, None) for i in (0, 1, 2, 4)],
        stores=(),
        scratch_shapes=[pltpu.VMEM(*out) for out in outs]
        + [
            pltpu.VMEM((group // 2 // cols // SUBS, width), F32),
            dma((cols,)),
            dma((4,)),
            dma((3, blocks)),
        ]
        + Reduce.scratch(cols, SUBS, group // 2, width)
        + Gather.scratch(cols, SUBS) * 2
        + Broadcast.scratch(dp, cols),
        compiler_params=params(2),
        cost_estimate=cost(95),
        name="middle_gate_up",
    )


def norm_two_back_kernel(
    cols,
    gate_up_grad,
    gate_up,
    middle,
    cotan_own,
    vectors,
    hidden,
    weight,
    grads,
    sums,
    mixed_part,
    part,
    down,
    sem,
    *scratch,
    load,
    store
):
    narrow = hidden.shape[1]
    copies = load_columns(weight, down, sem)
    half, width = part.shape[0] // 2, part.shape[1]
    own = half // cols
    step = own // SUBS
    total = scratch[11]
    enter(cols)
    load(0, 1)
    summing = Reduce(
        cols, SUBS, lambda d, s: (d * own + s * step, step, 0, width), part, *scratch[:3], scratch[3:7]
    )
    spread = Gather(cols, SUBS, row_spot(own, step, half, width), grads, scratch[7:11])
    blocks = part.shape[0] // BLOCK
    row = lax.axis_index("row")

    def product(r):
        @pl.loop(0, blocks // 2)
        def _(m):
            rows = pl.ds(pl.multiple_of(r * half + m * BLOCK, BLOCK), BLOCK)
            part[rows, :] = dot_nt(gate_up_grad[rows, :], gate_up[...]).astype(BF16)

    product(1 - row)
    summing.start()
    product(row)
    for copy in copies:
        copy.wait()
    load(2, 3, 4, 5)
    sums[...] = jnp.zeros_like(sums)

    def land(s):
        summing.land(s, total)
        rows = pl.ds(pl.multiple_of(s * step, step), step)
        centered, rstd = moments(middle[rows, :])
        xhat = centered * rstd
        grad = total[...]
        sums[0:1, :] += jnp.sum(grad * xhat, axis=0, keepdims=True)
        sums[1:2, :] += jnp.sum(grad, axis=0, keepdims=True)
        scaled = grad * vectors[2:3, :]
        inner = (
            scaled
            - jnp.mean(scaled, axis=1, keepdims=True)
            - xhat * jnp.mean(scaled * xhat, axis=1, keepdims=True)
        )
        result = cotan_own[rows, :].astype(F32) + rstd * inner
        grads[spread.spot(spread.r, spread.c, s)] = result.astype(BF16)
        spread.start(s)

    @pl.loop(0, summing.slots + LAG * (cols - 1))
    def _(t):
        summing.slot(t)
        summing.landed(t, land)
        spread.slot(t, summing.landing, summing.per_sub)

        @pl.when((lax.rem(t, PACE) == PACE - 1) & (t < PACE * blocks))
        def _():
            rows = pl.ds(pl.multiple_of(lax.div(t, PACE) * BLOCK, BLOCK), BLOCK)
            result = dot_nt(hidden[rows, :], down[:, :narrow])
            mixed_part[rows, :] = result.astype(BF16)

    store(2)
    spread.finish()
    store(0)
    summing.finish()


def norm_two_back(cols, gate_up_grad, gate_up, middle, cotan, vectors, hidden, weight):
    group, width = cotan.shape
    tall = weight.shape[3]
    own = group // 2 // cols

    def own_rows():
        row = lax.axis_index("row") * (group // 2) + lax.axis_index("col") * own
        return pl.ds(pl.multiple_of(row, own), own)

    args = (gate_up_grad, gate_up, middle, cotan, vectors, hidden, weight)
    return staged_call(
        functools.partial(norm_two_back_kernel, cols),
        args,
        out_shape=(
            jax.ShapeDtypeStruct((group, width), BF16),
            jax.ShapeDtypeStruct((8, width), F32),
            jax.ShapeDtypeStruct((group, width), BF16),
        ),
        in_specs=[VM] * 6 + [ANY],
        out_specs=[VM] * 3,
        loads=[(i, args[i].shape, None) for i in (0, 1, 2)]
        + [(3, (own, width), own_rows)]
        + [(i, args[i].shape, None) for i in (4, 5)],
        stores=(0, 2),
        scratch_shapes=[pltpu.VMEM((group, width), BF16), pltpu.VMEM((width, tall), BF16), pltpu.SemaphoreType.DMA(weight.shape[:2])]
        + Reduce.scratch(cols, SUBS, group // 2, width)
        + Gather.scratch(cols, SUBS)
        + [pltpu.VMEM((group // 2 // cols // SUBS, width), F32)],
        compiler_params=params(3),
        cost_estimate=cost(60),
        name="grad_sum_norm_gather",
    )


def mixed_sum(cols, part, middle, scratch):
    half, width = part.shape[0] // 2, part.shape[1]
    step, depth, own = half // SUBS, width // cols, half // cols
    c = lax.axis_index("col")

    def add(d, s):
        inside = s * step - c * own
        rows = pl.ds(pl.multiple_of(lax.rem(s * step, own), step), step)
        mine = middle[rows, pl.ds(pl.multiple_of(d * depth, 128), depth)]
        return jnp.where((inside >= 0) & (inside < own), mine, 0.0)

    return Reduce(
        cols,
        SUBS,
        lambda d, s: (s * step, step, d * depth, depth),
        part,
        *scratch[:3],
        scratch[3:7],
        add=add,
    )


MIXED_SLOT = 22
ARRANGE_SLOT = 24


def last_kernel(
    cols,
    part,
    xhat,
    rstd,
    gain,
    grad_middle,
    heads_grad,
    out_grad,
    second,
    mixed_part,
    middle,
    hidden_piece,
    bias,
    result,
    mixed,
    small,
    attention_all,
    hidden_all,
    total,
    grad,
    mine,
    theirs,
    sums,
    landed,
    slices,
    own_norms,
    pair_norms,
    arranged,
    own_small,
    all_small,
    out_sem,
    in_sem,
    pair_sem,
    small_send,
    small_recv,
    own_sem,
    *sems,
    load,
    store
):
    half, width = part.shape[0] // 2, part.shape[1]
    step, depth = half // SUBS, width // cols
    pairs, dp = heads_grad.shape[:2]
    two = heads_grad.shape[4] // 3
    narrow = sums.shape[2] // 4
    rows_each = hidden_piece.shape[1] // 2
    weights = hidden_piece.shape[0]
    enter(cols, everyone=True, dp=dp)
    r, c, me = (lax.axis_index(name) for name in ("row", "col", "dp"))
    load(0)
    summing = Reduce(
        cols, SUBS, lambda d, s: (s * step, step, d * depth, depth), part, *sems[:3], sems[3:7]
    )
    summing.start()
    rider = Exchange("col", cols, sums, landed, sems[14:17])
    names = Exchange("col", cols, second, slices, sems[17:20])
    names.start()

    def hidden_rows(u):
        return u % weights, pl.ds(u // weights * rows_each, rows_each)

    hidden_cast = Broadcast(
        dp,
        2 * weights,
        lambda u: hidden_piece.at[hidden_rows(u)],
        lambda p, u: hidden_all.at[(p,) + hidden_rows(u)],
        sems[20:22],
    )
    attention_cast = Broadcast(
        dp, 4, lambda u: arranged.at[u], lambda p, u: attention_all.at[p, u], sems[22:24]
    )
    hidden_own = pltpu.make_async_copy(hidden_piece, hidden_all.at[me], own_sem.at[0])
    attention_own = pltpu.make_async_copy(arranged, attention_all.at[me], own_sem.at[1])
    hidden_cast.start()
    hidden_own.start()
    load(5, 6)

    def over_dp(ref, to):
        value = ref[0, to].astype(F32)
        for p in range(1, dp):
            value = value + ref[p, to].astype(F32)
        return value.astype(BF16)

    def fill(to, target):
        for pair in range(pairs):
            value = over_dp(heads_grad.at[pair], to)
            for k in range(3):
                first = k * narrow + pair * two
                target[:, first : first + two] = value[:, k * two : (k + 1) * two]
        target[:, 3 * narrow :] = over_dp(out_grad, to)

    for k in range(1, cols):
        to = rider.peer(k)
        fill(to, sums.at[to])
        rider.hop(k).start()
    fill(c, landed.at[c])
    own_norms[...] = jnp.zeros_like(own_norms)
    load(8, 9)
    mixing = mixed_sum(cols, mixed_part, middle, sems[7:14])
    mixing.start()
    load(1, 2, 4)

    def land(s):
        summing.land(s, total)
        rows = pl.ds(pl.multiple_of(s * step, step), step)
        grad[rows, :] = total[...]
        standard = xhat[rows, :]
        own_norms[0:1, :] += jnp.sum(total[...] * standard, axis=0, keepdims=True)
        own_norms[1:2, :] += jnp.sum(total[...], axis=0, keepdims=True)

    def land_mixed(s):
        mixing.land(s, total)
        mixed[pl.ds(pl.multiple_of(s * step, step), step), :] = total[...].astype(BF16)

    def arrange():
        for k in range(1, cols):
            rider.hop(k).wait_recv()
        for k in range(4):
            for j in range(cols):
                arranged[k, :, j * narrow : (j + 1) * narrow] = landed[
                    j, :, k * narrow : (k + 1) * narrow
                ]
        attention_cast.start()
        attention_own.start()

    @pl.loop(0, summing.slots)
    def _(t):
        summing.slot(t)
        summing.landed(t, land)
        mixing.slot(t - MIXED_SLOT)
        mixing.landed(t - MIXED_SLOT, land_mixed)
        for u in range(weights):

            @pl.when(t == 8 + 6 * u)
            def _():
                hidden_cast.forward(u)
                hidden_cast.forward(weights + u)

        @pl.when(t == ARRANGE_SLOT)
        def _():
            arrange()

    lanes = lax.broadcasted_iota(jnp.int32, (128, 128), 1)
    for s in range(half // 128):
        rows = slice(s * 128, (s + 1) * 128)
        scaled = grad[rows, :] * gain[0:1, :]
        one = jnp.sum(scaled, axis=1, keepdims=True)
        two_sum = jnp.sum(scaled * xhat[rows, :], axis=1, keepdims=True)
        both = jnp.where(lanes == 0, one, jnp.where(lanes == 1, two_sum, 0.0))
        mine[:, rows] = both.T[0:8, :]

    def exchange_sums(k):
        return send(
            mine, theirs.at[k - 1], out_sem.at[k - 1], in_sem.at[k - 1], col=lax.rem(c + k, cols)
        )

    for k in range(1, cols):
        exchange_sums(k).start()
    names.finish()
    shift = slices[0]
    for j in range(1, cols):
        shift = shift + slices[j]
    own_norms[2:4, :] = shift[0:2, :]
    across = send(own_norms, pair_norms, pair_sem.at[0], pair_sem.at[1], row=1 - r)
    across.start()

    @pl.loop(summing.slots, MIXED_SLOT + mixing.slots)
    def _(t):
        mixing.slot(t - MIXED_SLOT)
        mixing.landed(t - MIXED_SLOT, land_mixed)
        for u in range(2):

            @pl.when(t == summing.slots + 6 + 8 * u)
            def _():
                attention_cast.forward(u)
                attention_cast.forward(2 + u)

    across.wait()
    own_small[:, :depth] = own_norms[...] + pair_norms[...]
    own_small[:, depth:] = bias[...]
    all_small[me] = own_small[...]

    def hop(k):
        to = lax.rem(me + k, dp)
        return send(
            own_small, all_small.at[me], small_send.at[k - 1], small_recv.at[k - 1], dp=to
        )

    for k in range(1, dp):
        hop(k).start()
    for k in range(1, cols):
        exchange_sums(k).wait_recv()
    for s in range(half // 128):
        rows = slice(s * 128, (s + 1) * 128)
        both = mine[:, rows]
        for k in range(1, cols):
            both = both + theirs[k - 1, :, rows]
        both = jnp.concatenate([both, jnp.zeros((120, 128), F32)], axis=0).T / (depth * cols)
        scaled = grad[rows, :] * gain[0:1, :]
        inner = scaled - both[:, 0:1] - xhat[rows, :] * both[:, 1:2]
        result[rows, :] = grad_middle[rows, :].astype(F32) + rstd[rows, 0:1] * inner
    store(0, 1)
    for k in range(1, dp):
        hop(k).wait()
    value = all_small[0]
    for p in range(1, dp):
        value = value + all_small[p]
    small[...] = value
    for k in range(1, cols):
        exchange_sums(k).wait_send()
        rider.hop(k).wait_send()
    summing.finish()
    mixing.finish()
    hidden_own.wait()
    attention_own.wait()
    hidden_cast.finish()
    attention_cast.finish()


def last_part(
    cols, part, xhat, rstd, gain, grad_middle, heads_grad, out_grad, second, mixed_part, middle, piece, bias
):
    group, width = part.shape
    half, depth = group // 2, width // cols
    dp, _, rows, narrow = out_grad.shape
    small = (8, depth + bias.shape[1])
    hops = max(dp - 1, 1)
    dma = pltpu.SemaphoreType.DMA

    def own_block():
        row = lax.axis_index("row") * half
        column = lax.axis_index("col") * depth
        return pl.ds(pl.multiple_of(row, half), half), pl.ds(pl.multiple_of(column, 128), depth)

    args = (
        part,
        xhat,
        rstd,
        gain,
        grad_middle,
        heads_grad,
        out_grad,
        second,
        mixed_part,
        middle,
        piece,
        bias,
    )
    return staged_call(
        functools.partial(last_kernel, cols),
        args,
        out_shape=(
            jax.ShapeDtypeStruct((half, depth), F32),
            jax.ShapeDtypeStruct((half, depth), BF16),
            jax.ShapeDtypeStruct(small, F32),
            jax.ShapeDtypeStruct((dp, 4, rows, cols * narrow), BF16),
            jax.ShapeDtypeStruct((dp,) + piece.shape, BF16),
        ),
        in_specs=[VM] * 10 + [ANY, VM],
        out_specs=[VM] * 3 + [ANY] * 2,
        loads=[(i, args[i].shape, None) for i in (0, 5, 6, 8, 9, 1, 2)]
        + [(4, (half, depth), own_block)],
        stores=(0, 1),
        scratch_shapes=[
            pltpu.VMEM((half // SUBS, depth), F32),
            pltpu.VMEM((half, depth), F32),
            pltpu.VMEM((8, half), F32),
            pltpu.VMEM((cols - 1, 8, half), F32),
            pltpu.VMEM((cols, rows, 4 * narrow), BF16),
            pltpu.VMEM((cols, rows, 4 * narrow), BF16),
            pltpu.VMEM((cols, 8, depth), F32),
            pltpu.VMEM((8, depth), F32),
            pltpu.VMEM((8, depth), F32),
            pltpu.VMEM((4, rows, cols * narrow), BF16),
            pltpu.VMEM(small, F32),
            pltpu.VMEM((dp,) + small, F32),
            dma((cols - 1,)),
            dma((cols - 1,)),
            dma((2,)),
            dma((hops,)),
            dma((hops,)),
            dma((2,)),
        ]
        + Reduce.scratch(cols, SUBS, half, width) * 2
        + Exchange.scratch(cols) * 2
        + Broadcast.scratch(dp, 2 * piece.shape[0])
        + Broadcast.scratch(dp, 4),
        compiler_params=params(5),
        cost_estimate=cost(110),
        name="input_grad_mixed_sum",
    )


def start_kernel(
    cols,
    tokens,
    one_gain,
    one_bias,
    two_gain,
    two_bias,
    heads_from,
    out_from,
    gate_up_from,
    down_from,
    normed,
    tokens_own,
    xhat,
    rstd,
    vectors,
    gate_up_piece,
    down_piece,
    attention_w,
    heads,
    out,
    gate_up,
    down,
    pieces,
    landed,
    full,
    in_sem,
    own_sem,
    pair_send,
    pair_recv,
    *sems,
    load,
    store
):
    half, depth = tokens.shape
    width = depth * cols
    step = half // cols
    dp, _, part, wide = attention_w.shape
    narrow = wide // 4
    tall = down.shape[0] // cols
    r, c, me = (lax.axis_index(name) for name in ("row", "col", "dp"))
    begin = pl.multiple_of(me * part, part)
    rows_in = pl.ds(begin, part)

    def share_of(ref):
        return ref if ref.shape[1] == part else ref.at[:, rows_in]

    loads = [
        pltpu.make_async_copy(heads_from.at[:, rows_in], heads, in_sem.at[0]),
        pltpu.make_async_copy(share_of(out_from), out, in_sem.at[1]),
        pltpu.make_async_copy(gate_up_from.at[rows_in], gate_up, in_sem.at[2]),
        pltpu.make_async_copy(share_of(down_from), down, in_sem.at[3]),
    ]
    for load in loads:
        load.start()
    enter(cols, everyone=True, dp=dp)
    loads[0].wait()
    loads[1].wait()
    for j in range(cols):
        share = slice(j * narrow, (j + 1) * narrow)
        for k in range(3):
            pieces[j, :, k * narrow : (k + 1) * narrow] = heads[k, :, share]
        pieces[j, :, 3 * narrow :] = out[share, :].T
    rider = Exchange("col", cols, pieces, landed, sems[:3])
    assert cols == 4
    landed[c] = pieces[c]
    units = [c] + [rider.peer(k) for k in range(1, cols)]
    cast = Broadcast(
        dp, cols, lambda k: landed.at[units[k]], lambda p, k: attention_w.at[p, units[k]], sems[11:13]
    )
    cast.start((0,))
    for k in range(1, cols):
        rider.hop(k).start()

    def columns(source):
        return pl.ds(pl.multiple_of(source * depth, 128), depth)

    names = Gather(
        cols, 1, lambda r, source, s: (pl.ds(0, 8), columns(source)), vectors, sems[3:7], pair=False
    )
    spread = Gather(
        cols,
        cols,
        lambda r, source, s: (pl.ds(s * step, step), columns(source)),
        full,
        sems[7:11],
        pair=False,
    )
    vectors[:, columns(c)] = jnp.zeros((8, depth), F32)
    for i, values in enumerate((one_gain, one_bias, two_gain, two_bias)):
        vectors[i : i + 1, columns(c)] = values[...]
    names.start(0)
    for s in range(cols):
        rows = pl.ds(s * step, step)
        full[rows, columns(c)] = tokens[rows, :]
        spread.start(s)
    loads[2].wait()
    for i in range(2):
        values = gate_up[:, i, :]
        for j in range(cols):
            gate_up_piece[j, :, i * tall : (i + 1) * tall] = values[:, j * tall : (j + 1) * tall]
    loads[3].wait()
    for j in range(cols):
        down_piece[j, :, :tall] = down[j * tall : (j + 1) * tall, :].T
        if down_piece.shape[2] > tall:
            down_piece[j, :, tall:] = jnp.zeros((part, down_piece.shape[2] - tall), BF16)

    store(5, 6)

    def across(r, s):
        where = normed.at[pl.ds(pl.multiple_of(r * half + s * step, 16), step), :]
        return send(where, where, pair_send.at[s], pair_recv.at[s], row=1 - lax.axis_index("row"))

    def own(k):
        u = units[k]
        return pltpu.make_async_copy(landed.at[u], attention_w.at[me, u], own_sem.at[k])

    def take(k):
        rider.hop(k).wait_recv()
        cast.start((k,))
        own(k).start()

    def norm(s):
        rows = slice(s * step, (s + 1) * step)
        state = full[rows, :].astype(F32)
        centered, inverse = moments(state)
        result = centered * inverse * vectors[0:1, :] + vectors[1:2, :]
        normed[pl.ds(pl.multiple_of(r * half + s * step, 16), step), :] = result.astype(BF16)
        across(r, s).start()
        rstd[rows, :] = jnp.broadcast_to(inverse, (step, 128))
        mean = jnp.mean(state, axis=1, keepdims=True)
        xhat[rows, :] = (tokens[rows, :].astype(F32) - mean) * inverse

        @pl.when(c == s)
        def _():
            tokens_own[...] = full[rows, :]

    own(0).start()
    take(1)
    for k in range(1, cols):
        names.relay(0, k)
    for s in range(cols):
        spread.relay(s, 1)
    cast.forward(0)
    take(2)
    take(3)
    for s in range(cols):
        spread.relay(s, 2)
    cast.forward(1)
    cast.forward(2)
    for s in range(cols):
        spread.relay(s, 3)
        norm(s)
        if s == 1:
            cast.forward(3)

    for s in range(cols):
        across(1 - r, s).wait_recv()
    store(0, 1, 2, 3)
    for s in range(cols):
        across(r, s).wait_send()
    for u in range(cols):
        own(u).wait()
    cast.finish()
    for k in range(1, cols):
        rider.hop(k).wait_send()
    names.finish()
    spread.finish()


def start_part(tokens, vectors, heads, out, gate_up, down, sizes):
    dp, cols = sizes["dp"], sizes["col"]
    half, depth = tokens.shape
    width = depth * cols
    part, wide, tall = depth // dp, heads.shape[2], down.shape[0]
    each = tall // cols
    dma = pltpu.SemaphoreType.DMA
    return staged_call(
        functools.partial(start_kernel, cols),
        (tokens, *vectors, heads, out, gate_up, down),
        out_shape=(
            jax.ShapeDtypeStruct((2 * half, width), BF16),
            jax.ShapeDtypeStruct((half // cols, width), BF16),
            jax.ShapeDtypeStruct((half, depth), F32),
            jax.ShapeDtypeStruct((half, 128), F32),
            jax.ShapeDtypeStruct((8, width), F32),
            jax.ShapeDtypeStruct((cols, part, 2 * each), BF16),
            jax.ShapeDtypeStruct((cols, part, each + -each % 128), BF16),
            jax.ShapeDtypeStruct((dp, cols, part, 4 * wide // cols), BF16),
        ),
        in_specs=[VM] * 5 + [ANY] * 4,
        out_specs=[VM] * 7 + [ANY],
        loads=(),
        stores=(0, 1, 2, 3, 5, 6),
        scratch_shapes=[
            pltpu.VMEM((3, part, wide), BF16),
            pltpu.VMEM((wide, part), BF16),
            pltpu.VMEM((part, 2, tall), BF16),
            pltpu.VMEM((tall, part), BF16),
            pltpu.VMEM((cols, part, 4 * wide // cols), BF16),
            pltpu.VMEM((cols, part, 4 * wide // cols), BF16),
            pltpu.VMEM((half, width), BF16),
            dma((4,)),
            dma((cols,)),
            dma((cols,)),
            dma((cols,)),
        ]
        + Exchange.scratch(cols)
        + Gather.scratch(cols, 1)
        + Gather.scratch(cols, cols)
        + Broadcast.scratch(dp, cols),
        compiler_params=params(1),
        cost_estimate=cost(60),
        name="tokens_norm_weights",
    )


def rope_tables(length):
    half_rot = ROT // 2
    lane = np.arange(2 * HD) % HD
    inverse = (ROPE_BASE ** (-2.0 * (lane % half_rot) / ROT)).astype(np.float32)
    angles = np.arange(length).astype(np.float32)[:, None] * inverse[None, :]
    turning = lane < ROT
    cosine = np.where(turning, np.cos(angles), 1.0)
    sine = np.where(turning, np.sin(angles), 0.0)
    lower = np.where(lane < half_rot, -sine, 0.0)
    upper = np.where(lane >= half_rot, sine, 0.0)
    return np.stack([cosine, lower, upper]).astype(np.float32)


def turn(x, tables, back=False):
    half_rot = ROT // 2
    width = x.shape[1]
    sines = pltpu.roll(x, width - half_rot, 1) * tables[1] + pltpu.roll(x, half_rot, 1) * tables[2]
    return x * tables[0] - sines if back else x * tables[0] + sines


def causal(rows):
    return lax.broadcasted_iota(jnp.int32, (rows, rows), 0) >= lax.broadcasted_iota(
        jnp.int32, (rows, rows), 1
    )


def attend_kernel(
    cols,
    normed,
    weight,
    bias,
    tables,
    one_from,
    two_from,
    heads_in,
    attn,
    logs,
    part,
    one_to,
    two_to,
    whole,
    sem,
    qkv,
    *sems,
    load,
    store
):
    length, wide = attn.shape
    two = 2 * HD
    copies = load_columns(weight, whole, sem)
    enter(cols, everyone=True)
    riders = (
        Exchange("col", cols, one_from, one_to, sems[:3]),
        Exchange("col", cols, two_from, two_to, sems[3:]),
    )
    for rider in riders:
        rider.start()
    for copy in copies:
        copy.wait()
    load(0, 3)
    first_head = lax.broadcasted_iota(jnp.int32, (BLOCK, two), 1) < HD

    @pl.loop(0, length // BLOCK)
    def _(m):
        rows = pl.ds(pl.multiple_of(m * BLOCK, BLOCK), BLOCK)
        qkv[rows, :] = dot_nn(normed[rows, :], whole[:, : 3 * wide])

    @pl.loop(0, wide // two)
    def _(pair):
        def lanes(k):
            return pl.ds(pl.multiple_of(k * wide + pair * two, two), two)

        for k in range(3):
            x = qkv[:, lanes(k)] + bias[k : k + 1, pl.ds(pl.multiple_of(pair * two, two), two)]
            if k < 2:
                x = turn(x, tables)
            if k == 0:
                x = x * HD ** (-0.5)
            heads_in[:, lanes(k)] = x.astype(BF16)
        for i in range(length // BLOCK):
            keep = (i + 1) * BLOCK
            rows = slice(i * BLOCK, keep)
            query = heads_in[rows, lanes(0)]
            keys = heads_in[0:keep, lanes(1)]
            values = heads_in[0:keep, lanes(2)]
            outs = []
            for h in range(2):
                mine = first_head if h == 0 else ~first_head
                scores = dot_nt(jnp.where(mine, query, jnp.zeros_like(query)), keys)
                last = jnp.where(causal(BLOCK), scores[:, i * BLOCK :], NEG_LARGE)
                scores = last if i == 0 else jnp.concatenate([scores[:, : i * BLOCK], last], axis=1)
                top = jnp.max(scores, axis=1, keepdims=True)
                expo = jnp.exp(scores - top)
                total = jnp.sum(expo, axis=1, keepdims=True)
                probs = (expo * (1.0 / total)).astype(BF16)
                outs.append(dot_nn(probs, values))
                logs[pair, h, rows, :] = jnp.broadcast_to(top + jnp.log(total), (BLOCK, 128))
            attn[rows, pl.ds(pl.multiple_of(pair * two, two), two)] = jnp.where(
                first_head, outs[0], outs[1]
            ).astype(BF16)

    store(0, 1, 2)

    @pl.loop(0, length // BLOCK)
    def _(m):
        rows = pl.ds(pl.multiple_of(m * BLOCK, BLOCK), BLOCK)
        part[rows, :] = dot_nt(attn[rows, :], whole[:, 3 * wide :]).astype(BF16)

    store(3)
    for rider in riders:
        rider.finish()


def attend(cols, normed, weight, bias, tables, one, two):
    length, width = normed.shape
    dp = weight.shape[0]
    wide = weight.shape[3] // 4
    args = (normed, weight, bias, tables, one, two)
    return staged_call(
        functools.partial(attend_kernel, cols),
        args,
        out_shape=(
            jax.ShapeDtypeStruct((length, 3 * wide), BF16),
            jax.ShapeDtypeStruct((length, wide), BF16),
            jax.ShapeDtypeStruct((wide // (2 * HD), 2, length, 128), F32),
            jax.ShapeDtypeStruct((length, width), BF16),
            jax.ShapeDtypeStruct(one.shape, BF16),
            jax.ShapeDtypeStruct(two.shape, BF16),
        ),
        in_specs=[VM, ANY, VM, VM, ANY, ANY],
        out_specs=[VM] * 4 + [ANY] * 2,
        loads=[(i, args[i].shape, None) for i in (0, 3)],
        stores=(0, 1, 2, 3),
        scratch_shapes=[
            pltpu.VMEM((width, 4 * wide), BF16),
            pltpu.SemaphoreType.DMA((dp, cols)),
            pltpu.VMEM((length, 3 * wide), F32),
        ]
        + Exchange.scratch(cols) * 2,
        compiler_params=params(6),
        cost_estimate=cost(50),
        name="attention_weight_exchange",
    )


def attend_back_kernel(
    cols,
    heads_in,
    logs,
    grad_middle,
    tables,
    weight,
    normed,
    attn,
    pieces_from,
    heads_to,
    out_to,
    normed_grad,
    sums,
    arranged,
    queries_grad,
    keys_grad,
    values_grad,
    whole,
    sem,
    grad,
    result,
    own,
    pieces_to,
    heads_from,
    out_from,
    *sems,
    load,
    store
):
    length, wide = attn.shape
    two = 2 * HD
    dp, _, part_rows, _ = weight.shape
    copies = load_columns(weight, whole, sem)
    enter(cols, everyone=True, dp=dp)
    rider = Exchange("col", cols, pieces_from, pieces_to, sems[:3])
    rider.start()
    out_rider = Exchange("dp", dp, out_from, out_to, sems[3:6])
    depth = normed.shape[1] // cols
    load(2, 6)

    def heads_rider(pair):
        return Exchange(
            "dp", dp, heads_from.at[pair], heads_to.at[pair], [sem.at[pair] for sem in sems[6:]]
        )

    def parts(j):
        return pl.ds(pl.multiple_of(j * depth, depth), depth)

    @pl.loop(0, cols)
    def _(j):
        out_grad = dot_tn(grad_middle[:, parts(j)], attn[...]).astype(BF16)
        for p in range(dp):
            out_from[p, j] = out_grad[p * part_rows : (p + 1) * part_rows, :]

    out_rider.start()
    for copy in copies:
        copy.wait()
    load(0, 1, 3, 5)
    sums[...] = jnp.zeros_like(sums)
    first_head = lax.broadcasted_iota(jnp.int32, (BLOCK, two), 1) < HD

    @pl.loop(0, length // BLOCK)
    def _(m):
        rows = pl.ds(pl.multiple_of(m * BLOCK, BLOCK), BLOCK)
        grad[rows, :] = dot_nn(grad_middle[rows, :], whole[:, 3 * wide :]).astype(BF16)

    @pl.loop(0, wide // two)
    def _(pair):
        def lanes(k):
            return pl.ds(pl.multiple_of(k * wide + pair * two, two), two)

        keys_grad[...] = jnp.zeros_like(keys_grad)
        values_grad[...] = jnp.zeros_like(values_grad)
        for i in range(length // BLOCK):
            keep = (i + 1) * BLOCK
            rows = slice(i * BLOCK, keep)
            query = heads_in[rows, lanes(0)]
            keys = heads_in[0:keep, lanes(1)]
            values = heads_in[0:keep, lanes(2)]
            out_grad = grad[rows, lanes(0)]
            outs = []
            for h in range(2):
                mine = first_head if h == 0 else ~first_head
                query_h = jnp.where(mine, query, jnp.zeros_like(query))
                grad_h = jnp.where(mine, out_grad, jnp.zeros_like(out_grad))
                scores = dot_nt(query_h, keys)
                probs = jnp.exp(scores - logs[pair, h, rows, 0:1])
                last = jnp.where(causal(BLOCK), probs[:, i * BLOCK :], 0.0)
                probs = last if i == 0 else jnp.concatenate([probs[:, : i * BLOCK], last], axis=1)
                probs_grad = dot_nt(grad_h, values)
                delta = jnp.sum(probs * probs_grad, axis=1, keepdims=True)
                scores_grad = (probs * (probs_grad - delta)).astype(BF16)
                outs.append(dot_nn(scores_grad, keys))
                keys_grad[0:keep, :] += dot_tn(scores_grad, query_h)
                values_grad[0:keep, :] += dot_tn(probs.astype(BF16), grad_h)
            queries_grad[rows, :] = jnp.where(first_head, outs[0], outs[1]) * HD ** (-0.5)
        grads = (
            turn(queries_grad[...], tables, back=True),
            turn(keys_grad[...], tables, back=True),
            values_grad[...],
        )
        for k in range(3):
            low = grads[k].astype(BF16)
            result[:, lanes(k)] = low
            own[:, k * two : (k + 1) * two] = low
            column_sum = jnp.sum(low.astype(F32), axis=0, keepdims=True)
            sums[0:1, lanes(k)] = column_sum

        @pl.loop(0, cols)
        def _(j):
            heads_grad = dot_tn(normed[:, parts(j)], own[...]).astype(BF16)
            for p in range(dp):
                heads_from[pair, p, j] = heads_grad[p * part_rows : (p + 1) * part_rows, :]

        heads_rider(pair).start()

    @pl.loop(0, length // BLOCK)
    def _(m):
        rows = pl.ds(pl.multiple_of(m * BLOCK, BLOCK), BLOCK)
        normed_grad[rows, :] = dot_nt(result[rows, :], whole[:, : 3 * wide]).astype(BF16)

    store(2)
    out_rider.finish()
    for pair in range(wide // two):
        heads_rider(pair).finish()
    rider.finish()
    share = arranged.shape[2] // cols
    for k in range(arranged.shape[0]):
        arranged[k] = jnp.concatenate(
            [pieces_to[j, :, k * share : (k + 1) * share] for j in range(cols)], axis=1
        )


def attend_back(cols, heads_in, logs, grad_middle, tables, weight, normed, attn, pieces, share):
    length, wide = attn.shape
    width = normed.shape[1]
    dp, _, part, _ = weight.shape
    pairs = wide // (2 * HD)
    heads = (pairs, dp, cols, part, 6 * HD)
    out = (dp, cols, part, wide)
    hops = max(dp - 1, 1)
    dma = pltpu.SemaphoreType.DMA
    args = (heads_in, logs, grad_middle, tables, weight, normed, attn, pieces)
    return staged_call(
        functools.partial(attend_back_kernel, cols),
        args,
        out_shape=(
            jax.ShapeDtypeStruct(heads, BF16),
            jax.ShapeDtypeStruct(out, BF16),
            jax.ShapeDtypeStruct((length, width), BF16),
            jax.ShapeDtypeStruct((8, 3 * wide), F32),
            jax.ShapeDtypeStruct((3, pieces.shape[1], cols * share), BF16),
        ),
        in_specs=[VM] * 4 + [ANY, VM, VM, ANY],
        out_specs=[ANY] * 2 + [VM] * 3,
        loads=[(i, args[i].shape, None) for i in (2, 6, 0, 1, 3, 5)],
        stores=(2,),
        scratch_shapes=[pltpu.VMEM((length, 2 * HD), F32)] * 3
        + [
            pltpu.VMEM((width, 4 * wide), BF16),
            pltpu.SemaphoreType.DMA(weight.shape[:2]),
            pltpu.VMEM((length, wide), BF16),
            pltpu.VMEM((length, 3 * wide), BF16),
            pltpu.VMEM((length, 6 * HD), BF16),
            pltpu.VMEM(pieces.shape, BF16),
            pltpu.VMEM(heads, BF16),
            pltpu.VMEM(out, BF16),
        ]
        + Exchange.scratch(cols)
        + Exchange.scratch(dp)
        + [dma((pairs, hops)), dma((pairs, hops)), dma((pairs, 1))],
        compiler_params=params(8),
        cost_estimate=cost(50),
        name="attention_back_exchange",
    )


def hidden_back_kernel(
    hidden_from,
    gate_from,
    up_from,
    cotan_from,
    down_from,
    normed_from,
    weight_to,
    grads_to,
    hidden,
    gate_part,
    up_part,
    cotan,
    down,
    normed,
    grads,
    weight_grad,
    down_sem,
    block_sem,
    whole_sem,
    out_sem,
    grad_sem,
):
    group, narrow = hidden.shape
    dp, cols, part_rows, _ = down_from.shape
    wide = weight_grad.shape[3]
    blocks = group // BLOCK
    depth = normed.shape[1] // cols

    def rows_of(m):
        return pl.ds(pl.multiple_of(m * BLOCK, BLOCK), BLOCK)

    def block_copies(m):
        rows = rows_of(m)
        pairs = ((cotan_from, cotan), (gate_from, gate_part), (up_from, up_part))
        return [
            pltpu.make_async_copy(a.at[rows, :], b.at[rows, :], block_sem.at[i, m])
            for i, (a, b) in enumerate(pairs)
        ]

    down_copies = load_columns(down_from, down, down_sem)
    for copy in block_copies(0):
        copy.start()
    for m in range(1, blocks):
        for copy in block_copies(m):
            copy.start()
    whole_copies = [
        pltpu.make_async_copy(hidden_from, hidden, whole_sem.at[0]),
        pltpu.make_async_copy(normed_from, normed, whole_sem.at[1]),
    ]
    for copy in whole_copies:
        copy.start()
    for copy in down_copies:
        copy.wait()

    def grads_out(m):
        rows = rows_of(m)
        return pltpu.make_async_copy(grads.at[rows, :], grads_to.at[rows, :], out_sem.at[m])

    def weight_out(p, j):
        return pltpu.make_async_copy(weight_grad.at[p, j], weight_to.at[p, j], grad_sem.at[p, j])

    @pl.loop(0, blocks)
    def _(m):
        rows = rows_of(m)
        for copy in block_copies(m):
            copy.wait()
        grad = dot_nn(cotan[rows, :], down[:, :narrow])
        both = jnp.concatenate(
            [grad * gate_part[rows, :].astype(F32), grad * up_part[rows, :].astype(F32)], axis=1
        )
        grads[rows, :] = both.astype(BF16)
        grads_out(m).start()

    for copy in whole_copies:
        copy.wait()

    @pl.loop(0, cols)
    def _(j):
        columns = pl.ds(pl.multiple_of(j * depth, depth), depth)
        gate_up_grad = dot_tn(normed[:, columns], grads[...]).astype(BF16)
        down_grad = dot_tn(cotan[:, columns], hidden[...]).astype(BF16)
        for p in range(dp):
            rows = slice(p * part_rows, (p + 1) * part_rows)
            weight_grad[p, j, :, : 2 * narrow] = gate_up_grad[rows, :]
            weight_grad[p, j, :, 2 * narrow : 3 * narrow] = down_grad[rows, :]
            if wide > 3 * narrow:
                weight_grad[p, j, :, 3 * narrow :] = jnp.zeros((part_rows, wide - 3 * narrow), BF16)
            weight_out(p, j).start()

    for m in range(blocks):
        grads_out(m).wait()
    for p in range(dp):
        for j in range(cols):
            weight_out(p, j).wait()


def hidden_back(hidden, gate_part, up_part, cotan, down, normed):
    group, width = normed.shape
    dp, cols, part, _ = down.shape
    double = 2 * hidden.shape[1]
    grad_shape = (dp, cols, part, double + down.shape[3])
    blocks = group // BLOCK
    dma = pltpu.SemaphoreType.DMA
    return pl.pallas_call(
        hidden_back_kernel,
        out_shape=(
            jax.ShapeDtypeStruct(grad_shape, BF16),
            jax.ShapeDtypeStruct((group, double), BF16),
        ),
        in_specs=[ANY] * 6,
        out_specs=(ANY,) * 2,
        scratch_shapes=[
            pltpu.VMEM(hidden.shape, BF16),
            pltpu.VMEM(gate_part.shape, BF16),
            pltpu.VMEM(up_part.shape, BF16),
            pltpu.VMEM(cotan.shape, BF16),
            pltpu.VMEM((width, down.shape[3]), BF16),
            pltpu.VMEM(normed.shape, BF16),
            pltpu.VMEM((group, double), BF16),
            pltpu.VMEM(grad_shape, BF16),
            dma((dp, cols)),
            dma((3, blocks)),
            dma((2,)),
            dma((blocks,)),
            dma((dp, cols)),
        ],
        compiler_params=pltpu.CompilerParams(vmem_limit_bytes=VMEM_LIMIT),
        cost_estimate=cost(30),
        name="hidden_back",
    )(hidden, gate_part, up_part, cotan, down, normed)


def split_kernel(hidden, attention, small, gate_up, down, heads, out, bias, *norms):
    def part(whole, k):
        return whole[:, k].reshape(whole.shape[0] * whole.shape[2], whole.shape[3]).astype(F32)

    for k in range(2):
        gate_up[:, k, :] = part(hidden, k)
    down[...] = part(hidden, 2).T
    for k in range(3):
        heads[k] = part(attention, k)
    out[...] = part(attention, 3).T
    depth, each = norms[0].shape[1], bias.shape[1]
    for i, norm in enumerate(norms):
        norm[...] = small[i : i + 1, :depth]
    for k in range(3):
        bias[k : k + 1, :] = small[0:1, depth + k * each : depth + (k + 1) * each]


def weights_split(hidden, attention, small):
    dp, _, part, _ = hidden.shape
    rows = min(part, 128)
    per = 128 // rows
    depth = dp * part
    tall, wide = hidden.shape[3], attention.shape[3]
    each = (small.shape[1] - depth) // 3

    def whole(shape):
        return pl.BlockSpec(shape, lambda b: (0, 0))

    def source(count, lanes):
        return pl.BlockSpec(
            (per, count, rows, lanes),
            lambda b: (b * 128 // (per * part), 0, lax.rem(b, max(part // 128, 1)), 0),
        )

    return pl.pallas_call(
        split_kernel,
        grid=(depth // 128,),
        out_shape=(
            jax.ShapeDtypeStruct((depth, 2, tall), F32),
            jax.ShapeDtypeStruct((tall, depth), F32),
            jax.ShapeDtypeStruct((3, depth, wide), F32),
            jax.ShapeDtypeStruct((wide, depth), F32),
            jax.ShapeDtypeStruct((3, each), F32),
        )
        + (jax.ShapeDtypeStruct((1, depth), F32),) * 4,
        in_specs=[source(3, tall), source(4, wide), whole(small.shape)],
        out_specs=(
            pl.BlockSpec((128, 2, tall), lambda b: (b, 0, 0)),
            pl.BlockSpec((tall, 128), lambda b: (0, b)),
            pl.BlockSpec((3, 128, wide), lambda b: (0, b, 0)),
            pl.BlockSpec((wide, 128), lambda b: (0, b)),
            whole((3, each)),
        )
        + (whole((1, depth)),) * 4,
        compiler_params=pltpu.CompilerParams(vmem_limit_bytes=VMEM_LIMIT),
        cost_estimate=cost(15),
        name="weight_gradients",
    )(hidden, attention, small)


def weights_whole(piece):
    return lax.all_gather(piece, "dp", axis=0)


def weights_sum(pieces):
    dp, cols, part, wide = pieces.shape
    piece = lax.psum_scatter(
        pieces.reshape(dp * cols * part, wide), "dp", scatter_dimension=0, tiled=True
    )
    return piece.reshape(cols, part, wide)


def make_body(sizes):
    cols = sizes["col"]

    def body(
        tokens,
        attention_norm_gain,
        attention_norm_bias,
        qkv_weight,
        qkv_bias,
        out_weight,
        feedforward_norm_gain,
        feedforward_norm_bias,
        gate_up_weight,
        down_weight,
        cotangent,
    ):
        my_dp = lax.axis_index("dp")
        depth = tokens.shape[1]
        tables = rope_tables(SEQ)
        part = depth // sizes["dp"]

        def share_of(rows):
            return rows if part % 128 == 0 else lax.dynamic_slice_in_dim(rows, my_dp * part, part, 1)

        (
            normed_one,
            tokens_own,
            xhat_one,
            rstd_one,
            vectors,
            gate_up_piece,
            down_piece,
            attention_w,
        ) = start_part(
            tokens,
            [
                values.reshape(1, -1)
                for values in (
                    attention_norm_gain,
                    attention_norm_bias,
                    feedforward_norm_gain,
                    feedforward_norm_bias,
                )
            ],
            qkv_weight.transpose(1, 0, 2),
            share_of(out_weight),
            gate_up_weight,
            share_of(down_weight),
            sizes,
        )
        heads_in, attn, logs, branch_part, gate_up_piece, down_piece = attend(
            cols,
            normed_one,
            attention_w,
            qkv_bias,
            tables,
            gate_up_piece,
            down_piece,
        )
        down_w = weights_whole(down_piece)
        narrow = down_weight.shape[0] // cols
        normed_two, middle, hidden, gate_part, up_part, gate_up_w, cotan_rows = middle_part(
            cols, branch_part, tokens_own, vectors, gate_up_piece, cotangent, sizes["dp"]
        )
        hidden_grad, gate_up_grad = hidden_back(
            hidden, gate_part, up_part, cotan_rows, down_w, normed_two
        )
        hidden_sum = weights_sum(hidden_grad)
        grad_middle, second, mixed_part = norm_two_back(
            cols, gate_up_grad, gate_up_w, middle, cotan_rows, vectors, hidden, down_w
        )
        second = second.reshape(8, cols, depth).transpose(1, 0, 2)
        heads_grad, out_grad, normed_part, bias_part, hidden_sum = attend_back(
            cols,
            heads_in,
            logs,
            grad_middle,
            tables,
            attention_w,
            normed_one,
            attn,
            hidden_sum,
            narrow,
        )
        input_grad, mixed, small, attention_sum, hidden_sum = last_part(
            cols,
            normed_part,
            xhat_one,
            rstd_one,
            attention_norm_gain.reshape(1, -1),
            grad_middle,
            heads_grad,
            out_grad,
            second,
            mixed_part,
            middle,
            hidden_sum,
            bias_part,
        )
        grad_gate_up, grad_down, grad_qkv_weight, grad_out, bias, *norms = weights_split(
            hidden_sum, attention_sum, small
        )
        norms = [norm.reshape(-1) for norm in norms]
        grad_qkv_weight = grad_qkv_weight.transpose(1, 0, 2)
        return (
            mixed,
            input_grad,
            norms[0],
            norms[1],
            grad_qkv_weight,
            bias,
            grad_out,
            norms[2],
            norms[3],
            grad_gate_up,
            grad_down,
        )

    return body


def solution(mesh):
    specs = (
        P(("dp", "row"), "col"),
        P("col"),
        P("col"),
        P("col", None, "row"),
        P(None, ("row", "col")),
        P("row", "col"),
        P("col"),
        P("col"),
        P("col", None, "row"),
        P("row", "col"),
    )
    return jax.shard_map(
        make_body(dict(mesh.shape)),
        mesh=mesh,
        in_specs=specs + (P(("dp", "row"), "col"),),
        out_specs=(P(("dp", "row"), "col"),) + specs,
        check_vma=False,
    )
```

```python
import functools

import jax
import jax.numpy as jnp
import numpy as np
from jax import lax
from jax.experimental import pallas as pl
from jax.experimental.pallas import tpu as pltpu
from jax.sharding import PartitionSpec as P

MODEL_WIDTH = 2048
HD = 64
ROT = 16
SEQ = 1024
EPSILON = 1e-05
ROPE_BASE = 10000.0
NEG_LARGE = -1e30
F32 = jnp.float32
BF16 = jnp.bfloat16
MESH = pl.DeviceIdType.MESH
VMEM_LIMIT = 56 * 1024 * 1024
SUBS = 8


def send(src, dst, send_sem, recv_sem, **where):
    return pltpu.make_async_remote_copy(
        src_ref=src,
        dst_ref=dst,
        send_sem=send_sem,
        recv_sem=recv_sem,
        device_id=where,
        device_id_type=MESH,
    )


def enter(cols, everyone=False, dp=1):
    r, c = lax.axis_index("row"), lax.axis_index("col")
    barrier = pltpu.get_barrier_semaphore()
    pl.semaphore_signal(barrier, inc=1, device_id={"row": 1 - r}, device_id_type=MESH)
    if everyone:
        for k in range(1, cols):
            pl.semaphore_signal(
                barrier, inc=1, device_id={"col": lax.rem(c + k, cols)}, device_id_type=MESH
            )
        for k in range(1, dp):
            pl.semaphore_signal(
                barrier,
                inc=1,
                device_id={"dp": lax.rem(lax.axis_index("dp") + k, dp)},
                device_id_type=MESH,
            )
        pl.semaphore_wait(barrier, cols + dp - 1)
        return

    @pl.when(c > 0)
    def _():
        pl.semaphore_signal(barrier, inc=1, device_id={"col": c - 1}, device_id_type=MESH)

    @pl.when(c < cols - 1)
    def _():
        pl.semaphore_signal(barrier, inc=1, device_id={"col": c + 1}, device_id_type=MESH)

    inner = (c > 0) & (c < cols - 1)

    @pl.when(inner)
    def _():
        pl.semaphore_wait(barrier, 3)

    @pl.when(jnp.logical_not(inner))
    def _():
        pl.semaphore_wait(barrier, 2)


LAG = 4
BLOCK = 256
PACE = 6


class Reduce:
    def __init__(self, cols, subs, spot, part, twin, going, coming, sems, add=None):
        self.cols, self.subs, self.spot, self.add = cols, subs, spot, add
        self.part, self.twin, self.going, self.coming = part, twin, going, coming
        self.twin_send, self.twin_recv, self.send, self.recv = sems
        self.r, self.c = lax.axis_index("row"), lax.axis_index("col")
        self.half = part.shape[0] // 2
        self.per_sub = cols - 1
        self.landing = LAG * (cols - 1)
        self.slots = self.per_sub * (subs - 1) + self.landing + 1

    def place(self, d, s, base=0):
        row, rows, column, columns = self.spot(d, s)
        if not isinstance(column, int):
            column = pl.multiple_of(column, 128)
        return pl.ds(pl.multiple_of(base + row, 16), rows), pl.ds(column, columns)

    def twin_copy(self, d, s):
        return send(
            self.part.at[self.place(d, s, (1 - self.r) * self.half)],
            self.twin.at[self.place(d, s)],
            self.twin_send.at[d, s],
            self.twin_recv.at[d, s],
            row=1 - self.r,
        )

    def start(self):
        @pl.loop(0, self.subs)
        def _(s):
            for j in range(self.cols):
                self.twin_copy(self.cols - 1 - j // 2 if j % 2 == 0 else j // 2, s).start()

    def hop(self, way, d, s):
        place = self.place(d, s)
        return send(
            self.going.at[(way,) + place],
            self.coming.at[(way,) + place],
            self.send.at[way, d, s],
            self.recv.at[way, d, s],
            col=self.c + 1 if way == 0 else self.c - 1,
        )

    def own(self, d, s):
        self.twin_copy(d, s).wait_recv()
        value = self.part[self.place(d, s, self.r * self.half)].astype(F32)
        value = value + self.twin[self.place(d, s)].astype(F32)
        if self.add is not None:
            value = value + self.add(d, s)
        return value

    def pass_on(self, way, d, s):
        place = (way,) + self.place(d, s)
        first = 0 if way == 0 else self.cols - 1

        @pl.when(self.c == first)
        def _():
            self.going[place] = self.own(d, s).astype(BF16)

        @pl.when(self.c != first)
        def _():
            value = self.own(d, s)
            self.hop(way, d, s).wait_recv()
            self.going[place] = (value + self.coming[place].astype(F32)).astype(BF16)

        self.hop(way, d, s).start()

    def slot(self, t):
        for way in range(2):
            made = self.c if way == 0 else self.cols - 1 - self.c
            event = t - LAG * made

            @pl.when((event >= 0) & (event < self.per_sub * self.subs))
            def _():
                s, j = lax.div(event, self.per_sub), lax.rem(event, self.per_sub)
                d = self.cols - 1 - j if way == 0 else j

                @pl.when(self.c < d if way == 0 else self.c > d)
                def _():
                    self.pass_on(way, d, s)

    def landed(self, t, do):
        after = t - self.landing

        @pl.when((after >= 0) & (lax.rem(after + self.per_sub * self.cols, self.per_sub) == 0))
        def _():
            s = lax.div(after, self.per_sub)

            @pl.when(s < self.subs)
            def _():
                do(s)

    def land(self, s, total):
        place = self.place(self.c, s)
        total[...] = self.own(self.c, s)

        @pl.when(self.c > 0)
        def _():
            self.hop(0, self.c, s).wait_recv()
            total[...] += self.coming[(0,) + place].astype(F32)

        @pl.when(self.c < self.cols - 1)
        def _():
            self.hop(1, self.c, s).wait_recv()
            total[...] += self.coming[(1,) + place].astype(F32)

    def finish(self):
        @pl.loop(0, self.subs)
        def _(s):
            for d in range(self.cols):
                self.twin_copy(d, s).wait_send()

                @pl.when(self.c < d)
                def _():
                    self.hop(0, d, s).wait_send()

                @pl.when(self.c > d)
                def _():
                    self.hop(1, d, s).wait_send()

    @staticmethod
    def scratch(cols, subs, half, width):
        return [
            pltpu.VMEM((half, width), BF16),
            pltpu.VMEM((2, half, width), BF16),
            pltpu.VMEM((2, half, width), BF16),
            pltpu.SemaphoreType.DMA((cols, subs)),
            pltpu.SemaphoreType.DMA((cols, subs)),
            pltpu.SemaphoreType.DMA((2, cols, subs)),
            pltpu.SemaphoreType.DMA((2, cols, subs)),
        ]


class Gather:
    def __init__(self, cols, subs, spot, whole, sems, pair=True):
        self.cols, self.subs, self.spot, self.whole, self.pair = cols, subs, spot, whole, pair
        self.send, self.recv, self.pair_send, self.pair_recv = sems
        self.r, self.c = lax.axis_index("row"), lax.axis_index("col")

    def hop(self, way, source, s):
        where = self.whole.at[self.spot(self.r, source, s)]
        return send(
            where,
            where,
            self.send.at[way, source, s],
            self.recv.at[way, source, s],
            col=self.c + 1 if way == 0 else self.c - 1,
        )

    def across(self, r, source, s):
        where = self.whole.at[self.spot(r, source, s)]
        return send(
            where, where, self.pair_send.at[source, s], self.pair_recv.at[source, s], row=1 - self.r
        )

    def start(self, s):
        @pl.when(self.c < self.cols - 1)
        def _():
            self.hop(0, self.c, s).start()

        @pl.when(self.c > 0)
        def _():
            self.hop(1, self.c, s).start()

        if self.pair:
            self.across(self.r, self.c, s).start()

    def relay(self, s, k):
        @pl.when(self.c >= k)
        def _():
            self.hop(0, self.c - k, s).wait_recv()

            @pl.when(self.c < self.cols - 1)
            def _():
                self.hop(0, self.c - k, s).start()

            if self.pair:
                self.across(self.r, self.c - k, s).start()

        @pl.when(self.c + k < self.cols)
        def _():
            self.hop(1, self.c + k, s).wait_recv()

            @pl.when(self.c > 0)
            def _():
                self.hop(1, self.c + k, s).start()

            if self.pair:
                self.across(self.r, self.c + k, s).start()

    def slot(self, t, begin, step, first=0, count=None):
        count = self.subs if count is None else count
        for k in range(1, self.cols):
            after = t - begin - LAG * k

            @pl.when((after >= 0) & (lax.rem(after + step * LAG * self.cols * 8, step) == 0))
            def _():
                s = lax.div(after, step)

                @pl.when(s < count)
                def _():
                    self.relay(first + s, k)

    def finish(self):
        @pl.loop(0, self.subs)
        def _(s):
            for source in range(self.cols):
                if self.pair:
                    self.across(1 - self.r, source, s).wait_recv()
                    self.across(self.r, source, s).wait_send()

                @pl.when((self.c >= source) & (self.c < self.cols - 1))
                def _():
                    self.hop(0, source, s).wait_send()

                @pl.when((self.c <= source) & (self.c > 0))
                def _():
                    self.hop(1, source, s).wait_send()

    @staticmethod
    def scratch(cols, subs):
        return [
            pltpu.SemaphoreType.DMA((2, cols, subs)),
            pltpu.SemaphoreType.DMA((2, cols, subs)),
            pltpu.SemaphoreType.DMA((cols, subs)),
            pltpu.SemaphoreType.DMA((cols, subs)),
        ]


class Exchange:
    def __init__(self, axis, size, source, target, sems):
        self.axis, self.size, self.source, self.target = axis, size, source, target
        self.send, self.recv, self.local = sems
        self.c = lax.axis_index(axis)

    def peer(self, k):
        if self.size == 4 and k != 2:
            return self.c + 1 - 2 * lax.rem(self.c, 2) if k == 1 else 3 - self.c
        return lax.rem(self.c + k, self.size)

    def hop(self, k):
        to = self.peer(k)
        return send(
            self.source.at[to],
            self.target.at[self.c],
            self.send.at[k - 1],
            self.recv.at[k - 1],
            **{self.axis: to},
        )

    def own(self):
        return pltpu.make_async_copy(
            self.source.at[self.c], self.target.at[self.c], self.local.at[0]
        )

    def start(self):
        for k in range(1, self.size):
            self.hop(k).start()
        self.own().start()

    def finish(self):
        self.own().wait()
        for k in range(1, self.size):
            self.hop(k).wait_recv()
        for k in range(1, self.size):
            self.hop(k).wait_send()

    @staticmethod
    def scratch(size):
        return [
            pltpu.SemaphoreType.DMA((size - 1,)),
            pltpu.SemaphoreType.DMA((size - 1,)),
            pltpu.SemaphoreType.DMA((1,)),
        ]


class Broadcast:
    def __init__(self, dp, units, source, target, sems):
        self.dp, self.units, self.source, self.target = dp, units, source, target
        self.send, self.recv = sems
        self.me = lax.axis_index("dp")
        self.near = self.me + 1 - 2 * lax.rem(self.me, 2)
        self.far = lax.rem(self.me + 2, dp)
        self.square = dp == 4

    def hop(self, i, u):
        if self.square:
            to = self.near if i == 0 else self.far
        else:
            to = lax.rem(self.me + i + 1, self.dp)
        return send(
            self.source(u), self.target(self.me, u), self.send.at[i, u], self.recv.at[i, u], dp=to
        )

    def across(self, u):
        low = u < self.units // 2
        where = self.target(self.near if low else self.far, u)
        return send(
            where,
            where,
            self.send.at[2, u],
            self.recv.at[2, u],
            dp=self.far if low else self.near,
        )

    def hops(self):
        return 2 if self.square else self.dp - 1

    def start(self, units=None):
        half = self.units // 2
        for n in range(self.units) if units is None else units:
            for i in range(self.hops()):
                u = (n + half) % self.units if self.square and i == 1 and units is None else n
                self.hop(i, u).start()

    def forward(self, u):
        if self.square:
            self.hop(0 if u < self.units // 2 else 1, u).wait_recv()
            self.across(u).start()

    def finish(self):
        for u in range(self.units):
            for i in range(self.hops()):
                if not self.square or (i == 0) != (u < self.units // 2):
                    self.hop(i, u).wait_recv()
                self.hop(i, u).wait_send()
            if self.square:
                self.across(u).wait()

    @staticmethod
    def scratch(dp, units):
        return [
            pltpu.SemaphoreType.DMA((max(dp - 1, 1), units)),
            pltpu.SemaphoreType.DMA((max(dp - 1, 1), units)),
        ]


ANY = pl.BlockSpec(memory_space=pl.ANY)


def staged_call(kernel, args, out_shape, in_specs, out_specs, scratch_shapes, loads, stores, **kinds):
    counts = len(args), len(out_shape)
    dma = pltpu.SemaphoreType.DMA
    buffers = [pltpu.VMEM(shape, args[i].dtype) for i, shape, _ in loads]
    buffers += [pltpu.VMEM(out_shape[j].shape, out_shape[j].dtype) for j in stores]
    in_specs, out_specs = list(in_specs), list(out_specs)
    for i, _, _ in loads:
        in_specs[i] = ANY
    for j in stores:
        out_specs[j] = ANY

    def run(*refs):
        ins, outs = list(refs[: counts[0]]), list(refs[counts[0] : sum(counts)])
        own = refs[len(refs) - len(buffers) - 2 :]
        in_sem, out_sem = own[-2:]
        coming, going = {}, {}
        for n, (i, _, part) in enumerate(loads):
            source = ins[i] if part is None else ins[i].at[part()]
            coming[i] = pltpu.make_async_copy(source, own[n], in_sem.at[n])
            ins[i] = own[n]
        for n, j in enumerate(stores):
            buffer = own[len(loads) + n]
            going[j] = pltpu.make_async_copy(buffer, outs[j], out_sem.at[n])
            outs[j] = buffer
        for copy in coming.values():
            copy.start()

        def load(*which):
            for i in which:
                coming[i].wait()

        def store(*which):
            for j in which:
                going[j].start()

        kernel(*ins, *outs, *refs[sum(counts) : len(refs) - len(own)], load=load, store=store)
        for copy in going.values():
            copy.wait()

    return pl.pallas_call(
        run,
        out_shape=tuple(out_shape),
        in_specs=in_specs,
        out_specs=tuple(out_specs),
        scratch_shapes=list(scratch_shapes)
        + buffers
        + [dma((max(len(loads), 1),)), dma((max(len(stores), 1),))],
        **kinds,
    )(*args)


def load_columns(weight, whole, sem):
    dp, cols, part, _ = weight.shape
    copies = [
        pltpu.make_async_copy(
            weight.at[p, j],
            whole.at[pl.ds((j * dp + p) * part, part), :],
            sem.at[p, j],
        )
        for p in range(dp)
        for j in range(cols)
    ]
    for copy in copies:
        copy.start()
    return copies


def dot_nt(a, b):
    return lax.dot_general(a, b, (((1,), (1,)), ((), ())), preferred_element_type=F32)


def dot_tn(a, b):
    return lax.dot_general(a, b, (((0,), (0,)), ((), ())), preferred_element_type=F32)


def dot_nn(a, b):
    return jnp.dot(a, b, preferred_element_type=F32)


def moments(rows):
    mean = jnp.mean(rows, axis=1, keepdims=True)
    centered = rows - mean
    return centered, lax.rsqrt(jnp.mean(centered * centered, axis=1, keepdims=True) + EPSILON)


def cost(us):
    return pl.CostEstimate(flops=us * 10**9, bytes_accessed=10**7, transcendentals=0)


def params(number):
    return pltpu.CompilerParams(
        collective_id=number, has_side_effects=True, vmem_limit_bytes=VMEM_LIMIT
    )


VM = pl.BlockSpec(memory_space=pltpu.VMEM)


def row_spot(own, step, half, width):
    def spot(r, source, s):
        return pl.ds(pl.multiple_of(r * half + source * own + s * step, 16), step), pl.ds(0, width)

    return spot


COTANGENT_SLOTS = (0, 36)


def middle_kernel(
    cols,
    part,
    tokens_own,
    vectors,
    piece,
    cotan,
    normed_to,
    middle_to,
    hidden_to,
    gate_to,
    up_to,
    weight_to,
    cotan_to,
    normed,
    middle,
    hidden,
    gate_part,
    up_part,
    weight,
    cotan_rows,
    total,
    own_sem,
    out_sem,
    block_sem,
    *scratch,
    load,
    store
):
    group, width = part.shape
    half = group // 2
    own = half // cols
    step = own // SUBS
    depth = cotan.shape[1]
    rows_each = half // SUBS
    _, part_rows, double = piece.shape
    narrow = double // 2
    dp = weight.shape[0] // cols // part_rows
    me = lax.axis_index("dp")
    enter(cols, everyone=True, dp=dp)
    load(0)
    summing = Reduce(
        cols, SUBS, lambda d, s: (d * own + s * step, step, 0, width), part, *scratch[:3], scratch[3:7]
    )
    summing.start()
    spread = Gather(cols, SUBS, row_spot(own, step, half, width), normed, scratch[7:11])

    def cotan_spot(r, source, s):
        rows = pl.ds(pl.multiple_of(r * half + s * rows_each, 16), rows_each)
        return rows, pl.ds(pl.multiple_of(source * depth, 128), depth)

    cotan_spread = Gather(cols, SUBS, cotan_spot, cotan_rows, scratch[11:15])

    def weight_rows(p, j):
        return weight.at[pl.ds(pl.multiple_of((j * dp + p) * part_rows, 16), part_rows), :]

    rider = Broadcast(dp, cols, lambda u: piece.at[u], weight_rows, scratch[15:17])
    rider.start()
    own_copies = [
        pltpu.make_async_copy(piece.at[j], weight_rows(me, j), own_sem.at[j]) for j in range(cols)
    ]
    for copy in own_copies:
        copy.start()
    load(1, 2, 4)

    def land(s):
        summing.land(s, total)
        rows = pl.ds(pl.multiple_of(s * step, step), step)
        state = tokens_own[rows, :].astype(F32) + total[...]
        middle[rows, :] = state
        centered, rstd = moments(state)
        result = centered * rstd * vectors[2:3, :] + vectors[3:4, :]
        normed[spread.spot(spread.r, spread.c, s)] = result.astype(BF16)
        spread.start(s)

    batch = SUBS // len(COTANGENT_SLOTS)

    def cotan_slot(t):
        for i, begin in enumerate(COTANGENT_SLOTS):
            after = t - begin

            @pl.when((after >= 0) & (lax.rem(after + 60, 3) == 0) & (after < 3 * batch))
            def _():
                s = i * batch + lax.div(after, 3)
                rows = pl.ds(pl.multiple_of(s * rows_each, 16), rows_each)
                cotan_rows[cotan_spot(spread.r, spread.c, s)] = cotan[rows, :]
                cotan_spread.start(s)

            cotan_spread.slot(t, begin, 3, i * batch, batch)

    first = summing.slots + LAG * (cols - 1)
    last = COTANGENT_SLOTS[-1] + 3 * (batch - 1) + LAG * (cols - 1) + 1
    blocks = group // BLOCK

    @pl.loop(0, first)
    def _(t):
        summing.slot(t)
        summing.landed(t, land)
        spread.slot(t, summing.landing, summing.per_sub)
        cotan_slot(t)
        for u in range(cols):

            @pl.when(t == 14 + 8 * (u % 2))
            def _():
                rider.forward(u)

    spread.finish()
    normed_out = pltpu.make_async_copy(normed, normed_to, out_sem.at[0])
    normed_out.start()
    middle_out = pltpu.make_async_copy(middle, middle_to, out_sem.at[1])
    middle_out.start()
    for copy in own_copies:
        copy.wait()
    rider.finish()
    weight_out = pltpu.make_async_copy(weight, weight_to, out_sem.at[2])
    weight_out.start()

    def block_out(m):
        rows = pl.ds(pl.multiple_of(m * BLOCK, BLOCK), BLOCK)
        pairs = ((hidden, hidden_to), (gate_part, gate_to), (up_part, up_to))
        return [
            pltpu.make_async_copy(a.at[rows, :], b.at[rows, :], block_sem.at[i, m])
            for i, (a, b) in enumerate(pairs)
        ]

    @pl.loop(0, max(last - first, blocks))
    def _(m):
        @pl.when(m < blocks)
        def _():
            rows = pl.ds(pl.multiple_of(m * BLOCK, BLOCK), BLOCK)
            both = dot_nn(normed[rows, :], weight[...])
            gate, up = both[:, :narrow], both[:, narrow:]
            sig = 1.0 / (1.0 + jnp.exp(-gate))
            active = gate * sig
            hidden[rows, :] = (active * up).astype(BF16)
            up_part[rows, :] = active.astype(BF16)
            gate_part[rows, :] = (up * sig * (1.0 + gate * (1.0 - sig))).astype(BF16)
            for copy in block_out(m):
                copy.start()

        cotan_slot(first + m)

    cotan_spread.finish()
    cotan_out = pltpu.make_async_copy(cotan_rows, cotan_to, out_sem.at[3])
    cotan_out.start()
    summing.finish()
    for m in range(blocks):
        for copy in block_out(m):
            copy.wait()
    for copy in (normed_out, middle_out, weight_out, cotan_out):
        copy.wait()


def middle_part(cols, part, tokens_own, vectors, piece, cotan, dp):
    group, width = part.shape
    _, part_rows, double = piece.shape
    narrow = double // 2
    blocks = group // BLOCK
    dma = pltpu.SemaphoreType.DMA
    outs = (
        ((group, width), BF16),
        (tokens_own.shape, F32),
        ((group, narrow), BF16),
        ((group, narrow), BF16),
        ((group, narrow), BF16),
        ((dp * cols * part_rows, double), BF16),
        ((group, width), BF16),
    )
    args = (part, tokens_own, vectors, piece, cotan)
    return staged_call(
        functools.partial(middle_kernel, cols),
        args,
        out_shape=tuple(jax.ShapeDtypeStruct(*out) for out in outs),
        in_specs=[VM] * 3 + [ANY, VM],
        out_specs=[ANY] * len(outs),
        loads=[(i, args[i].shape, None) for i in (0, 1, 2, 4)],
        stores=(),
        scratch_shapes=[pltpu.VMEM(*out) for out in outs]
        + [
            pltpu.VMEM((group // 2 // cols // SUBS, width), F32),
            dma((cols,)),
            dma((4,)),
            dma((3, blocks)),
        ]
        + Reduce.scratch(cols, SUBS, group // 2, width)
        + Gather.scratch(cols, SUBS) * 2
        + Broadcast.scratch(dp, cols),
        compiler_params=params(2),
        cost_estimate=cost(95),
        name="middle_gate_up",
    )


def norm_two_back_kernel(
    cols,
    gate_up_grad,
    gate_up,
    middle,
    cotan_own,
    vectors,
    hidden,
    weight,
    grads,
    sums,
    mixed_part,
    part,
    down,
    sem,
    *scratch,
    load,
    store
):
    narrow = hidden.shape[1]
    copies = load_columns(weight, down, sem)
    half, width = part.shape[0] // 2, part.shape[1]
    own = half // cols
    step = own // SUBS
    total = scratch[11]
    enter(cols)
    load(0, 1)
    summing = Reduce(
        cols, SUBS, lambda d, s: (d * own + s * step, step, 0, width), part, *scratch[:3], scratch[3:7]
    )
    spread = Gather(cols, SUBS, row_spot(own, step, half, width), grads, scratch[7:11])
    blocks = part.shape[0] // BLOCK
    row = lax.axis_index("row")

    def product(r):
        @pl.loop(0, blocks // 2)
        def _(m):
            rows = pl.ds(pl.multiple_of(r * half + m * BLOCK, BLOCK), BLOCK)
            part[rows, :] = dot_nt(gate_up_grad[rows, :], gate_up[...]).astype(BF16)

    product(1 - row)
    summing.start()
    product(row)
    for copy in copies:
        copy.wait()
    load(2, 3, 4, 5)
    sums[...] = jnp.zeros_like(sums)

    def land(s):
        summing.land(s, total)
        rows = pl.ds(pl.multiple_of(s * step, step), step)
        centered, rstd = moments(middle[rows, :])
        xhat = centered * rstd
        grad = total[...]
        sums[0:1, :] += jnp.sum(grad * xhat, axis=0, keepdims=True)
        sums[1:2, :] += jnp.sum(grad, axis=0, keepdims=True)
        scaled = grad * vectors[2:3, :]
        inner = (
            scaled
            - jnp.mean(scaled, axis=1, keepdims=True)
            - xhat * jnp.mean(scaled * xhat, axis=1, keepdims=True)
        )
        result = cotan_own[rows, :].astype(F32) + rstd * inner
        grads[spread.spot(spread.r, spread.c, s)] = result.astype(BF16)
        spread.start(s)

    @pl.loop(0, summing.slots + LAG * (cols - 1))
    def _(t):
        summing.slot(t)
        summing.landed(t, land)
        spread.slot(t, summing.landing, summing.per_sub)

        @pl.when((lax.rem(t, PACE) == PACE - 1) & (t < PACE * blocks))
        def _():
            rows = pl.ds(pl.multiple_of(lax.div(t, PACE) * BLOCK, BLOCK), BLOCK)
            result = dot_nt(hidden[rows, :], down[:, :narrow])
            mixed_part[rows, :] = result.astype(BF16)

    store(2)
    spread.finish()
    store(0)
    summing.finish()


def norm_two_back(cols, gate_up_grad, gate_up, middle, cotan, vectors, hidden, weight):
    group, width = cotan.shape
    tall = weight.shape[3]
    own = group // 2 // cols

    def own_rows():
        row = lax.axis_index("row") * (group // 2) + lax.axis_index("col") * own
        return pl.ds(pl.multiple_of(row, own), own)

    args = (gate_up_grad, gate_up, middle, cotan, vectors, hidden, weight)
    return staged_call(
        functools.partial(norm_two_back_kernel, cols),
        args,
        out_shape=(
            jax.ShapeDtypeStruct((group, width), BF16),
            jax.ShapeDtypeStruct((8, width), F32),
            jax.ShapeDtypeStruct((group, width), BF16),
        ),
        in_specs=[VM] * 6 + [ANY],
        out_specs=[VM] * 3,
        loads=[(i, args[i].shape, None) for i in (0, 1, 2)]
        + [(3, (own, width), own_rows)]
        + [(i, args[i].shape, None) for i in (4, 5)],
        stores=(0, 2),
        scratch_shapes=[pltpu.VMEM((group, width), BF16), pltpu.VMEM((width, tall), BF16), pltpu.SemaphoreType.DMA(weight.shape[:2])]
        + Reduce.scratch(cols, SUBS, group // 2, width)
        + Gather.scratch(cols, SUBS)
        + [pltpu.VMEM((group // 2 // cols // SUBS, width), F32)],
        compiler_params=params(3),
        cost_estimate=cost(60),
        name="grad_sum_norm_gather",
    )


def mixed_sum(cols, part, middle, scratch):
    half, width = part.shape[0] // 2, part.shape[1]
    step, depth, own = half // SUBS, width // cols, half // cols
    c = lax.axis_index("col")

    def add(d, s):
        inside = s * step - c * own
        rows = pl.ds(pl.multiple_of(lax.rem(s * step, own), step), step)
        mine = middle[rows, pl.ds(pl.multiple_of(d * depth, 128), depth)]
        return jnp.where((inside >= 0) & (inside < own), mine, 0.0)

    return Reduce(
        cols,
        SUBS,
        lambda d, s: (s * step, step, d * depth, depth),
        part,
        *scratch[:3],
        scratch[3:7],
        add=add,
    )


MIXED_SLOT = 22
ARRANGE_SLOT = 24


def last_kernel(
    cols,
    part,
    xhat,
    rstd,
    gain,
    grad_middle,
    heads_grad,
    out_grad,
    second,
    mixed_part,
    middle,
    hidden_piece,
    bias,
    result,
    mixed,
    small,
    attention_all,
    hidden_all,
    total,
    grad,
    mine,
    theirs,
    sums,
    landed,
    slices,
    own_norms,
    pair_norms,
    arranged,
    own_small,
    all_small,
    out_sem,
    in_sem,
    pair_sem,
    small_send,
    small_recv,
    own_sem,
    *sems,
    load,
    store
):
    half, width = part.shape[0] // 2, part.shape[1]
    step, depth = half // SUBS, width // cols
    pairs, dp = heads_grad.shape[:2]
    two = heads_grad.shape[4] // 3
    narrow = sums.shape[2] // 4
    rows_each = hidden_piece.shape[1] // 2
    weights = hidden_piece.shape[0]
    enter(cols, everyone=True, dp=dp)
    r, c, me = (lax.axis_index(name) for name in ("row", "col", "dp"))
    load(0)
    summing = Reduce(
        cols, SUBS, lambda d, s: (s * step, step, d * depth, depth), part, *sems[:3], sems[3:7]
    )
    summing.start()
    rider = Exchange("col", cols, sums, landed, sems[14:17])
    names = Exchange("col", cols, second, slices, sems[17:20])
    names.start()

    def hidden_rows(u):
        return u % weights, pl.ds(u // weights * rows_each, rows_each)

    hidden_cast = Broadcast(
        dp,
        2 * weights,
        lambda u: hidden_piece.at[hidden_rows(u)],
        lambda p, u: hidden_all.at[(p,) + hidden_rows(u)],
        sems[20:22],
    )
    attention_cast = Broadcast(
        dp, 4, lambda u: arranged.at[u], lambda p, u: attention_all.at[p, u], sems[22:24]
    )
    hidden_own = pltpu.make_async_copy(hidden_piece, hidden_all.at[me], own_sem.at[0])
    attention_own = pltpu.make_async_copy(arranged, attention_all.at[me], own_sem.at[1])
    hidden_cast.start()
    hidden_own.start()
    load(5, 6)

    def over_dp(ref, to):
        value = ref[0, to].astype(F32)
        for p in range(1, dp):
            value = value + ref[p, to].astype(F32)
        return value.astype(BF16)

    def fill(to, target):
        for pair in range(pairs):
            value = over_dp(heads_grad.at[pair], to)
            for k in range(3):
                first = k * narrow + pair * two
                target[:, first : first + two] = value[:, k * two : (k + 1) * two]
        target[:, 3 * narrow :] = over_dp(out_grad, to)

    for k in range(1, cols):
        to = rider.peer(k)
        fill(to, sums.at[to])
        rider.hop(k).start()
    fill(c, landed.at[c])
    own_norms[...] = jnp.zeros_like(own_norms)
    load(8, 9)
    mixing = mixed_sum(cols, mixed_part, middle, sems[7:14])
    mixing.start()
    load(1, 2, 4)

    def land(s):
        summing.land(s, total)
        rows = pl.ds(pl.multiple_of(s * step, step), step)
        grad[rows, :] = total[...]
        standard = xhat[rows, :]
        own_norms[0:1, :] += jnp.sum(total[...] * standard, axis=0, keepdims=True)
        own_norms[1:2, :] += jnp.sum(total[...], axis=0, keepdims=True)

    def land_mixed(s):
        mixing.land(s, total)
        mixed[pl.ds(pl.multiple_of(s * step, step), step), :] = total[...].astype(BF16)

    def arrange():
        for k in range(1, cols):
            rider.hop(k).wait_recv()
        for k in range(4):
            for j in range(cols):
                arranged[k, :, j * narrow : (j + 1) * narrow] = landed[
                    j, :, k * narrow : (k + 1) * narrow
                ]
        attention_cast.start()
        attention_own.start()

    @pl.loop(0, summing.slots)
    def _(t):
        summing.slot(t)
        summing.landed(t, land)
        mixing.slot(t - MIXED_SLOT)
        mixing.landed(t - MIXED_SLOT, land_mixed)
        for u in range(weights):

            @pl.when(t == 8 + 6 * u)
            def _():
                hidden_cast.forward(u)
                hidden_cast.forward(weights + u)

        @pl.when(t == ARRANGE_SLOT)
        def _():
            arrange()

    lanes = lax.broadcasted_iota(jnp.int32, (128, 128), 1)
    for s in range(half // 128):
        rows = slice(s * 128, (s + 1) * 128)
        scaled = grad[rows, :] * gain[0:1, :]
        one = jnp.sum(scaled, axis=1, keepdims=True)
        two_sum = jnp.sum(scaled * xhat[rows, :], axis=1, keepdims=True)
        both = jnp.where(lanes == 0, one, jnp.where(lanes == 1, two_sum, 0.0))
        mine[:, rows] = both.T[0:8, :]

    def exchange_sums(k):
        return send(
            mine, theirs.at[k - 1], out_sem.at[k - 1], in_sem.at[k - 1], col=lax.rem(c + k, cols)
        )

    for k in range(1, cols):
        exchange_sums(k).start()
    names.finish()
    shift = slices[0]
    for j in range(1, cols):
        shift = shift + slices[j]
    own_norms[2:4, :] = shift[0:2, :]
    across = send(own_norms, pair_norms, pair_sem.at[0], pair_sem.at[1], row=1 - r)
    across.start()

    @pl.loop(summing.slots, MIXED_SLOT + mixing.slots)
    def _(t):
        mixing.slot(t - MIXED_SLOT)
        mixing.landed(t - MIXED_SLOT, land_mixed)
        for u in range(2):

            @pl.when(t == summing.slots + 6 + 8 * u)
            def _():
                attention_cast.forward(u)
                attention_cast.forward(2 + u)

    across.wait()
    own_small[:, :depth] = own_norms[...] + pair_norms[...]
    own_small[:, depth:] = bias[...]
    all_small[me] = own_small[...]

    def hop(k):
        to = lax.rem(me + k, dp)
        return send(
            own_small, all_small.at[me], small_send.at[k - 1], small_recv.at[k - 1], dp=to
        )

    for k in range(1, dp):
        hop(k).start()
    for k in range(1, cols):
        exchange_sums(k).wait_recv()
    for s in range(half // 128):
        rows = slice(s * 128, (s + 1) * 128)
        both = mine[:, rows]
        for k in range(1, cols):
            both = both + theirs[k - 1, :, rows]
        both = jnp.concatenate([both, jnp.zeros((120, 128), F32)], axis=0).T / (depth * cols)
        scaled = grad[rows, :] * gain[0:1, :]
        inner = scaled - both[:, 0:1] - xhat[rows, :] * both[:, 1:2]
        result[rows, :] = grad_middle[rows, :].astype(F32) + rstd[rows, 0:1] * inner
    store(0, 1)
    for k in range(1, dp):
        hop(k).wait()
    value = all_small[0]
    for p in range(1, dp):
        value = value + all_small[p]
    small[...] = value
    for k in range(1, cols):
        exchange_sums(k).wait_send()
        rider.hop(k).wait_send()
    summing.finish()
    mixing.finish()
    hidden_own.wait()
    attention_own.wait()
    hidden_cast.finish()
    attention_cast.finish()


def last_part(
    cols, part, xhat, rstd, gain, grad_middle, heads_grad, out_grad, second, mixed_part, middle, piece, bias
):
    group, width = part.shape
    half, depth = group // 2, width // cols
    dp, _, rows, narrow = out_grad.shape
    small = (8, depth + bias.shape[1])
    hops = max(dp - 1, 1)
    dma = pltpu.SemaphoreType.DMA

    def own_block():
        row = lax.axis_index("row") * half
        column = lax.axis_index("col") * depth
        return pl.ds(pl.multiple_of(row, half), half), pl.ds(pl.multiple_of(column, 128), depth)

    args = (
        part,
        xhat,
        rstd,
        gain,
        grad_middle,
        heads_grad,
        out_grad,
        second,
        mixed_part,
        middle,
        piece,
        bias,
    )
    return staged_call(
        functools.partial(last_kernel, cols),
        args,
        out_shape=(
            jax.ShapeDtypeStruct((half, depth), F32),
            jax.ShapeDtypeStruct((half, depth), BF16),
            jax.ShapeDtypeStruct(small, F32),
            jax.ShapeDtypeStruct((dp, 4, rows, cols * narrow), BF16),
            jax.ShapeDtypeStruct((dp,) + piece.shape, BF16),
        ),
        in_specs=[VM] * 10 + [ANY, VM],
        out_specs=[VM] * 3 + [ANY] * 2,
        loads=[(i, args[i].shape, None) for i in (0, 5, 6, 8, 9, 1, 2)]
        + [(4, (half, depth), own_block)],
        stores=(0, 1),
        scratch_shapes=[
            pltpu.VMEM((half // SUBS, depth), F32),
            pltpu.VMEM((half, depth), F32),
            pltpu.VMEM((8, half), F32),
            pltpu.VMEM((cols - 1, 8, half), F32),
            pltpu.VMEM((cols, rows, 4 * narrow), BF16),
            pltpu.VMEM((cols, rows, 4 * narrow), BF16),
            pltpu.VMEM((cols, 8, depth), F32),
            pltpu.VMEM((8, depth), F32),
            pltpu.VMEM((8, depth), F32),
            pltpu.VMEM((4, rows, cols * narrow), BF16),
            pltpu.VMEM(small, F32),
            pltpu.VMEM((dp,) + small, F32),
            dma((cols - 1,)),
            dma((cols - 1,)),
            dma((2,)),
            dma((hops,)),
            dma((hops,)),
            dma((2,)),
        ]
        + Reduce.scratch(cols, SUBS, half, width) * 2
        + Exchange.scratch(cols) * 2
        + Broadcast.scratch(dp, 2 * piece.shape[0])
        + Broadcast.scratch(dp, 4),
        compiler_params=params(5),
        cost_estimate=cost(110),
        name="input_grad_mixed_sum",
    )


def start_kernel(
    cols,
    tokens,
    one_gain,
    one_bias,
    two_gain,
    two_bias,
    heads_from,
    out_from,
    gate_up_from,
    down_from,
    normed,
    tokens_own,
    xhat,
    rstd,
    vectors,
    gate_up_piece,
    down_piece,
    attention_w,
    heads,
    out,
    gate_up,
    down,
    pieces,
    landed,
    full,
    in_sem,
    own_sem,
    pair_send,
    pair_recv,
    *sems,
    load,
    store
):
    half, depth = tokens.shape
    width = depth * cols
    step = half // cols
    dp, _, part, wide = attention_w.shape
    narrow = wide // 4
    tall = down.shape[0] // cols
    r, c, me = (lax.axis_index(name) for name in ("row", "col", "dp"))
    begin = pl.multiple_of(me * part, part)
    rows_in = pl.ds(begin, part)

    def share_of(ref):
        return ref if ref.shape[1] == part else ref.at[:, rows_in]

    loads = [
        pltpu.make_async_copy(heads_from.at[:, rows_in], heads, in_sem.at[0]),
        pltpu.make_async_copy(share_of(out_from), out, in_sem.at[1]),
        pltpu.make_async_copy(gate_up_from.at[rows_in], gate_up, in_sem.at[2]),
        pltpu.make_async_copy(share_of(down_from), down, in_sem.at[3]),
    ]
    for load in loads:
        load.start()
    enter(cols, everyone=True, dp=dp)
    loads[0].wait()
    loads[1].wait()
    for j in range(cols):
        share = slice(j * narrow, (j + 1) * narrow)
        for k in range(3):
            pieces[j, :, k * narrow : (k + 1) * narrow] = heads[k, :, share]
        pieces[j, :, 3 * narrow :] = out[share, :].T
    rider = Exchange("col", cols, pieces, landed, sems[:3])
    assert cols == 4
    landed[c] = pieces[c]
    units = [c] + [rider.peer(k) for k in range(1, cols)]
    cast = Broadcast(
        dp, cols, lambda k: landed.at[units[k]], lambda p, k: attention_w.at[p, units[k]], sems[11:13]
    )
    cast.start((0,))
    for k in range(1, cols):
        rider.hop(k).start()

    def columns(source):
        return pl.ds(pl.multiple_of(source * depth, 128), depth)

    names = Gather(
        cols, 1, lambda r, source, s: (pl.ds(0, 8), columns(source)), vectors, sems[3:7], pair=False
    )
    spread = Gather(
        cols,
        cols,
        lambda r, source, s: (pl.ds(s * step, step), columns(source)),
        full,
        sems[7:11],
        pair=False,
    )
    vectors[:, columns(c)] = jnp.zeros((8, depth), F32)
    for i, values in enumerate((one_gain, one_bias, two_gain, two_bias)):
        vectors[i : i + 1, columns(c)] = values[...]
    names.start(0)
    for s in range(cols):
        rows = pl.ds(s * step, step)
        full[rows, columns(c)] = tokens[rows, :]
        spread.start(s)
    loads[2].wait()
    for i in range(2):
        values = gate_up[:, i, :]
        for j in range(cols):
            gate_up_piece[j, :, i * tall : (i + 1) * tall] = values[:, j * tall : (j + 1) * tall]
    loads[3].wait()
    for j in range(cols):
        down_piece[j, :, :tall] = down[j * tall : (j + 1) * tall, :].T
        if down_piece.shape[2] > tall:
            down_piece[j, :, tall:] = jnp.zeros((part, down_piece.shape[2] - tall), BF16)

    store(5, 6)

    def across(r, s):
        where = normed.at[pl.ds(pl.multiple_of(r * half + s * step, 16), step), :]
        return send(where, where, pair_send.at[s], pair_recv.at[s], row=1 - lax.axis_index("row"))

    def own(k):
        u = units[k]
        return pltpu.make_async_copy(landed.at[u], attention_w.at[me, u], own_sem.at[k])

    def take(k):
        rider.hop(k).wait_recv()
        cast.start((k,))
        own(k).start()

    def norm(s):
        rows = slice(s * step, (s + 1) * step)
        state = full[rows, :].astype(F32)
        centered, inverse = moments(state)
        result = centered * inverse * vectors[0:1, :] + vectors[1:2, :]
        normed[pl.ds(pl.multiple_of(r * half + s * step, 16), step), :] = result.astype(BF16)
        across(r, s).start()
        rstd[rows, :] = jnp.broadcast_to(inverse, (step, 128))
        mean = jnp.mean(state, axis=1, keepdims=True)
        xhat[rows, :] = (tokens[rows, :].astype(F32) - mean) * inverse

        @pl.when(c == s)
        def _():
            tokens_own[...] = full[rows, :]

    own(0).start()
    take(1)
    for k in range(1, cols):
        names.relay(0, k)
    for s in range(cols):
        spread.relay(s, 1)
    cast.forward(0)
    take(2)
    take(3)
    for s in range(cols):
        spread.relay(s, 2)
    cast.forward(1)
    cast.forward(2)
    for s in range(cols):
        spread.relay(s, 3)
        norm(s)
        if s == 1:
            cast.forward(3)

    for s in range(cols):
        across(1 - r, s).wait_recv()
    store(0, 1, 2, 3)
    for s in range(cols):
        across(r, s).wait_send()
    for u in range(cols):
        own(u).wait()
    cast.finish()
    for k in range(1, cols):
        rider.hop(k).wait_send()
    names.finish()
    spread.finish()


def start_part(tokens, vectors, heads, out, gate_up, down, sizes):
    dp, cols = sizes["dp"], sizes["col"]
    half, depth = tokens.shape
    width = depth * cols
    part, wide, tall = depth // dp, heads.shape[2], down.shape[0]
    each = tall // cols
    dma = pltpu.SemaphoreType.DMA
    return staged_call(
        functools.partial(start_kernel, cols),
        (tokens, *vectors, heads, out, gate_up, down),
        out_shape=(
            jax.ShapeDtypeStruct((2 * half, width), BF16),
            jax.ShapeDtypeStruct((half // cols, width), BF16),
            jax.ShapeDtypeStruct((half, depth), F32),
            jax.ShapeDtypeStruct((half, 128), F32),
            jax.ShapeDtypeStruct((8, width), F32),
            jax.ShapeDtypeStruct((cols, part, 2 * each), BF16),
            jax.ShapeDtypeStruct((cols, part, each + -each % 128), BF16),
            jax.ShapeDtypeStruct((dp, cols, part, 4 * wide // cols), BF16),
        ),
        in_specs=[VM] * 5 + [ANY] * 4,
        out_specs=[VM] * 7 + [ANY],
        loads=(),
        stores=(0, 1, 2, 3, 5, 6),
        scratch_shapes=[
            pltpu.VMEM((3, part, wide), BF16),
            pltpu.VMEM((wide, part), BF16),
            pltpu.VMEM((part, 2, tall), BF16),
            pltpu.VMEM((tall, part), BF16),
            pltpu.VMEM((cols, part, 4 * wide // cols), BF16),
            pltpu.VMEM((cols, part, 4 * wide // cols), BF16),
            pltpu.VMEM((half, width), BF16),
            dma((4,)),
            dma((cols,)),
            dma((cols,)),
            dma((cols,)),
        ]
        + Exchange.scratch(cols)
        + Gather.scratch(cols, 1)
        + Gather.scratch(cols, cols)
        + Broadcast.scratch(dp, cols),
        compiler_params=params(1),
        cost_estimate=cost(60),
        name="tokens_norm_weights",
    )


def rope_tables(length):
    half_rot = ROT // 2
    lane = np.arange(2 * HD) % HD
    inverse = (ROPE_BASE ** (-2.0 * (lane % half_rot) / ROT)).astype(np.float32)
    angles = np.arange(length).astype(np.float32)[:, None] * inverse[None, :]
    turning = lane < ROT
    cosine = np.where(turning, np.cos(angles), 1.0)
    sine = np.where(turning, np.sin(angles), 0.0)
    lower = np.where(lane < half_rot, -sine, 0.0)
    upper = np.where(lane >= half_rot, sine, 0.0)
    return np.stack([cosine, lower, upper]).astype(np.float32)


def turn(x, tables, back=False):
    half_rot = ROT // 2
    width = x.shape[1]
    sines = pltpu.roll(x, width - half_rot, 1) * tables[1] + pltpu.roll(x, half_rot, 1) * tables[2]
    return x * tables[0] - sines if back else x * tables[0] + sines


def causal(rows):
    return lax.broadcasted_iota(jnp.int32, (rows, rows), 0) >= lax.broadcasted_iota(
        jnp.int32, (rows, rows), 1
    )


def attend_kernel(
    cols,
    normed,
    weight,
    bias,
    tables,
    one_from,
    two_from,
    heads_in,
    attn,
    logs,
    part,
    one_to,
    two_to,
    whole,
    sem,
    qkv,
    *sems,
    load,
    store
):
    length, wide = attn.shape
    two = 2 * HD
    copies = load_columns(weight, whole, sem)
    enter(cols, everyone=True)
    riders = (
        Exchange("col", cols, one_from, one_to, sems[:3]),
        Exchange("col", cols, two_from, two_to, sems[3:]),
    )
    for rider in riders:
        rider.start()
    for copy in copies:
        copy.wait()
    load(0, 3)
    first_head = lax.broadcasted_iota(jnp.int32, (BLOCK, two), 1) < HD

    @pl.loop(0, length // BLOCK)
    def _(m):
        rows = pl.ds(pl.multiple_of(m * BLOCK, BLOCK), BLOCK)
        qkv[rows, :] = dot_nn(normed[rows, :], whole[:, : 3 * wide])

    @pl.loop(0, wide // two)
    def _(pair):
        def lanes(k):
            return pl.ds(pl.multiple_of(k * wide + pair * two, two), two)

        for k in range(3):
            x = qkv[:, lanes(k)] + bias[k : k + 1, pl.ds(pl.multiple_of(pair * two, two), two)]
            if k < 2:
                x = turn(x, tables)
            if k == 0:
                x = x * HD ** (-0.5)
            heads_in[:, lanes(k)] = x.astype(BF16)
        for i in range(length // BLOCK):
            keep = (i + 1) * BLOCK
            rows = slice(i * BLOCK, keep)
            query = heads_in[rows, lanes(0)]
            keys = heads_in[0:keep, lanes(1)]
            values = heads_in[0:keep, lanes(2)]
            outs = []
            for h in range(2):
                mine = first_head if h == 0 else ~first_head
                scores = dot_nt(jnp.where(mine, query, jnp.zeros_like(query)), keys)
                last = jnp.where(causal(BLOCK), scores[:, i * BLOCK :], NEG_LARGE)
                scores = last if i == 0 else jnp.concatenate([scores[:, : i * BLOCK], last], axis=1)
                top = jnp.max(scores, axis=1, keepdims=True)
                expo = jnp.exp(scores - top)
                total = jnp.sum(expo, axis=1, keepdims=True)
                probs = (expo * (1.0 / total)).astype(BF16)
                outs.append(dot_nn(probs, values))
                logs[pair, h, rows, :] = jnp.broadcast_to(top + jnp.log(total), (BLOCK, 128))
            attn[rows, pl.ds(pl.multiple_of(pair * two, two), two)] = jnp.where(
                first_head, outs[0], outs[1]
            ).astype(BF16)

    store(0, 1, 2)

    @pl.loop(0, length // BLOCK)
    def _(m):
        rows = pl.ds(pl.multiple_of(m * BLOCK, BLOCK), BLOCK)
        part[rows, :] = dot_nt(attn[rows, :], whole[:, 3 * wide :]).astype(BF16)

    store(3)
    for rider in riders:
        rider.finish()


def attend(cols, normed, weight, bias, tables, one, two):
    length, width = normed.shape
    dp = weight.shape[0]
    wide = weight.shape[3] // 4
    args = (normed, weight, bias, tables, one, two)
    return staged_call(
        functools.partial(attend_kernel, cols),
        args,
        out_shape=(
            jax.ShapeDtypeStruct((length, 3 * wide), BF16),
            jax.ShapeDtypeStruct((length, wide), BF16),
            jax.ShapeDtypeStruct((wide // (2 * HD), 2, length, 128), F32),
            jax.ShapeDtypeStruct((length, width), BF16),
            jax.ShapeDtypeStruct(one.shape, BF16),
            jax.ShapeDtypeStruct(two.shape, BF16),
        ),
        in_specs=[VM, ANY, VM, VM, ANY, ANY],
        out_specs=[VM] * 4 + [ANY] * 2,
        loads=[(i, args[i].shape, None) for i in (0, 3)],
        stores=(0, 1, 2, 3),
        scratch_shapes=[
            pltpu.VMEM((width, 4 * wide), BF16),
            pltpu.SemaphoreType.DMA((dp, cols)),
            pltpu.VMEM((length, 3 * wide), F32),
        ]
        + Exchange.scratch(cols) * 2,
        compiler_params=params(6),
        cost_estimate=cost(50),
        name="attention_weight_exchange",
    )


def attend_back_kernel(
    cols,
    heads_in,
    logs,
    grad_middle,
    tables,
    weight,
    normed,
    attn,
    pieces_from,
    heads_to,
    out_to,
    normed_grad,
    sums,
    arranged,
    queries_grad,
    keys_grad,
    values_grad,
    whole,
    sem,
    grad,
    result,
    own,
    pieces_to,
    heads_from,
    out_from,
    *sems,
    load,
    store
):
    length, wide = attn.shape
    two = 2 * HD
    dp, _, part_rows, _ = weight.shape
    copies = load_columns(weight, whole, sem)
    enter(cols, everyone=True, dp=dp)
    rider = Exchange("col", cols, pieces_from, pieces_to, sems[:3])
    rider.start()
    out_rider = Exchange("dp", dp, out_from, out_to, sems[3:6])
    depth = normed.shape[1] // cols
    load(2, 6)

    def heads_rider(pair):
        return Exchange(
            "dp", dp, heads_from.at[pair], heads_to.at[pair], [sem.at[pair] for sem in sems[6:]]
        )

    def parts(j):
        return pl.ds(pl.multiple_of(j * depth, depth), depth)

    @pl.loop(0, cols)
    def _(j):
        out_grad = dot_tn(grad_middle[:, parts(j)], attn[...]).astype(BF16)
        for p in range(dp):
            out_from[p, j] = out_grad[p * part_rows : (p + 1) * part_rows, :]

    out_rider.start()
    for copy in copies:
        copy.wait()
    load(0, 1, 3, 5)
    sums[...] = jnp.zeros_like(sums)
    first_head = lax.broadcasted_iota(jnp.int32, (BLOCK, two), 1) < HD

    @pl.loop(0, length // BLOCK)
    def _(m):
        rows = pl.ds(pl.multiple_of(m * BLOCK, BLOCK), BLOCK)
        grad[rows, :] = dot_nn(grad_middle[rows, :], whole[:, 3 * wide :]).astype(BF16)

    @pl.loop(0, wide // two)
    def _(pair):
        def lanes(k):
            return pl.ds(pl.multiple_of(k * wide + pair * two, two), two)

        keys_grad[...] = jnp.zeros_like(keys_grad)
        values_grad[...] = jnp.zeros_like(values_grad)
        for i in range(length // BLOCK):
            keep = (i + 1) * BLOCK
            rows = slice(i * BLOCK, keep)
            query = heads_in[rows, lanes(0)]
            keys = heads_in[0:keep, lanes(1)]
            values = heads_in[0:keep, lanes(2)]
            out_grad = grad[rows, lanes(0)]
            outs = []
            for h in range(2):
                mine = first_head if h == 0 else ~first_head
                query_h = jnp.where(mine, query, jnp.zeros_like(query))
                grad_h = jnp.where(mine, out_grad, jnp.zeros_like(out_grad))
                scores = dot_nt(query_h, keys)
                probs = jnp.exp(scores - logs[pair, h, rows, 0:1])
                last = jnp.where(causal(BLOCK), probs[:, i * BLOCK :], 0.0)
                probs = last if i == 0 else jnp.concatenate([probs[:, : i * BLOCK], last], axis=1)
                probs_grad = dot_nt(grad_h, values)
                delta = jnp.sum(probs * probs_grad, axis=1, keepdims=True)
                scores_grad = (probs * (probs_grad - delta)).astype(BF16)
                outs.append(dot_nn(scores_grad, keys))
                keys_grad[0:keep, :] += dot_tn(scores_grad, query_h)
                values_grad[0:keep, :] += dot_tn(probs.astype(BF16), grad_h)
            queries_grad[rows, :] = jnp.where(first_head, outs[0], outs[1]) * HD ** (-0.5)
        grads = (
            turn(queries_grad[...], tables, back=True),
            turn(keys_grad[...], tables, back=True),
            values_grad[...],
        )
        for k in range(3):
            low = grads[k].astype(BF16)
            result[:, lanes(k)] = low
            own[:, k * two : (k + 1) * two] = low
            column_sum = jnp.sum(low.astype(F32), axis=0, keepdims=True)
            sums[0:1, lanes(k)] = column_sum

        @pl.loop(0, cols)
        def _(j):
            heads_grad = dot_tn(normed[:, parts(j)], own[...]).astype(BF16)
            for p in range(dp):
                heads_from[pair, p, j] = heads_grad[p * part_rows : (p + 1) * part_rows, :]

        heads_rider(pair).start()

    @pl.loop(0, length // BLOCK)
    def _(m):
        rows = pl.ds(pl.multiple_of(m * BLOCK, BLOCK), BLOCK)
        normed_grad[rows, :] = dot_nt(result[rows, :], whole[:, : 3 * wide]).astype(BF16)

    store(2)
    out_rider.finish()
    for pair in range(wide // two):
        heads_rider(pair).finish()
    rider.finish()
    share = arranged.shape[2] // cols
    for k in range(arranged.shape[0]):
        arranged[k] = jnp.concatenate(
            [pieces_to[j, :, k * share : (k + 1) * share] for j in range(cols)], axis=1
        )


def attend_back(cols, heads_in, logs, grad_middle, tables, weight, normed, attn, pieces, share):
    length, wide = attn.shape
    width = normed.shape[1]
    dp, _, part, _ = weight.shape
    pairs = wide // (2 * HD)
    heads = (pairs, dp, cols, part, 6 * HD)
    out = (dp, cols, part, wide)
    hops = max(dp - 1, 1)
    dma = pltpu.SemaphoreType.DMA
    args = (heads_in, logs, grad_middle, tables, weight, normed, attn, pieces)
    return staged_call(
        functools.partial(attend_back_kernel, cols),
        args,
        out_shape=(
            jax.ShapeDtypeStruct(heads, BF16),
            jax.ShapeDtypeStruct(out, BF16),
            jax.ShapeDtypeStruct((length, width), BF16),
            jax.ShapeDtypeStruct((8, 3 * wide), F32),
            jax.ShapeDtypeStruct((3, pieces.shape[1], cols * share), BF16),
        ),
        in_specs=[VM] * 4 + [ANY, VM, VM, ANY],
        out_specs=[ANY] * 2 + [VM] * 3,
        loads=[(i, args[i].shape, None) for i in (2, 6, 0, 1, 3, 5)],
        stores=(2,),
        scratch_shapes=[pltpu.VMEM((length, 2 * HD), F32)] * 3
        + [
            pltpu.VMEM((width, 4 * wide), BF16),
            pltpu.SemaphoreType.DMA(weight.shape[:2]),
            pltpu.VMEM((length, wide), BF16),
            pltpu.VMEM((length, 3 * wide), BF16),
            pltpu.VMEM((length, 6 * HD), BF16),
            pltpu.VMEM(pieces.shape, BF16),
            pltpu.VMEM(heads, BF16),
            pltpu.VMEM(out, BF16),
        ]
        + Exchange.scratch(cols)
        + Exchange.scratch(dp)
        + [dma((pairs, hops)), dma((pairs, hops)), dma((pairs, 1))],
        compiler_params=params(8),
        cost_estimate=cost(50),
        name="attention_back_exchange",
    )


def hidden_back_kernel(
    hidden_from,
    gate_from,
    up_from,
    cotan_from,
    down_from,
    normed_from,
    weight_to,
    grads_to,
    hidden,
    gate_part,
    up_part,
    cotan,
    down,
    normed,
    grads,
    weight_grad,
    down_sem,
    block_sem,
    whole_sem,
    out_sem,
    grad_sem,
):
    group, narrow = hidden.shape
    dp, cols, part_rows, _ = down_from.shape
    wide = weight_grad.shape[3]
    blocks = group // BLOCK
    depth = normed.shape[1] // cols

    def rows_of(m):
        return pl.ds(pl.multiple_of(m * BLOCK, BLOCK), BLOCK)

    def block_copies(m):
        rows = rows_of(m)
        pairs = ((cotan_from, cotan), (gate_from, gate_part), (up_from, up_part))
        return [
            pltpu.make_async_copy(a.at[rows, :], b.at[rows, :], block_sem.at[i, m])
            for i, (a, b) in enumerate(pairs)
        ]

    down_copies = load_columns(down_from, down, down_sem)
    for copy in block_copies(0):
        copy.start()
    for m in range(1, blocks):
        for copy in block_copies(m):
            copy.start()
    whole_copies = [
        pltpu.make_async_copy(hidden_from, hidden, whole_sem.at[0]),
        pltpu.make_async_copy(normed_from, normed, whole_sem.at[1]),
    ]
    for copy in whole_copies:
        copy.start()
    for copy in down_copies:
        copy.wait()

    def grads_out(m):
        rows = rows_of(m)
        return pltpu.make_async_copy(grads.at[rows, :], grads_to.at[rows, :], out_sem.at[m])

    def weight_out(p, j):
        return pltpu.make_async_copy(weight_grad.at[p, j], weight_to.at[p, j], grad_sem.at[p, j])

    @pl.loop(0, blocks)
    def _(m):
        rows = rows_of(m)
        for copy in block_copies(m):
            copy.wait()
        grad = dot_nn(cotan[rows, :], down[:, :narrow])
        both = jnp.concatenate(
            [grad * gate_part[rows, :].astype(F32), grad * up_part[rows, :].astype(F32)], axis=1
        )
        grads[rows, :] = both.astype(BF16)
        grads_out(m).start()

    for copy in whole_copies:
        copy.wait()

    @pl.loop(0, cols)
    def _(j):
        columns = pl.ds(pl.multiple_of(j * depth, depth), depth)
        gate_up_grad = dot_tn(normed[:, columns], grads[...]).astype(BF16)
        down_grad = dot_tn(cotan[:, columns], hidden[...]).astype(BF16)
        for p in range(dp):
            rows = slice(p * part_rows, (p + 1) * part_rows)
            weight_grad[p, j, :, : 2 * narrow] = gate_up_grad[rows, :]
            weight_grad[p, j, :, 2 * narrow : 3 * narrow] = down_grad[rows, :]
            if wide > 3 * narrow:
                weight_grad[p, j, :, 3 * narrow :] = jnp.zeros((part_rows, wide - 3 * narrow), BF16)
            weight_out(p, j).start()

    for m in range(blocks):
        grads_out(m).wait()
    for p in range(dp):
        for j in range(cols):
            weight_out(p, j).wait()


def hidden_back(hidden, gate_part, up_part, cotan, down, normed):
    group, width = normed.shape
    dp, cols, part, _ = down.shape
    double = 2 * hidden.shape[1]
    grad_shape = (dp, cols, part, double + down.shape[3])
    blocks = group // BLOCK
    dma = pltpu.SemaphoreType.DMA
    return pl.pallas_call(
        hidden_back_kernel,
        out_shape=(
            jax.ShapeDtypeStruct(grad_shape, BF16),
            jax.ShapeDtypeStruct((group, double), BF16),
        ),
        in_specs=[ANY] * 6,
        out_specs=(ANY,) * 2,
        scratch_shapes=[
            pltpu.VMEM(hidden.shape, BF16),
            pltpu.VMEM(gate_part.shape, BF16),
            pltpu.VMEM(up_part.shape, BF16),
            pltpu.VMEM(cotan.shape, BF16),
            pltpu.VMEM((width, down.shape[3]), BF16),
            pltpu.VMEM(normed.shape, BF16),
            pltpu.VMEM((group, double), BF16),
            pltpu.VMEM(grad_shape, BF16),
            dma((dp, cols)),
            dma((3, blocks)),
            dma((2,)),
            dma((blocks,)),
            dma((dp, cols)),
        ],
        compiler_params=pltpu.CompilerParams(vmem_limit_bytes=VMEM_LIMIT),
        cost_estimate=cost(30),
        name="hidden_back",
    )(hidden, gate_part, up_part, cotan, down, normed)


def split_kernel(hidden, attention, small, gate_up, down, heads, out, bias, *norms):
    def part(whole, k):
        return whole[:, k].reshape(whole.shape[0] * whole.shape[2], whole.shape[3]).astype(F32)

    for k in range(2):
        gate_up[:, k, :] = part(hidden, k)
    down[...] = part(hidden, 2).T
    for k in range(3):
        heads[k] = part(attention, k)
    out[...] = part(attention, 3).T
    depth, each = norms[0].shape[1], bias.shape[1]
    for i, norm in enumerate(norms):
        norm[...] = small[i : i + 1, :depth]
    for k in range(3):
        bias[k : k + 1, :] = small[0:1, depth + k * each : depth + (k + 1) * each]


def weights_split(hidden, attention, small):
    dp, _, part, _ = hidden.shape
    rows = min(part, 128)
    per = 128 // rows
    depth = dp * part
    tall, wide = hidden.shape[3], attention.shape[3]
    each = (small.shape[1] - depth) // 3

    def whole(shape):
        return pl.BlockSpec(shape, lambda b: (0, 0))

    def source(count, lanes):
        return pl.BlockSpec(
            (per, count, rows, lanes),
            lambda b: (b * 128 // (per * part), 0, lax.rem(b, max(part // 128, 1)), 0),
        )

    return pl.pallas_call(
        split_kernel,
        grid=(depth // 128,),
        out_shape=(
            jax.ShapeDtypeStruct((depth, 2, tall), F32),
            jax.ShapeDtypeStruct((tall, depth), F32),
            jax.ShapeDtypeStruct((3, depth, wide), F32),
            jax.ShapeDtypeStruct((wide, depth), F32),
            jax.ShapeDtypeStruct((3, each), F32),
        )
        + (jax.ShapeDtypeStruct((1, depth), F32),) * 4,
        in_specs=[source(3, tall), source(4, wide), whole(small.shape)],
        out_specs=(
            pl.BlockSpec((128, 2, tall), lambda b: (b, 0, 0)),
            pl.BlockSpec((tall, 128), lambda b: (0, b)),
            pl.BlockSpec((3, 128, wide), lambda b: (0, b, 0)),
            pl.BlockSpec((wide, 128), lambda b: (0, b)),
            whole((3, each)),
        )
        + (whole((1, depth)),) * 4,
        compiler_params=pltpu.CompilerParams(vmem_limit_bytes=VMEM_LIMIT),
        cost_estimate=cost(15),
        name="weight_gradients",
    )(hidden, attention, small)


def weights_whole(piece):
    return lax.all_gather(piece, "dp", axis=0)


def weights_sum(pieces):
    dp, cols, part, wide = pieces.shape
    piece = lax.psum_scatter(
        pieces.reshape(dp * cols * part, wide), "dp", scatter_dimension=0, tiled=True
    )
    return piece.reshape(cols, part, wide)


def make_body(sizes):
    cols = sizes["col"]

    def body(
        tokens,
        attention_norm_gain,
        attention_norm_bias,
        qkv_weight,
        qkv_bias,
        out_weight,
        feedforward_norm_gain,
        feedforward_norm_bias,
        gate_up_weight,
        down_weight,
        cotangent,
    ):
        my_dp = lax.axis_index("dp")
        depth = tokens.shape[1]
        tables = rope_tables(SEQ)
        part = depth // sizes["dp"]

        def share_of(rows):
            return rows if part % 128 == 0 else lax.dynamic_slice_in_dim(rows, my_dp * part, part, 1)

        (
            normed_one,
            tokens_own,
            xhat_one,
            rstd_one,
            vectors,
            gate_up_piece,
            down_piece,
            attention_w,
        ) = start_part(
            tokens,
            [
                values.reshape(1, -1)
                for values in (
                    attention_norm_gain,
                    attention_norm_bias,
                    feedforward_norm_gain,
                    feedforward_norm_bias,
                )
            ],
            qkv_weight.transpose(1, 0, 2),
            share_of(out_weight),
            gate_up_weight,
            share_of(down_weight),
            sizes,
        )
        heads_in, attn, logs, branch_part, gate_up_piece, down_piece = attend(
            cols,
            normed_one,
            attention_w,
            qkv_bias,
            tables,
            gate_up_piece,
            down_piece,
        )
        down_w = weights_whole(down_piece)
        narrow = down_weight.shape[0] // cols
        normed_two, middle, hidden, gate_part, up_part, gate_up_w, cotan_rows = middle_part(
            cols, branch_part, tokens_own, vectors, gate_up_piece, cotangent, sizes["dp"]
        )
        hidden_grad, gate_up_grad = hidden_back(
            hidden, gate_part, up_part, cotan_rows, down_w, normed_two
        )
        hidden_sum = weights_sum(hidden_grad)
        grad_middle, second, mixed_part = norm_two_back(
            cols, gate_up_grad, gate_up_w, middle, cotan_rows, vectors, hidden, down_w
        )
        second = second.reshape(8, cols, depth).transpose(1, 0, 2)
        heads_grad, out_grad, normed_part, bias_part, hidden_sum = attend_back(
            cols,
            heads_in,
            logs,
            grad_middle,
            tables,
            attention_w,
            normed_one,
            attn,
            hidden_sum,
            narrow,
        )
        input_grad, mixed, small, attention_sum, hidden_sum = last_part(
            cols,
            normed_part,
            xhat_one,
            rstd_one,
            attention_norm_gain.reshape(1, -1),
            grad_middle,
            heads_grad,
            out_grad,
            second,
            mixed_part,
            middle,
            hidden_sum,
            bias_part,
        )
        grad_gate_up, grad_down, grad_qkv_weight, grad_out, bias, *norms = weights_split(
            hidden_sum, attention_sum, small
        )
        norms = [norm.reshape(-1) for norm in norms]
        grad_qkv_weight = grad_qkv_weight.transpose(1, 0, 2)
        return (
            mixed,
            input_grad,
            norms[0],
            norms[1],
            grad_qkv_weight,
            bias,
            grad_out,
            norms[2],
            norms[3],
            grad_gate_up,
            grad_down,
        )

    return body


def solution(mesh):
    specs = (
        P(("dp", "row"), "col"),
        P("col"),
        P("col"),
        P("col", None, "row"),
        P(None, ("row", "col")),
        P("row", "col"),
        P("col"),
        P("col"),
        P("col", None, "row"),
        P("row", "col"),
    )
    return jax.shard_map(
        make_body(dict(mesh.shape)),
        mesh=mesh,
        in_specs=specs + (P(("dp", "row"), "col"),),
        out_specs=(P(("dp", "row"), "col"),) + specs,
        check_vma=False,
    )
```
